128 devices in a mesh: dp: 32 (over y, z, core), mp: 4 (over x).
Axes of the slice: x: 4, y: 4, z: 4, core: 2. Of those that a mesh axis runs over, the one named last changes fastest.
Arguments:
- layer_in: bfloat16 [8192, 2048], P('dp'), may hold values from -6 to 6
- cotangent: bfloat16 [8192, 2048], P('dp', 'mp'), may hold values from -6 to 6
- segments: int32 [8192], P('dp'), may hold values from 0 to 7, as said below
- adapters: int32 [8], replicated, may hold values from 0 to 7
- norm_one: float32 [2048], replicated, may hold values from 0.5 to 1.5
- norm_two: float32 [2048], replicated, may hold values from 0.5 to 1.5
- out_gain: float32 [128], replicated, may hold values from 0.5 to 1.5
- beta_bias: float32 [16], P('mp'), may hold values from -7.5 to 0
- conv_taps: bfloat16 [4, 3, 2048], P(None, None, 'mp'), may hold values from -3 to 3
- w_qkv: bfloat16 [2048, 3, 2048], P('dp', None, 'mp'), may hold values from -0.125 to 0.125
- w_beta: bfloat16 [2048, 16], P('dp', 'mp'), may hold values from -0.125 to 0.125
- w_out: bfloat16 [2048, 2048], P('mp', 'dp'), may hold values from -0.125 to 0.125
- w_gate_up: bfloat16 [2048, 2, 5632], P('dp', None, 'mp'), may hold values from -0.125 to 0.125
- w_down: bfloat16 [5632, 2048], P('mp', 'dp'), may hold values from -0.078125 to 0.078125
- a_in: bfloat16 [2048, 6, 128], P(('dp', 'mp')), may hold values from -0.125 to 0.125
- b_heads: bfloat16 [3, 128, 2048], P(None, 'dp', 'mp'), may hold values from -0.75 to 0.75
- b_beta: bfloat16 [128, 16], P('dp', 'mp'), may hold values from -0.75 to 0.75
- a_out: bfloat16 [2048, 128], P('mp', 'dp'), may hold values from -0.125 to 0.125
- b_ffn: bfloat16 [2, 128, 5632], P(None, 'dp', 'mp'), may hold values from -0.75 to 0.75
- a_down: bfloat16 [5632, 128], P('mp', 'dp'), may hold values from -0.078125 to 0.078125
- b_res: bfloat16 [2, 128, 2048], P(None, None, ('dp', 'mp')), may hold values from -0.75 to 0.75
Outputs:
- output: bfloat16 [8192, 2048], P('dp', 'mp')
- grad_input: float32 [8192, 2048], P('dp', 'mp')
- grad_a_in: float32 [2048, 6, 128], P(('dp', 'mp'))
- grad_b_heads: float32 [3, 128, 2048], P(None, 'dp', 'mp')
- grad_b_beta: float32 [128, 16], P('dp', 'mp')
- grad_a_out: float32 [2048, 128], P('mp', 'dp')
- grad_b_ffn: float32 [2, 128, 5632], P(None, 'dp', 'mp')
- grad_a_down: float32 [5632, 128], P('mp', 'dp')
- grad_b_res: float32 [2, 128, 2048], P(None, None, ('dp', 'mp'))
The draws below stay inside these ranges and needn't reach their ends.
Inputs may be any that keep to these rules, and one draw needn't show every extreme that they name: `segments`: document numbers start at 0, never fall, and rise by one at every multiple of 8192 tokens and at 7 further places inside each packed sequence, never at the first token of an index of dp and one of them within the first 256 tokens of the sequence; a packed sequence spans 32 indices of dp.
All inputs are finite; a program needn't handle non-finite values.
Results may differ from the reference program's by a relative error of at most 0.03.
Values may be sent and summed in bfloat16 or wider, within the bound.
A program may use at most 256 MiB of HBM per device.

```python
from functools import partial
import jax
import jax.numpy as jnp
from jax import lax

H = 16
DH = 128
D = 2048
FF = 5632
KW = 4
BLOCK = 64
RANK = 16
NADAPT = 8
NR = 128
DOCS_SEQ = 8
TOK_DEV = 256
SEQ_LEN = 8192
TOKENS = 8192
SEGS = 8


def draw_segments(key, part):
    key = jax.random.fold_in(key, 5)
    first_key, rest_key = jax.random.split(key)
    seq_count = TOKENS // SEQ_LEN
    places = jnp.arange(SEQ_LEN, dtype=jnp.int32)
    allowed = places % TOK_DEV != 0
    head_zone = allowed & (places < TOK_DEV)
    first_scores = jax.random.randint(first_key, (seq_count, SEQ_LEN), 0, 65536) * SEQ_LEN + places[None, :]
    first_scores = jnp.where(head_zone[None, :], first_scores, 1 << 30)
    first_cut = jnp.argsort(first_scores, axis=1, stable=True)[:, :1].astype(jnp.int32)
    rest_scores = jax.random.randint(rest_key, (seq_count, SEQ_LEN), 0, 65536) * SEQ_LEN + places[None, :]
    rest_scores = jnp.where(allowed[None, :] & (places[None, :] != first_cut), rest_scores, 1 << 30)
    rest_cuts = jnp.argsort(rest_scores, axis=1, stable=True)[:, :DOCS_SEQ - 2].astype(jnp.int32)
    chosen = jnp.concatenate([first_cut, rest_cuts], axis=1)
    rows = jnp.arange(seq_count, dtype=jnp.int32)[:, None]
    marks = jnp.zeros((seq_count, SEQ_LEN), jnp.int32).at[rows, chosen].set(1)
    marks = marks.at[:, 0].set(1).reshape(TOKENS)
    marks = marks.at[0].set(0)
    return jnp.cumsum(marks).astype(jnp.int32)


def draw_beta_bias(key, part):
    key = jax.random.fold_in(key, 11)
    pick_key, fast_key, slow_key = jax.random.split(key, 3)
    fast_heads = jax.random.uniform(pick_key, (H,), jnp.float32) < 0.5
    slow_values = jax.random.uniform(slow_key, (H,), jnp.float32, -7.0, -5.5)
    fast_values = jax.random.uniform(fast_key, (H,), jnp.float32, -2.0, 0.0)
    return jnp.where(fast_heads, fast_values, slow_values).astype(jnp.float32)


def set_ends(values, own_key, smallest, largest):
    longest = values.shape.index(max(values.shape))
    spots = []
    for shift in (0, 1):
        where = [jax.random.randint(jax.random.fold_in(own_key, axis), (), 0, length) for axis, length in enumerate(values.shape)]
        where[longest] = (where[longest] + shift) % values.shape[longest]
        spots.append(tuple(where))
    return values.at[spots[0]].set(smallest).at[spots[1]].set(largest)


def block_scale(key, shape, pieces, least, largest):
    loudness = 1.0
    for dim, shards_of in pieces:
        heights = jax.random.uniform(jax.random.fold_in(jax.random.fold_in(key, 6), dim), (shards_of,), jnp.float32, least / len(pieces), largest / len(pieces))
        loudness = loudness * jnp.repeat(jnp.exp(heights), shape[dim] // shards_of).reshape((-1,) + (1,) * (len(shape) - 1 - dim))
    return loudness


def centred(stream_key, extent, scale, most, pieces=(), held_as=jnp.bfloat16):
    factor_of = block_scale(stream_key, extent, pieces, -0.22, 0.18) if pieces else 1.0
    values = jax.random.normal(stream_key, extent, jnp.float32) * scale * factor_of
    return jnp.minimum(jnp.maximum(values, -most), most).astype(held_as)


def setup_inputs(seed: int = 0) -> dict:
    splits = jax.random.split(jax.random.key(seed), 22)
    return {
        "layer_in": centred(splits[0], (TOKENS, D), 1.0, 6.0, ((0, 32),)),
        "cotangent": centred(splits[1], (TOKENS, D), 1.0, 6.0, ((0, 32), (1, 4))),
        "segments": draw_segments(jax.random.fold_in(splits[21], 71), 0),
        "adapters": set_ends(jax.random.randint(splits[3], (SEGS,), 0, NADAPT), jax.random.fold_in(splits[3], 1), 0, NADAPT - 1).astype(jnp.int32),
        "norm_one": jnp.clip(1.0 + 0.1 * jax.random.normal(splits[4], (D,), jnp.float32), 0.5, 1.5),
        "norm_two": jnp.clip(1.0 + 0.1 * jax.random.normal(splits[5], (D,), jnp.float32), 0.5, 1.5),
        "out_gain": jnp.clip(1.0 + 0.1 * jax.random.normal(splits[6], (DH,), jnp.float32), 0.5, 1.5),
        "beta_bias": draw_beta_bias(jax.random.fold_in(splits[21], 71), 0),
        "conv_taps": centred(splits[8], (KW, 3, D), KW ** -0.5, 3.0, ((2, 4),)),
        "w_qkv": centred(splits[9], (D, 3, D), D ** -0.5, 0.125, ((0, 32), (2, 4))),
        "w_beta": centred(splits[10], (D, H), D ** -0.5, 0.125, ((0, 32), (1, 4))),
        "w_out": centred(splits[11], (D, D), D ** -0.5, 0.125, ((0, 4), (1, 32))),
        "w_gate_up": centred(splits[12], (D, 2, FF), D ** -0.5, 0.125, ((0, 32), (2, 4))),
        "w_down": centred(splits[13], (FF, D), FF ** -0.5, 0.078125, ((0, 4), (1, 32))),
        "a_in": centred(splits[14], (D, 6, NR), D ** -0.5, 0.125, ((0, 128),)),
        "b_heads": centred(splits[15], (3, NR, D), (4 * RANK) ** -0.5, 0.75, ((1, 32), (2, 4))),
        "b_beta": centred(splits[16], (NR, H), (4 * RANK) ** -0.5, 0.75, ((0, 32), (1, 4))),
        "a_out": centred(splits[17], (D, NR), D ** -0.5, 0.125, ((0, 4), (1, 32))),
        "b_ffn": centred(splits[18], (2, NR, FF), (4 * RANK) ** -0.5, 0.75, ((1, 32), (2, 4))),
        "a_down": centred(splits[19], (FF, NR), FF ** -0.5, 0.078125, ((0, 4), (1, 32))),
        "b_res": centred(splits[20], (2, NR, D), (4 * RANK) ** -0.5, 0.75, ((2, 128),)),
    }


EXACT_PRECISION = lax.Precision.HIGHEST
EPSILON = 1e-06

@jax.custom_vjp
def low(v):
    return lax.optimization_barrier(v.astype(jnp.bfloat16)).astype(jnp.float32)

@jax.custom_vjp
def low_back(v):
    return v

def low_keep(v):
    return (low(v), None)

def low_pass(kept, grad):
    return (grad,)

def back_keep(v):
    return (v, None)

def back_low(kept, grad):
    return (low(grad),)
low.defvjp(low_keep, low_pass)
low_back.defvjp(back_keep, back_low)

def inverse_rms(values):
    return lax.rsqrt(lax.optimization_barrier(jnp.mean(values * values, axis=-1, keepdims=True)) + EPSILON)

def unit_rows(values):
    return values * lax.rsqrt(lax.optimization_barrier(jnp.sum(values * values, axis=-1, keepdims=True)) + EPSILON)

def product(left, right):
    return jnp.dot(left, right, precision=EXACT_PRECISION)

def delta_rule(queries, key_rows, value_rows, strength, resets):

    def token_step(running_memory_state, current):
        current_query_rows, current_key_rows, v_now, b_now, s_now = current
        running_memory_state = running_memory_state * (1.0 - s_now)
        retrieved_value_rows = jnp.einsum('oqf,oq->of', running_memory_state, current_key_rows, precision=EXACT_PRECISION)
        written_value_rows = b_now[:, None] * (v_now - retrieved_value_rows)
        running_memory_state = running_memory_state + current_key_rows[:, :, None] * written_value_rows[:, None, :]
        return (running_memory_state, jnp.einsum('oqf,oq->of', running_memory_state, current_query_rows, precision=EXACT_PRECISION))

    def block_step(running_memory_state, block_inputs):
        return lax.scan(token_step, running_memory_state, block_inputs)
    block_count = TOKENS // BLOCK
    blocks = tuple((member.reshape((block_count, BLOCK) + member.shape[1:]) for member in (queries, key_rows, value_rows, strength, resets)))
    _, result = lax.scan(jax.checkpoint(block_step), jnp.zeros((H, DH, DH), jnp.float32), blocks)
    return result.reshape(TOKENS, H, DH)

def block_forward(frozen, adapter_picks, same_masks, resets, layer_in, a_in, b_heads, b_beta, a_out, b_ffn, a_down, b_res):
    norm_one, norm_two, out_gain, beta_bias, conv_taps, w_qkv, w_beta, w_out, w_gate_up, w_down = frozen
    scale_one = inverse_rms(layer_in)
    xn_one = low(layer_in * scale_one * norm_one)
    u_one = low(jnp.einsum('td,djr->tjr', xn_one, a_in[:, :4], precision=EXACT_PRECISION) * adapter_picks[:, None, :])
    projected = jnp.einsum('td,djc->tjc', xn_one, w_qkv, precision=EXACT_PRECISION) + jnp.einsum('tjr,jrc->tjc', u_one[:, :3], b_heads, precision=EXACT_PRECISION)
    pre_conv = low_back(low(projected))
    strength = jax.nn.sigmoid(product(xn_one, w_beta) + product(u_one[:, 3], b_beta) + beta_bias)
    summed = jnp.zeros_like(pre_conv)
    for tap_index in range(KW):
        shifted = jnp.pad(pre_conv, ((tap_index, 0), (0, 0), (0, 0)))[:TOKENS]
        summed = summed + conv_taps[tap_index] * shifted * same_masks[tap_index][:, None, None]
    activated = jax.nn.silu(summed)
    queries = unit_rows(activated[:, 0].reshape(TOKENS, H, DH))
    key_rows = unit_rows(activated[:, 1].reshape(TOKENS, H, DH))
    value_rows = activated[:, 2].reshape(TOKENS, H, DH)
    mixer_output_rows = delta_rule(queries, key_rows, value_rows, strength, resets)
    normed = low((mixer_output_rows * inverse_rms(mixer_output_rows) * out_gain).reshape(TOKENS, D))
    u_out = product(normed, a_out) * adapter_picks
    branch = low_back(product(normed, w_out) + product(u_out, b_res[0]))
    hidden_one = layer_in + branch
    xn_two = low(hidden_one * inverse_rms(hidden_one) * norm_two)
    u_two = low(jnp.einsum('td,djr->tjr', xn_two, a_in[:, 4:], precision=EXACT_PRECISION) * adapter_picks[:, None, :])
    gate_up = low_back(jnp.einsum('td,djf->tjf', xn_two, w_gate_up, precision=EXACT_PRECISION) + jnp.einsum('tjr,jrf->tjf', u_two, b_ffn, precision=EXACT_PRECISION))
    hidden = low(jax.nn.silu(gate_up[:, 0]) * gate_up[:, 1])
    u_down = product(hidden, a_down) * adapter_picks
    return hidden_one + product(hidden, w_down) + product(u_down, b_res[1])

def reference(layer_in, cotangent, segments, adapters, norm_one, norm_two, out_gain, beta_bias, conv_taps, w_qkv, w_beta, w_out, w_gate_up, w_down, a_in, b_heads, b_beta, a_out, b_ffn, a_down, b_res):
    per_token = adapters[segments]
    owner_ids = jnp.arange(NADAPT * RANK, dtype=jnp.int32) // RANK
    adapter_picks = (per_token[:, None] == owner_ids[None, :]).astype(jnp.float32)
    same_masks = []
    for tap_index in range(KW):
        earlier = jnp.pad(segments, (tap_index, 0), constant_values=-1)[:TOKENS]
        same_masks.append((earlier == segments).astype(jnp.float32))
    resets = 1.0 - same_masks[1]
    frozen = (norm_one, norm_two, out_gain, beta_bias) + tuple((member.astype(jnp.float32) for member in (conv_taps, w_qkv, w_beta, w_out, w_gate_up, w_down)))
    trained = tuple((member.astype(jnp.float32) for member in (layer_in, a_in, b_heads, b_beta, a_out, b_ffn, a_down, b_res)))
    result, pullback = jax.vjp(partial(block_forward, frozen, adapter_picks, same_masks, resets), *trained)
    gradients = pullback(cotangent.astype(jnp.float32))
    return (result.astype(jnp.bfloat16), gradients[0], gradients[1], gradients[2], gradients[3], gradients[4], gradients[5], gradients[6], gradients[7])
```

```python
import functools

import jax
import jax.numpy as jnp
from jax import lax
from jax.experimental import pallas as pl
from jax.experimental.pallas import tpu as pltpu
from jax.sharding import PartitionSpec as P

DH = 128
KW = 4
RANK = 16
HALO = 16
EPSILON = 1e-06
WIDE = jnp.float32
NARROW = jnp.bfloat16
MESH = pl.DeviceIdType.MESH
EXACT = lax.Precision.HIGHEST


def coords():
    place = lax.axis_index("dp")
    return place // 8, lax.rem(place // 2, 4), lax.rem(place, 2)


def place_of(y, z, c):
    return (y * 4 + z) * 2 + c


def moved(dy, dz, other_core=False):
    y, z, c = coords()
    return place_of(lax.rem(y + dy + 4, 4), lax.rem(z + dz + 4, 4), 1 - c if other_core else c)


def greet(dp_peers=(), mp_peers=()):
    barrier = pltpu.get_barrier_semaphore()
    for peer in dp_peers:
        pl.semaphore_signal(barrier, inc=1, device_id={"dp": peer}, device_id_type=MESH)
    for peer in mp_peers:
        pl.semaphore_signal(barrier, inc=1, device_id={"mp": peer}, device_id_type=MESH)
    pl.semaphore_wait(barrier, len(dp_peers) + len(mp_peers))


class Mailbox:
    def __init__(self, send, recv):
        self.send, self.recv, self.copies = send, recv, []

    def push(self, src, dst, **device):
        k = len(self.copies)
        copy = pltpu.make_async_remote_copy(
            src_ref=src,
            dst_ref=dst,
            send_sem=self.send.at[k],
            recv_sem=self.recv.at[k],
            device_id=device,
            device_id_type=MESH,
        )
        copy.start()
        self.copies.append(copy)
        return copy

    def drain(self):
        for copy in self.copies:
            copy.wait_send()


def gather_steps(box, own, out):
    me = moved(0, 0)
    half = own.shape[0] // 2
    quarter = half // 2
    sibling = moved(0, 0, True)
    kinds = []
    for kind in range(2):
        base = kind * half
        parts = (pl.ds(base, half), pl.ds(base, quarter), pl.ds(base + quarter, quarter))
        if kind == 0:
            kinds.append((parts, lambda a, b: moved(a, b)))
        else:
            kinds.append((parts, lambda a, b: moved(b, a)))
    near, across, far, far_across, shared = [], [{}, {}], [[], []], [{}, {}], []

    def open_up():
        for parts, at in kinds:
            near.append([box.push(own.at[parts[0]], out.at[me, parts[0]], dp=at(s, 0)) for s in (1, -1)])
        for k, (parts, at) in enumerate(kinds):
            across[k][0] = [box.push(own.at[parts[0]], out.at[me, parts[0]], dp=at(0, s)) for s in (1, -1)]
        shared.append(box.push(own, out.at[me], dp=sibling))

    def pass_on(k, slot):
        parts, at = kinds[k]
        block = out.at[slot, parts[0]]
        return [box.push(block, block, dp=at(0, t)) for t in (1, -1)]

    def to_sibling(k, slot):
        block = out.at[slot, kinds[k][0][0]]
        shared.append(box.push(block, block, dp=sibling))

    def from_near(i, s):
        def step():
            for k, (parts, at) in enumerate(kinds):
                near[k][i].wait_recv()
                block = out.at[at(s, 0), parts[1 + i]]
                far[k].append(box.push(block, block, dp=at(-s, 0)))
            for k, (parts, at) in enumerate(kinds):
                across[k][s] = pass_on(k, at(s, 0))
                to_sibling(k, at(s, 0))

        return step

    def from_far(k):
        def step():
            for copy in far[k]:
                copy.wait_recv()
            slot = kinds[k][1](2, 0)
            across[k][2] = pass_on(k, slot)
            to_sibling(k, slot)

        return step

    def from_across(k, f):
        def step():
            parts, at = kinds[k]
            far_across[k][f] = []
            for i, s in enumerate((-1, 1)):
                across[k][f][i].wait_recv()
                slot = at(f, s)
                block = out.at[slot, parts[1 + i]]
                far_across[k][f].append(box.push(block, block, dp=at(0, -s)))
                to_sibling(k, slot)

        return step

    def from_far_across(k, f):
        def step():
            for copy in far_across[k][f]:
                copy.wait_recv()
            to_sibling(k, kinds[k][1](f, 2))

        return step

    def close():
        for copy in shared:
            copy.wait_recv()

    steps = [open_up, from_near(0, -1), from_near(1, 1), from_far(0), from_far(1)]
    steps += [from_across(k, f) for f in (0, -1, 1, 2) for k in range(2)]
    steps += [from_far_across(k, f) for f in (0, -1, 1, 2) for k in range(2)]
    return steps + [close]


def gather_peers():
    return [moved(1, 0), moved(-1, 0), moved(0, 1), moved(0, -1), moved(0, 0, True)]


GATHER_COPIES = 71


def first_gather_kernel(wide_ref, thin_ref, wide_out, thin_out, thin_own, send, recv, local):
    m = lax.axis_index("mp")
    mp_peers = [lax.rem(m + k, 4) for k in (1, 2, 3)]
    greet(gather_peers(), mp_peers)
    me = moved(0, 0)
    box = Mailbox(send, recv)
    rows = thin_ref.shape[0]
    mine = pl.ds(pl.multiple_of(m * rows, rows), rows)
    crossing = [box.push(thin_ref, thin_own.at[mine], mp=peer) for peer in mp_peers]
    keep_wide = pltpu.make_async_copy(wide_ref, wide_out.at[me], local.at[0])
    keep_wide.start()
    keep_thin = pltpu.make_async_copy(thin_ref, thin_own.at[mine], local.at[1])
    keep_thin.start()
    wide_steps = gather_steps(box, wide_ref, wide_out)
    thin_steps = gather_steps(box, thin_own, thin_out)
    wide_steps[0]()
    keep_thin.wait()
    for copy in crossing:
        copy.wait_recv()
    keep_thin_out = pltpu.make_async_copy(thin_own, thin_out.at[me], local.at[2])
    keep_thin_out.start()
    thin_steps[0]()
    for one, two in zip(wide_steps[1:], thin_steps[1:]):
        one()
        two()
    keep_wide.wait()
    keep_thin_out.wait()
    box.drain()


def first_gather(wide, thin):
    count = 2 * GATHER_COPIES + 3
    rows, cols = thin.shape
    anywhere = pl.BlockSpec(memory_space=pl.ANY)
    return pl.pallas_call(
        first_gather_kernel,
        out_shape=(
            jax.ShapeDtypeStruct((32,) + wide.shape, wide.dtype),
            jax.ShapeDtypeStruct((32, 4 * rows, cols), thin.dtype),
        ),
        in_specs=[anywhere, anywhere],
        out_specs=(anywhere, anywhere),
        scratch_shapes=[
            pltpu.VMEM((4 * rows, cols), thin.dtype),
            pltpu.SemaphoreType.DMA((count,)),
            pltpu.SemaphoreType.DMA((count,)),
            pltpu.SemaphoreType.DMA((3,)),
        ],
        compiler_params=pltpu.CompilerParams(collective_id=0, has_side_effects=True),
        name="gather_first",
    )(wide, thin)


def second_gather_kernel(wide_ref, wide_out, send, recv, local):
    greet(gather_peers())
    box = Mailbox(send, recv)
    keep = pltpu.make_async_copy(wide_ref, wide_out.at[moved(0, 0)], local)
    keep.start()
    for step in gather_steps(box, wide_ref, wide_out):
        step()
    keep.wait()
    box.drain()


def second_gather(wide):
    anywhere = pl.BlockSpec(memory_space=pl.ANY)
    return pl.pallas_call(
        second_gather_kernel,
        out_shape=jax.ShapeDtypeStruct((32,) + wide.shape, wide.dtype),
        in_specs=[anywhere],
        out_specs=anywhere,
        scratch_shapes=[
            pltpu.SemaphoreType.DMA((GATHER_COPIES,)),
            pltpu.SemaphoreType.DMA((GATHER_COPIES,)),
            pltpu.SemaphoreType.DMA,
        ],
        compiler_params=pltpu.CompilerParams(collective_id=1, has_side_effects=True),
        name="gather_second",
    )(wide)


def sum_kernel(n_extra, x_ref, *refs):
    if n_extra:
        e_ref, out_ref, e_out, landed, e_landed, send, recv = refs
    else:
        out_ref, landed, send, recv = refs
    m = lax.axis_index("mp")
    rows = x_ref.shape[0] // 2
    width = x_ref.shape[1] // 4
    peers = {k: lax.rem(m + k, 4) for k in (1, 2, 3)}
    greet((), list(peers.values()))
    box = Mailbox(send, recv)

    def columns(i, w):
        return pl.ds(pl.multiple_of(i * w, w), w)

    arriving = []
    for part in range(2):
        r = pl.ds(part * rows, rows)
        arriving.append(
            [
                box.push(x_ref.at[r, columns(peers[k], width)], landed.at[k - 1, r], mp=peers[k])
                for k in (2, 1, 3)
            ]
        )
    if n_extra:
        extra = [
            box.push(e_ref.at[:, columns(peers[k], n_extra)], e_landed.at[k - 1], mp=peers[k])
            for k in (2, 1, 3)
        ]
    gathered = []
    for part in range(2):
        r = pl.ds(part * rows, rows)
        for copy in arriving[part]:
            copy.wait_recv()
        total = x_ref[r, columns(m, width)].astype(WIDE)
        for k in range(3):
            total = total + landed[k, r].astype(WIDE)
        out_ref[r, columns(m, width)] = total.astype(out_ref.dtype)
        block = out_ref.at[r, columns(m, width)]
        gathered += [box.push(block, block, mp=peers[k]) for k in (2, 1, 3)]
    if n_extra:
        for copy in extra:
            copy.wait_recv()
        total = e_ref[:, columns(m, n_extra)].astype(WIDE)
        for k in range(3):
            total = total + e_landed[k].astype(WIDE)
        e_out[...] = total
    for copy in gathered:
        copy.wait_recv()
    box.drain()


def sum_over_mp(x, extra=None, collective_id=0):
    rows, cols = x.shape
    vmem = pl.BlockSpec(memory_space=pltpu.VMEM)
    n_extra = 0 if extra is None else extra.shape[1] // 4
    out_shape = [jax.ShapeDtypeStruct(x.shape, x.dtype)]
    scratch = [pltpu.VMEM((3, rows, cols // 4), x.dtype)]
    count = 12
    if n_extra:
        out_shape.append(jax.ShapeDtypeStruct((rows, n_extra), WIDE))
        scratch.append(pltpu.VMEM((3, rows, n_extra), extra.dtype))
        count += 3
    return pl.pallas_call(
        functools.partial(sum_kernel, n_extra),
        out_shape=tuple(out_shape),
        in_specs=[vmem] * len(out_shape),
        out_specs=tuple([vmem] * len(out_shape)),
        scratch_shapes=scratch
        + [pltpu.SemaphoreType.DMA((count,)), pltpu.SemaphoreType.DMA((count,))],
        compiler_params=pltpu.CompilerParams(
            collective_id=collective_id, has_side_effects=True, vmem_limit_bytes=32 << 20
        ),
        name="sum_over_mp",
    )(*([x] if extra is None else [x, extra]))


def half_dot(left, right, dims=(((1,), (0,)), ((), ()))):
    high = right.astype(NARROW)
    low = (right - high.astype(WIDE)).astype(NARROW)
    return lax.dot_general(left, high, dims, preferred_element_type=WIDE) + lax.dot_general(
        left, low, dims, preferred_element_type=WIDE
    )


TURNED = (((0,), (0,)), ((), ()))


def chain_forward_kernel(
    a_ref, b_ref, state_out, sib_a, chip_a, row_a, sib_b, chip_b, row_b, states, send, recv
):
    y, z, c = coords()
    sibling = moved(0, 0, True)
    z_peers = {k: moved(0, k) for k in (1, 2, 3)}
    y_peers = {k: moved(k, 0) for k in (1, 2, 3)}
    greet([sibling] + list(z_peers.values()) + list(y_peers.values()))
    box = Mailbox(send, recv)
    mine = pl.ds(pl.multiple_of(2 * c, 2), 2)
    theirs = pl.ds(pl.multiple_of(2 * (1 - c), 2), 2)
    pair = [box.push(a_ref.at[theirs], sib_a, dp=sibling), box.push(b_ref.at[theirs], sib_b, dp=sibling)]
    for copy in pair:
        copy.wait_recv()
    first = c == 0
    lower_b = []
    for h in range(2):
        own_a, own_b = a_ref[2 * c + h], b_ref[2 * c + h]
        a_low, a_high = jnp.where(first, own_a, sib_a[h]), jnp.where(first, sib_a[h], own_a)
        b_low, b_high = jnp.where(first, own_b, sib_b[h]), jnp.where(first, sib_b[h], own_b)
        lower_b.append((a_low, b_low))
        chip_a[z, h] = lax.dot(a_high, a_low, preferred_element_type=WIDE).astype(NARROW)
        chip_b[z, h] = (
            lax.dot(a_high, b_low, preferred_element_type=WIDE) + b_high.astype(WIDE)
        ).astype(NARROW)
    ring = []
    for k in (2, 1, 3):
        ring.append(box.push(chip_a.at[z], chip_a.at[z], dp=z_peers[k]))
        ring.append(box.push(chip_b.at[z], chip_b.at[z], dp=z_peers[k]))
    for copy in ring:
        copy.wait_recv()
    for h in range(2):
        total_a, total_b = chip_a[0, h].astype(WIDE), chip_b[0, h].astype(WIDE)
        for i in range(1, 4):
            total_a = half_dot(chip_a[i, h], total_a)
            total_b = half_dot(chip_a[i, h], total_b) + chip_b[i, h].astype(WIDE)
        row_a[y, h] = total_a.astype(NARROW)
        row_b[y, h] = total_b.astype(NARROW)
    column = []
    for k in (2, 1, 3):
        column.append(box.push(row_a.at[y], row_a.at[y], dp=y_peers[k]))
        column.append(box.push(row_b.at[y], row_b.at[y], dp=y_peers[k]))
    for copy in column:
        copy.wait_recv()
    for h in range(2):
        state = jnp.zeros((DH, DH), WIDE)
        for i in range(3):
            longer = half_dot(row_a[i, h], state) + row_b[i, h].astype(WIDE)
            state = jnp.where(i < y, longer, state)
        for i in range(3):
            longer = half_dot(chip_a[i, h], state) + chip_b[i, h].astype(WIDE)
            state = jnp.where(i < z, longer, state)
        a_low, b_low = lower_b[h]
        middle = half_dot(a_low, state) + b_low.astype(WIDE)
        state_out[2 * c + h] = jnp.where(first, state, middle)
        states[h] = jnp.where(first, middle, state)
    back = box.push(states, state_out.at[mine], dp=sibling)
    back.wait_recv()
    box.drain()


def chain_forward(maps, offsets):
    vmem = pl.BlockSpec(memory_space=pltpu.VMEM)
    heads = maps.shape[0]
    two = (2, DH, DH)
    count = 2 + 6 + 6 + 1
    return pl.pallas_call(
        chain_forward_kernel,
        out_shape=(
            jax.ShapeDtypeStruct((heads, DH, DH), WIDE),
            jax.ShapeDtypeStruct(two, NARROW),
            jax.ShapeDtypeStruct((4,) + two, NARROW),
            jax.ShapeDtypeStruct((4,) + two, NARROW),
        ),
        in_specs=[vmem] * 2,
        out_specs=(vmem,) * 4,
        scratch_shapes=[
            pltpu.VMEM(two, NARROW),
            pltpu.VMEM((4,) + two, NARROW),
            pltpu.VMEM((4,) + two, NARROW),
            pltpu.VMEM(two, WIDE),
            pltpu.SemaphoreType.DMA((count,)),
            pltpu.SemaphoreType.DMA((count,)),
        ],
        compiler_params=pltpu.CompilerParams(
            collective_id=4, has_side_effects=True, vmem_limit_bytes=32 << 20
        ),
        name="chain_forward",
    )(maps, offsets)


def chain_backward_kernel(
    a_ref, sib_a, chip_a, row_a, g_ref, grad_out, sib_g, chip_g, row_g, grads, send, recv
):
    y, z, c = coords()
    sibling = moved(0, 0, True)
    z_peers = {k: moved(0, k) for k in (1, 2, 3)}
    y_peers = {k: moved(k, 0) for k in (1, 2, 3)}
    greet([sibling] + list(z_peers.values()) + list(y_peers.values()))
    box = Mailbox(send, recv)
    mine = pl.ds(pl.multiple_of(2 * c, 2), 2)
    theirs = pl.ds(pl.multiple_of(2 * (1 - c), 2), 2)
    box.push(g_ref.at[theirs], sib_g, dp=sibling).wait_recv()
    first = c == 0
    upper = []
    for h in range(2):
        own_a, own_g = a_ref[2 * c + h], g_ref[2 * c + h]
        a_low, a_high = jnp.where(first, own_a, sib_a[h]), jnp.where(first, sib_a[h], own_a)
        g_low, g_high = jnp.where(first, own_g, sib_g[h]), jnp.where(first, sib_g[h], own_g)
        upper.append((a_high, g_high))
        chip_g[z, h] = (
            lax.dot_general(a_low, g_high, TURNED, preferred_element_type=WIDE) + g_low.astype(WIDE)
        ).astype(NARROW)
    ring = [box.push(chip_g.at[z], chip_g.at[z], dp=z_peers[k]) for k in (2, 1, 3)]
    for copy in ring:
        copy.wait_recv()
    for h in range(2):
        total = chip_g[3, h].astype(WIDE)
        for i in (2, 1, 0):
            total = half_dot(chip_a[i, h], total, TURNED) + chip_g[i, h].astype(WIDE)
        row_g[y, h] = total.astype(NARROW)
    column = [box.push(row_g.at[y], row_g.at[y], dp=y_peers[k]) for k in (2, 1, 3)]
    for copy in column:
        copy.wait_recv()
    for h in range(2):
        grad = jnp.zeros((DH, DH), WIDE)
        for i in (3, 2, 1):
            longer = half_dot(row_a[i, h], grad, TURNED) + row_g[i, h].astype(WIDE)
            grad = jnp.where(i > y, longer, grad)
        for i in (3, 2, 1):
            longer = half_dot(chip_a[i, h], grad, TURNED) + chip_g[i, h].astype(WIDE)
            grad = jnp.where(i > z, longer, grad)
        a_high, g_high = upper[h]
        middle = half_dot(a_high, grad, TURNED) + g_high.astype(WIDE)
        grad_out[2 * c + h] = jnp.where(first, middle, grad)
        grads[h] = jnp.where(first, grad, middle)
    box.push(grads, grad_out.at[mine], dp=sibling).wait_recv()
    box.drain()


def chain_backward(maps, kept, offsets):
    vmem = pl.BlockSpec(memory_space=pltpu.VMEM)
    heads = maps.shape[0]
    two = (2, DH, DH)
    count = 1 + 3 + 3 + 1
    return pl.pallas_call(
        chain_backward_kernel,
        out_shape=jax.ShapeDtypeStruct((heads, DH, DH), WIDE),
        in_specs=[vmem] * 5,
        out_specs=vmem,
        scratch_shapes=[
            pltpu.VMEM(two, NARROW),
            pltpu.VMEM((4,) + two, NARROW),
            pltpu.VMEM((4,) + two, NARROW),
            pltpu.VMEM(two, WIDE),
            pltpu.SemaphoreType.DMA((count,)),
            pltpu.SemaphoreType.DMA((count,)),
        ],
        compiler_params=pltpu.CompilerParams(
            collective_id=5, has_side_effects=True, vmem_limit_bytes=32 << 20
        ),
        name="chain_backward",
    )(maps, *kept, offsets)


def wide_dot(left, right, left_dim=1, right_dim=0):
    return lax.dot_general(
        left,
        right,
        (((left_dim,), (right_dim,)), ((), ())),
        precision=EXACT,
        preferred_element_type=WIDE,
    )


def column_of(aux, index):
    lanes = lax.broadcasted_iota(jnp.int32, aux.shape, 1)
    return jnp.sum(jnp.where(lanes == index, aux, 0.0), axis=1, keepdims=True)


def convolve(pre_ref, taps_ref, part, aux, work):
    count = aux.shape[0]
    work[...] = pre_ref[...].astype(WIDE)
    total = work[pl.ds(HALO, count)] * taps_ref[part : part + 1, :]
    for j in range(1, KW):
        total = total + (
            work[pl.ds(HALO - j, count)] * aux[:, j : j + 1] * taps_ref[3 * j + part : 3 * j + part + 1, :]
        )
    return total


def masks(aux, seg_row):
    same = aux[:, 6:7] == seg_row
    shape = (aux.shape[0], aux.shape[0])
    row = lax.broadcasted_iota(jnp.int32, shape, 0)
    col = lax.broadcasted_iota(jnp.int32, shape, 1)
    return row, col, same


def lower_inverse(lower, row, col):
    near = jnp.where(row // 8 == col // 8, lower, 0.0)
    square = wide_dot(near, near)
    inverse = jnp.where(row == col, 1.0, 0.0) - near
    inverse = inverse + wide_dot(inverse, square)
    inverse = inverse + wide_dot(inverse, wide_dot(square, square))
    size = 8
    while size < lower.shape[0]:
        link = jnp.where((row // (2 * size) == col // (2 * size)) & (row // size != col // size), lower, 0.0)
        inverse = inverse - wide_dot(inverse, wide_dot(link, inverse))
        size *= 2
    return inverse


def mixer_forward_kernel(
    q_pre, k_pre, v_pre, taps_ref, aux_ref, seg_ref,
    out_ref, reach_ref, map_ref, offset_ref, q_ref, k_ref, v_ref, t_ref, w_ref, u_ref, work,
):
    head = pl.program_id(0)
    aux = aux_ref[...]
    rate = column_of(aux, 8 + head)
    linked, ending = aux[:, 4:5], aux[:, 5:6]
    row, col, same = masks(aux, seg_ref[0:1, :])
    acts = []
    for part, pre_ref in enumerate((q_pre, k_pre, v_pre)):
        conv = convolve(pre_ref, taps_ref, part, aux, work)
        acts.append(conv * jax.nn.sigmoid(conv))
    q = acts[0] * lax.rsqrt(jnp.sum(acts[0] * acts[0], axis=1, keepdims=True) + EPSILON)
    k = acts[1] * lax.rsqrt(jnp.sum(acts[1] * acts[1], axis=1, keepdims=True) + EPSILON)
    v = acts[2]
    q_ref[...] = q
    k_ref[...] = k
    v_ref[...] = v
    gram = wide_dot(k, k, 1, 1)
    inverse = lower_inverse(jnp.where((row > col) & same, gram * rate, 0.0), row, col)
    t_ref[0] = inverse
    written = wide_dot(inverse, jnp.concatenate([v, k * linked], axis=1) * rate)
    w_ref[...] = written[:, :DH]
    u_ref[...] = written[:, DH:]
    scores = jnp.where((row >= col) & same, wide_dot(q, k, 1, 1), 0.0)
    mixed = wide_dot(scores, written)
    out_ref[...] = mixed[:, :DH]
    reach_ref[...] = q * linked - mixed[:, DH:]
    ends = wide_dot(k * ending, written, 0, 0)
    offset_ref[0] = ends[:, :DH].astype(offset_ref.dtype)
    eye = jnp.where(row[:DH, :DH] == col[:DH, :DH], 1.0, 0.0)
    last = aux[aux.shape[0] - 1 :, 4:5]
    map_ref[0] = (eye * last - ends[:, DH:]).astype(map_ref.dtype)


def mixer_forward(pre, taps, aux, seg_row):
    count = aux.shape[0]
    heads = pre.shape[1] // (3 * DH)

    def part(p):
        return pl.BlockSpec((pre.shape[0], DH), lambda h: (0, p * heads + h))

    whole = lambda x: pl.BlockSpec(x.shape, lambda h: (0,) * x.ndim)
    by_head = pl.BlockSpec((count, DH), lambda h: (0, h))
    square = lambda n: pl.BlockSpec((1, n, n), lambda h: (h, 0, 0))
    wide = jax.ShapeDtypeStruct((count, heads * DH), WIDE)
    small = jax.ShapeDtypeStruct((heads, DH, DH), NARROW)
    return pl.pallas_call(
        mixer_forward_kernel,
        grid=(heads,),
        out_shape=(wide, wide, small, small, wide, wide, wide,
                   jax.ShapeDtypeStruct((heads, count, count), WIDE), wide, wide),
        in_specs=[part(0), part(1), part(2), pl.BlockSpec((16, DH), lambda h: (0, h)), whole(aux), whole(seg_row)],
        out_specs=(by_head, by_head, square(DH), square(DH), by_head, by_head, by_head, square(count), by_head, by_head),
        scratch_shapes=[pltpu.VMEM((pre.shape[0], DH), WIDE)],
        compiler_params=pltpu.CompilerParams(vmem_limit_bytes=40 << 20),
        name="mixer_forward",
    )(pre, pre, pre, taps, aux, seg_row)


def mixer_backward_kernel(
    q_pre, k_pre, v_pre, taps_ref, aux_ref, seg_ref,
    q_ref, k_ref, v_ref, t_ref, w_ref, u_ref, state_ref, grad_ref, d_out_ref,
    dq_pre, dk_pre, dv_pre, d_rate_ref, work,
):
    head = pl.program_id(0)
    aux = aux_ref[...]
    count = aux.shape[0]
    rate = column_of(aux, 8 + head)
    linked, ending = aux[:, 4:5], aux[:, 5:6]
    row, col, same = masks(aux, seg_ref[0:1, :])
    q, k, v = q_ref[...], k_ref[...], v_ref[...]
    state, grad, d_out = state_ref[0], grad_ref[0], d_out_ref[...]
    written = w_ref[...] - wide_dot(u_ref[...], state)
    upto = (row >= col) & same
    scores = jnp.where(upto, wide_dot(q, k, 1, 1), 0.0)
    d_written = wide_dot(scores, d_out, 0, 0) + wide_dot(k * ending, grad)
    d_scores = jnp.where(upto, wide_dot(d_out, written, 1, 1), 0.0)
    d_q = wide_dot(d_scores, k) + linked * wide_dot(d_out, state, 1, 1)
    d_k = wide_dot(d_scores, q, 0, 0) + ending * wide_dot(written, grad, 1, 1)
    d_right = wide_dot(t_ref[0], d_written, 0, 0)
    d_v = rate * d_right
    d_rate = jnp.sum(d_right * (v - linked * wide_dot(k, state)), axis=1, keepdims=True)
    d_k = d_k - (linked * rate) * wide_dot(d_right, state, 1, 1)
    d_lower = jnp.where((row > col) & same, -wide_dot(d_right, written, 1, 1), 0.0)
    d_rate = d_rate + jnp.sum(d_lower * wide_dot(k, k, 1, 1), axis=1, keepdims=True)
    d_gram = d_lower * rate
    d_k = d_k + wide_dot(d_gram, k) + wide_dot(d_gram, k, 0, 0)

    @pl.when(head == 0)
    def _():
        d_rate_ref[...] = jnp.zeros_like(d_rate_ref)

    lanes = lax.broadcasted_iota(jnp.int32, aux.shape, 1)
    d_rate_ref[...] += jnp.where(lanes == head, d_rate, 0.0)
    for part, (pre_ref, out_ref, unit, d) in enumerate(
        ((q_pre, dq_pre, q, d_q), (k_pre, dk_pre, k, d_k), (v_pre, dv_pre, None, d_v))
    ):
        conv = convolve(pre_ref, taps_ref, part, aux, work)
        gate = jax.nn.sigmoid(conv)
        if unit is not None:
            act = conv * gate
            scale = lax.rsqrt(jnp.sum(act * act, axis=1, keepdims=True) + EPSILON)
            d = (d - unit * jnp.sum(unit * d, axis=1, keepdims=True)) * scale
        d_conv = d * gate * (1.0 + conv * (1.0 - gate))
        out_ref[...] = jnp.zeros_like(out_ref)
        for j in range(KW):
            term = d_conv * taps_ref[3 * j + part : 3 * j + part + 1, :]
            if j:
                term = term * aux[:, j : j + 1]
            out_ref[pl.ds(HALO - j, count)] += term


def mixer_backward(pre, taps, aux, seg_row, kept, state, grad, d_out):
    count = aux.shape[0]
    heads = pre.shape[1] // (3 * DH)

    def part(p):
        return pl.BlockSpec((pre.shape[0], DH), lambda h: (0, p * heads + h))

    whole = lambda x: pl.BlockSpec(x.shape, lambda h: (0,) * x.ndim)
    by_head = pl.BlockSpec((count, DH), lambda h: (0, h))
    long_by_head = pl.BlockSpec((pre.shape[0], DH), lambda h: (0, h))
    square = lambda n: pl.BlockSpec((1, n, n), lambda h: (h, 0, 0))
    wide = jax.ShapeDtypeStruct((pre.shape[0], heads * DH), WIDE)
    return pl.pallas_call(
        mixer_backward_kernel,
        grid=(heads,),
        out_shape=(wide, wide, wide, jax.ShapeDtypeStruct(aux.shape, WIDE)),
        in_specs=[part(0), part(1), part(2), pl.BlockSpec((16, DH), lambda h: (0, h)), whole(aux), whole(seg_row),
                  by_head, by_head, by_head, square(count), by_head, by_head, square(DH), square(DH), by_head],
        out_specs=(long_by_head, long_by_head, long_by_head, whole(aux)),
        scratch_shapes=[pltpu.VMEM((pre.shape[0], DH), WIDE)],
        compiler_params=pltpu.CompilerParams(vmem_limit_bytes=40 << 20),
        name="mixer_backward",
    )(pre, pre, pre, taps, aux, seg_row, *kept, state, grad, d_out)


def inverse_rms(values):
    return lax.rsqrt(jnp.mean(values * values, axis=-1, keepdims=True) + EPSILON)


def norm_back(values, scale, gain, grad_out):
    weighted = grad_out * gain
    return scale * weighted - values * scale**3 * jnp.mean(weighted * values, axis=-1, keepdims=True)


def dot(left, right):
    return jnp.dot(left, right, preferred_element_type=WIDE)


def dot_nt(left, right):
    return lax.dot_general(left, right, (((1,), (1,)), ((), ())), preferred_element_type=WIDE)


def dot_tn(left, right):
    return lax.dot_general(left, right, (((0,), (0,)), ((), ())), preferred_element_type=WIDE)


def shifted(value, steps):
    count = lax.axis_size("dp")
    pairs = [(i, i + steps) for i in range(max(0, -steps), min(count, count - steps))]
    return lax.ppermute(value, "dp", pairs)


def pack_ranks(ranks, blocks):
    flat = ranks.reshape(-1, 128)
    flat = jnp.pad(flat, ((0, 64 * blocks - flat.shape[0]), (0, 0)))
    return flat.reshape(blocks, 64, 128).transpose(1, 0, 2).reshape(64, blocks * 128)


def unpack_ranks(packed, tiles):
    blocks = packed.shape[2] // 128
    flat = packed.reshape(32, 64, blocks, 128).transpose(0, 2, 1, 3).reshape(32, 64 * blocks, 128)
    return flat[:, : 4 * tiles].reshape(128, tiles * 128)


def on_device(
    layer_in, cotangent, segments, adapters, norm_one, norm_two, out_gain, beta_bias, conv_taps,
    w_qkv, w_beta, w_out, w_gate_up, w_down, a_in, b_heads, b_beta, a_out, b_ffn, a_down, b_res,
):
    count = layer_in.shape[0]
    m = lax.axis_index("mp")
    heads = w_beta.shape[1]
    inner = heads * DH
    ff = w_down.shape[0]

    pad_beta = jnp.pad(w_beta, ((0, 0), (0, 128 - heads)))
    ranks_one = pack_ranks(
        jnp.concatenate(
            [b_heads.transpose(1, 0, 2).reshape(4, 3 * inner), jnp.pad(b_beta, ((0, 0), (0, 128 - heads)))],
            axis=1,
        ),
        1,
    )
    wide_one = jnp.concatenate([w_qkv.reshape(64, 3 * inner), pad_beta, ranks_one], axis=1)
    thin_one = jnp.concatenate([a_in.reshape(16, 768), b_res.transpose(2, 0, 1).reshape(16, 256)], axis=1)
    ranks_two = pack_ranks(
        jnp.concatenate([b_ffn.transpose(1, 0, 2).reshape(4, 2 * ff), a_out.T, a_down.T], axis=1), 3
    )
    wide_two = jnp.concatenate([w_out.T, w_gate_up.reshape(64, 2 * ff), w_down.T, ranks_two], axis=1)
    full_one, full_thin = first_gather(wide_one, thin_one)
    wide_two, full_one, full_thin = lax.optimization_barrier((wide_two, full_one, full_thin))
    full_two = second_gather(wide_two)

    ranks = unpack_ranks(full_one[:, :, 3 * inner + 128 :], 13)
    full_one = full_one.reshape(2048, -1)
    w_qkv_full = full_one[:, : 3 * inner]
    w_beta_full = full_one[:, 3 * inner : 3 * inner + 128]
    b_heads_full = [ranks[:, j * inner : (j + 1) * inner] for j in range(3)]
    b_beta_full = ranks[:, 3 * inner :]
    full_thin = full_thin.reshape(2048, 1024)
    a_one, a_two = full_thin[:, :512], full_thin[:, 512:768]
    b_res_mix, b_res_down = full_thin[:, 768:896], full_thin[:, 896:]

    ranks = unpack_ranks(full_two[:, :, inner + 3 * ff :], 37)
    full_two = full_two.reshape(2048, -1)
    w_out_full = full_two[:, :inner]
    w_gate_up_full = full_two[:, inner : inner + 2 * ff]
    w_down_full = full_two[:, inner + 2 * ff : inner + 3 * ff]
    b_ffn_full = [ranks[:, j * ff : (j + 1) * ff] for j in range(2)]
    a_out_full = ranks[:, 2 * ff : 2 * ff + inner]
    a_down_full = ranks[:, 2 * ff + inner :]

    before_rows = shifted(layer_in[count - HALO :], 1)
    before_ids = shifted(segments[count - HALO :] + 1, 1) - 1
    rows_ext = jnp.concatenate([before_rows, layer_in]).astype(WIDE)
    seg_ext = jnp.concatenate([before_ids, segments])
    seg_count = adapters.shape[0]
    per_token = jnp.sum(
        jnp.where(seg_ext[:, None] == jnp.arange(seg_count, dtype=jnp.int32)[None, :], adapters[None, :], 0), axis=1
    )
    owner_ids = jnp.arange(128, dtype=jnp.int32) // RANK
    picks_ext = (per_token[:, None] == owner_ids[None, :]).astype(WIDE)
    picks = picks_ext[HALO:]
    same = [
        (seg_ext[HALO - j : HALO - j + count] == segments).astype(WIDE) for j in range(KW)
    ]
    seg_float = segments.astype(WIDE)
    g_full = lax.all_gather(cotangent, "mp", axis=1, tiled=True)

    scale_ext = inverse_rms(rows_ext)
    xn_ext = (rows_ext * scale_ext * norm_one).astype(NARROW)
    u_ext = (dot(xn_ext, a_one) * jnp.tile(picks_ext, (1, 4))).astype(NARROW)
    pre = (
        dot(xn_ext, w_qkv_full)
        + jnp.concatenate([dot(u_ext[:, j * 128 : (j + 1) * 128], b_heads_full[j]) for j in range(3)], axis=1)
    ).astype(NARROW)
    xn_one, u_one = xn_ext[HALO:], u_ext[HALO:]
    logits = dot(xn_one, w_beta_full) + dot(u_one[:, 384:], b_beta_full)
    strength = jax.nn.sigmoid(logits[:, :heads] + beta_bias)
    aux = jnp.concatenate(
        [s[:, None] for s in same]
        + [
            (segments == before_ids[HALO - 1]).astype(WIDE)[:, None],
            (segments == segments[count - 1]).astype(WIDE)[:, None],
            seg_float[:, None],
            jnp.zeros((count, 1), WIDE),
            strength,
            jnp.zeros((count, 128 - 8 - heads), WIDE),
        ],
        axis=1,
    )
    seg_row = jnp.broadcast_to(seg_float[None, :], (8, count))
    taps = jnp.pad(conv_taps.reshape(3 * KW, inner).astype(WIDE), ((0, 4), (0, 0)))
    out_zero, reach, maps, offsets, *kept = mixer_forward(pre, taps, aux, seg_row)
    state_in, *kept_maps = chain_forward(maps, offsets)
    by_head = lambda x: x.reshape(count, heads, DH)
    mixer_out = by_head(out_zero) + jnp.einsum(
        "thk,hkv->thv", by_head(reach), state_in, precision=EXACT
    )
    mixer_scale = inverse_rms(mixer_out)
    normed = (mixer_out * mixer_scale * out_gain).astype(NARROW).reshape(count, inner)
    u_out = dot_nt(normed, a_out_full) * picks
    u_out_narrow = u_out.astype(NARROW)
    branch_part = dot_nt(normed, w_out_full) + dot_nt(u_out_narrow, b_res_mix)
    (branch,) = sum_over_mp(branch_part.astype(NARROW), collective_id=2)

    rows = rows_ext[HALO:]
    hidden_one = rows + branch.astype(WIDE)
    scale_two = inverse_rms(hidden_one)
    xn_two = (hidden_one * scale_two * norm_two).astype(NARROW)
    u_two = (dot(xn_two, a_two) * jnp.tile(picks, (1, 2))).astype(NARROW)
    gate_up = dot(xn_two, w_gate_up_full) + jnp.concatenate(
        [dot(u_two[:, j * 128 : (j + 1) * 128], b_ffn_full[j]) for j in range(2)], axis=1
    )
    gate, up = gate_up[:, :ff], gate_up[:, ff:]
    sig = jax.nn.sigmoid(gate)
    hidden = (gate * sig * up).astype(NARROW)
    u_down = (dot_nt(hidden, a_down_full) * picks).astype(NARROW)
    ffn_part = dot_nt(hidden, w_down_full) + dot_nt(u_down, b_res_down)
    ffn_share = lax.psum_scatter(ffn_part.astype(NARROW), "mp", scatter_dimension=1, tiled=True)
    share = ffn_share.shape[1]
    start_col = m * share
    output = (
        lax.dynamic_slice_in_dim(hidden_one, start_col, share, 1) + ffn_share.astype(WIDE)
    ).astype(NARROW)

    g_wide = g_full.astype(WIDE)
    e_down = (dot(g_full, b_res_down) * picks).astype(NARROW)
    grad_a_down = dot_tn(e_down, hidden)
    d_hidden = dot(g_full, w_down_full) + dot(e_down, a_down_full)
    d_gate = d_hidden * up * sig * (1.0 + gate * (1.0 - sig))
    d_up = d_hidden * gate * sig
    d_gate_up = jnp.concatenate([d_gate, d_up], axis=1).astype(NARROW)
    e_two = jnp.concatenate(
        [dot_nt(d_gate_up[:, j * ff : (j + 1) * ff], b_ffn_full[j]) * picks for j in range(2)], axis=1
    ).astype(NARROW)
    grad_b_ffn = jnp.concatenate(
        [dot_tn(u_two[:, j * 128 : (j + 1) * 128], d_gate_up[:, j * ff : (j + 1) * ff]) for j in range(2)], axis=1
    )
    d_xn_two_part = dot_nt(d_gate_up, w_gate_up_full) + dot_nt(e_two, a_two)
    extra = jnp.concatenate([e_two, u_out_narrow, u_down], axis=1)
    d_xn_two, shared_two = sum_over_mp(d_xn_two_part.astype(NARROW), extra, collective_id=3)
    d_hidden_one = g_wide + norm_back(hidden_one, scale_two, norm_two, d_xn_two.astype(WIDE))

    d_branch = d_hidden_one.astype(NARROW)
    e_out = (dot(d_branch, b_res_mix) * picks).astype(NARROW)
    grad_a_out = dot_tn(e_out, normed)
    d_normed = dot(d_branch, w_out_full) + dot(e_out, a_out_full)
    d_mixer = norm_back(mixer_out, mixer_scale, out_gain, by_head(d_normed))
    d_state = jnp.einsum("thk,thv->hkv", by_head(reach), d_mixer, precision=EXACT)
    state_grad = chain_backward(maps, kept_maps, d_state.astype(NARROW))
    dq_pre, dk_pre, dv_pre, d_rate = mixer_backward(
        pre, taps, aux, seg_row, kept, state_in, state_grad, d_mixer.reshape(count, inner)
    )
    d_pre_ext = jnp.concatenate([dq_pre, dk_pre, dv_pre], axis=1)
    from_next = shifted(d_pre_ext[HALO - KW + 1 : HALO], -1)
    d_pre = d_pre_ext[HALO:].at[count - KW + 1 :].add(from_next).astype(NARROW)
    d_logit = (d_rate[:, :heads] * strength * (1.0 - strength)).astype(NARROW)
    d_logit_pad = jnp.pad(d_logit, ((0, 0), (0, 128 - heads)))
    e_one = (
        jnp.concatenate(
            [dot_nt(d_pre[:, j * inner : (j + 1) * inner], b_heads_full[j]) for j in range(3)]
            + [dot_nt(d_logit_pad, b_beta_full)],
            axis=1,
        )
        * jnp.tile(picks, (1, 4))
    ).astype(NARROW)
    grad_b_heads = jnp.concatenate(
        [dot_tn(u_one[:, j * 128 : (j + 1) * 128], d_pre[:, j * inner : (j + 1) * inner]) for j in range(3)], axis=1
    )
    grad_b_beta = dot_tn(u_one[:, 384:], d_logit)
    d_xn_one_part = dot_nt(d_pre, w_qkv_full) + dot_nt(d_logit_pad, w_beta_full) + dot_nt(e_one, a_one)
    d_xn_one, shared_one = sum_over_mp(d_xn_one_part.astype(NARROW), e_one, collective_id=6)
    grad_full = d_hidden_one + norm_back(rows, scale_ext[HALO:], norm_one, d_xn_one.astype(WIDE))
    grad_input = lax.dynamic_slice_in_dim(grad_full, start_col, share, 1)

    left_two = jnp.where(m < 2, xn_two, jnp.where(m == 2, d_branch, g_full))
    shared_two = dot_tn(left_two, shared_two.astype(NARROW))
    shared_one = dot_tn(xn_one, shared_one.astype(NARROW))

    def rank_rows(x):
        return x.reshape(32, 4, -1)

    early = jnp.concatenate(
        [rank_rows(x).reshape(32, -1, 128) for x in (grad_b_ffn, grad_a_out, grad_a_down)]
        + [shared_two.reshape(32, 64, 128)],
        axis=1,
    ).astype(NARROW)
    early = lax.psum_scatter(early, "dp", scatter_dimension=0, tiled=True)[0].astype(WIDE)
    late = jnp.concatenate(
        [
            rank_rows(grad_b_heads).reshape(32, -1, 128),
            jnp.pad(rank_rows(grad_b_beta), ((0, 0), (0, 0), (0, 128 - heads))),
            shared_one.reshape(32, 64, 128),
        ],
        axis=1,
    ).astype(NARROW)
    late = jnp.sum(lax.all_to_all(late, "dp", 0, 0, tiled=True).astype(WIDE), axis=0)
    shared = jnp.stack([late[-64:].reshape(4, 16, 128), early[-64:].reshape(4, 16, 128)], axis=1)
    shared = lax.all_to_all(shared, "mp", 0, 0, tiled=True)
    out_grad_a_in = jnp.concatenate(
        [shared[j, 0][:, None] for j in range(4)] + [shared[j, 1][:, None] for j in range(2)], axis=1
    )
    out_grad_b_res = jnp.stack([shared[2, 1].T, shared[3, 1].T])
    n_ffn, n_out, n_down = 2 * ff * 4 // 128, inner * 4 // 128, ff * 4 // 128
    out_b_ffn = early[:n_ffn].reshape(4, 2, ff).transpose(1, 0, 2)
    out_a_out = early[n_ffn : n_ffn + n_out].reshape(4, inner).T
    out_a_down = early[n_ffn + n_out : n_ffn + n_out + n_down].reshape(4, ff).T
    n_heads = 3 * inner * 4 // 128
    out_b_heads = late[:n_heads].reshape(4, 3, inner).transpose(1, 0, 2)
    out_b_beta = late[n_heads : n_heads + 4, :heads]
    return (
        output, grad_input, out_grad_a_in, out_b_heads, out_b_beta, out_a_out, out_b_ffn, out_a_down, out_grad_b_res,
    )


def solution(mesh):
    placed = (
        P("dp", None),
        P("dp", "mp"),
        P("dp"),
        P(),
        P(),
        P(),
        P(),
        P("mp"),
        P(None, None, "mp"),
        P("dp", None, "mp"),
        P("dp", "mp"),
        P("mp", "dp"),
        P("dp", None, "mp"),
        P("mp", "dp"),
        P(("dp", "mp"), None, None),
        P(None, "dp", "mp"),
        P("dp", "mp"),
        P("mp", "dp"),
        P(None, "dp", "mp"),
        P("mp", "dp"),
        P(None, None, ("dp", "mp")),
    )
    return jax.shard_map(
        on_device,
        mesh=mesh,
        in_specs=placed,
        out_specs=(
            P("dp", "mp"),
            P("dp", "mp"),
            P(("dp", "mp"), None, None),
            P(None, "dp", "mp"),
            P("dp", "mp"),
            P("mp", "dp"),
            P(None, "dp", "mp"),
            P("mp", "dp"),
            P(None, None, ("dp", "mp")),
        ),
        check_vma=False,
    )
```

```python
import functools

import jax
import jax.numpy as jnp
from jax import lax
from jax.experimental import pallas as pl
from jax.experimental.pallas import tpu as pltpu
from jax.sharding import PartitionSpec as P

DH = 128
KW = 4
RANK = 16
HALO = 16
EPSILON = 1e-06
WIDE = jnp.float32
NARROW = jnp.bfloat16
MESH = pl.DeviceIdType.MESH
EXACT = lax.Precision.HIGHEST


def coords():
    place = lax.axis_index("dp")
    return place // 8, lax.rem(place // 2, 4), lax.rem(place, 2)


def place_of(y, z, c):
    return (y * 4 + z) * 2 + c


def moved(dy, dz, other_core=False):
    y, z, c = coords()
    return place_of(lax.rem(y + dy + 4, 4), lax.rem(z + dz + 4, 4), 1 - c if other_core else c)


def greet(dp_peers=(), mp_peers=()):
    barrier = pltpu.get_barrier_semaphore()
    for peer in dp_peers:
        pl.semaphore_signal(barrier, inc=1, device_id={"dp": peer}, device_id_type=MESH)
    for peer in mp_peers:
        pl.semaphore_signal(barrier, inc=1, device_id={"mp": peer}, device_id_type=MESH)
    pl.semaphore_wait(barrier, len(dp_peers) + len(mp_peers))


class Mailbox:
    def __init__(self, send, recv):
        self.send, self.recv, self.copies = send, recv, []

    def push(self, src, dst, **device):
        k = len(self.copies)
        copy = pltpu.make_async_remote_copy(
            src_ref=src,
            dst_ref=dst,
            send_sem=self.send.at[k],
            recv_sem=self.recv.at[k],
            device_id=device,
            device_id_type=MESH,
        )
        copy.start()
        self.copies.append(copy)
        return copy

    def drain(self):
        for copy in self.copies:
            copy.wait_send()


def gather_steps(box, own, out):
    me = moved(0, 0)
    half = own.shape[0] // 2
    quarter = half // 2
    sibling = moved(0, 0, True)
    kinds = []
    for kind in range(2):
        base = kind * half
        parts = (pl.ds(base, half), pl.ds(base, quarter), pl.ds(base + quarter, quarter))
        if kind == 0:
            kinds.append((parts, lambda a, b: moved(a, b)))
        else:
            kinds.append((parts, lambda a, b: moved(b, a)))
    near, across, far, far_across, shared = [], [{}, {}], [[], []], [{}, {}], []

    def open_up():
        for parts, at in kinds:
            near.append([box.push(own.at[parts[0]], out.at[me, parts[0]], dp=at(s, 0)) for s in (1, -1)])
        for k, (parts, at) in enumerate(kinds):
            across[k][0] = [box.push(own.at[parts[0]], out.at[me, parts[0]], dp=at(0, s)) for s in (1, -1)]
        shared.append(box.push(own, out.at[me], dp=sibling))

    def pass_on(k, slot):
        parts, at = kinds[k]
        block = out.at[slot, parts[0]]
        return [box.push(block, block, dp=at(0, t)) for t in (1, -1)]

    def to_sibling(k, slot):
        block = out.at[slot, kinds[k][0][0]]
        shared.append(box.push(block, block, dp=sibling))

    def from_near(i, s):
        def step():
            for k, (parts, at) in enumerate(kinds):
                near[k][i].wait_recv()
                block = out.at[at(s, 0), parts[1 + i]]
                far[k].append(box.push(block, block, dp=at(-s, 0)))
            for k, (parts, at) in enumerate(kinds):
                across[k][s] = pass_on(k, at(s, 0))
                to_sibling(k, at(s, 0))

        return step

    def from_far(k):
        def step():
            for copy in far[k]:
                copy.wait_recv()
            slot = kinds[k][1](2, 0)
            across[k][2] = pass_on(k, slot)
            to_sibling(k, slot)

        return step

    def from_across(k, f):
        def step():
            parts, at = kinds[k]
            far_across[k][f] = []
            for i, s in enumerate((-1, 1)):
                across[k][f][i].wait_recv()
                slot = at(f, s)
                block = out.at[slot, parts[1 + i]]
                far_across[k][f].append(box.push(block, block, dp=at(0, -s)))
                to_sibling(k, slot)

        return step

    def from_far_across(k, f):
        def step():
            for copy in far_across[k][f]:
                copy.wait_recv()
            to_sibling(k, kinds[k][1](f, 2))

        return step

    def close():
        for copy in shared:
            copy.wait_recv()

    steps = [open_up, from_near(0, -1), from_near(1, 1), from_far(0), from_far(1)]
    steps += [from_across(k, f) for f in (0, -1, 1, 2) for k in range(2)]
    steps += [from_far_across(k, f) for f in (0, -1, 1, 2) for k in range(2)]
    return steps + [close]


def gather_peers():
    return [moved(1, 0), moved(-1, 0), moved(0, 1), moved(0, -1), moved(0, 0, True)]


GATHER_COPIES = 71


def first_gather_kernel(wide_ref, thin_ref, wide_out, thin_out, thin_own, send, recv, local):
    m = lax.axis_index("mp")
    mp_peers = [lax.rem(m + k, 4) for k in (1, 2, 3)]
    greet(gather_peers(), mp_peers)
    me = moved(0, 0)
    box = Mailbox(send, recv)
    rows = thin_ref.shape[0]
    mine = pl.ds(pl.multiple_of(m * rows, rows), rows)
    crossing = [box.push(thin_ref, thin_own.at[mine], mp=peer) for peer in mp_peers]
    keep_wide = pltpu.make_async_copy(wide_ref, wide_out.at[me], local.at[0])
    keep_wide.start()
    keep_thin = pltpu.make_async_copy(thin_ref, thin_own.at[mine], local.at[1])
    keep_thin.start()
    wide_steps = gather_steps(box, wide_ref, wide_out)
    thin_steps = gather_steps(box, thin_own, thin_out)
    wide_steps[0]()
    keep_thin.wait()
    for copy in crossing:
        copy.wait_recv()
    keep_thin_out = pltpu.make_async_copy(thin_own, thin_out.at[me], local.at[2])
    keep_thin_out.start()
    thin_steps[0]()
    for one, two in zip(wide_steps[1:], thin_steps[1:]):
        one()
        two()
    keep_wide.wait()
    keep_thin_out.wait()
    box.drain()


def first_gather(wide, thin):
    count = 2 * GATHER_COPIES + 3
    rows, cols = thin.shape
    anywhere = pl.BlockSpec(memory_space=pl.ANY)
    return pl.pallas_call(
        first_gather_kernel,
        out_shape=(
            jax.ShapeDtypeStruct((32,) + wide.shape, wide.dtype),
            jax.ShapeDtypeStruct((32, 4 * rows, cols), thin.dtype),
        ),
        in_specs=[anywhere, anywhere],
        out_specs=(anywhere, anywhere),
        scratch_shapes=[
            pltpu.VMEM((4 * rows, cols), thin.dtype),
            pltpu.SemaphoreType.DMA((count,)),
            pltpu.SemaphoreType.DMA((count,)),
            pltpu.SemaphoreType.DMA((3,)),
        ],
        compiler_params=pltpu.CompilerParams(collective_id=0, has_side_effects=True),
        name="gather_first",
    )(wide, thin)


def sum_kernel(n_extra, x_ref, *refs):
    if n_extra:
        e_ref, out_ref, e_out, landed, e_landed, send, recv = refs
    else:
        out_ref, landed, send, recv = refs
    m = lax.axis_index("mp")
    rows = x_ref.shape[0] // 2
    width = x_ref.shape[1] // 4
    peers = {k: lax.rem(m + k, 4) for k in (1, 2, 3)}
    greet((), list(peers.values()))
    box = Mailbox(send, recv)

    def columns(i, w):
        return pl.ds(pl.multiple_of(i * w, w), w)

    arriving = []
    for part in range(2):
        r = pl.ds(part * rows, rows)
        arriving.append(
            [
                box.push(x_ref.at[r, columns(peers[k], width)], landed.at[k - 1, r], mp=peers[k])
                for k in (2, 1, 3)
            ]
        )
    if n_extra:
        extra = [
            box.push(e_ref.at[:, columns(peers[k], n_extra)], e_landed.at[k - 1], mp=peers[k])
            for k in (2, 1, 3)
        ]
    gathered = []
    for part in range(2):
        r = pl.ds(part * rows, rows)
        for copy in arriving[part]:
            copy.wait_recv()
        total = x_ref[r, columns(m, width)].astype(WIDE)
        for k in range(3):
            total = total + landed[k, r].astype(WIDE)
        out_ref[r, columns(m, width)] = total.astype(out_ref.dtype)
        block = out_ref.at[r, columns(m, width)]
        gathered += [box.push(block, block, mp=peers[k]) for k in (2, 1, 3)]
    if n_extra:
        for copy in extra:
            copy.wait_recv()
        total = e_ref[:, columns(m, n_extra)].astype(WIDE)
        for k in range(3):
            total = total + e_landed[k].astype(WIDE)
        e_out[...] = total
    for copy in gathered:
        copy.wait_recv()
    box.drain()


def sum_over_mp(x, extra=None, collective_id=0):
    rows, cols = x.shape
    vmem = pl.BlockSpec(memory_space=pltpu.VMEM)
    n_extra = 0 if extra is None else extra.shape[1] // 4
    out_shape = [jax.ShapeDtypeStruct(x.shape, x.dtype)]
    scratch = [pltpu.VMEM((3, rows, cols // 4), x.dtype)]
    count = 12
    if n_extra:
        out_shape.append(jax.ShapeDtypeStruct((rows, n_extra), WIDE))
        scratch.append(pltpu.VMEM((3, rows, n_extra), extra.dtype))
        count += 3
    return pl.pallas_call(
        functools.partial(sum_kernel, n_extra),
        out_shape=tuple(out_shape),
        in_specs=[vmem] * len(out_shape),
        out_specs=tuple([vmem] * len(out_shape)),
        scratch_shapes=scratch
        + [pltpu.SemaphoreType.DMA((count,)), pltpu.SemaphoreType.DMA((count,))],
        compiler_params=pltpu.CompilerParams(
            collective_id=collective_id, has_side_effects=True, vmem_limit_bytes=32 << 20
        ),
        name="sum_over_mp",
    )(*([x] if extra is None else [x, extra]))


def half_dot(left, right, dims=(((1,), (0,)), ((), ()))):
    high = right.astype(NARROW)
    low = (right - high.astype(WIDE)).astype(NARROW)
    return lax.dot_general(left, high, dims, preferred_element_type=WIDE) + lax.dot_general(
        left, low, dims, preferred_element_type=WIDE
    )


TURNED = (((0,), (0,)), ((), ()))


def two_parts(value):
    high = value.astype(NARROW)
    return high, (value - high.astype(WIDE)).astype(NARROW)


def wide_dot(left, right, left_dim=1, right_dim=0):
    left_high, left_low = two_parts(left)
    right_high, right_low = two_parts(right)

    def part(one, two):
        return lax.dot_general(one, two, (((left_dim,), (right_dim,)), ((), ())), preferred_element_type=WIDE)

    return part(left_high, right_high) + (part(left_high, right_low) + part(left_low, right_high))


def column_of(aux, index):
    lanes = lax.broadcasted_iota(jnp.int32, aux.shape, 1)
    return jnp.sum(jnp.where(lanes == index, aux, 0.0), axis=1, keepdims=True)


def convolve(pre_ref, taps_ref, part, aux, work):
    count = aux.shape[0]
    work[...] = pre_ref[...].astype(WIDE)
    total = work[pl.ds(HALO, count)] * taps_ref[part : part + 1, :]
    for j in range(1, KW):
        total = total + (
            work[pl.ds(HALO - j, count)] * aux[:, j : j + 1] * taps_ref[3 * j + part : 3 * j + part + 1, :]
        )
    return total


def masks(aux, seg_row):
    same = aux[:, 6:7] == seg_row
    shape = (aux.shape[0], aux.shape[0])
    row = lax.broadcasted_iota(jnp.int32, shape, 0)
    col = lax.broadcasted_iota(jnp.int32, shape, 1)
    return row, col, same


def lower_inverse(lower, row, col):
    near = jnp.where(row // 8 == col // 8, lower, 0.0)
    square = wide_dot(near, near)
    inverse = jnp.where(row == col, 1.0, 0.0) - near
    inverse = inverse + wide_dot(inverse, square)
    inverse = inverse + wide_dot(inverse, wide_dot(square, square))
    size = 8
    while size < lower.shape[0]:
        link = jnp.where((row // (2 * size) == col // (2 * size)) & (row // size != col // size), lower, 0.0)
        inverse = inverse - wide_dot(inverse, wide_dot(link, inverse))
        size *= 2
    return inverse


def mixer_forward_kernel(
    q_pre, k_pre, v_pre, taps_ref, aux_ref, seg_ref,
    out_ref, reach_ref, map_ref, offset_ref, q_ref, k_ref, v_ref, t_ref, w_ref, u_ref, work,
):
    head = pl.program_id(0)
    aux = aux_ref[...]
    rate = column_of(aux, 8 + head)
    linked, ending = aux[:, 4:5], aux[:, 5:6]
    row, col, same = masks(aux, seg_ref[0:1, :])
    acts = []
    for part, pre_ref in enumerate((q_pre, k_pre, v_pre)):
        conv = convolve(pre_ref, taps_ref, part, aux, work)
        acts.append(conv * jax.nn.sigmoid(conv))
    q = acts[0] * lax.rsqrt(jnp.sum(acts[0] * acts[0], axis=1, keepdims=True) + EPSILON)
    k = acts[1] * lax.rsqrt(jnp.sum(acts[1] * acts[1], axis=1, keepdims=True) + EPSILON)
    v = acts[2]
    q_ref[...] = q
    k_ref[...] = k
    v_ref[...] = v
    gram = wide_dot(k, k, 1, 1)
    inverse = lower_inverse(jnp.where((row > col) & same, gram * rate, 0.0), row, col)
    t_ref[0] = inverse
    written = wide_dot(inverse, jnp.concatenate([v, k * linked], axis=1) * rate)
    w_ref[...] = written[:, :DH]
    u_ref[...] = written[:, DH:]
    scores = jnp.where((row >= col) & same, wide_dot(q, k, 1, 1), 0.0)
    mixed = wide_dot(scores, written)
    out_ref[...] = mixed[:, :DH]
    reach_ref[...] = q * linked - mixed[:, DH:]
    ends = wide_dot(k * ending, written, 0, 0)
    offset_ref[0] = ends[:, :DH].astype(offset_ref.dtype)
    eye = jnp.where(row[:DH, :DH] == col[:DH, :DH], 1.0, 0.0)
    last = aux[aux.shape[0] - 1 :, 4:5]
    map_ref[0] = (eye * last - ends[:, DH:]).astype(map_ref.dtype)


def mixer_forward(pre, taps, aux, seg_row):
    count = aux.shape[0]
    heads = pre.shape[1] // (3 * DH)

    def part(p):
        return pl.BlockSpec((pre.shape[0], DH), lambda h: (0, p * heads + h))

    whole = lambda x: pl.BlockSpec(x.shape, lambda h: (0,) * x.ndim)
    by_head = pl.BlockSpec((count, DH), lambda h: (0, h))
    square = lambda n: pl.BlockSpec((1, n, n), lambda h: (h, 0, 0))
    wide = jax.ShapeDtypeStruct((count, heads * DH), WIDE)
    small = jax.ShapeDtypeStruct((heads, DH, DH), NARROW)
    return pl.pallas_call(
        mixer_forward_kernel,
        grid=(heads,),
        out_shape=(wide, wide, small, small, wide, wide, wide,
                   jax.ShapeDtypeStruct((heads, count, count), WIDE), wide, wide),
        in_specs=[part(0), part(1), part(2), pl.BlockSpec((16, DH), lambda h: (0, h)), whole(aux), whole(seg_row)],
        out_specs=(by_head, by_head, square(DH), square(DH), by_head, by_head, by_head, square(count), by_head, by_head),
        scratch_shapes=[pltpu.VMEM((pre.shape[0], DH), WIDE)],
        compiler_params=pltpu.CompilerParams(vmem_limit_bytes=40 << 20),
        name="mixer_forward",
    )(pre, pre, pre, taps, aux, seg_row)


def mixer_backward_kernel(
    q_pre, k_pre, v_pre, taps_ref, aux_ref, seg_ref,
    q_ref, k_ref, v_ref, t_ref, w_ref, u_ref, state_ref, grad_ref, d_out_ref,
    dq_pre, dk_pre, dv_pre, d_rate_ref, work,
):
    head = pl.program_id(0)
    aux = aux_ref[...]
    count = aux.shape[0]
    rate = column_of(aux, 8 + head)
    linked, ending = aux[:, 4:5], aux[:, 5:6]
    row, col, same = masks(aux, seg_ref[0:1, :])
    q, k, v = q_ref[...], k_ref[...], v_ref[...]
    state, grad, d_out = state_ref[0], grad_ref[0], d_out_ref[...]
    written = w_ref[...] - wide_dot(u_ref[...], state)
    upto = (row >= col) & same
    scores = jnp.where(upto, wide_dot(q, k, 1, 1), 0.0)
    d_written = wide_dot(scores, d_out, 0, 0) + wide_dot(k * ending, grad)
    d_scores = jnp.where(upto, wide_dot(d_out, written, 1, 1), 0.0)
    d_q = wide_dot(d_scores, k) + linked * wide_dot(d_out, state, 1, 1)
    d_k = wide_dot(d_scores, q, 0, 0) + ending * wide_dot(written, grad, 1, 1)
    d_right = wide_dot(t_ref[0], d_written, 0, 0)
    d_v = rate * d_right
    d_rate = jnp.sum(d_right * (v - linked * wide_dot(k, state)), axis=1, keepdims=True)
    d_k = d_k - (linked * rate) * wide_dot(d_right, state, 1, 1)
    d_lower = jnp.where((row > col) & same, -wide_dot(d_right, written, 1, 1), 0.0)
    d_rate = d_rate + jnp.sum(d_lower * wide_dot(k, k, 1, 1), axis=1, keepdims=True)
    d_gram = d_lower * rate
    d_k = d_k + wide_dot(d_gram, k) + wide_dot(d_gram, k, 0, 0)

    @pl.when(head == 0)
    def _():
        d_rate_ref[...] = jnp.zeros_like(d_rate_ref)

    lanes = lax.broadcasted_iota(jnp.int32, aux.shape, 1)
    d_rate_ref[...] += jnp.where(lanes == head, d_rate, 0.0)
    for part, (pre_ref, out_ref, unit, d) in enumerate(
        ((q_pre, dq_pre, q, d_q), (k_pre, dk_pre, k, d_k), (v_pre, dv_pre, None, d_v))
    ):
        conv = convolve(pre_ref, taps_ref, part, aux, work)
        gate = jax.nn.sigmoid(conv)
        if unit is not None:
            act = conv * gate
            scale = lax.rsqrt(jnp.sum(act * act, axis=1, keepdims=True) + EPSILON)
            d = (d - unit * jnp.sum(unit * d, axis=1, keepdims=True)) * scale
        d_conv = d * gate * (1.0 + conv * (1.0 - gate))
        out_ref[...] = jnp.zeros_like(out_ref)
        for j in range(KW):
            term = d_conv * taps_ref[3 * j + part : 3 * j + part + 1, :]
            if j:
                term = term * aux[:, j : j + 1]
            out_ref[pl.ds(HALO - j, count)] += term


def mixer_backward(pre, taps, aux, seg_row, kept, state, grad, d_out):
    count = aux.shape[0]
    heads = pre.shape[1] // (3 * DH)

    def part(p):
        return pl.BlockSpec((pre.shape[0], DH), lambda h: (0, p * heads + h))

    whole = lambda x: pl.BlockSpec(x.shape, lambda h: (0,) * x.ndim)
    by_head = pl.BlockSpec((count, DH), lambda h: (0, h))
    long_by_head = pl.BlockSpec((pre.shape[0], DH), lambda h: (0, h))
    square = lambda n: pl.BlockSpec((1, n, n), lambda h: (h, 0, 0))
    wide = jax.ShapeDtypeStruct((pre.shape[0], heads * DH), WIDE)
    return pl.pallas_call(
        mixer_backward_kernel,
        grid=(heads,),
        out_shape=(wide, wide, wide, jax.ShapeDtypeStruct(aux.shape, WIDE)),
        in_specs=[part(0), part(1), part(2), pl.BlockSpec((16, DH), lambda h: (0, h)), whole(aux), whole(seg_row),
                  by_head, by_head, by_head, square(count), by_head, by_head, square(DH), square(DH), by_head],
        out_specs=(long_by_head, long_by_head, long_by_head, whole(aux)),
        scratch_shapes=[pltpu.VMEM((pre.shape[0], DH), WIDE)],
        compiler_params=pltpu.CompilerParams(vmem_limit_bytes=40 << 20),
        name="mixer_backward",
    )(pre, pre, pre, taps, aux, seg_row, *kept, state, grad, d_out)


def inverse_rms(values):
    return lax.rsqrt(jnp.mean(values * values, axis=-1, keepdims=True) + EPSILON)


def norm_back(values, scale, gain, grad_out):
    weighted = grad_out * gain
    return scale * weighted - values * scale**3 * jnp.mean(weighted * values, axis=-1, keepdims=True)


def dot(left, right):
    return jnp.dot(left, right, preferred_element_type=WIDE)


def dot_nt(left, right):
    return lax.dot_general(left, right, (((1,), (1,)), ((), ())), preferred_element_type=WIDE)


def dot_tn(left, right):
    return lax.dot_general(left, right, (((0,), (0,)), ((), ())), preferred_element_type=WIDE)


def shifted(value, steps):
    count = lax.axis_size("dp")
    pairs = [(i, i + steps) for i in range(max(0, -steps), min(count, count - steps))]
    return lax.ppermute(value, "dp", pairs)


def pack_ranks(ranks, blocks):
    flat = ranks.reshape(-1, 128)
    flat = jnp.pad(flat, ((0, 64 * blocks - flat.shape[0]), (0, 0)))
    return flat.reshape(blocks, 64, 128).transpose(1, 0, 2).reshape(64, blocks * 128)


def unpack_ranks(packed, tiles):
    blocks = packed.shape[2] // 128
    flat = packed.reshape(32, 64, blocks, 128).transpose(0, 2, 1, 3).reshape(32, 64 * blocks, 128)
    return flat[:, : 4 * tiles].reshape(128, tiles * 128)


class Chain:
    def __init__(self, box, a_ref, b_ref, g_ref, sib, chip_a, chip_b, chip_g, row_a, row_b, row_g, pass_on):
        self.box, self.a_ref, self.b_ref, self.g_ref = box, a_ref, b_ref, g_ref
        self.sib, self.pass_on = sib, pass_on
        self.chip_a, self.chip_b, self.chip_g = chip_a, chip_b, chip_g
        self.row_a, self.row_b, self.row_g = row_a, row_b, row_g
        self.y, self.z, self.c = coords()
        self.first = self.c == 0
        self.sibling = moved(0, 0, True)
        self.z_peers = {k: moved(0, k) for k in (1, 2, 3)}
        self.y_peers = {k: moved(k, 0) for k in (1, 2, 3)}
        self.mine = pl.ds(pl.multiple_of(2 * self.c, 2), 2)
        self.theirs = pl.ds(pl.multiple_of(2 * (1 - self.c), 2), 2)

    def peers(self):
        return [self.sibling] + list(self.z_peers.values()) + list(self.y_peers.values())

    def swap(self, ref, slot):
        return self.box.push(ref.at[self.theirs], self.sib.at[slot], dp=self.sibling)

    def ordered(self, ref, slot, h):
        own, other = ref[2 * self.c + h], self.sib[slot, h]
        return jnp.where(self.first, own, other), jnp.where(self.first, other, own)

    def spread(self, refs, place, peers):
        return [self.box.push(ref.at[place], ref.at[place], dp=peers[k]) for k in (2, 1, 3) for ref in refs]

    def start_forward(self):
        self.pair = [self.swap(self.a_ref, 0), self.swap(self.b_ref, 1)]

    def chips_forward(self):
        for copy in self.pair:
            copy.wait_recv()
        self.lower, self.upper_a = [], []
        for h in range(2):
            a_low, a_high = self.ordered(self.a_ref, 0, h)
            b_low, b_high = self.ordered(self.b_ref, 1, h)
            self.lower.append((a_low, b_low))
            self.upper_a.append(a_high)
            self.chip_a[self.z, h] = lax.dot(a_high, a_low, preferred_element_type=WIDE).astype(NARROW)
            self.chip_b[self.z, h] = (
                lax.dot(a_high, b_low, preferred_element_type=WIDE) + b_high.astype(WIDE)
            ).astype(NARROW)
        self.ring = self.spread((self.chip_a, self.chip_b), self.z, self.z_peers)

    def rows_forward(self):
        for copy in self.ring:
            copy.wait_recv()
        for h in range(2):
            total_a, total_b = self.chip_a[0, h].astype(WIDE), self.chip_b[0, h].astype(WIDE)
            for i in range(1, 4):
                total_a = half_dot(self.chip_a[i, h], total_a)
                total_b = half_dot(self.chip_a[i, h], total_b) + self.chip_b[i, h].astype(WIDE)
            self.row_a[self.y, h] = total_a.astype(NARROW)
            self.row_b[self.y, h] = total_b.astype(NARROW)
        self.ring = self.spread((self.row_a, self.row_b), self.y, self.y_peers)

    def finish_forward(self, out):
        for copy in self.ring:
            copy.wait_recv()
        for h in range(2):
            state = jnp.zeros((DH, DH), WIDE)
            for i in range(3):
                longer = half_dot(self.row_a[i, h], state) + self.row_b[i, h].astype(WIDE)
                state = jnp.where(i < self.y, longer, state)
            for i in range(3):
                longer = half_dot(self.chip_a[i, h], state) + self.chip_b[i, h].astype(WIDE)
                state = jnp.where(i < self.z, longer, state)
            a_low, b_low = self.lower[h]
            middle = half_dot(a_low, state) + b_low.astype(WIDE)
            out[2 * self.c + h] = jnp.where(self.first, state, middle)
            self.pass_on[0, h] = jnp.where(self.first, middle, state)
        self.box.push(self.pass_on.at[0], out.at[self.mine], dp=self.sibling).wait_recv()

    def start_backward(self):
        self.pair = [self.swap(self.g_ref, 2)]

    def chips_backward(self):
        for copy in self.pair:
            copy.wait_recv()
        self.upper_g = []
        for h in range(2):
            a_low, _ = self.ordered(self.a_ref, 0, h)
            g_low, g_high = self.ordered(self.g_ref, 2, h)
            self.upper_g.append(g_high)
            self.chip_g[self.z, h] = (
                lax.dot_general(a_low, g_high, TURNED, preferred_element_type=WIDE) + g_low.astype(WIDE)
            ).astype(NARROW)
        self.ring = self.spread((self.chip_g,), self.z, self.z_peers)

    def rows_backward(self):
        for copy in self.ring:
            copy.wait_recv()
        for h in range(2):
            total = self.chip_g[3, h].astype(WIDE)
            for i in (2, 1, 0):
                total = half_dot(self.chip_a[i, h], total, TURNED) + self.chip_g[i, h].astype(WIDE)
            self.row_g[self.y, h] = total.astype(NARROW)
        self.ring = self.spread((self.row_g,), self.y, self.y_peers)

    def finish_backward(self, out):
        for copy in self.ring:
            copy.wait_recv()
        for h in range(2):
            grad = jnp.zeros((DH, DH), WIDE)
            for i in (3, 2, 1):
                longer = half_dot(self.row_a[i, h], grad, TURNED) + self.row_g[i, h].astype(WIDE)
                grad = jnp.where(i > self.y, longer, grad)
            for i in (3, 2, 1):
                longer = half_dot(self.chip_a[i, h], grad, TURNED) + self.chip_g[i, h].astype(WIDE)
                grad = jnp.where(i > self.z, longer, grad)
            _, a_high = self.ordered(self.a_ref, 0, h)
            middle = half_dot(a_high, grad, TURNED) + self.upper_g[h].astype(WIDE)
            out[2 * self.c + h] = jnp.where(self.first, middle, grad)
            self.pass_on[1, h] = jnp.where(self.first, grad, middle)
        self.box.push(self.pass_on.at[1], out.at[self.mine], dp=self.sibling).wait_recv()


def columns(i, width):
    return pl.ds(pl.multiple_of(i * width, width), width)


class MpSum:
    ORDER = (2, 1, 3)

    def __init__(self, box, part, landed):
        self.box, self.part, self.landed = box, part, landed
        self.m = lax.axis_index("mp")
        self.peers = {k: lax.rem(self.m + k, 4) for k in (1, 2, 3)}
        self.copies = []

    def owner(self, k):
        return lax.rem(self.m + k, 4)

    def send(self, k):
        self.copies.append(self.box.push(self.part.at[k], self.landed.at[k - 1], mp=self.peers[k]))

    def total(self):
        for copy in self.copies:
            copy.wait_recv()
        total = self.part[0].astype(WIDE)
        for k in range(3):
            total = total + self.landed[k].astype(WIDE)
        return total

    def share(self, out, width):
        block = out.at[:, columns(self.m, width)]
        return [self.box.push(block, block, mp=self.peers[k]) for k in self.ORDER]


def middle_kernel(
    a_ref, b_ref, out_zero, reach, picks_ref, x_ref, g_own, norm_ref, gain_ref, ranks_ref, thin_ref, wide_ref,
    output, state_out, grad_out, d_one_out, d_mixer_out, g_b_ffn, g_a_down, g_a_out, g_shared,
    w_out, w_gu, w_down, a_two, b_res, ranks, g_full, sib, chip_a, chip_b, chip_g, row_a, row_b, row_g, pass_on, g_maps,
    mixer_out, normed, part, landed, branch, hidden_one, xn_two, gate, up, hidden, ffn_part, ffn_landed,
    d_gate_up, d_xn, extra, extra_landed, d_branch, e_down_ref, u_two_ref,
    send, recv, local,
):
    count = x_ref.shape[0]
    heads = a_ref.shape[0]
    inner = heads * DH
    ff = gate.shape[1]
    m = lax.axis_index("mp")
    box = Mailbox(send, recv)
    chain = Chain(box, a_ref, b_ref, g_maps, sib, chip_a, chip_b, chip_g, row_a, row_b, row_g, pass_on)
    mp_peers = {k: lax.rem(m + k, 4) for k in (1, 2, 3)}
    greet(chain.peers(), list(mp_peers.values()))
    chain.start_forward()
    share = g_own.shape[1]
    g_full[:, columns(m, share)] = g_own[...]
    g_sent = [box.push(g_own, g_full.at[:, columns(m, share)], mp=mp_peers[k]) for k in MpSum.ORDER]
    loads = [
        pltpu.make_async_copy(wide_ref.at[:, pl.ds(0, inner)], w_out, local.at[0]),
        pltpu.make_async_copy(thin_ref.at[:, pl.ds(512, 256)], a_two, local.at[1]),
        pltpu.make_async_copy(thin_ref.at[:, pl.ds(768, 256)], b_res, local.at[2]),
        pltpu.make_async_copy(wide_ref.at[:, pl.ds(inner, 2 * ff)], w_gu, local.at[3]),
        pltpu.make_async_copy(wide_ref.at[:, pl.ds(inner + 2 * ff, ff)], w_down, local.at[4]),
    ]
    for load in loads:
        load.start()
    row = lax.broadcasted_iota(jnp.int32, (128, 256), 0)
    col = lax.broadcasted_iota(jnp.int32, (128, 256), 1)
    pick_rows = jnp.where(col == (row // 4) * 8 + lax.rem(row, 4), 1.0, 0.0).astype(NARROW)
    width = ranks_ref.shape[1]
    for start in range(0, width, 1280):
        piece = slice(start, min(start + 1280, width))
        ranks[:, piece] = dot(pick_rows, ranks_ref[:, piece]).astype(NARROW)
    picks = picks_ref[...]
    chain.chips_forward()
    chain.rows_forward()
    chain.finish_forward(state_out)

    for h in range(heads):
        cols = slice(h * DH, (h + 1) * DH)
        rows = out_zero[:, cols] + wide_dot(reach[:, cols], state_out[h])
        mixer_out[:, cols] = rows
        normed[:, cols] = (rows * inverse_rms(rows) * gain_ref[0:1, :]).astype(NARROW)
    at_gate, at_up, at_out, at_down = 0, ff, 2 * ff, 2 * ff + inner
    a_out = ranks.at[:, pl.ds(at_out, inner)]
    a_down = ranks.at[:, pl.ds(at_down, ff)]
    u_out = (dot_nt(normed[...], a_out[...]) * picks).astype(NARROW)
    for load in loads[:3]:
        load.wait()
    b_mix, b_down = b_res.at[:, pl.ds(0, 128)], b_res.at[:, pl.ds(128, 128)]
    one = MpSum(box, part.at[0], landed.at[0])
    for k in (2, 1, 3, 0):
        rows = columns(one.owner(k), share)
        part[0, k] = (dot_nt(normed[...], w_out[rows, :]) + dot_nt(u_out, b_mix[rows, :])).astype(NARROW)
        if k:
            one.send(k)
    branch[:, columns(m, share)] = one.total().astype(NARROW)
    shared = one.share(branch, share)
    for copy in g_sent + shared:
        copy.wait_recv()

    rows = x_ref[...].astype(WIDE) + branch[...].astype(WIDE)
    hidden_one[...] = rows
    scale_two = inverse_rms(rows)
    xn_two[...] = (rows * scale_two * norm_ref[0:1, :]).astype(NARROW)
    two_picks = jnp.concatenate([picks, picks], axis=1)
    u_two_ref[...] = (dot(xn_two[...], a_two[...]) * two_picks).astype(NARROW)
    loads[3].wait()
    gate[...] = dot(xn_two[...], w_gu[:, :ff]) + dot(u_two_ref[:, :128], ranks[:, at_gate : at_gate + ff])
    up[...] = dot(xn_two[...], w_gu[:, ff:]) + dot(u_two_ref[:, 128:], ranks[:, at_up : at_up + ff])
    hidden[...] = (gate[...] * jax.nn.sigmoid(gate[...]) * up[...]).astype(NARROW)
    loads[4].wait()

    e_down = (dot(g_full[...], b_down[...]) * picks).astype(NARROW)
    e_down_ref[...] = e_down
    d_hidden = dot(g_full[...], w_down[...]) + dot(e_down, a_down[...])
    sig = jax.nn.sigmoid(gate[...])
    d_gate_up[:, :ff] = (d_hidden * up[...] * sig * (1.0 + gate[...] * (1.0 - sig))).astype(NARROW)
    d_gate_up[:, ff:] = (d_hidden * gate[...] * sig).astype(NARROW)
    e_two = [
        (dot_nt(d_gate_up[:, j * ff : (j + 1) * ff], ranks[:, j * ff : (j + 1) * ff]) * picks).astype(NARROW)
        for j in range(2)
    ]
    two = MpSum(box, part.at[1], landed.at[1])
    for k in (2, 1, 3, 0):
        rows = columns(two.owner(k), share)
        part[1, k] = (
            dot_nt(d_gate_up[...], w_gu[rows, :]) + dot_nt(jnp.concatenate(e_two, axis=1), a_two[rows, :])
        ).astype(NARROW)
        if k:
            two.send(k)
    u_down = (dot_nt(hidden[...], a_down[...]) * picks).astype(NARROW)
    for j, value in enumerate((e_two[0], e_two[1], u_out, u_down)):
        extra[j] = value
    d_xn[:, columns(m, share)] = two.total().astype(NARROW)
    shared = two.share(d_xn, share)
    extra_sent = [box.push(extra.at[mp_peers[k]], extra_landed.at[k - 1], mp=mp_peers[k]) for k in MpSum.ORDER]
    three = MpSum(box, ffn_part, ffn_landed)
    for k in (2, 1, 3, 0):
        rows = columns(three.owner(k), share)
        ffn_part[k] = (dot_nt(hidden[...], w_down[rows, :]) + dot_nt(u_down, b_down[rows, :])).astype(NARROW)
    for copy in shared:
        copy.wait_recv()
    for k in MpSum.ORDER:
        three.send(k)

    rows = hidden_one[...]
    scale_two = inverse_rms(rows)
    d_one = g_full[...].astype(WIDE) + norm_back(rows, scale_two, norm_ref[0:1, :], d_xn[...].astype(WIDE))
    d_one_out[...] = d_one
    d_branch[...] = d_one.astype(NARROW)
    e_out = (dot(d_branch[...], b_mix[...]) * picks).astype(NARROW)
    d_normed = dot(d_branch[...], w_out[...]) + dot(e_out, a_out[...])
    for h in range(heads):
        cols = slice(h * DH, (h + 1) * DH)
        rows = mixer_out[:, cols]
        d_rows = norm_back(rows, inverse_rms(rows), gain_ref[0:1, :], d_normed[:, cols])
        d_mixer_out[:, cols] = d_rows
        g_maps[h] = wide_dot(reach[:, cols], d_rows, 0, 0).astype(NARROW)
    chain.start_backward()
    g_a_out[...] = dot_tn(e_out, normed[...]).astype(NARROW)
    chain.chips_backward()
    for j in range(2):
        cols = slice(j * ff, (j + 1) * ff)
        g_b_ffn[:, cols] = dot_tn(u_two_ref[:, j * 128 : (j + 1) * 128], d_gate_up[:, cols]).astype(NARROW)
    chain.rows_backward()
    g_a_down[...] = dot_tn(e_down_ref[...], hidden[...]).astype(NARROW)
    for copy in extra_sent:
        copy.wait_recv()
    factor = extra[m].astype(WIDE)
    for k in range(3):
        factor = factor + extra_landed[k].astype(WIDE)
    left = jnp.where(m < 2, xn_two[...], jnp.where(m == 2, d_branch[...], g_full[...]))
    g_shared[...] = dot_tn(left, factor.astype(NARROW)).astype(NARROW)
    chain.finish_backward(grad_out)
    output[...] = (hidden_one[:, columns(m, share)] + three.total()).astype(NARROW)
    box.drain()


def middle(maps, offsets, out_zero, reach, picks, x, g, norm, gain, ranks, thin, wide):
    count, inner = out_zero.shape
    heads = maps.shape[0]
    model = x.shape[1]
    share = g.shape[1]
    ff = (wide.shape[1] - inner) // 3
    vmem = pl.BlockSpec(memory_space=pltpu.VMEM)
    anywhere = pl.BlockSpec(memory_space=pl.ANY)
    two = (2, DH, DH)
    copies = 2 + 6 + 6 + 1 + 1 + 3 + 3 + 1 + 3 + 6 + 6 + 3 + 3
    results = [
        ((count, share), NARROW),
        ((heads, DH, DH), WIDE),
        ((heads, DH, DH), WIDE),
        ((count, model), WIDE),
        ((count, inner), WIDE),
        ((128, 2 * ff), NARROW),
        ((128, ff), NARROW),
        ((128, inner), NARROW),
        ((model, 128), NARROW),
    ]
    scratch = [
        ((model, inner), NARROW),
        ((model, 2 * ff), NARROW),
        ((model, ff), NARROW),
        ((model, 256), NARROW),
        ((model, 256), NARROW),
        ((128, 3 * ff + inner), NARROW),
        ((count, model), NARROW),
        ((3,) + two, NARROW),
        ((4,) + two, NARROW),
        ((4,) + two, NARROW),
        ((4,) + two, NARROW),
        ((4,) + two, NARROW),
        ((4,) + two, NARROW),
        ((4,) + two, NARROW),
        ((2,) + two, WIDE),
        ((heads, DH, DH), NARROW),
        ((count, inner), WIDE),
        ((count, inner), NARROW),
        ((2, 4, count, share), NARROW),
        ((2, 3, count, share), NARROW),
        ((count, model), NARROW),
        ((count, model), WIDE),
        ((count, model), NARROW),
        ((count, ff), WIDE),
        ((count, ff), WIDE),
        ((count, ff), NARROW),
        ((4, count, share), NARROW),
        ((3, count, share), NARROW),
        ((count, 2 * ff), NARROW),
        ((count, model), NARROW),
        ((4, count, 128), NARROW),
        ((3, count, 128), NARROW),
        ((count, model), NARROW),
        ((count, 128), NARROW),
        ((count, 256), NARROW),
    ]
    return pl.pallas_call(
        middle_kernel,
        out_shape=tuple(jax.ShapeDtypeStruct(*r) for r in results),
        in_specs=[vmem] * 10 + [anywhere] * 2,
        out_specs=tuple([vmem] * len(results)),
        scratch_shapes=[pltpu.VMEM(*s) for s in scratch]
        + [
            pltpu.SemaphoreType.DMA((copies,)),
            pltpu.SemaphoreType.DMA((copies,)),
            pltpu.SemaphoreType.DMA((5,)),
        ],
        compiler_params=pltpu.CompilerParams(
            collective_id=2, has_side_effects=True, vmem_limit_bytes=60 << 20
        ),
        name="middle",
    )(maps, offsets, out_zero, reach, picks, x, g, norm, gain, ranks, thin, wide)


def on_device(
    layer_in, cotangent, segments, adapters, norm_one, norm_two, out_gain, beta_bias, conv_taps,
    w_qkv, w_beta, w_out, w_gate_up, w_down, a_in, b_heads, b_beta, a_out, b_ffn, a_down, b_res,
):
    count = layer_in.shape[0]
    m = lax.axis_index("mp")
    heads = w_beta.shape[1]
    inner = heads * DH
    ff = w_down.shape[0]

    pad_beta = jnp.pad(w_beta, ((0, 0), (0, 128 - heads)))
    ranks_one = pack_ranks(
        jnp.concatenate(
            [b_heads.transpose(1, 0, 2).reshape(4, 3 * inner), jnp.pad(b_beta, ((0, 0), (0, 128 - heads)))],
            axis=1,
        ),
        1,
    )
    wide_one = jnp.concatenate([w_qkv.reshape(64, 3 * inner), pad_beta, ranks_one], axis=1)
    thin_one = jnp.concatenate([a_in.reshape(16, 768), b_res.transpose(2, 0, 1).reshape(16, 256)], axis=1)
    ranks_two = jnp.concatenate([b_ffn.transpose(1, 0, 2).reshape(4, 2 * ff), a_out.T, a_down.T], axis=1)
    ranks_two = jnp.pad(ranks_two, ((0, 4), (0, 0)))
    wide_two = jnp.concatenate([w_out.T, w_gate_up.reshape(64, 2 * ff), w_down.T], axis=1)
    full_ranks = lax.all_gather(ranks_two, "dp", axis=0, tiled=True)
    full_two = lax.all_gather(wide_two, "dp", axis=0, tiled=True)
    full_one, full_thin = first_gather(wide_one, thin_one)

    ranks = unpack_ranks(full_one[:, :, 3 * inner + 128 :], 13)
    full_one = full_one.reshape(2048, -1)
    w_qkv_full = full_one[:, : 3 * inner]
    w_beta_full = full_one[:, 3 * inner : 3 * inner + 128]
    b_heads_full = [ranks[:, j * inner : (j + 1) * inner] for j in range(3)]
    b_beta_full = ranks[:, 3 * inner :]
    full_thin = full_thin.reshape(2048, 1024)
    a_one = full_thin[:, :512]

    before_rows = shifted(layer_in[count - HALO :], 1)
    before_ids = shifted(segments[count - HALO :] + 1, 1) - 1
    rows_ext = jnp.concatenate([before_rows, layer_in]).astype(WIDE)
    seg_ext = jnp.concatenate([before_ids, segments])
    seg_count = adapters.shape[0]
    per_token = jnp.sum(
        jnp.where(seg_ext[:, None] == jnp.arange(seg_count, dtype=jnp.int32)[None, :], adapters[None, :], 0), axis=1
    )
    owner_ids = jnp.arange(128, dtype=jnp.int32) // RANK
    picks_ext = (per_token[:, None] == owner_ids[None, :]).astype(WIDE)
    picks = picks_ext[HALO:]
    same = [
        (seg_ext[HALO - j : HALO - j + count] == segments).astype(WIDE) for j in range(KW)
    ]
    seg_float = segments.astype(WIDE)

    scale_ext = inverse_rms(rows_ext)
    xn_ext = (rows_ext * scale_ext * norm_one).astype(NARROW)
    u_ext = (dot(xn_ext, a_one) * jnp.tile(picks_ext, (1, 4))).astype(NARROW)
    pre = (
        dot(xn_ext, w_qkv_full)
        + jnp.concatenate([dot(u_ext[:, j * 128 : (j + 1) * 128], b_heads_full[j]) for j in range(3)], axis=1)
    ).astype(NARROW)
    xn_one, u_one = xn_ext[HALO:], u_ext[HALO:]
    logits = dot(xn_one, w_beta_full) + dot(u_one[:, 384:], b_beta_full)
    strength = jax.nn.sigmoid(logits[:, :heads] + beta_bias)
    aux = jnp.concatenate(
        [s[:, None] for s in same]
        + [
            (segments == before_ids[HALO - 1]).astype(WIDE)[:, None],
            (segments == segments[count - 1]).astype(WIDE)[:, None],
            seg_float[:, None],
            jnp.zeros((count, 1), WIDE),
            strength,
            jnp.zeros((count, 128 - 8 - heads), WIDE),
        ],
        axis=1,
    )
    seg_row = jnp.broadcast_to(seg_float[None, :], (8, count))
    taps = jnp.pad(conv_taps.reshape(3 * KW, inner).astype(WIDE), ((0, 4), (0, 0)))
    out_zero, reach, maps, offsets, *kept = mixer_forward(pre, taps, aux, seg_row)
    (
        output, state_in, state_grad, d_hidden_one, d_mixer,
        grad_b_ffn, grad_a_down, grad_a_out, shared_two,
    ) = middle(
        maps, offsets, out_zero, reach, picks, layer_in, cotangent,
        jnp.broadcast_to(norm_two[None, :], (8, norm_two.shape[0])),
        jnp.broadcast_to(out_gain[None, :], (8, DH)),
        full_ranks, full_thin, full_two,
    )
    dq_pre, dk_pre, dv_pre, d_rate = mixer_backward(
        pre, taps, aux, seg_row, kept, state_in, state_grad, d_mixer
    )
    d_pre_ext = jnp.concatenate([dq_pre, dk_pre, dv_pre], axis=1)
    from_next = shifted(d_pre_ext[HALO - KW + 1 : HALO], -1)
    d_pre = d_pre_ext[HALO:].at[count - KW + 1 :].add(from_next).astype(NARROW)
    d_logit = (d_rate[:, :heads] * strength * (1.0 - strength)).astype(NARROW)
    d_logit_pad = jnp.pad(d_logit, ((0, 0), (0, 128 - heads)))
    e_one = (
        jnp.concatenate(
            [dot_nt(d_pre[:, j * inner : (j + 1) * inner], b_heads_full[j]) for j in range(3)]
            + [dot_nt(d_logit_pad, b_beta_full)],
            axis=1,
        )
        * jnp.tile(picks, (1, 4))
    ).astype(NARROW)
    grad_b_heads = jnp.concatenate(
        [dot_tn(u_one[:, j * 128 : (j + 1) * 128], d_pre[:, j * inner : (j + 1) * inner]) for j in range(3)], axis=1
    )
    grad_b_beta = dot_tn(u_one[:, 384:], d_logit)
    d_xn_one_part = dot_nt(d_pre, w_qkv_full) + dot_nt(d_logit_pad, w_beta_full) + dot_nt(e_one, a_one)
    d_xn_one, shared_one = sum_over_mp(d_xn_one_part.astype(NARROW), e_one, collective_id=6)
    rows = rows_ext[HALO:]
    share = cotangent.shape[1]
    start_col = m * share
    grad_full = d_hidden_one + norm_back(rows, scale_ext[HALO:], norm_one, d_xn_one.astype(WIDE))
    grad_input = lax.dynamic_slice_in_dim(grad_full, start_col, share, 1)

    shared_one = dot_tn(xn_one, shared_one.astype(NARROW))

    def rank_rows(x):
        return x.reshape(32, 4, -1)

    early = jnp.concatenate(
        [rank_rows(x).reshape(32, -1, 128) for x in (grad_b_ffn, grad_a_out, grad_a_down)]
        + [shared_two.reshape(32, 64, 128)],
        axis=1,
    ).astype(NARROW)
    early = lax.psum_scatter(early, "dp", scatter_dimension=0, tiled=True)[0].astype(WIDE)
    late = jnp.concatenate(
        [
            rank_rows(grad_b_heads).reshape(32, -1, 128),
            jnp.pad(rank_rows(grad_b_beta), ((0, 0), (0, 0), (0, 128 - heads))),
            shared_one.reshape(32, 64, 128),
        ],
        axis=1,
    ).astype(NARROW)
    late = jnp.sum(lax.all_to_all(late, "dp", 0, 0, tiled=True).astype(WIDE), axis=0)
    shared = jnp.stack([late[-64:].reshape(4, 16, 128), early[-64:].reshape(4, 16, 128)], axis=1)
    shared = lax.all_to_all(shared, "mp", 0, 0, tiled=True)
    out_grad_a_in = jnp.concatenate(
        [shared[j, 0][:, None] for j in range(4)] + [shared[j, 1][:, None] for j in range(2)], axis=1
    )
    out_grad_b_res = jnp.stack([shared[2, 1].T, shared[3, 1].T])
    n_ffn, n_out, n_down = 2 * ff * 4 // 128, inner * 4 // 128, ff * 4 // 128
    out_b_ffn = early[:n_ffn].reshape(4, 2, ff).transpose(1, 0, 2)
    out_a_out = early[n_ffn : n_ffn + n_out].reshape(4, inner).T
    out_a_down = early[n_ffn + n_out : n_ffn + n_out + n_down].reshape(4, ff).T
    n_heads = 3 * inner * 4 // 128
    out_b_heads = late[:n_heads].reshape(4, 3, inner).transpose(1, 0, 2)
    out_b_beta = late[n_heads : n_heads + 4, :heads]
    return (
        output, grad_input, out_grad_a_in, out_b_heads, out_b_beta, out_a_out, out_b_ffn, out_a_down, out_grad_b_res,
    )


def solution(mesh):
    placed = (
        P("dp", None),
        P("dp", "mp"),
        P("dp"),
        P(),
        P(),
        P(),
        P(),
        P("mp"),
        P(None, None, "mp"),
        P("dp", None, "mp"),
        P("dp", "mp"),
        P("mp", "dp"),
        P("dp", None, "mp"),
        P("mp", "dp"),
        P(("dp", "mp"), None, None),
        P(None, "dp", "mp"),
        P("dp", "mp"),
        P("mp", "dp"),
        P(None, "dp", "mp"),
        P("mp", "dp"),
        P(None, None, ("dp", "mp")),
    )
    return jax.shard_map(
        on_device,
        mesh=mesh,
        in_specs=placed,
        out_specs=(
            P("dp", "mp"),
            P("dp", "mp"),
            P(("dp", "mp"), None, None),
            P(None, "dp", "mp"),
            P("dp", "mp"),
            P("mp", "dp"),
            P(None, "dp", "mp"),
            P("mp", "dp"),
            P(None, None, ("dp", "mp")),
        ),
        check_vma=False,
    )
```

```python
import functools

import jax
import jax.numpy as jnp
from jax import lax
from jax.experimental import pallas as pl
from jax.experimental.pallas import tpu as pltpu
from jax.sharding import PartitionSpec as P

DH = 128
KW = 4
RANK = 16
HALO = 16
EPSILON = 1e-06
WIDE = jnp.float32
NARROW = jnp.bfloat16
MESH = pl.DeviceIdType.MESH
EXACT = lax.Precision.HIGHEST


def coords():
    place = lax.axis_index("dp")
    return place // 8, lax.rem(place // 2, 4), lax.rem(place, 2)


def place_of(y, z, c):
    return (y * 4 + z) * 2 + c


def moved(dy, dz, other_core=False):
    y, z, c = coords()
    return place_of(lax.rem(y + dy + 4, 4), lax.rem(z + dz + 4, 4), 1 - c if other_core else c)


def greet(dp_peers=(), mp_peers=()):
    barrier = pltpu.get_barrier_semaphore()
    for peer in dp_peers:
        pl.semaphore_signal(barrier, inc=1, device_id={"dp": peer}, device_id_type=MESH)
    for peer in mp_peers:
        pl.semaphore_signal(barrier, inc=1, device_id={"mp": peer}, device_id_type=MESH)
    pl.semaphore_wait(barrier, len(dp_peers) + len(mp_peers))


class Mailbox:
    def __init__(self, send, recv):
        self.send, self.recv, self.copies = send, recv, []

    def push(self, src, dst, **device):
        k = len(self.copies)
        copy = pltpu.make_async_remote_copy(
            src_ref=src,
            dst_ref=dst,
            send_sem=self.send.at[k],
            recv_sem=self.recv.at[k],
            device_id=device,
            device_id_type=MESH,
        )
        copy.start()
        self.copies.append(copy)
        return copy

    def drain(self):
        for copy in self.copies:
            copy.wait_send()


def gather_steps(box, own, out):
    me = moved(0, 0)
    half = own.shape[0] // 2
    quarter = half // 2
    sibling = moved(0, 0, True)
    kinds = []
    for kind in range(2):
        base = kind * half
        parts = (pl.ds(base, half), pl.ds(base, quarter), pl.ds(base + quarter, quarter))
        if kind == 0:
            kinds.append((parts, lambda a, b: moved(a, b)))
        else:
            kinds.append((parts, lambda a, b: moved(b, a)))
    near, across, far, far_across, shared = [], [{}, {}], [[], []], [{}, {}], []

    def open_up():
        for parts, at in kinds:
            near.append([box.push(own.at[parts[0]], out.at[me, parts[0]], dp=at(s, 0)) for s in (1, -1)])
        for k, (parts, at) in enumerate(kinds):
            across[k][0] = [box.push(own.at[parts[0]], out.at[me, parts[0]], dp=at(0, s)) for s in (1, -1)]
        shared.append(box.push(own, out.at[me], dp=sibling))

    def pass_on(k, slot):
        parts, at = kinds[k]
        block = out.at[slot, parts[0]]
        return [box.push(block, block, dp=at(0, t)) for t in (1, -1)]

    def to_sibling(k, slot):
        block = out.at[slot, kinds[k][0][0]]
        shared.append(box.push(block, block, dp=sibling))

    def from_near(i, s):
        def step():
            for k, (parts, at) in enumerate(kinds):
                near[k][i].wait_recv()
                block = out.at[at(s, 0), parts[1 + i]]
                far[k].append(box.push(block, block, dp=at(-s, 0)))
            for k, (parts, at) in enumerate(kinds):
                across[k][s] = pass_on(k, at(s, 0))
                to_sibling(k, at(s, 0))

        return step

    def from_far(k):
        def step():
            for copy in far[k]:
                copy.wait_recv()
            slot = kinds[k][1](2, 0)
            across[k][2] = pass_on(k, slot)
            to_sibling(k, slot)

        return step

    def from_across(k, f):
        def step():
            parts, at = kinds[k]
            far_across[k][f] = []
            for i, s in enumerate((-1, 1)):
                across[k][f][i].wait_recv()
                slot = at(f, s)
                block = out.at[slot, parts[1 + i]]
                far_across[k][f].append(box.push(block, block, dp=at(0, -s)))
                to_sibling(k, slot)

        return step

    def from_far_across(k, f):
        def step():
            for copy in far_across[k][f]:
                copy.wait_recv()
            to_sibling(k, kinds[k][1](f, 2))

        return step

    def close():
        for copy in shared:
            copy.wait_recv()

    steps = [open_up, from_near(0, -1), from_near(1, 1), from_far(0), from_far(1)]
    steps += [from_across(k, f) for f in (0, -1, 1, 2) for k in range(2)]
    steps += [from_far_across(k, f) for f in (0, -1, 1, 2) for k in range(2)]
    return steps + [close]


def gather_peers():
    return [moved(1, 0), moved(-1, 0), moved(0, 1), moved(0, -1), moved(0, 0, True)]


GATHER_COPIES = 71


def first_gather_kernel(wide_ref, thin_ref, wide_out, thin_out, thin_own, send, recv, local):
    m = lax.axis_index("mp")
    mp_peers = [lax.rem(m + k, 4) for k in (1, 2, 3)]
    greet(gather_peers(), mp_peers)
    me = moved(0, 0)
    box = Mailbox(send, recv)
    rows = thin_ref.shape[0]
    mine = pl.ds(pl.multiple_of(m * rows, rows), rows)
    crossing = [box.push(thin_ref, thin_own.at[mine], mp=peer) for peer in mp_peers]
    keep_wide = pltpu.make_async_copy(wide_ref, wide_out.at[me], local.at[0])
    keep_wide.start()
    keep_thin = pltpu.make_async_copy(thin_ref, thin_own.at[mine], local.at[1])
    keep_thin.start()
    wide_steps = gather_steps(box, wide_ref, wide_out)
    thin_steps = gather_steps(box, thin_own, thin_out)
    wide_steps[0]()
    keep_thin.wait()
    for copy in crossing:
        copy.wait_recv()
    keep_thin_out = pltpu.make_async_copy(thin_own, thin_out.at[me], local.at[2])
    keep_thin_out.start()
    thin_steps[0]()
    for one, two in zip(wide_steps[1:], thin_steps[1:]):
        one()
        two()
    keep_wide.wait()
    keep_thin_out.wait()
    box.drain()


def first_gather(wide, thin):
    count = 2 * GATHER_COPIES + 3
    rows, cols = thin.shape
    anywhere = pl.BlockSpec(memory_space=pl.ANY)
    return pl.pallas_call(
        first_gather_kernel,
        out_shape=(
            jax.ShapeDtypeStruct((32,) + wide.shape, wide.dtype),
            jax.ShapeDtypeStruct((32, 4 * rows, cols), thin.dtype),
        ),
        in_specs=[anywhere, anywhere],
        out_specs=(anywhere, anywhere),
        scratch_shapes=[
            pltpu.VMEM((4 * rows, cols), thin.dtype),
            pltpu.SemaphoreType.DMA((count,)),
            pltpu.SemaphoreType.DMA((count,)),
            pltpu.SemaphoreType.DMA((3,)),
        ],
        compiler_params=pltpu.CompilerParams(collective_id=0, has_side_effects=True),
        name="gather_first",
    )(wide, thin)


def half_dot(left, right, dims=(((1,), (0,)), ((), ()))):
    high = right.astype(NARROW)
    low = (right - high.astype(WIDE)).astype(NARROW)
    return lax.dot_general(left, high, dims, preferred_element_type=WIDE) + lax.dot_general(
        left, low, dims, preferred_element_type=WIDE
    )


TURNED = (((0,), (0,)), ((), ()))


def two_parts(value):
    high = value.astype(NARROW)
    return high, (value - high.astype(WIDE)).astype(NARROW)


def wide_dot(left, right, left_dim=1, right_dim=0):
    left_high, left_low = two_parts(left)
    right_high, right_low = two_parts(right)

    def part(one, two):
        return lax.dot_general(one, two, (((left_dim,), (right_dim,)), ((), ())), preferred_element_type=WIDE)

    return part(left_high, right_high) + (part(left_high, right_low) + part(left_low, right_high))


def column_of(aux, index):
    lanes = lax.broadcasted_iota(jnp.int32, aux.shape, 1)
    return jnp.sum(jnp.where(lanes == index, aux, 0.0), axis=1, keepdims=True)


def convolve(pre_ref, taps_ref, part, aux, work):
    count = aux.shape[0]
    work[...] = pre_ref[...].astype(WIDE)
    total = work[pl.ds(HALO, count)] * taps_ref[part : part + 1, :]
    for j in range(1, KW):
        total = total + (
            work[pl.ds(HALO - j, count)] * aux[:, j : j + 1] * taps_ref[3 * j + part : 3 * j + part + 1, :]
        )
    return total


def masks(aux, seg_row):
    same = aux[:, 6:7] == seg_row
    shape = (aux.shape[0], aux.shape[0])
    row = lax.broadcasted_iota(jnp.int32, shape, 0)
    col = lax.broadcasted_iota(jnp.int32, shape, 1)
    return row, col, same


def lower_inverse(lower, row, col):
    near = jnp.where(row // 8 == col // 8, lower, 0.0)
    square = wide_dot(near, near)
    inverse = jnp.where(row == col, 1.0, 0.0) - near
    inverse = inverse + wide_dot(inverse, square)
    inverse = inverse + wide_dot(inverse, wide_dot(square, square))
    size = 8
    while size < lower.shape[0]:
        link = jnp.where((row // (2 * size) == col // (2 * size)) & (row // size != col // size), lower, 0.0)
        inverse = inverse - wide_dot(inverse, wide_dot(link, inverse))
        size *= 2
    return inverse


def mixer_forward_kernel(
    q_pre, k_pre, v_pre, taps_ref, aux_ref, seg_ref,
    out_ref, reach_ref, map_ref, offset_ref, q_ref, k_ref, v_ref, t_ref, w_ref, u_ref, work,
):
    head = pl.program_id(0)
    aux = aux_ref[...]
    rate = column_of(aux, 8 + head)
    linked, ending = aux[:, 4:5], aux[:, 5:6]
    row, col, same = masks(aux, seg_ref[0:1, :])
    acts = []
    for part, pre_ref in enumerate((q_pre, k_pre, v_pre)):
        conv = convolve(pre_ref, taps_ref, part, aux, work)
        acts.append(conv * jax.nn.sigmoid(conv))
    q = acts[0] * lax.rsqrt(jnp.sum(acts[0] * acts[0], axis=1, keepdims=True) + EPSILON)
    k = acts[1] * lax.rsqrt(jnp.sum(acts[1] * acts[1], axis=1, keepdims=True) + EPSILON)
    v = acts[2]
    q_ref[...] = q
    k_ref[...] = k
    v_ref[...] = v
    gram = wide_dot(k, k, 1, 1)
    inverse = lower_inverse(jnp.where((row > col) & same, gram * rate, 0.0), row, col)
    t_ref[0] = inverse
    written = wide_dot(inverse, jnp.concatenate([v, k * linked], axis=1) * rate)
    w_ref[...] = written[:, :DH]
    u_ref[...] = written[:, DH:]
    scores = jnp.where((row >= col) & same, wide_dot(q, k, 1, 1), 0.0)
    mixed = wide_dot(scores, written)
    out_ref[...] = mixed[:, :DH]
    reach_ref[...] = q * linked - mixed[:, DH:]
    ends = wide_dot(k * ending, written, 0, 0)
    offset_ref[0] = ends[:, :DH].astype(offset_ref.dtype)
    eye = jnp.where(row[:DH, :DH] == col[:DH, :DH], 1.0, 0.0)
    last = aux[aux.shape[0] - 1 :, 4:5]
    map_ref[0] = (eye * last - ends[:, DH:]).astype(map_ref.dtype)


def mixer_forward(pre, taps, aux, seg_row):
    count = aux.shape[0]
    heads = pre.shape[1] // (3 * DH)

    def part(p):
        return pl.BlockSpec((pre.shape[0], DH), lambda h: (0, p * heads + h))

    whole = lambda x: pl.BlockSpec(x.shape, lambda h: (0,) * x.ndim)
    by_head = pl.BlockSpec((count, DH), lambda h: (0, h))
    square = lambda n: pl.BlockSpec((1, n, n), lambda h: (h, 0, 0))
    wide = jax.ShapeDtypeStruct((count, heads * DH), WIDE)
    small = jax.ShapeDtypeStruct((heads, DH, DH), NARROW)
    return pl.pallas_call(
        mixer_forward_kernel,
        grid=(heads,),
        out_shape=(wide, wide, small, small, wide, wide, wide,
                   jax.ShapeDtypeStruct((heads, count, count), WIDE), wide, wide),
        in_specs=[part(0), part(1), part(2), pl.BlockSpec((16, DH), lambda h: (0, h)), whole(aux), whole(seg_row)],
        out_specs=(by_head, by_head, square(DH), square(DH), by_head, by_head, by_head, square(count), by_head, by_head),
        scratch_shapes=[pltpu.VMEM((pre.shape[0], DH), WIDE)],
        compiler_params=pltpu.CompilerParams(vmem_limit_bytes=40 << 20),
        name="mixer_forward",
    )(pre, pre, pre, taps, aux, seg_row)


def each(step, *lists):
    return [step(*items) for items in zip(*lists)]


def mixer_backward(heads, pre_ref, taps_ref, aux, seg_row, kept, state_ref, grad_ref, d_out_ref, d_ext, work):
    q_ref, k_ref, v_ref, t_ref, w_ref, u_ref = kept
    count = aux.shape[0]
    inner = d_out_ref.shape[1]
    linked, ending = aux[:, 4:5], aux[:, 5:6]
    row, col, same = masks(aux, seg_row)
    upto = (row >= col) & same
    below = (row > col) & same

    def take(ref):
        return [ref[:, h * DH : (h + 1) * DH] for h in heads]

    rate = [aux[:, 8 + h : 9 + h] for h in heads]
    q, k, v, d_out = take(q_ref), take(k_ref), take(v_ref), take(d_out_ref)
    state, grad = [state_ref[h] for h in heads], [grad_ref[h] for h in heads]
    written = each(lambda w, u, s: w - wide_dot(u, s), take(w_ref), take(u_ref), state)
    scores = each(lambda a, b: jnp.where(upto, wide_dot(a, b, 1, 1), 0.0), q, k)
    d_written = each(
        lambda a, d, b, g: wide_dot(a, d, 0, 0) + wide_dot(b * ending, g), scores, d_out, k, grad
    )
    d_right = each(lambda t, d: wide_dot(t, d, 0, 0), [t_ref[h] for h in heads], d_written)
    d_scores = each(lambda d, w: jnp.where(upto, wide_dot(d, w, 1, 1), 0.0), d_out, written)
    d_lower = each(lambda d, w: jnp.where(below, -wide_dot(d, w, 1, 1), 0.0), d_right, written)
    d_q = each(
        lambda ds, b, d, s: wide_dot(ds, b) + linked * wide_dot(d, s, 1, 1), d_scores, k, d_out, state
    )
    d_k = each(
        lambda ds, a, w, g: wide_dot(ds, a, 0, 0) + ending * wide_dot(w, g, 1, 1), d_scores, q, written, grad
    )
    d_rate = each(
        lambda d, a, b, s: jnp.sum(d * (a - linked * wide_dot(b, s)), axis=1, keepdims=True), d_right, v, k, state
    )
    d_rate = each(
        lambda r, d, b: r + jnp.sum(d * wide_dot(b, b, 1, 1), axis=1, keepdims=True), d_rate, d_lower, k
    )
    d_k = each(lambda dk, r, d, s: dk - (linked * r) * wide_dot(d, s, 1, 1), d_k, rate, d_right, state)
    d_gram = each(lambda d, r: d * r, d_lower, rate)
    d_k = each(lambda dk, d, b: dk + wide_dot(d, b) + wide_dot(d, b, 0, 0), d_k, d_gram, k)
    d_v = each(lambda r, d: r * d, rate, d_right)
    for i, h in enumerate(heads):
        for part, (unit, d) in enumerate(((q[i], d_q[i]), (k[i], d_k[i]), (None, d_v[i]))):
            cols = slice(h * DH, (h + 1) * DH)
            pre_cols = slice(part * inner + h * DH, part * inner + (h + 1) * DH)
            conv = convolve(pre_ref.at[:, pre_cols], taps_ref.at[:, cols], part, aux, work)
            gate = jax.nn.sigmoid(conv)
            if unit is not None:
                act = conv * gate
                scale = lax.rsqrt(jnp.sum(act * act, axis=1, keepdims=True) + EPSILON)
                d = (d - unit * jnp.sum(unit * d, axis=1, keepdims=True)) * scale
            d_conv = d * gate * (1.0 + conv * (1.0 - gate))
            d_ext[part, :HALO, cols] = jnp.zeros((HALO, DH), WIDE)
            d_ext[part, HALO:, cols] = d_conv * taps_ref[part : part + 1, cols]
            for j in range(1, KW):
                term = d_conv * taps_ref[3 * j + part : 3 * j + part + 1, cols] * aux[:, j : j + 1]
                d_ext[part, pl.ds(HALO - j, count), cols] += term
    return each(lambda d, r: d * r * (1.0 - r), d_rate, rate)


def inverse_rms(values):
    return lax.rsqrt(jnp.mean(values * values, axis=-1, keepdims=True) + EPSILON)


def norm_back(values, scale, gain, grad_out):
    weighted = grad_out * gain
    return scale * weighted - values * scale**3 * jnp.mean(weighted * values, axis=-1, keepdims=True)


def dot(left, right):
    return jnp.dot(left, right, preferred_element_type=WIDE)


def dot_nt(left, right):
    return lax.dot_general(left, right, (((1,), (1,)), ((), ())), preferred_element_type=WIDE)


def dot_tn(left, right):
    return lax.dot_general(left, right, (((0,), (0,)), ((), ())), preferred_element_type=WIDE)


def shifted(value, steps):
    count = lax.axis_size("dp")
    pairs = [(i, i + steps) for i in range(max(0, -steps), min(count, count - steps))]
    return lax.ppermute(value, "dp", pairs)


def pack_ranks(ranks, blocks):
    flat = ranks.reshape(-1, 128)
    flat = jnp.pad(flat, ((0, 64 * blocks - flat.shape[0]), (0, 0)))
    return flat.reshape(blocks, 64, 128).transpose(1, 0, 2).reshape(64, blocks * 128)


def unpack_ranks(packed, tiles):
    blocks = packed.shape[2] // 128
    flat = packed.reshape(32, 64, blocks, 128).transpose(0, 2, 1, 3).reshape(32, 64 * blocks, 128)
    return flat[:, : 4 * tiles].reshape(128, tiles * 128)


class Chain:
    def __init__(self, box, a_ref, b_ref, g_ref, sib, chip_a, chip_b, chip_g, row_a, row_b, row_g, pass_on):
        self.box, self.a_ref, self.b_ref, self.g_ref = box, a_ref, b_ref, g_ref
        self.sib, self.pass_on = sib, pass_on
        self.chip_a, self.chip_b, self.chip_g = chip_a, chip_b, chip_g
        self.row_a, self.row_b, self.row_g = row_a, row_b, row_g
        self.y, self.z, self.c = coords()
        self.first = self.c == 0
        self.sibling = moved(0, 0, True)
        self.z_peers = {k: moved(0, k) for k in (1, 2, 3)}
        self.y_peers = {k: moved(k, 0) for k in (1, 2, 3)}
        self.mine = pl.ds(pl.multiple_of(2 * self.c, 2), 2)
        self.theirs = pl.ds(pl.multiple_of(2 * (1 - self.c), 2), 2)

    def peers(self):
        return [self.sibling] + list(self.z_peers.values()) + list(self.y_peers.values())

    def swap(self, ref, slot):
        return self.box.push(ref.at[self.theirs], self.sib.at[slot], dp=self.sibling)

    def ordered(self, ref, slot, h):
        own, other = ref[2 * self.c + h], self.sib[slot, h]
        return jnp.where(self.first, own, other), jnp.where(self.first, other, own)

    def spread(self, refs, place, peers):
        return [self.box.push(ref.at[place], ref.at[place], dp=peers[k]) for k in (2, 1, 3) for ref in refs]

    def start_forward(self):
        self.pair = [self.swap(self.a_ref, 0), self.swap(self.b_ref, 1)]

    def chips_forward(self):
        for copy in self.pair:
            copy.wait_recv()
        self.lower, self.upper_a = [], []
        for h in range(2):
            a_low, a_high = self.ordered(self.a_ref, 0, h)
            b_low, b_high = self.ordered(self.b_ref, 1, h)
            self.lower.append((a_low, b_low))
            self.upper_a.append(a_high)
            self.chip_a[self.z, h] = lax.dot(a_high, a_low, preferred_element_type=WIDE).astype(NARROW)
            self.chip_b[self.z, h] = (
                lax.dot(a_high, b_low, preferred_element_type=WIDE) + b_high.astype(WIDE)
            ).astype(NARROW)
        self.ring = self.spread((self.chip_a, self.chip_b), self.z, self.z_peers)

    def rows_forward(self):
        for copy in self.ring:
            copy.wait_recv()
        for h in range(2):
            total_a, total_b = self.chip_a[0, h].astype(WIDE), self.chip_b[0, h].astype(WIDE)
            for i in range(1, 4):
                total_a = half_dot(self.chip_a[i, h], total_a)
                total_b = half_dot(self.chip_a[i, h], total_b) + self.chip_b[i, h].astype(WIDE)
            self.row_a[self.y, h] = total_a.astype(NARROW)
            self.row_b[self.y, h] = total_b.astype(NARROW)
        self.ring = self.spread((self.row_a, self.row_b), self.y, self.y_peers)

    def finish_forward(self, out):
        for copy in self.ring:
            copy.wait_recv()
        for h in range(2):
            state = jnp.zeros((DH, DH), WIDE)
            for i in range(3):
                longer = half_dot(self.row_a[i, h], state) + self.row_b[i, h].astype(WIDE)
                state = jnp.where(i < self.y, longer, state)
            for i in range(3):
                longer = half_dot(self.chip_a[i, h], state) + self.chip_b[i, h].astype(WIDE)
                state = jnp.where(i < self.z, longer, state)
            a_low, b_low = self.lower[h]
            middle = half_dot(a_low, state) + b_low.astype(WIDE)
            out[2 * self.c + h] = jnp.where(self.first, state, middle)
            self.pass_on[0, h] = jnp.where(self.first, middle, state)
        self.box.push(self.pass_on.at[0], out.at[self.mine], dp=self.sibling).wait_recv()

    def start_backward(self):
        self.pair = [self.swap(self.g_ref, 2)]

    def chips_backward(self):
        for copy in self.pair:
            copy.wait_recv()
        self.upper_g = []
        for h in range(2):
            a_low, _ = self.ordered(self.a_ref, 0, h)
            g_low, g_high = self.ordered(self.g_ref, 2, h)
            self.upper_g.append(g_high)
            self.chip_g[self.z, h] = (
                lax.dot_general(a_low, g_high, TURNED, preferred_element_type=WIDE) + g_low.astype(WIDE)
            ).astype(NARROW)
        self.ring = self.spread((self.chip_g,), self.z, self.z_peers)

    def rows_backward(self):
        for copy in self.ring:
            copy.wait_recv()
        for h in range(2):
            total = self.chip_g[3, h].astype(WIDE)
            for i in (2, 1, 0):
                total = half_dot(self.chip_a[i, h], total, TURNED) + self.chip_g[i, h].astype(WIDE)
            self.row_g[self.y, h] = total.astype(NARROW)
        self.ring = self.spread((self.row_g,), self.y, self.y_peers)

    def finish_backward(self, out):
        for copy in self.ring:
            copy.wait_recv()
        for h in range(2):
            grad = jnp.zeros((DH, DH), WIDE)
            for i in (3, 2, 1):
                longer = half_dot(self.row_a[i, h], grad, TURNED) + self.row_g[i, h].astype(WIDE)
                grad = jnp.where(i > self.y, longer, grad)
            for i in (3, 2, 1):
                longer = half_dot(self.chip_a[i, h], grad, TURNED) + self.chip_g[i, h].astype(WIDE)
                grad = jnp.where(i > self.z, longer, grad)
            _, a_high = self.ordered(self.a_ref, 0, h)
            middle = half_dot(a_high, grad, TURNED) + self.upper_g[h].astype(WIDE)
            out[2 * self.c + h] = jnp.where(self.first, middle, grad)
            self.pass_on[1, h] = jnp.where(self.first, grad, middle)
        self.box.push(self.pass_on.at[1], out.at[self.mine], dp=self.sibling).wait_recv()


def columns(i, width):
    return pl.ds(pl.multiple_of(i * width, width), width)


class MpSum:
    ORDER = (2, 1, 3)

    def __init__(self, box, part, landed):
        self.box, self.part, self.landed = box, part, landed
        self.m = lax.axis_index("mp")
        self.peers = {k: lax.rem(self.m + k, 4) for k in (1, 2, 3)}
        self.copies = []

    def owner(self, k):
        return lax.rem(self.m + k, 4)

    def send(self, k):
        self.copies.append(self.box.push(self.part.at[k], self.landed.at[k - 1], mp=self.peers[k]))

    def total(self):
        for copy in self.copies:
            copy.wait_recv()
        total = self.part[0].astype(WIDE)
        for k in range(3):
            total = total + self.landed[k].astype(WIDE)
        return total

    def share(self, out, width):
        block = out.at[:, columns(self.m, width)]
        return [self.box.push(block, block, mp=self.peers[k]) for k in self.ORDER]


def middle_kernel(
    a_ref, b_ref, out_zero, reach, picks_ref, x_ref, g_own, norm_ref, gain_ref, ranks_ref, thin_ref, wide_ref,
    output, state_out, grad_out, d_one_out, d_mixer_out, g_b_ffn, g_a_down, g_a_out, g_shared,
    w_out, w_gu, w_down, a_two, b_res, ranks, g_full, sib, chip_a, chip_b, chip_g, row_a, row_b, row_g, pass_on, g_maps,
    mixer_out, normed, part, landed, branch, hidden_one, xn_two, gate, up, hidden, ffn_part, ffn_landed,
    d_gate_up, d_xn, extra, extra_landed, d_branch, e_down_ref, u_two_ref,
    send, recv, local,
):
    count = x_ref.shape[0]
    heads = a_ref.shape[0]
    inner = heads * DH
    ff = gate.shape[1]
    m = lax.axis_index("mp")
    box = Mailbox(send, recv)
    chain = Chain(box, a_ref, b_ref, g_maps, sib, chip_a, chip_b, chip_g, row_a, row_b, row_g, pass_on)
    mp_peers = {k: lax.rem(m + k, 4) for k in (1, 2, 3)}
    greet(chain.peers(), list(mp_peers.values()))
    chain.start_forward()
    share = g_own.shape[1]
    g_full[:, columns(m, share)] = g_own[...]
    g_sent = [box.push(g_own, g_full.at[:, columns(m, share)], mp=mp_peers[k]) for k in MpSum.ORDER]
    loads = [
        pltpu.make_async_copy(wide_ref.at[:, pl.ds(0, inner)], w_out, local.at[0]),
        pltpu.make_async_copy(thin_ref.at[:, pl.ds(512, 256)], a_two, local.at[1]),
        pltpu.make_async_copy(thin_ref.at[:, pl.ds(768, 256)], b_res, local.at[2]),
        pltpu.make_async_copy(wide_ref.at[:, pl.ds(inner, 2 * ff)], w_gu, local.at[3]),
        pltpu.make_async_copy(wide_ref.at[:, pl.ds(inner + 2 * ff, ff)], w_down, local.at[4]),
    ]
    for load in loads:
        load.start()
    row = lax.broadcasted_iota(jnp.int32, (128, 256), 0)
    col = lax.broadcasted_iota(jnp.int32, (128, 256), 1)
    pick_rows = jnp.where(col == (row // 4) * 8 + lax.rem(row, 4), 1.0, 0.0).astype(NARROW)
    width = ranks_ref.shape[1]
    for start in range(0, width, 1280):
        piece = slice(start, min(start + 1280, width))
        ranks[:, piece] = dot(pick_rows, ranks_ref[:, piece]).astype(NARROW)
    picks = picks_ref[...]
    chain.chips_forward()
    chain.rows_forward()
    chain.finish_forward(state_out)

    for h in range(heads):
        cols = slice(h * DH, (h + 1) * DH)
        rows = out_zero[:, cols] + wide_dot(reach[:, cols], state_out[h])
        mixer_out[:, cols] = rows
        normed[:, cols] = (rows * inverse_rms(rows) * gain_ref[0:1, :]).astype(NARROW)
    at_gate, at_up, at_out, at_down = 0, ff, 2 * ff, 2 * ff + inner
    a_out = ranks.at[:, pl.ds(at_out, inner)]
    a_down = ranks.at[:, pl.ds(at_down, ff)]
    u_out = (dot_nt(normed[...], a_out[...]) * picks).astype(NARROW)
    for load in loads[:3]:
        load.wait()
    b_mix, b_down = b_res.at[:, pl.ds(0, 128)], b_res.at[:, pl.ds(128, 128)]
    one = MpSum(box, part.at[0], landed.at[0])
    for k in (2, 1, 3, 0):
        rows = columns(one.owner(k), share)
        part[0, k] = (dot_nt(normed[...], w_out[rows, :]) + dot_nt(u_out, b_mix[rows, :])).astype(NARROW)
        if k:
            one.send(k)
    branch[:, columns(m, share)] = one.total().astype(NARROW)
    shared = one.share(branch, share)
    for copy in g_sent + shared:
        copy.wait_recv()

    rows = x_ref[...].astype(WIDE) + branch[...].astype(WIDE)
    hidden_one[...] = rows
    scale_two = inverse_rms(rows)
    xn_two[...] = (rows * scale_two * norm_ref[0:1, :]).astype(NARROW)
    two_picks = jnp.concatenate([picks, picks], axis=1)
    u_two_ref[...] = (dot(xn_two[...], a_two[...]) * two_picks).astype(NARROW)
    loads[3].wait()
    gate[...] = dot(xn_two[...], w_gu[:, :ff]) + dot(u_two_ref[:, :128], ranks[:, at_gate : at_gate + ff])
    up[...] = dot(xn_two[...], w_gu[:, ff:]) + dot(u_two_ref[:, 128:], ranks[:, at_up : at_up + ff])
    hidden[...] = (gate[...] * jax.nn.sigmoid(gate[...]) * up[...]).astype(NARROW)
    loads[4].wait()

    e_down = (dot(g_full[...], b_down[...]) * picks).astype(NARROW)
    e_down_ref[...] = e_down
    d_hidden = dot(g_full[...], w_down[...]) + dot(e_down, a_down[...])
    sig = jax.nn.sigmoid(gate[...])
    d_gate_up[:, :ff] = (d_hidden * up[...] * sig * (1.0 + gate[...] * (1.0 - sig))).astype(NARROW)
    d_gate_up[:, ff:] = (d_hidden * gate[...] * sig).astype(NARROW)
    e_two = [
        (dot_nt(d_gate_up[:, j * ff : (j + 1) * ff], ranks[:, j * ff : (j + 1) * ff]) * picks).astype(NARROW)
        for j in range(2)
    ]
    two = MpSum(box, part.at[1], landed.at[1])
    for k in (2, 1, 3, 0):
        rows = columns(two.owner(k), share)
        part[1, k] = (
            dot_nt(d_gate_up[...], w_gu[rows, :]) + dot_nt(jnp.concatenate(e_two, axis=1), a_two[rows, :])
        ).astype(NARROW)
        if k:
            two.send(k)
    u_down = (dot_nt(hidden[...], a_down[...]) * picks).astype(NARROW)
    for j, value in enumerate((e_two[0], e_two[1], u_out, u_down)):
        extra[j] = value
    d_xn[:, columns(m, share)] = two.total().astype(NARROW)
    shared = two.share(d_xn, share)
    extra_sent = [box.push(extra.at[mp_peers[k]], extra_landed.at[k - 1], mp=mp_peers[k]) for k in MpSum.ORDER]
    three = MpSum(box, ffn_part, ffn_landed)
    for k in (2, 1, 3, 0):
        rows = columns(three.owner(k), share)
        ffn_part[k] = (dot_nt(hidden[...], w_down[rows, :]) + dot_nt(u_down, b_down[rows, :])).astype(NARROW)
    for copy in shared:
        copy.wait_recv()
    for k in MpSum.ORDER:
        three.send(k)

    rows = hidden_one[...]
    scale_two = inverse_rms(rows)
    d_one = g_full[...].astype(WIDE) + norm_back(rows, scale_two, norm_ref[0:1, :], d_xn[...].astype(WIDE))
    d_one_out[...] = d_one
    d_branch[...] = d_one.astype(NARROW)
    e_out = (dot(d_branch[...], b_mix[...]) * picks).astype(NARROW)
    d_normed = dot(d_branch[...], w_out[...]) + dot(e_out, a_out[...])
    for h in range(heads):
        cols = slice(h * DH, (h + 1) * DH)
        rows = mixer_out[:, cols]
        d_rows = norm_back(rows, inverse_rms(rows), gain_ref[0:1, :], d_normed[:, cols])
        d_mixer_out[:, cols] = d_rows
        g_maps[h] = wide_dot(reach[:, cols], d_rows, 0, 0).astype(NARROW)
    chain.start_backward()
    g_a_out[...] = dot_tn(e_out, normed[...]).astype(NARROW)
    chain.chips_backward()
    for j in range(2):
        cols = slice(j * ff, (j + 1) * ff)
        g_b_ffn[:, cols] = dot_tn(u_two_ref[:, j * 128 : (j + 1) * 128], d_gate_up[:, cols]).astype(NARROW)
    chain.rows_backward()
    g_a_down[...] = dot_tn(e_down_ref[...], hidden[...]).astype(NARROW)
    for copy in extra_sent:
        copy.wait_recv()
    factor = extra[m].astype(WIDE)
    for k in range(3):
        factor = factor + extra_landed[k].astype(WIDE)
    left = jnp.where(m < 2, xn_two[...], jnp.where(m == 2, d_branch[...], g_full[...]))
    g_shared[...] = dot_tn(left, factor.astype(NARROW)).astype(NARROW)
    chain.finish_backward(grad_out)
    output[...] = (hidden_one[:, columns(m, share)] + three.total()).astype(NARROW)
    box.drain()


def middle(maps, offsets, out_zero, reach, picks, x, g, norm, gain, ranks, thin, wide):
    count, inner = out_zero.shape
    heads = maps.shape[0]
    model = x.shape[1]
    share = g.shape[1]
    ff = (wide.shape[1] - inner) // 3
    vmem = pl.BlockSpec(memory_space=pltpu.VMEM)
    anywhere = pl.BlockSpec(memory_space=pl.ANY)
    two = (2, DH, DH)
    copies = 2 + 6 + 6 + 1 + 1 + 3 + 3 + 1 + 3 + 6 + 6 + 3 + 3
    results = [
        ((count, share), NARROW),
        ((heads, DH, DH), WIDE),
        ((heads, DH, DH), WIDE),
        ((count, model), WIDE),
        ((count, inner), WIDE),
        ((128, 2 * ff), NARROW),
        ((128, ff), NARROW),
        ((128, inner), NARROW),
        ((model, 128), NARROW),
    ]
    scratch = [
        ((model, inner), NARROW),
        ((model, 2 * ff), NARROW),
        ((model, ff), NARROW),
        ((model, 256), NARROW),
        ((model, 256), NARROW),
        ((128, 3 * ff + inner), NARROW),
        ((count, model), NARROW),
        ((3,) + two, NARROW),
        ((4,) + two, NARROW),
        ((4,) + two, NARROW),
        ((4,) + two, NARROW),
        ((4,) + two, NARROW),
        ((4,) + two, NARROW),
        ((4,) + two, NARROW),
        ((2,) + two, WIDE),
        ((heads, DH, DH), NARROW),
        ((count, inner), WIDE),
        ((count, inner), NARROW),
        ((2, 4, count, share), NARROW),
        ((2, 3, count, share), NARROW),
        ((count, model), NARROW),
        ((count, model), WIDE),
        ((count, model), NARROW),
        ((count, ff), WIDE),
        ((count, ff), WIDE),
        ((count, ff), NARROW),
        ((4, count, share), NARROW),
        ((3, count, share), NARROW),
        ((count, 2 * ff), NARROW),
        ((count, model), NARROW),
        ((4, count, 128), NARROW),
        ((3, count, 128), NARROW),
        ((count, model), NARROW),
        ((count, 128), NARROW),
        ((count, 256), NARROW),
    ]
    return pl.pallas_call(
        middle_kernel,
        out_shape=tuple(jax.ShapeDtypeStruct(*r) for r in results),
        in_specs=[vmem] * 10 + [anywhere] * 2,
        out_specs=tuple([vmem] * len(results)),
        scratch_shapes=[pltpu.VMEM(*s) for s in scratch]
        + [
            pltpu.SemaphoreType.DMA((copies,)),
            pltpu.SemaphoreType.DMA((copies,)),
            pltpu.SemaphoreType.DMA((5,)),
        ],
        compiler_params=pltpu.CompilerParams(
            collective_id=2, has_side_effects=True, vmem_limit_bytes=60 << 20
        ),
        name="middle",
    )(maps, offsets, out_zero, reach, picks, x, g, norm, gain, ranks, thin, wide)


class DpSum:
    SCRATCH = 6

    @staticmethod
    def scratch(rows, width):
        small = rows // 4
        return [
            ((2, 4, rows, width), NARROW),
            ((4, rows, width), NARROW),
            ((3, rows, width), NARROW),
            ((4, small, width), WIDE),
            ((3, small, width), WIDE),
            ((small, width), WIDE),
        ]

    def __init__(self, box, full, landed_core, landed_y, by_z, landed_z, result):
        self.box, self.full, self.landed_core = box, full, landed_core
        self.landed_y, self.by_z, self.landed_z, self.result = landed_y, by_z, landed_z, result
        self.y, self.z, self.c = coords()

    def over_cores(self):
        self.pair = self.box.push(self.full.at[1 - self.c], self.landed_core, dp=moved(0, 0, True))

    def over_y(self):
        self.pair.wait_recv()
        mine = self.full.at[self.c]
        for i in range(4):
            mine[i] = (mine[i].astype(WIDE) + self.landed_core[i].astype(WIDE)).astype(NARROW)
        self.copies = [
            self.box.push(mine.at[lax.rem(self.y + k, 4)], self.landed_y.at[k - 1], dp=moved(k, 0)) for k in (2, 1, 3)
        ]

    def over_z(self):
        for copy in self.copies:
            copy.wait_recv()
        total = self.full[self.c, self.y].astype(WIDE)
        for k in range(3):
            total = total + self.landed_y[k].astype(WIDE)
        self.by_z[...] = total.reshape(self.by_z.shape)
        self.copies = [
            self.box.push(self.by_z.at[lax.rem(self.z + k, 4)], self.landed_z.at[k - 1], dp=moved(0, k))
            for k in (2, 1, 3)
        ]

    def finish(self):
        for copy in self.copies:
            copy.wait_recv()
        total = self.by_z[self.z]
        for k in range(3):
            total = total + self.landed_z[k]
        self.result[...] = total


def tail_kernel(
    pre_ref, taps_ref, aux_ref, seg_ref, q_ref, k_ref, v_ref, t_ref, w_ref, u_map_ref, state_ref, grad_ref, d_out_ref,
    u_ref, xn_ref, x_ref, d_one_ref, norm_ref, picks_ref, ranks, shared_two, g_b_ffn, g_a_out, g_a_down,
    wide_ref, thin_ref,
    grad_input, out_a_in, out_heads, out_beta, out_a_out, out_ffn, out_a_down, out_res,
    w_in, a_one, d_ext, work, halo, d_pre, e_one, part, landed, extra_landed, sums, sums_landed, pair, early_pair, ends,
    *rest,
):
    one, two, three, four = (rest[i * DpSum.SCRATCH : (i + 1) * DpSum.SCRATCH] for i in range(4))
    send, recv, local = rest[4 * DpSum.SCRATCH :]
    count, model = x_ref.shape
    inner = d_out_ref.shape[1]
    heads = inner // DH
    ff = g_a_down.shape[1]
    m = lax.axis_index("mp")
    c = lax.rem(lax.axis_index("dp"), 2)
    before, after = (lax.rem(lax.axis_index("dp") + k, 32) for k in (31, 1))
    mp_peers = {k: lax.rem(m + k, 4) for k in (1, 2, 3)}
    dp_peers = [before, after, moved(0, 0, True)]
    dp_peers += [moved(k, 0) for k in (1, 2, 3)] + [moved(0, k) for k in (1, 2, 3)]
    greet(dp_peers, list(mp_peers.values()))
    box = Mailbox(send, recv)
    early_sum, heads_sum, two_sum, one_sum = (DpSum(box, *refs) for refs in (four, one, two, three))

    def halves(refs, values):
        half = refs[0].shape[3]
        missing = 2 * half - sum(value.shape[1] for value in values)
        values = values + [jnp.zeros((128, missing), NARROW)] if missing else values
        values = jnp.concatenate(values, axis=1)
        for i in range(2):
            refs[0][i] = values[:, i * half : (i + 1) * half].reshape(4, 32, half)

    def by_core(value):
        value = value.reshape(4, 4, 2, model // 32, 128)
        return [value[:, :, i].reshape(4, model // 8, 128) for i in range(2)]

    halves(four, [g_b_ffn[...], g_a_out[...], g_a_down[...]])
    early_sum.over_cores()
    for i, value in enumerate(by_core(shared_two[...])):
        two[0][i] = value
    two_sum.over_cores()
    loads = [
        pltpu.make_async_copy(wide_ref.at[:, pl.ds(0, w_in.shape[1])], w_in, local.at[0]),
        pltpu.make_async_copy(thin_ref.at[:, pl.ds(0, a_one.shape[1])], a_one, local.at[1]),
    ]
    for load in loads:
        load.start()
    aux = aux_ref[...]
    kept = (q_ref, k_ref, v_ref, t_ref, w_ref, u_map_ref)
    lanes = lax.broadcasted_iota(jnp.int32, aux.shape, 1)
    d_logit = jnp.zeros(aux.shape, WIDE)
    for first in range(0, heads, 2):
        some = list(range(first, min(first + 2, heads)))
        found = mixer_backward(
            some, pre_ref, taps_ref, aux, seg_ref[0:1, :], kept, state_ref, grad_ref, d_out_ref, d_ext, work
        )
        for h, value in zip(some, found):
            d_logit = jnp.where(lanes == h, value, d_logit)
        if first == 0:
            early_sum.over_y()
            two_sum.over_y()
    edges = [box.push(d_ext.at[i, pl.ds(HALO - 8, 8)], halo.at[i], dp=before) for i in range(3)]
    early_sum.over_z()
    two_sum.over_z()
    picks = picks_ref[...]
    d_logit = d_logit.astype(NARROW)
    for copy in edges:
        copy.wait_recv()
    for i in range(3):
        ref = d_ext.at[i]
        cols = slice(i * inner, (i + 1) * inner)
        d_pre[: count - 16, cols] = ref[HALO : HALO + count - 16].astype(NARROW)
        ending = ref[HALO + count - 16 :]
        d_pre[count - 16 :, cols] = jnp.concatenate([ending[:8], ending[8:] + halo[i]], axis=0).astype(NARROW)
    for j in range(3):
        cols = slice(j * inner, (j + 1) * inner)
        e_one[j] = (dot_nt(d_pre[:, cols], ranks[:, cols]) * picks).astype(NARROW)
    e_one[3] = (dot_nt(d_logit, ranks[:, 3 * inner :]) * picks).astype(NARROW)
    extra_sent = [box.push(e_one.at[mp_peers[k]], extra_landed.at[k - 1], mp=mp_peers[k]) for k in MpSum.ORDER]
    grads = [dot_tn(u_ref[:, j * 128 : (j + 1) * 128], d_pre[:, j * inner : (j + 1) * inner]) for j in range(3)]
    grads.append(dot_tn(u_ref[:, 384:], d_logit))
    halves(one, [value.astype(NARROW) for value in grads])
    heads_sum.over_cores()
    for load in loads:
        load.wait()
    share = grad_input.shape[1]
    total = MpSum(box, part, landed)
    row_sum = jnp.zeros((count, 128), WIDE)
    all_e = jnp.concatenate([e_one[j] for j in range(4)], axis=1)
    for k in (2, 1, 3, 0):
        owner = total.owner(k)
        rows = columns(owner, share)
        value = (
            dot_nt(d_pre[...], w_in[rows, : 3 * inner])
            + dot_nt(d_logit, w_in[rows, 3 * inner :])
            + dot_nt(all_e, a_one[rows, :])
        )
        part[k] = value.astype(NARROW)
        if k:
            total.send(k)
        weighted = value * norm_ref[0:1, rows] * x_ref[:, rows].astype(WIDE)
        row_sum = row_sum + jnp.sum(weighted, axis=1, keepdims=True)
    sums[...] = row_sum.T[:8]
    sums_sent = [box.push(sums, sums_landed.at[k - 1], mp=mp_peers[k]) for k in MpSum.ORDER]
    heads_sum.over_y()
    early_sum.finish()
    early_pair[c] = four[5][...]
    early_paired = box.push(four[5], early_pair.at[c], dp=moved(0, 0, True))
    for copy in extra_sent:
        copy.wait_recv()
    factor = e_one[m].astype(WIDE)
    for k in range(3):
        factor = factor + extra_landed[k].astype(WIDE)
    for i, value in enumerate(by_core(dot_tn(xn_ref[...], factor.astype(NARROW)).astype(NARROW))):
        three[0][i] = value
    one_sum.over_cores()
    heads_sum.over_z()
    one_sum.over_y()
    x_all = x_ref[...].astype(WIDE)
    scale = inverse_rms(x_all)
    mine = columns(m, share)
    d_xn = total.total()
    for copy in sums_sent:
        copy.wait_recv()
    rows = sums[...] + sums_landed[0] + sums_landed[1] + sums_landed[2]
    mean = jnp.concatenate([rows] * 16, axis=0).T[:, :1] / model
    grad_input[...] = d_one_ref[:, mine] + (
        scale * norm_ref[0:1, mine] * d_xn - x_ref[:, mine].astype(WIDE) * (scale * scale * scale * mean)
    )
    heads_sum.finish()
    pair[c] = one[5][...]
    paired = box.push(one[5], pair.at[c], dp=moved(0, 0, True))
    two_sum.finish()
    rank_rows = model // 128
    one_sum.over_z()

    def to_owners(slot, result):
        ends[slot, m] = result[columns(m, rank_rows)]
        return [
            box.push(result.at[columns(mp_peers[k], rank_rows)], ends.at[slot, m], mp=mp_peers[k])
            for k in MpSum.ORDER
        ]

    owners = to_owners(1, two[5])
    one_sum.finish()
    owners += to_owners(0, three[5])
    paired.wait_recv()
    early_paired.wait_recv()

    def own_ranks(pair):
        both = jnp.concatenate([pair[0], pair[1]], axis=1)
        return jnp.where(c == 0, both[:4], both[4:])

    rows = own_ranks(pair)
    for j in range(3):
        out_heads[j] = rows[:, j * inner : (j + 1) * inner]
    out_beta[...] = rows[:, 3 * inner : 3 * inner + heads]
    rows = own_ranks(early_pair)
    for j in range(2):
        out_ffn[j] = rows[:, j * ff : (j + 1) * ff]
    out_a_out[...] = rows[:, 2 * ff : 2 * ff + inner]
    out_a_down[...] = rows[:, 2 * ff + inner : 3 * ff + inner]
    for copy in owners:
        copy.wait_recv()
    for j in range(4):
        out_a_in[j] = ends[0, j]
    for j in range(2):
        out_a_in[4 + j] = ends[1, j]
        out_res[j] = ends[1, 2 + j]
    box.drain()


def tail(mixer, tokens, grads, wide, thin):
    model = tokens[2].shape[1]
    count, inner = mixer[-1].shape
    heads = inner // DH
    share = model // 4
    ranks, ff = tokens[-1], grads[3].shape[1]

    def half_of(width):
        return -(-width // 256) * 128

    half, early_half = half_of(ranks.shape[1]), half_of(3 * ff + inner)
    vmem = pl.BlockSpec(memory_space=pltpu.VMEM)
    anywhere = pl.BlockSpec(memory_space=pl.ANY)
    copies = 3 + 3 + 3 + 3 + 4 * 7 + 2 + 6
    results = [
        (count, share), (6, model // 128, 128), (3, 4, inner), (4, heads),
        (4, inner), (2, 4, ff), (4, ff), (2, model // 128, 128),
    ]
    scratch = [
        ((model, 3 * inner + 128), NARROW),
        ((model, 512), NARROW),
        ((3, HALO + count, inner), WIDE),
        ((HALO + count, DH), WIDE),
        ((3, 8, inner), WIDE),
        ((count, 3 * inner), NARROW),
        ((4, count, 128), NARROW),
        ((4, count, share), NARROW),
        ((3, count, share), NARROW),
        ((3, count, 128), NARROW),
        ((8, count), WIDE),
        ((3, 8, count), WIDE),
        ((2, 8, half), WIDE),
        ((2, 8, early_half), WIDE),
        ((2, 4, model // 128, 128), WIDE),
    ]
    scratch += DpSum.scratch(32, half) + DpSum.scratch(model // 8, 128) + DpSum.scratch(model // 8, 128)
    scratch += DpSum.scratch(32, early_half)
    operands = (*mixer, *tokens, *grads)
    return pl.pallas_call(
        tail_kernel,
        out_shape=tuple(jax.ShapeDtypeStruct(r, WIDE) for r in results),
        in_specs=[vmem] * len(operands) + [anywhere] * 2,
        out_specs=tuple([vmem] * len(results)),
        scratch_shapes=[pltpu.VMEM(*s) for s in scratch]
        + [
            pltpu.SemaphoreType.DMA((copies,)),
            pltpu.SemaphoreType.DMA((copies,)),
            pltpu.SemaphoreType.DMA((2,)),
        ],
        compiler_params=pltpu.CompilerParams(
            collective_id=3, has_side_effects=True, vmem_limit_bytes=60 << 20
        ),
        name="tail",
    )(*operands, wide, thin)


def on_device(
    layer_in, cotangent, segments, adapters, norm_one, norm_two, out_gain, beta_bias, conv_taps,
    w_qkv, w_beta, w_out, w_gate_up, w_down, a_in, b_heads, b_beta, a_out, b_ffn, a_down, b_res,
):
    count = layer_in.shape[0]
    m = lax.axis_index("mp")
    heads = w_beta.shape[1]
    inner = heads * DH
    ff = w_down.shape[0]

    pad_beta = jnp.pad(w_beta, ((0, 0), (0, 128 - heads)))
    ranks_one = pack_ranks(
        jnp.concatenate(
            [b_heads.transpose(1, 0, 2).reshape(4, 3 * inner), jnp.pad(b_beta, ((0, 0), (0, 128 - heads)))],
            axis=1,
        ),
        1,
    )
    wide_one = jnp.concatenate([w_qkv.reshape(64, 3 * inner), pad_beta, ranks_one], axis=1)
    thin_one = jnp.concatenate([a_in.reshape(16, 768), b_res.transpose(2, 0, 1).reshape(16, 256)], axis=1)
    ranks_two = jnp.concatenate([b_ffn.transpose(1, 0, 2).reshape(4, 2 * ff), a_out.T, a_down.T], axis=1)
    ranks_two = jnp.pad(ranks_two, ((0, 4), (0, 0)))
    wide_two = jnp.concatenate([w_out.T, w_gate_up.reshape(64, 2 * ff), w_down.T], axis=1)
    full_ranks = lax.all_gather(ranks_two, "dp", axis=0, tiled=True)
    full_two = lax.all_gather(wide_two, "dp", axis=0, tiled=True)
    full_one, full_thin = first_gather(wide_one, thin_one)

    ranks = unpack_ranks(full_one[:, :, 3 * inner + 128 :], 13)
    full_one = full_one.reshape(2048, -1)
    w_qkv_full = full_one[:, : 3 * inner]
    w_beta_full = full_one[:, 3 * inner : 3 * inner + 128]
    b_heads_full = [ranks[:, j * inner : (j + 1) * inner] for j in range(3)]
    b_beta_full = ranks[:, 3 * inner :]
    full_thin = full_thin.reshape(2048, 1024)
    a_one = full_thin[:, :512]

    before_rows = shifted(layer_in[count - HALO :], 1)
    before_ids = shifted(segments[count - HALO :] + 1, 1) - 1
    rows_ext = jnp.concatenate([before_rows, layer_in]).astype(WIDE)
    seg_ext = jnp.concatenate([before_ids, segments])
    seg_count = adapters.shape[0]
    per_token = jnp.sum(
        jnp.where(seg_ext[:, None] == jnp.arange(seg_count, dtype=jnp.int32)[None, :], adapters[None, :], 0), axis=1
    )
    owner_ids = jnp.arange(128, dtype=jnp.int32) // RANK
    picks_ext = (per_token[:, None] == owner_ids[None, :]).astype(WIDE)
    picks = picks_ext[HALO:]
    same = [
        (seg_ext[HALO - j : HALO - j + count] == segments).astype(WIDE) for j in range(KW)
    ]
    seg_float = segments.astype(WIDE)

    scale_ext = inverse_rms(rows_ext)
    xn_ext = (rows_ext * scale_ext * norm_one).astype(NARROW)
    u_ext = (dot(xn_ext, a_one) * jnp.tile(picks_ext, (1, 4))).astype(NARROW)
    pre = (
        dot(xn_ext, w_qkv_full)
        + jnp.concatenate([dot(u_ext[:, j * 128 : (j + 1) * 128], b_heads_full[j]) for j in range(3)], axis=1)
    ).astype(NARROW)
    xn_one, u_one = xn_ext[HALO:], u_ext[HALO:]
    logits = dot(xn_one, w_beta_full) + dot(u_one[:, 384:], b_beta_full)
    strength = jax.nn.sigmoid(logits[:, :heads] + beta_bias)
    aux = jnp.concatenate(
        [s[:, None] for s in same]
        + [
            (segments == before_ids[HALO - 1]).astype(WIDE)[:, None],
            (segments == segments[count - 1]).astype(WIDE)[:, None],
            seg_float[:, None],
            jnp.zeros((count, 1), WIDE),
            strength,
            jnp.zeros((count, 128 - 8 - heads), WIDE),
        ],
        axis=1,
    )
    seg_row = jnp.broadcast_to(seg_float[None, :], (8, count))
    taps = jnp.pad(conv_taps.reshape(3 * KW, inner).astype(WIDE), ((0, 4), (0, 0)))
    out_zero, reach, maps, offsets, *kept = mixer_forward(pre, taps, aux, seg_row)
    (
        output, state_in, state_grad, d_hidden_one, d_mixer,
        grad_b_ffn, grad_a_down, grad_a_out, shared_two,
    ) = middle(
        maps, offsets, out_zero, reach, picks, layer_in, cotangent,
        jnp.broadcast_to(norm_two[None, :], (8, norm_two.shape[0])),
        jnp.broadcast_to(out_gain[None, :], (8, DH)),
        full_ranks, full_thin, full_two,
    )
    grad_input, d_a_in, d_b_heads, d_b_beta, d_a_out, d_b_ffn, d_a_down, d_b_res = tail(
        (pre, taps, aux, seg_row, *kept, state_in, state_grad, d_mixer),
        (
            u_one, xn_one, layer_in, d_hidden_one,
            jnp.broadcast_to(norm_one[None, :], (8, norm_one.shape[0])),
            picks,
            ranks,
        ),
        (shared_two, grad_b_ffn, grad_a_out, grad_a_down),
        full_one,
        full_thin,
    )
    return (
        output, grad_input, d_a_in.transpose(1, 0, 2), d_b_heads, d_b_beta, d_a_out.T, d_b_ffn, d_a_down.T,
        d_b_res.transpose(0, 2, 1),
    )


def solution(mesh):
    placed = (
        P("dp", None),
        P("dp", "mp"),
        P("dp"),
        P(),
        P(),
        P(),
        P(),
        P("mp"),
        P(None, None, "mp"),
        P("dp", None, "mp"),
        P("dp", "mp"),
        P("mp", "dp"),
        P("dp", None, "mp"),
        P("mp", "dp"),
        P(("dp", "mp"), None, None),
        P(None, "dp", "mp"),
        P("dp", "mp"),
        P("mp", "dp"),
        P(None, "dp", "mp"),
        P("mp", "dp"),
        P(None, None, ("dp", "mp")),
    )
    return jax.shard_map(
        on_device,
        mesh=mesh,
        in_specs=placed,
        out_specs=(
            P("dp", "mp"),
            P("dp", "mp"),
            P(("dp", "mp"), None, None),
            P(None, "dp", "mp"),
            P("dp", "mp"),
            P("mp", "dp"),
            P(None, "dp", "mp"),
            P("mp", "dp"),
            P(None, None, ("dp", "mp")),
        ),
        check_vma=False,
    )
```

```python
import functools

import jax
import jax.numpy as jnp
from jax import lax
from jax.experimental import pallas as pl
from jax.experimental.pallas import tpu as pltpu
from jax.sharding import PartitionSpec as P

DH = 128
KW = 4
RANK = 16
HALO = 16
EPSILON = 1e-06
WIDE = jnp.float32
NARROW = jnp.bfloat16
MESH = pl.DeviceIdType.MESH
EXACT = lax.Precision.HIGHEST


def coords():
    place = lax.axis_index("dp")
    return place // 8, lax.rem(place // 2, 4), lax.rem(place, 2)


def place_of(y, z, c):
    return (y * 4 + z) * 2 + c


def moved(dy, dz, other_core=False):
    y, z, c = coords()
    return place_of(lax.rem(y + dy + 4, 4), lax.rem(z + dz + 4, 4), 1 - c if other_core else c)


def greet(dp_peers=(), mp_peers=()):
    barrier = pltpu.get_barrier_semaphore()
    for peer in dp_peers:
        pl.semaphore_signal(barrier, inc=1, device_id={"dp": peer}, device_id_type=MESH)
    for peer in mp_peers:
        pl.semaphore_signal(barrier, inc=1, device_id={"mp": peer}, device_id_type=MESH)
    pl.semaphore_wait(barrier, len(dp_peers) + len(mp_peers))


class Mailbox:
    def __init__(self, send, recv):
        self.send, self.recv, self.copies = send, recv, []

    def push(self, src, dst, **device):
        k = len(self.copies)
        copy = pltpu.make_async_remote_copy(
            src_ref=src,
            dst_ref=dst,
            send_sem=self.send.at[k],
            recv_sem=self.recv.at[k],
            device_id=device,
            device_id_type=MESH,
        )
        copy.start()
        self.copies.append(copy)
        return copy

    def drain(self):
        for copy in self.copies:
            copy.wait_send()


def gather_steps(box, own, out):
    me = moved(0, 0)
    half = own.shape[0] // 2
    quarter = half // 2
    sibling = moved(0, 0, True)
    kinds = []
    for kind in range(2):
        base = kind * half
        parts = (pl.ds(base, half), pl.ds(base, quarter), pl.ds(base + quarter, quarter))
        if kind == 0:
            kinds.append((parts, lambda a, b: moved(a, b)))
        else:
            kinds.append((parts, lambda a, b: moved(b, a)))
    near, across, far, far_across, shared = [], [{}, {}], [[], []], [{}, {}], []

    def open_up():
        for parts, at in kinds:
            near.append([box.push(own.at[parts[0]], out.at[me, parts[0]], dp=at(s, 0)) for s in (1, -1)])
        for k, (parts, at) in enumerate(kinds):
            across[k][0] = [box.push(own.at[parts[0]], out.at[me, parts[0]], dp=at(0, s)) for s in (1, -1)]
        shared.append(box.push(own, out.at[me], dp=sibling))

    def pass_on(k, slot):
        parts, at = kinds[k]
        block = out.at[slot, parts[0]]
        return [box.push(block, block, dp=at(0, t)) for t in (1, -1)]

    def to_sibling(k, slot):
        block = out.at[slot, kinds[k][0][0]]
        shared.append(box.push(block, block, dp=sibling))

    def from_near(i, s):
        def step():
            for k, (parts, at) in enumerate(kinds):
                near[k][i].wait_recv()
                block = out.at[at(s, 0), parts[1 + i]]
                far[k].append(box.push(block, block, dp=at(-s, 0)))
            for k, (parts, at) in enumerate(kinds):
                across[k][s] = pass_on(k, at(s, 0))
                to_sibling(k, at(s, 0))

        return step

    def from_far(k):
        def step():
            for copy in far[k]:
                copy.wait_recv()
            slot = kinds[k][1](2, 0)
            across[k][2] = pass_on(k, slot)
            to_sibling(k, slot)

        return step

    def from_across(k, f):
        def step():
            parts, at = kinds[k]
            far_across[k][f] = []
            for i, s in enumerate((-1, 1)):
                across[k][f][i].wait_recv()
                slot = at(f, s)
                block = out.at[slot, parts[1 + i]]
                far_across[k][f].append(box.push(block, block, dp=at(0, -s)))
                to_sibling(k, slot)

        return step

    def from_far_across(k, f):
        def step():
            for copy in far_across[k][f]:
                copy.wait_recv()
            to_sibling(k, kinds[k][1](f, 2))

        return step

    def close():
        for copy in shared:
            copy.wait_recv()

    steps = [open_up, from_near(0, -1), from_near(1, 1), from_far(0), from_far(1)]
    steps += [from_across(k, f) for f in (0, -1, 1, 2) for k in range(2)]
    steps += [from_far_across(k, f) for f in (0, -1, 1, 2) for k in range(2)]
    return steps + [close]


def gather_peers():
    return [moved(1, 0), moved(-1, 0), moved(0, 1), moved(0, -1), moved(0, 0, True)]


GATHER_COPIES = 71


def half_dot(left, right, dims=(((1,), (0,)), ((), ()))):
    high = right.astype(NARROW)
    low = (right - high.astype(WIDE)).astype(NARROW)
    return lax.dot_general(left, high, dims, preferred_element_type=WIDE) + lax.dot_general(
        left, low, dims, preferred_element_type=WIDE
    )


TURNED = (((0,), (0,)), ((), ()))


def two_parts(value):
    high = value.astype(NARROW)
    return high, (value - high.astype(WIDE)).astype(NARROW)


def wide_dot(left, right, left_dim=1, right_dim=0):
    left_high, left_low = two_parts(left)
    right_high, right_low = two_parts(right)

    def part(one, two):
        return lax.dot_general(one, two, (((left_dim,), (right_dim,)), ((), ())), preferred_element_type=WIDE)

    return part(left_high, right_high) + (part(left_high, right_low) + part(left_low, right_high))


def convolve(pre_ref, taps_ref, part, head, inner, aux):
    count = aux.shape[0]
    cols = slice(part * inner + head * DH, part * inner + (head + 1) * DH)
    taps = taps_ref[:, head * DH : (head + 1) * DH]
    total = pre_ref[pl.ds(HALO, count), cols] * taps[part : part + 1]
    for j in range(1, KW):
        shifted = pre_ref[pl.ds(HALO - j, count), cols]
        total = total + shifted * aux[:, j : j + 1] * taps[3 * j + part : 3 * j + part + 1]
    return total


def masks(aux, seg_row):
    same = aux[:, 6:7] == seg_row
    shape = (aux.shape[0], aux.shape[0])
    row = lax.broadcasted_iota(jnp.int32, shape, 0)
    col = lax.broadcasted_iota(jnp.int32, shape, 1)
    return row, col, same


def each(step, *lists):
    return [step(*items) for items in zip(*lists)]


def lower_inverses(lowers, row, col, tick):
    near = [jnp.where(row // 8 == col // 8, lower, 0.0) for lower in lowers]
    square = each(lambda a: wide_dot(a, a), near)
    inverse = [jnp.where(row == col, 1.0, 0.0) - a for a in near]
    inverse = each(lambda x, s: x + wide_dot(x, s), inverse, square)
    square = each(lambda s: wide_dot(s, s), square)
    inverse = each(lambda x, s: x + wide_dot(x, s), inverse, square)
    size = 8
    while size < row.shape[0]:
        link = (row // (2 * size) == col // (2 * size)) & (row // size != col // size)
        middle = each(lambda lower, x: wide_dot(jnp.where(link, lower, 0.0), x), lowers, inverse)
        inverse = each(lambda x, y: x - wide_dot(x, y), inverse, middle)
        size *= 2
        tick()
    return inverse


def mixer_forward(heads, pre_ref, taps_ref, aux, seg_row, out_ref, reach_ref, map_ref, offset_ref, kept, tick):
    q_ref, k_ref, v_ref, t_ref, w_ref, u_ref = kept
    count = aux.shape[0]
    inner = out_ref.shape[1]
    linked, ending = aux[:, 4:5], aux[:, 5:6]
    row, col, same = masks(aux, seg_row)
    rate = [aux[:, 8 + h : 9 + h] for h in heads]
    cols = [slice(h * DH, (h + 1) * DH) for h in heads]

    def act(part):
        convs = [convolve(pre_ref, taps_ref, part, h, inner, aux) for h in heads]
        return [conv * jax.nn.sigmoid(conv) for conv in convs]

    def unit(a):
        return a * lax.rsqrt(jnp.sum(a * a, axis=1, keepdims=True) + EPSILON)

    k = each(unit, act(1))
    gram = each(lambda b: wide_dot(b, b, 1, 1), k)
    lowers = each(lambda g, r: jnp.where((row > col) & same, g * r, 0.0), gram, rate)
    q, v = each(unit, act(0)), act(2)
    for i in range(len(heads)):
        q_ref[:, cols[i]] = q[i]
        k_ref[:, cols[i]] = k[i]
        v_ref[:, cols[i]] = v[i]
    scores = each(lambda a, b: jnp.where((row >= col) & same, wide_dot(a, b, 1, 1), 0.0), q, k)
    tick()
    inverse = lower_inverses(lowers, row, col, tick)
    written = each(
        lambda t, a, b, r: wide_dot(t, jnp.concatenate([a, b * linked], axis=1) * r), inverse, v, k, rate
    )
    ends = each(lambda b, w: wide_dot(b * ending, w, 0, 0), k, written)
    mixed = each(wide_dot, scores, written)
    eye = jnp.where(row[:DH, :DH] == col[:DH, :DH], 1.0, 0.0)
    last = aux[count - 1 :, 4:5]
    for i, h in enumerate(heads):
        t_ref[h] = inverse[i]
        w_ref[:, cols[i]] = written[i][:, :DH]
        u_ref[:, cols[i]] = written[i][:, DH:]
        offset_ref[h] = ends[i][:, :DH].astype(offset_ref.dtype)
        map_ref[h] = (eye * last - ends[i][:, DH:]).astype(map_ref.dtype)
        out_ref[:, cols[i]] = mixed[i][:, :DH]
        reach_ref[:, cols[i]] = q[i] * linked - mixed[i][:, DH:]
    tick()


def mixer_backward(heads, pre_ref, taps_ref, aux, seg_row, kept, state_ref, grad_ref, d_out_ref, d_ext):
    q_ref, k_ref, v_ref, t_ref, w_ref, u_ref = kept
    count = aux.shape[0]
    inner = d_out_ref.shape[1]
    linked, ending = aux[:, 4:5], aux[:, 5:6]
    row, col, same = masks(aux, seg_row)
    upto = (row >= col) & same
    below = (row > col) & same

    def take(ref):
        return [ref[:, h * DH : (h + 1) * DH] for h in heads]

    rate = [aux[:, 8 + h : 9 + h] for h in heads]
    q, k, v, d_out = take(q_ref), take(k_ref), take(v_ref), take(d_out_ref)
    state, grad = [state_ref[h] for h in heads], [grad_ref[h] for h in heads]
    written = each(lambda w, u, s: w - wide_dot(u, s), take(w_ref), take(u_ref), state)
    scores = each(lambda a, b: jnp.where(upto, wide_dot(a, b, 1, 1), 0.0), q, k)
    d_written = each(
        lambda a, d, b, g: wide_dot(a, d, 0, 0) + wide_dot(b * ending, g), scores, d_out, k, grad
    )
    d_right = each(lambda t, d: wide_dot(t, d, 0, 0), [t_ref[h] for h in heads], d_written)
    d_scores = each(lambda d, w: jnp.where(upto, wide_dot(d, w, 1, 1), 0.0), d_out, written)
    d_lower = each(lambda d, w: jnp.where(below, -wide_dot(d, w, 1, 1), 0.0), d_right, written)
    d_q = each(
        lambda ds, b, d, s: wide_dot(ds, b) + linked * wide_dot(d, s, 1, 1), d_scores, k, d_out, state
    )
    d_k = each(
        lambda ds, a, w, g: wide_dot(ds, a, 0, 0) + ending * wide_dot(w, g, 1, 1), d_scores, q, written, grad
    )
    d_rate = each(
        lambda d, a, b, s: jnp.sum(d * (a - linked * wide_dot(b, s)), axis=1, keepdims=True), d_right, v, k, state
    )
    d_rate = each(
        lambda r, d, b: r + jnp.sum(d * wide_dot(b, b, 1, 1), axis=1, keepdims=True), d_rate, d_lower, k
    )
    d_k = each(lambda dk, r, d, s: dk - (linked * r) * wide_dot(d, s, 1, 1), d_k, rate, d_right, state)
    d_gram = each(lambda d, r: d * r, d_lower, rate)
    d_k = each(lambda dk, d, b: dk + wide_dot(d, b) + wide_dot(d, b, 0, 0), d_k, d_gram, k)
    d_v = each(lambda r, d: r * d, rate, d_right)
    for i, h in enumerate(heads):
        for part, (unit, d) in enumerate(((q[i], d_q[i]), (k[i], d_k[i]), (None, d_v[i]))):
            cols = slice(h * DH, (h + 1) * DH)
            conv = convolve(pre_ref, taps_ref, part, h, inner, aux)
            gate = jax.nn.sigmoid(conv)
            if unit is not None:
                act = conv * gate
                scale = lax.rsqrt(jnp.sum(act * act, axis=1, keepdims=True) + EPSILON)
                d = (d - unit * jnp.sum(unit * d, axis=1, keepdims=True)) * scale
            d_conv = d * gate * (1.0 + conv * (1.0 - gate))
            d_ext[part, :HALO, cols] = jnp.zeros((HALO, DH), WIDE)
            d_ext[part, HALO:, cols] = d_conv * taps_ref[part : part + 1, cols]
            for j in range(1, KW):
                term = d_conv * taps_ref[3 * j + part : 3 * j + part + 1, cols] * aux[:, j : j + 1]
                d_ext[part, pl.ds(HALO - j, count), cols] += term
    return each(lambda d, r: d * r * (1.0 - r), d_rate, rate)


def inverse_rms(values):
    return lax.rsqrt(jnp.mean(values * values, axis=-1, keepdims=True) + EPSILON)


def norm_back(values, scale, gain, grad_out):
    weighted = grad_out * gain
    return scale * weighted - values * scale**3 * jnp.mean(weighted * values, axis=-1, keepdims=True)


def dot(left, right):
    return jnp.dot(left, right, preferred_element_type=WIDE)


def dot_nt(left, right):
    return lax.dot_general(left, right, (((1,), (1,)), ((), ())), preferred_element_type=WIDE)


def dot_tn(left, right):
    return lax.dot_general(left, right, (((0,), (0,)), ((), ())), preferred_element_type=WIDE)


class Chain:
    def __init__(self, box, a_ref, sib_a, chip_a, row_a):
        self.box, self.a_ref, self.sib_a, self.chip_a, self.row_a = box, a_ref, sib_a, chip_a, row_a
        self.y, self.z, self.c = coords()
        self.first = self.c == 0
        self.sibling = moved(0, 0, True)
        self.z_peers = {k: moved(0, k) for k in (1, 2, 3)}
        self.y_peers = {k: moved(k, 0) for k in (1, 2, 3)}
        self.mine = pl.ds(pl.multiple_of(2 * self.c, 2), 2)
        self.theirs = pl.ds(pl.multiple_of(2 * (1 - self.c), 2), 2)

    def peers(self):
        return [self.sibling] + list(self.z_peers.values()) + list(self.y_peers.values())

    def swap(self, ref, sib):
        return self.box.push(ref.at[self.theirs], sib, dp=self.sibling)

    def ordered(self, ref, sib, h):
        own, other = ref[2 * self.c + h], sib[h]
        return jnp.where(self.first, own, other), jnp.where(self.first, other, own)

    def spread(self, refs, place, peers):
        return [self.box.push(ref.at[place], ref.at[place], dp=peers[k]) for k in (2, 1, 3) for ref in refs]

    def start_forward(self, b_ref, sib_b, chip_b, row_b, pass_on):
        self.b_ref, self.sib_b, self.chip_b, self.row_b, self.pass_on = b_ref, sib_b, chip_b, row_b, pass_on
        self.pair = [self.swap(self.a_ref, self.sib_a), self.swap(b_ref, sib_b)]

    def chips_forward(self):
        for copy in self.pair:
            copy.wait_recv()
        self.lower = []
        for h in range(2):
            a_low, a_high = self.ordered(self.a_ref, self.sib_a, h)
            b_low, b_high = self.ordered(self.b_ref, self.sib_b, h)
            self.lower.append((a_low, b_low))
            self.chip_a[self.z, h] = lax.dot(a_high, a_low, preferred_element_type=WIDE).astype(NARROW)
            self.chip_b[self.z, h] = (
                lax.dot(a_high, b_low, preferred_element_type=WIDE) + b_high.astype(WIDE)
            ).astype(NARROW)
        self.ring = self.spread((self.chip_a, self.chip_b), self.z, self.z_peers)

    def rows_forward(self):
        for copy in self.ring:
            copy.wait_recv()
        for h in range(2):
            total_a, total_b = self.chip_a[0, h].astype(WIDE), self.chip_b[0, h].astype(WIDE)
            for i in range(1, 4):
                total_a = half_dot(self.chip_a[i, h], total_a)
                total_b = half_dot(self.chip_a[i, h], total_b) + self.chip_b[i, h].astype(WIDE)
            self.row_a[self.y, h] = total_a.astype(NARROW)
            self.row_b[self.y, h] = total_b.astype(NARROW)
        self.ring = self.spread((self.row_a, self.row_b), self.y, self.y_peers)

    def finish_forward(self, out):
        for copy in self.ring:
            copy.wait_recv()
        for h in range(2):
            state = jnp.zeros((DH, DH), WIDE)
            for i in range(3):
                longer = half_dot(self.row_a[i, h], state) + self.row_b[i, h].astype(WIDE)
                state = jnp.where(i < self.y, longer, state)
            for i in range(3):
                longer = half_dot(self.chip_a[i, h], state) + self.chip_b[i, h].astype(WIDE)
                state = jnp.where(i < self.z, longer, state)
            a_low, b_low = self.lower[h]
            middle = half_dot(a_low, state) + b_low.astype(WIDE)
            out[2 * self.c + h] = jnp.where(self.first, state, middle)
            self.pass_on[h] = jnp.where(self.first, middle, state)
        self.box.push(self.pass_on, out.at[self.mine], dp=self.sibling).wait_recv()

    def start_backward(self, g_ref, sib_g, chip_g, row_g, pass_on):
        self.g_ref, self.sib_g, self.chip_g, self.row_g, self.pass_on = g_ref, sib_g, chip_g, row_g, pass_on
        self.pair = [self.swap(g_ref, sib_g)]

    def chips_backward(self):
        for copy in self.pair:
            copy.wait_recv()
        self.upper_g = []
        for h in range(2):
            a_low, _ = self.ordered(self.a_ref, self.sib_a, h)
            g_low, g_high = self.ordered(self.g_ref, self.sib_g, h)
            self.upper_g.append(g_high)
            self.chip_g[self.z, h] = (
                lax.dot_general(a_low, g_high, TURNED, preferred_element_type=WIDE) + g_low.astype(WIDE)
            ).astype(NARROW)
        self.ring = self.spread((self.chip_g,), self.z, self.z_peers)

    def rows_backward(self):
        for copy in self.ring:
            copy.wait_recv()
        for h in range(2):
            total = self.chip_g[3, h].astype(WIDE)
            for i in (2, 1, 0):
                total = half_dot(self.chip_a[i, h], total, TURNED) + self.chip_g[i, h].astype(WIDE)
            self.row_g[self.y, h] = total.astype(NARROW)
        self.ring = self.spread((self.row_g,), self.y, self.y_peers)

    def finish_backward(self, out):
        for copy in self.ring:
            copy.wait_recv()
        for h in range(2):
            grad = jnp.zeros((DH, DH), WIDE)
            for i in (3, 2, 1):
                longer = half_dot(self.row_a[i, h], grad, TURNED) + self.row_g[i, h].astype(WIDE)
                grad = jnp.where(i > self.y, longer, grad)
            for i in (3, 2, 1):
                longer = half_dot(self.chip_a[i, h], grad, TURNED) + self.chip_g[i, h].astype(WIDE)
                grad = jnp.where(i > self.z, longer, grad)
            _, a_high = self.ordered(self.a_ref, self.sib_a, h)
            middle = half_dot(a_high, grad, TURNED) + self.upper_g[h].astype(WIDE)
            out[2 * self.c + h] = jnp.where(self.first, middle, grad)
            self.pass_on[h] = jnp.where(self.first, grad, middle)
        self.box.push(self.pass_on, out.at[self.mine], dp=self.sibling).wait_recv()


def columns(i, width):
    return pl.ds(pl.multiple_of(i * width, width), width)


class MpSum:
    ORDER = (2, 1, 3)

    def __init__(self, box, part, landed):
        self.box, self.part, self.landed = box, part, landed
        self.m = lax.axis_index("mp")
        self.peers = {k: lax.rem(self.m + k, 4) for k in (1, 2, 3)}
        self.copies = []

    def owner(self, k):
        return lax.rem(self.m + k, 4)

    def send(self, k):
        self.copies.append(self.box.push(self.part.at[k], self.landed.at[k - 1], mp=self.peers[k]))

    def total(self):
        for copy in self.copies:
            copy.wait_recv()
        total = self.part[0].astype(WIDE)
        for k in range(3):
            total = total + self.landed[k].astype(WIDE)
        return total

    def share(self, out, width):
        block = out.at[:, columns(self.m, width)]
        return [self.box.push(block, block, mp=self.peers[k]) for k in self.ORDER]


def unpack_ranks(block, spread, ranks, first, tiles):
    for q in range(4):
        for t in range(tiles):
            at = first + q * tiles + t
            spread[t, pl.ds(q, 32, stride=4), :] = block[at // 64, pl.ds(at % 64, 32, stride=64), :]
    for t in range(tiles):
        ranks[:, t * 128 : (t + 1) * 128] = spread[t].astype(ranks.dtype)


def front_kernel(
    x_ref, g_own, seg_ref, adapters, norm_ref, gain_ref, bias_ref, taps_ref, wide_ref, thin_ref, late_ref, late_thin,
    wide_out, thin_out, late_out, pre, aux_ref, picks_ref, xn_ref, u_ref, q_ref, k_ref, v_ref, t_ref, w_ref, u_map_ref,
    reach, ranks, a_ref, sib_a, chip_a, row_a, state_out, mixer_out, normed, u_out_ref, branch, g_full,
    wide_all, thin_all, late_all, thin_own, late_own, halo_x, seg_ext, xn_ext, pre_wide, block, spread, b_beta,
    b_ref, out_zero, sib_b, chip_b, row_b, pass_on, part, landed, send, recv, local,
):
    count, model = x_ref.shape
    heads = a_ref.shape[0]
    inner = heads * DH
    m = lax.axis_index("mp")
    place = lax.axis_index("dp")
    before, after = lax.rem(place + 31, 32), lax.rem(place + 1, 32)
    mp_peers = {k: lax.rem(m + k, 4) for k in (1, 2, 3)}
    box = Mailbox(send, recv)
    chain = Chain(box, a_ref, sib_a, chip_a, row_a)
    greet([before, after] + chain.peers(), list(mp_peers.values()))
    me = moved(0, 0)
    seg_ext[HALO:] = jnp.concatenate([seg_ref[...]] * 16, axis=0).T
    edges = [
        box.push(x_ref.at[pl.ds(count - HALO, HALO)], halo_x, dp=after),
        box.push(seg_ext.at[pl.ds(count, HALO)], seg_ext.at[pl.ds(0, HALO)], dp=after),
    ]
    thin_rows = thin_ref.shape[0]
    mine = pl.ds(pl.multiple_of(m * thin_rows, thin_rows), thin_rows)
    crossing = [box.push(thin_ref, thin_own.at[mine], mp=peer) for peer in mp_peers.values()]
    late_cols = pl.ds(late_ref.shape[1], late_thin.shape[1])
    late_crossing = [box.push(late_thin, late_own.at[mine, late_cols], mp=peer) for peer in mp_peers.values()]
    keep = [
        pltpu.make_async_copy(wide_ref, wide_all.at[me], local.at[0]),
        pltpu.make_async_copy(thin_ref, thin_own.at[mine], local.at[1]),
        pltpu.make_async_copy(late_ref, late_own.at[:, pl.ds(0, late_ref.shape[1])], local.at[2]),
        pltpu.make_async_copy(late_thin, late_own.at[mine, late_cols], local.at[3]),
    ]
    for copy in keep:
        copy.start()
    wide_steps = gather_steps(box, wide_ref, wide_all)
    thin_steps = gather_steps(box, thin_own, thin_all)
    late_steps = gather_steps(box, late_own, late_all)
    wide_steps.pop(0)()
    share = g_own.shape[1]
    g_full[:, columns(m, share)] = g_own[...]
    keep[1].wait()
    for copy in crossing:
        copy.wait_recv()
    keep_thin = pltpu.make_async_copy(thin_own, thin_all.at[me], local.at[4])
    keep_thin.start()
    thin_steps.pop(0)()
    g_sent = [box.push(g_own, g_full.at[:, columns(m, share)], mp=mp_peers[k]) for k in MpSum.ORDER]

    def normal(rows):
        rows = rows.astype(WIDE)
        return (rows * inverse_rms(rows) * norm_ref[0:1, :]).astype(NARROW)

    xn_ref[...] = normal(x_ref[...])
    xn_ext[HALO:] = xn_ref[...]
    for one, two in zip(wide_steps, thin_steps):
        one()
        two()
    keep[0].wait()
    keep_thin.wait()
    keep[2].wait()
    keep[3].wait()
    for copy in late_crossing:
        copy.wait_recv()
    keep_late = pltpu.make_async_copy(late_own, late_all.at[me], local.at[5])
    keep_late.start()
    late_steps.pop(0)()
    to_hbm = [
        pltpu.make_async_copy(wide_all, wide_out, local.at[6]),
        pltpu.make_async_copy(thin_all, thin_out, local.at[7]),
    ]
    for copy in to_hbm:
        copy.start()

    def tick(steps=1):
        for _ in range(min(steps, len(late_steps))):
            late_steps.pop(0)()

    for copy in edges:
        copy.wait_recv()
    xn_ext[:HALO] = normal(halo_x[...])
    seg_ext[:HALO] = jnp.where(place == 0, -1.0, seg_ext[:HALO])
    lanes = lax.broadcasted_iota(jnp.int32, seg_ext.shape, 1)
    seg_all = seg_ext[...]
    per_token = jnp.zeros(seg_all.shape, WIDE)
    for s in range(adapters.shape[0]):
        per_token = jnp.where(seg_all == float(s), adapters[s].astype(WIDE), per_token)
    picks_ext = jnp.where(per_token == (lanes // RANK).astype(WIDE), 1.0, 0.0)
    picks_ref[...] = picks_ext[HALO:]
    tiles = inner // 128
    for i in range(2):
        lane_block = slice(3 * inner + i * 128, 3 * inner + (i + 1) * 128)
        block[i] = wide_all[:, :, lane_block].reshape(model, 128).astype(WIDE)
    for q in range(4):
        b_beta[pl.ds(q, 32, stride=4), :] = block[0, pl.ds(q, 32, stride=64), :]
    unpack_ranks(block.at[pl.ds(1, 1)], spread, ranks.at[:, pl.ds(0, 4 * inner)], 0, 4 * tiles)
    beta = pltpu.roll(b_beta[...], 64, 1)
    beta_lane = lax.broadcasted_iota(jnp.int32, beta.shape, 1)
    beta = jnp.where((beta_lane >= 8) & (beta_lane < 8 + heads), beta, 0.0)
    ranks[:, 4 * inner :] = beta.astype(NARROW)
    tick()
    u_ext = dot(xn_ext[...], thin_all[...].reshape(model, thin_all.shape[2]))
    u_ext = (u_ext * jnp.concatenate([picks_ext] * 4, axis=1)).astype(NARROW)
    u_ref[...] = u_ext[HALO:]
    tick()
    for j in range(3):
        cols = slice(j * inner, (j + 1) * inner)
        value = dot(xn_ext[...], wide_all[:, :, cols].reshape(model, inner)) + dot(
            u_ext[:, j * 128 : (j + 1) * 128], ranks[:, cols]
        )
        value = value.astype(NARROW)
        pre[:, cols] = value
        pre_wide[:, cols] = value.astype(WIDE)
        tick()
    w_beta = wide_all[:, :, 3 * inner : 3 * inner + 128].reshape(model, 128)
    logits = dot(xn_ref[...], w_beta) + dot(u_ref[:, 384:], ranks[:, 4 * inner :]) + bias_ref[0:1, :]
    seg = seg_all[HALO:]
    lane = lanes[HALO:]
    aux = jnp.where((lane >= 8) & (lane < 8 + heads), jax.nn.sigmoid(logits), 0.0)
    for j in range(KW):
        aux = jnp.where((lane == j) & (seg_ext[pl.ds(HALO - j, count)] == seg), 1.0, aux)
    aux = jnp.where((lane == 4) & (seg == seg_ext[HALO - 1 : HALO]), 1.0, aux)
    aux = jnp.where((lane == 5) & (seg == seg_ext[HALO + count - 1 : HALO + count]), 1.0, aux)
    aux = jnp.where(lane == 6, seg, aux)
    aux_ref[...] = aux
    for first in range(0, heads, 2):
        mixer_forward(
            list(range(first, min(first + 2, heads))), pre_wide, taps_ref, aux, seg_ref[0:1, :],
            out_zero, reach, a_ref, b_ref, (q_ref, k_ref, v_ref, t_ref, w_ref, u_map_ref), tick,
        )
    chain.start_forward(b_ref, sib_b, chip_b, row_b, pass_on)
    tick(len(late_steps))
    keep_late.wait()
    keep_late_out = pltpu.make_async_copy(late_all, late_out, local.at[8])
    keep_late_out.start()
    chain.chips_forward()
    chain.rows_forward()
    chain.finish_forward(state_out)
    for h in range(heads):
        cols = slice(h * DH, (h + 1) * DH)
        rows = out_zero[:, cols] + wide_dot(reach[:, cols], state_out[h])
        mixer_out[:, cols] = rows
        normed[:, cols] = (rows * inverse_rms(rows) * gain_ref[0:1, :]).astype(NARROW)
    u_out = (dot_nt(normed[...], ranks[:, 3 * inner : 4 * inner]) * picks_ref[...]).astype(NARROW)
    u_out_ref[...] = u_out
    one = MpSum(box, part, landed)
    for k in (2, 1, 3, 0):
        groups = pl.ds(one.owner(k) * (share // 64), share // 64)
        w_out = late_all[groups, :, :inner].reshape(share, inner)
        b_mix = late_all[groups, :, inner + 256 : inner + 384].reshape(share, 128)
        part[k] = (dot_nt(normed[...], w_out) + dot_nt(u_out, b_mix)).astype(NARROW)
        if k:
            one.send(k)
    branch[:, columns(m, share)] = one.total().astype(NARROW)
    for copy in g_sent + one.share(branch, share):
        copy.wait_recv()
    for copy in to_hbm + [keep_late_out]:
        copy.wait()
    box.drain()


def front(x, g, seg_row, adapters, norm, gain, bias, taps, wide, thin, late, late_thin):
    count, model = x.shape
    inner = taps.shape[1]
    heads = inner // DH
    share = g.shape[1]
    vmem = pl.BlockSpec(memory_space=pltpu.VMEM)
    anywhere = pl.BlockSpec(memory_space=pl.ANY)
    two = (2, DH, DH)
    square = (heads, DH, DH)
    by_head = ((count, inner), WIDE)
    thin_all, late_all = (32, 64, thin.shape[1]), (32, 64, late.shape[1] + late_thin.shape[1])
    results = [
        ((32,) + wide.shape, NARROW),
        (thin_all, NARROW),
        (late_all, NARROW),
        ((HALO + count, 3 * inner), NARROW),
        ((count, 128), WIDE),
        ((count, 128), WIDE),
        ((count, model), NARROW),
        ((count, 512), NARROW),
        by_head,
        by_head,
        by_head,
        ((heads, count, count), WIDE),
        by_head,
        by_head,
        by_head,
        ((128, 4 * inner + 128), NARROW),
        (square, NARROW),
        (two, NARROW),
        ((4,) + two, NARROW),
        ((4,) + two, NARROW),
        (square, WIDE),
        by_head,
        ((count, inner), NARROW),
        ((count, 128), NARROW),
        ((count, model), NARROW),
        ((count, model), NARROW),
    ]
    scratch = [
        ((32,) + wide.shape, NARROW),
        (thin_all, NARROW),
        (late_all, NARROW),
        (thin_all[1:], NARROW),
        (late_all[1:], NARROW),
        ((HALO, model), NARROW),
        ((HALO + count, 128), WIDE),
        ((HALO + count, model), NARROW),
        ((HALO + count, 3 * inner), WIDE),
        ((2, model, 128), WIDE),
        ((4 * inner // 128, 128, 128), WIDE),
        ((128, 128), WIDE),
        (square, NARROW),
        by_head,
        (two, NARROW),
        ((4,) + two, NARROW),
        ((4,) + two, NARROW),
        (two, WIDE),
        ((4, count, share), NARROW),
        ((3, count, share), NARROW),
    ]
    copies = 3 * GATHER_COPIES + 2 + 3 + 3 + 3 + 2 + 6 + 6 + 1 + 6
    return pl.pallas_call(
        front_kernel,
        out_shape=tuple(jax.ShapeDtypeStruct(*r) for r in results),
        in_specs=[vmem] * 3 + [pl.BlockSpec(memory_space=pltpu.SMEM)] + [vmem] * 4 + [anywhere] * 4,
        out_specs=tuple([anywhere] * 3 + [vmem] * (len(results) - 3)),
        scratch_shapes=[pltpu.VMEM(*s) for s in scratch]
        + [
            pltpu.SemaphoreType.DMA((copies,)),
            pltpu.SemaphoreType.DMA((copies,)),
            pltpu.SemaphoreType.DMA((9,)),
        ],
        compiler_params=pltpu.CompilerParams(
            collective_id=0, has_side_effects=True, vmem_limit_bytes=60 << 20
        ),
        name="front",
    )(x, g, seg_row, adapters, norm, gain, bias, taps, wide, thin, late, late_thin)


def middle_kernel(
    a_ref, sib_a, chip_a, row_a, reach, mixer_out, normed, u_out_ref, branch, picks_ref, x_ref, g_full, norm_ref, gain_ref,
    ranks_one, late_ref, wide_ref,
    output, grad_out, d_one_out, d_mixer_out, g_b_ffn, g_a_down, g_a_out, g_shared,
    late, w_gu, w_down, packed, block, spread, ranks, sib_g, chip_g, row_g, pass_on, g_maps,
    part, landed, hidden_one, xn_two, gate, up, hidden, ffn_part, ffn_landed,
    d_gate_up, d_xn, extra, extra_landed, d_branch, e_down_ref, u_two_ref,
    send, recv, local,
):
    count = x_ref.shape[0]
    heads = a_ref.shape[0]
    inner = heads * DH
    ff = gate.shape[1]
    model = x_ref.shape[1]
    share = output.shape[1]
    m = lax.axis_index("mp")
    loads = [
        pltpu.make_async_copy(late_ref, late, local.at[0]),
        pltpu.make_async_copy(wide_ref.at[:, pl.ds(3 * ff, packed.shape[1])], packed, local.at[1]),
        pltpu.make_async_copy(wide_ref.at[:, pl.ds(0, ff)], w_gu.at[:, pl.ds(0, ff)], local.at[2]),
        pltpu.make_async_copy(wide_ref.at[:, pl.ds(ff, ff)], w_gu.at[:, pl.ds(ff, ff)], local.at[3]),
        pltpu.make_async_copy(wide_ref.at[:, pl.ds(2 * ff, ff)], w_down, local.at[4]),
    ]
    for load in loads:
        load.start()
    box = Mailbox(send, recv)
    chain = Chain(box, a_ref, sib_a, chip_a, row_a)
    mp_peers = {k: lax.rem(m + k, 4) for k in (1, 2, 3)}
    greet(chain.peers(), list(mp_peers.values()))
    picks = picks_ref[...]
    u_out = u_out_ref[...]
    a_out = ranks_one.at[:, pl.ds(3 * inner, inner)]
    a_down = ranks.at[:, pl.ds(2 * ff, ff)]
    w_out, a_two = late.at[:, pl.ds(0, inner)], late.at[:, pl.ds(inner, 256)]
    b_mix, b_down = late.at[:, pl.ds(inner + 256, 128)], late.at[:, pl.ds(inner + 384, 128)]

    rows = x_ref[...].astype(WIDE) + branch[...].astype(WIDE)
    hidden_one[...] = rows
    scale_two = inverse_rms(rows)
    xn_two[...] = (rows * scale_two * norm_ref[0:1, :]).astype(NARROW)
    two_picks = jnp.concatenate([picks, picks], axis=1)
    loads[0].wait()
    u_two_ref[...] = (dot(xn_two[...], a_two[...]) * two_picks).astype(NARROW)
    loads[1].wait()
    for i in range(3):
        block[i] = packed[:, i * 128 : (i + 1) * 128].astype(WIDE)
    unpack_ranks(block, spread, ranks, 0, 3 * ff // 128)
    loads[2].wait()
    gate[...] = dot(xn_two[...], w_gu[:, :ff]) + dot(u_two_ref[:, :128], ranks[:, :ff])
    loads[3].wait()
    up[...] = dot(xn_two[...], w_gu[:, ff:]) + dot(u_two_ref[:, 128:], ranks[:, ff : 2 * ff])
    hidden[...] = (gate[...] * jax.nn.sigmoid(gate[...]) * up[...]).astype(NARROW)
    loads[4].wait()

    e_down = (dot(g_full[...], b_down[...]) * picks).astype(NARROW)
    e_down_ref[...] = e_down
    d_hidden = dot(g_full[...], w_down[...]) + dot(e_down, a_down[...])
    sig = jax.nn.sigmoid(gate[...])
    d_gate_up[:, :ff] = (d_hidden * up[...] * sig * (1.0 + gate[...] * (1.0 - sig))).astype(NARROW)
    d_gate_up[:, ff:] = (d_hidden * gate[...] * sig).astype(NARROW)
    e_two = [
        (dot_nt(d_gate_up[:, j * ff : (j + 1) * ff], ranks[:, j * ff : (j + 1) * ff]) * picks).astype(NARROW)
        for j in range(2)
    ]
    two = MpSum(box, part, landed)
    for k in (2, 1, 3, 0):
        rows = columns(two.owner(k), share)
        part[k] = (
            dot_nt(d_gate_up[...], w_gu[rows, :]) + dot_nt(jnp.concatenate(e_two, axis=1), a_two[rows, :])
        ).astype(NARROW)
        if k:
            two.send(k)
    u_down = (dot_nt(hidden[...], a_down[...]) * picks).astype(NARROW)
    for j, value in enumerate((e_two[0], e_two[1], u_out, u_down)):
        extra[j] = value
    d_xn[:, columns(m, share)] = two.total().astype(NARROW)
    shared = two.share(d_xn, share)
    extra_sent = [box.push(extra.at[mp_peers[k]], extra_landed.at[k - 1], mp=mp_peers[k]) for k in MpSum.ORDER]
    three = MpSum(box, ffn_part, ffn_landed)
    for k in (2, 1, 3, 0):
        rows = columns(three.owner(k), share)
        ffn_part[k] = (dot_nt(hidden[...], w_down[rows, :]) + dot_nt(u_down, b_down[rows, :])).astype(NARROW)
    for copy in shared:
        copy.wait_recv()
    for k in MpSum.ORDER:
        three.send(k)

    rows = hidden_one[...]
    scale_two = inverse_rms(rows)
    d_one = g_full[...].astype(WIDE) + norm_back(rows, scale_two, norm_ref[0:1, :], d_xn[...].astype(WIDE))
    d_one_out[...] = d_one
    d_branch[...] = d_one.astype(NARROW)
    e_out = (dot(d_branch[...], b_mix[...]) * picks).astype(NARROW)
    d_normed = dot(d_branch[...], w_out[...]) + dot(e_out, a_out[...])
    for h in range(heads):
        cols = slice(h * DH, (h + 1) * DH)
        rows = mixer_out[:, cols]
        d_rows = norm_back(rows, inverse_rms(rows), gain_ref[0:1, :], d_normed[:, cols])
        d_mixer_out[:, cols] = d_rows
        g_maps[h] = wide_dot(reach[:, cols], d_rows, 0, 0).astype(NARROW)
    chain.start_backward(g_maps, sib_g, chip_g, row_g, pass_on)
    g_a_out[...] = dot_tn(e_out, normed[...]).astype(NARROW)
    chain.chips_backward()
    for j in range(2):
        cols = slice(j * ff, (j + 1) * ff)
        g_b_ffn[:, cols] = dot_tn(u_two_ref[:, j * 128 : (j + 1) * 128], d_gate_up[:, cols]).astype(NARROW)
    chain.rows_backward()
    g_a_down[...] = dot_tn(e_down_ref[...], hidden[...]).astype(NARROW)
    for copy in extra_sent:
        copy.wait_recv()
    factor = extra[m].astype(WIDE)
    for k in range(3):
        factor = factor + extra_landed[k].astype(WIDE)
    left = jnp.where(m < 2, xn_two[...], jnp.where(m == 2, d_branch[...], g_full[...]))
    g_shared[...] = dot_tn(left, factor.astype(NARROW)).astype(NARROW)
    chain.finish_backward(grad_out)
    output[...] = (hidden_one[:, columns(m, share)] + three.total()).astype(NARROW)
    box.drain()


def middle(kept_maps, forward, x, g, norm, gain, ranks, late, wide):
    operands = (*kept_maps, *forward, x, g, norm, gain, ranks)
    count, inner = forward[0].shape
    heads = inner // DH
    model = x.shape[1]
    share = model // 4
    ff = (wide.shape[1] - 384) // 3
    vmem = pl.BlockSpec(memory_space=pltpu.VMEM)
    anywhere = pl.BlockSpec(memory_space=pl.ANY)
    two = (2, DH, DH)
    copies = 1 + 3 + 3 + 1 + 6 + 3 + 3
    results = [
        ((count, share), NARROW),
        ((heads, DH, DH), WIDE),
        ((count, model), WIDE),
        ((count, inner), WIDE),
        ((128, 2 * ff), NARROW),
        ((128, ff), NARROW),
        ((128, inner), NARROW),
        ((model, 128), NARROW),
    ]
    scratch = [
        (late.shape, NARROW),
        ((model, 2 * ff), NARROW),
        ((model, ff), NARROW),
        ((model, 384), NARROW),
        ((3, model, 128), WIDE),
        ((3 * ff // 128, 128, 128), WIDE),
        ((128, 3 * ff), NARROW),
        (two, NARROW),
        ((4,) + two, NARROW),
        ((4,) + two, NARROW),
        (two, WIDE),
        ((heads, DH, DH), NARROW),
        ((4, count, share), NARROW),
        ((3, count, share), NARROW),
        ((count, model), WIDE),
        ((count, model), NARROW),
        ((count, ff), WIDE),
        ((count, ff), WIDE),
        ((count, ff), NARROW),
        ((4, count, share), NARROW),
        ((3, count, share), NARROW),
        ((count, 2 * ff), NARROW),
        ((count, model), NARROW),
        ((4, count, 128), NARROW),
        ((3, count, 128), NARROW),
        ((count, model), NARROW),
        ((count, 128), NARROW),
        ((count, 256), NARROW),
    ]
    return pl.pallas_call(
        middle_kernel,
        out_shape=tuple(jax.ShapeDtypeStruct(*r) for r in results),
        in_specs=[vmem] * len(operands) + [anywhere] * 2,
        out_specs=tuple([vmem] * len(results)),
        scratch_shapes=[pltpu.VMEM(*v) for v in scratch]
        + [
            pltpu.SemaphoreType.DMA((copies,)),
            pltpu.SemaphoreType.DMA((copies,)),
            pltpu.SemaphoreType.DMA((5,)),
        ],
        compiler_params=pltpu.CompilerParams(
            collective_id=2, has_side_effects=True, vmem_limit_bytes=60 << 20
        ),
        name="middle",
    )(*operands, late, wide)


class DpSum:
    SCRATCH = 6

    @staticmethod
    def scratch(rows, width):
        small = rows // 4
        return [
            ((2, 4, rows, width), NARROW),
            ((4, rows, width), NARROW),
            ((3, rows, width), NARROW),
            ((4, small, width), WIDE),
            ((3, small, width), WIDE),
            ((small, width), WIDE),
        ]

    def __init__(self, box, full, landed_core, landed_y, by_z, landed_z, result):
        self.box, self.full, self.landed_core = box, full, landed_core
        self.landed_y, self.by_z, self.landed_z, self.result = landed_y, by_z, landed_z, result
        self.y, self.z, self.c = coords()

    def over_cores(self):
        self.pair = self.box.push(self.full.at[1 - self.c], self.landed_core, dp=moved(0, 0, True))

    def over_y(self):
        self.pair.wait_recv()
        mine = self.full.at[self.c]
        for i in range(4):
            mine[i] = (mine[i].astype(WIDE) + self.landed_core[i].astype(WIDE)).astype(NARROW)
        self.copies = [
            self.box.push(mine.at[lax.rem(self.y + k, 4)], self.landed_y.at[k - 1], dp=moved(k, 0)) for k in (2, 1, 3)
        ]

    def over_z(self):
        for copy in self.copies:
            copy.wait_recv()
        total = self.full[self.c, self.y].astype(WIDE)
        for k in range(3):
            total = total + self.landed_y[k].astype(WIDE)
        self.by_z[...] = total.reshape(self.by_z.shape)
        self.copies = [
            self.box.push(self.by_z.at[lax.rem(self.z + k, 4)], self.landed_z.at[k - 1], dp=moved(0, k))
            for k in (2, 1, 3)
        ]

    def finish(self):
        for copy in self.copies:
            copy.wait_recv()
        total = self.by_z[self.z]
        for k in range(3):
            total = total + self.landed_z[k]
        self.result[...] = total


def tail_kernel(
    pre_ref, taps_ref, aux_ref, seg_ref, q_ref, k_ref, v_ref, t_ref, w_ref, u_map_ref, state_ref, grad_ref, d_out_ref,
    u_ref, xn_ref, x_ref, d_one_ref, norm_ref, picks_ref, ranks, shared_two, g_b_ffn, g_a_out, g_a_down,
    wide_ref, thin_ref,
    grad_input, out_a_in, out_heads, out_beta, out_a_out, out_ffn, out_a_down, out_res,
    w_in, a_one, d_ext, pre_wide, halo, d_pre, e_one, part, landed, extra_landed, sums, sums_landed, pair, early_pair, ends,
    *rest,
):
    one, two, three, four = (rest[i * DpSum.SCRATCH : (i + 1) * DpSum.SCRATCH] for i in range(4))
    send, recv, local = rest[4 * DpSum.SCRATCH :]
    count, model = x_ref.shape
    inner = d_out_ref.shape[1]
    heads = inner // DH
    ff = g_a_down.shape[1]
    m = lax.axis_index("mp")
    c = lax.rem(lax.axis_index("dp"), 2)
    before, after = (lax.rem(lax.axis_index("dp") + k, 32) for k in (31, 1))
    mp_peers = {k: lax.rem(m + k, 4) for k in (1, 2, 3)}
    dp_peers = [before, after, moved(0, 0, True)]
    dp_peers += [moved(k, 0) for k in (1, 2, 3)] + [moved(0, k) for k in (1, 2, 3)]
    greet(dp_peers, list(mp_peers.values()))
    box = Mailbox(send, recv)
    early_sum, heads_sum, two_sum, one_sum = (DpSum(box, *refs) for refs in (four, one, two, three))

    def halves(refs, values):
        half = refs[0].shape[3]
        missing = 2 * half - sum(value.shape[1] for value in values)
        values = values + [jnp.zeros((128, missing), NARROW)] if missing else values
        values = jnp.concatenate(values, axis=1)
        for i in range(2):
            refs[0][i] = values[:, i * half : (i + 1) * half].reshape(4, 32, half)

    def by_core(value):
        value = value.reshape(4, 4, 2, model // 32, 128)
        return [value[:, :, i].reshape(4, model // 8, 128) for i in range(2)]

    halves(four, [g_b_ffn[...], g_a_out[...], g_a_down[...]])
    early_sum.over_cores()
    for i, value in enumerate(by_core(shared_two[...])):
        two[0][i] = value
    two_sum.over_cores()
    loads = [
        pltpu.make_async_copy(wide_ref.at[:, pl.ds(0, w_in.shape[1])], w_in, local.at[0]),
        pltpu.make_async_copy(thin_ref.at[:, pl.ds(0, a_one.shape[1])], a_one, local.at[1]),
    ]
    for load in loads:
        load.start()
    aux = aux_ref[...]
    pre_wide[...] = pre_ref[...].astype(WIDE)
    kept = (q_ref, k_ref, v_ref, t_ref, w_ref, u_map_ref)
    lanes = lax.broadcasted_iota(jnp.int32, aux.shape, 1)
    d_logit = jnp.zeros(aux.shape, WIDE)
    for first in range(0, heads, 2):
        some = list(range(first, min(first + 2, heads)))
        found = mixer_backward(
            some, pre_wide, taps_ref, aux, seg_ref[0:1, :], kept, state_ref, grad_ref, d_out_ref, d_ext
        )
        for h, value in zip(some, found):
            d_logit = jnp.where(lanes == 8 + h, value, d_logit)
        if first == 0:
            early_sum.over_y()
            two_sum.over_y()
    edges = [box.push(d_ext.at[i, pl.ds(HALO - 8, 8)], halo.at[i], dp=before) for i in range(3)]
    early_sum.over_z()
    two_sum.over_z()
    picks = picks_ref[...]
    d_logit = d_logit.astype(NARROW)
    for copy in edges:
        copy.wait_recv()
    for i in range(3):
        ref = d_ext.at[i]
        cols = slice(i * inner, (i + 1) * inner)
        d_pre[: count - 16, cols] = ref[HALO : HALO + count - 16].astype(NARROW)
        ending = ref[HALO + count - 16 :]
        d_pre[count - 16 :, cols] = jnp.concatenate([ending[:8], ending[8:] + halo[i]], axis=0).astype(NARROW)
    for j in range(3):
        cols = slice(j * inner, (j + 1) * inner)
        e_one[j] = (dot_nt(d_pre[:, cols], ranks[:, cols]) * picks).astype(NARROW)
    e_one[3] = (dot_nt(d_logit, ranks[:, 4 * inner :]) * picks).astype(NARROW)
    extra_sent = [box.push(e_one.at[mp_peers[k]], extra_landed.at[k - 1], mp=mp_peers[k]) for k in MpSum.ORDER]
    grads = [dot_tn(u_ref[:, j * 128 : (j + 1) * 128], d_pre[:, j * inner : (j + 1) * inner]) for j in range(3)]
    grads.append(dot_tn(u_ref[:, 384:], d_logit))
    halves(one, [value.astype(NARROW) for value in grads])
    heads_sum.over_cores()
    for load in loads:
        load.wait()
    share = grad_input.shape[1]
    total = MpSum(box, part, landed)
    row_sum = jnp.zeros((count, 128), WIDE)
    all_e = jnp.concatenate([e_one[j] for j in range(4)], axis=1)
    for k in (2, 1, 3, 0):
        owner = total.owner(k)
        rows = columns(owner, share)
        value = (
            dot_nt(d_pre[...], w_in[rows, : 3 * inner])
            + dot_nt(d_logit, w_in[rows, 3 * inner :])
            + dot_nt(all_e, a_one[rows, :])
        )
        part[k] = value.astype(NARROW)
        if k:
            total.send(k)
        weighted = value * norm_ref[0:1, rows] * x_ref[:, rows].astype(WIDE)
        row_sum = row_sum + jnp.sum(weighted, axis=1, keepdims=True)
    sums[...] = row_sum.T[:8]
    sums_sent = [box.push(sums, sums_landed.at[k - 1], mp=mp_peers[k]) for k in MpSum.ORDER]
    heads_sum.over_y()
    early_sum.finish()
    early_pair[c] = four[5][...]
    early_paired = box.push(four[5], early_pair.at[c], dp=moved(0, 0, True))
    for copy in extra_sent:
        copy.wait_recv()
    factor = e_one[m].astype(WIDE)
    for k in range(3):
        factor = factor + extra_landed[k].astype(WIDE)
    for i, value in enumerate(by_core(dot_tn(xn_ref[...], factor.astype(NARROW)).astype(NARROW))):
        three[0][i] = value
    one_sum.over_cores()
    heads_sum.over_z()
    one_sum.over_y()
    x_all = x_ref[...].astype(WIDE)
    scale = inverse_rms(x_all)
    mine = columns(m, share)
    d_xn = total.total()
    for copy in sums_sent:
        copy.wait_recv()
    rows = sums[...] + sums_landed[0] + sums_landed[1] + sums_landed[2]
    mean = jnp.concatenate([rows] * 16, axis=0).T[:, :1] / model
    grad_input[...] = d_one_ref[:, mine] + (
        scale * norm_ref[0:1, mine] * d_xn - x_ref[:, mine].astype(WIDE) * (scale * scale * scale * mean)
    )
    heads_sum.finish()
    pair[c] = one[5][...]
    paired = box.push(one[5], pair.at[c], dp=moved(0, 0, True))
    two_sum.finish()
    rank_rows = model // 128
    one_sum.over_z()

    def to_owners(slot, result):
        ends[slot, m] = result[columns(m, rank_rows)]
        return [
            box.push(result.at[columns(mp_peers[k], rank_rows)], ends.at[slot, m], mp=mp_peers[k])
            for k in MpSum.ORDER
        ]

    owners = to_owners(1, two[5])
    one_sum.finish()
    owners += to_owners(0, three[5])
    paired.wait_recv()
    early_paired.wait_recv()

    def own_ranks(pair):
        both = jnp.concatenate([pair[0], pair[1]], axis=1)
        return jnp.where(c == 0, both[:4], both[4:])

    rows = own_ranks(pair)
    for j in range(3):
        out_heads[j] = rows[:, j * inner : (j + 1) * inner]
    out_beta[...] = rows[:, 3 * inner + 8 : 3 * inner + 8 + heads]
    rows = own_ranks(early_pair)
    for j in range(2):
        out_ffn[j] = rows[:, j * ff : (j + 1) * ff]
    out_a_out[...] = rows[:, 2 * ff : 2 * ff + inner]
    out_a_down[...] = rows[:, 2 * ff + inner : 3 * ff + inner]
    for copy in owners:
        copy.wait_recv()
    for j in range(4):
        out_a_in[j] = ends[0, j]
    for j in range(2):
        out_a_in[4 + j] = ends[1, j]
        out_res[j] = ends[1, 2 + j]
    box.drain()


def tail(mixer, tokens, grads, wide, thin):
    model = tokens[2].shape[1]
    count, inner = mixer[-1].shape
    heads = inner // DH
    share = model // 4
    ff = grads[3].shape[1]

    def half_of(width):
        return -(-width // 256) * 128

    half, early_half = half_of(3 * inner + 128), half_of(3 * ff + inner)
    vmem = pl.BlockSpec(memory_space=pltpu.VMEM)
    anywhere = pl.BlockSpec(memory_space=pl.ANY)
    copies = 3 + 3 + 3 + 3 + 4 * 7 + 2 + 6
    results = [
        (count, share), (6, model // 128, 128), (3, 4, inner), (4, heads),
        (4, inner), (2, 4, ff), (4, ff), (2, model // 128, 128),
    ]
    scratch = [
        ((model, 3 * inner + 128), NARROW),
        ((model, 512), NARROW),
        ((3, HALO + count, inner), WIDE),
        ((HALO + count, 3 * inner), WIDE),
        ((3, 8, inner), WIDE),
        ((count, 3 * inner), NARROW),
        ((4, count, 128), NARROW),
        ((4, count, share), NARROW),
        ((3, count, share), NARROW),
        ((3, count, 128), NARROW),
        ((8, count), WIDE),
        ((3, 8, count), WIDE),
        ((2, 8, half), WIDE),
        ((2, 8, early_half), WIDE),
        ((2, 4, model // 128, 128), WIDE),
    ]
    scratch += DpSum.scratch(32, half) + DpSum.scratch(model // 8, 128) + DpSum.scratch(model // 8, 128)
    scratch += DpSum.scratch(32, early_half)
    operands = (*mixer, *tokens, *grads)
    return pl.pallas_call(
        tail_kernel,
        out_shape=tuple(jax.ShapeDtypeStruct(r, WIDE) for r in results),
        in_specs=[vmem] * len(operands) + [anywhere] * 2,
        out_specs=tuple([vmem] * len(results)),
        scratch_shapes=[pltpu.VMEM(*s) for s in scratch]
        + [
            pltpu.SemaphoreType.DMA((copies,)),
            pltpu.SemaphoreType.DMA((copies,)),
            pltpu.SemaphoreType.DMA((2,)),
        ],
        compiler_params=pltpu.CompilerParams(
            collective_id=3, has_side_effects=True, vmem_limit_bytes=60 << 20
        ),
        name="tail",
    )(*operands, wide, thin)


def on_device(
    layer_in, cotangent, segments, adapters, norm_one, norm_two, out_gain, beta_bias, conv_taps,
    w_qkv, w_beta, w_out, w_gate_up, w_down, a_in, b_heads, b_beta, a_out, b_ffn, a_down, b_res,
):
    heads = w_beta.shape[1]
    inner = heads * DH
    ff = w_down.shape[0]

    def rows_of(vector, count=8):
        return jnp.broadcast_to(vector[None, :], (count, vector.shape[0]))

    def pack_ranks(parts, blocks):
        flat = jnp.concatenate(parts, axis=1).reshape(-1, 128)
        flat = jnp.pad(flat, ((0, 64 * blocks - flat.shape[0]), (0, 0)))
        return flat.reshape(blocks, 64, 128).transpose(1, 0, 2).reshape(64, blocks * 128)

    last = jnp.concatenate(
        [
            w_gate_up.reshape(64, 2 * ff),
            w_down.T,
            pack_ranks([b_ffn.transpose(1, 0, 2).reshape(4, 2 * ff), a_down.T], 3),
        ],
        axis=1,
    )
    last = lax.all_gather(last, "dp", axis=0, tiled=True)
    beta = jnp.concatenate([w_beta, jnp.zeros((64, 64 - heads), NARROW), jnp.pad(b_beta, ((0, 60), (0, 0)))], axis=1)
    wide = jnp.concatenate(
        [
            w_qkv.reshape(64, 3 * inner),
            jnp.pad(beta, ((0, 0), (8, 56 - heads))),
            pack_ranks([b_heads.transpose(1, 0, 2).reshape(4, 3 * inner), a_out.T], 1),
        ],
        axis=1,
    )
    a_flat = a_in.reshape(16, 768)
    late_thin = jnp.concatenate([a_flat[:, 512:], b_res.transpose(2, 0, 1).reshape(16, 256)], axis=1)
    seg_row = rows_of(segments.astype(WIDE))
    taps = jnp.pad(conv_taps.reshape(3 * KW, inner).astype(WIDE), ((0, 4), (0, 0)))
    (
        wide, thin, late, pre, aux, picks, xn_one, u_one, q, k, v, t_map, w_map, u_map, reach, ranks,
        maps, sib_a, chip_a, row_a, state_in, mixer_out, normed, u_out, branch, g_full,
    ) = front(
        layer_in, cotangent, seg_row, adapters, rows_of(norm_one), rows_of(out_gain),
        rows_of(jnp.pad(beta_bias, (8, 120 - heads))), taps, wide, a_flat[:, :512], w_out.T, late_thin,
    )
    wide, thin, late = (x.reshape(2048, -1) for x in (wide, thin, late))
    output, state_grad, d_hidden_one, d_mixer, grad_b_ffn, grad_a_down, grad_a_out, shared_two = middle(
        (maps, sib_a, chip_a, row_a), (reach, mixer_out, normed, u_out, branch, picks),
        layer_in, g_full, rows_of(norm_two), rows_of(out_gain), ranks, late, last,
    )
    grad_input, d_a_in, d_b_heads, d_b_beta, d_a_out, d_b_ffn, d_a_down, d_b_res = tail(
        (pre, taps, aux, seg_row, q, k, v, t_map, w_map, u_map, state_in, state_grad, d_mixer),
        (u_one, xn_one, layer_in, d_hidden_one, rows_of(norm_one), picks, ranks),
        (shared_two, grad_b_ffn, grad_a_out, grad_a_down),
        wide,
        thin,
    )
    return (
        output, grad_input, d_a_in.transpose(1, 0, 2), d_b_heads, d_b_beta, d_a_out.T, d_b_ffn, d_a_down.T,
        d_b_res.transpose(0, 2, 1),
    )


def solution(mesh):
    placed = (
        P("dp", None),
        P("dp", "mp"),
        P("dp"),
        P(),
        P(),
        P(),
        P(),
        P("mp"),
        P(None, None, "mp"),
        P("dp", None, "mp"),
        P("dp", "mp"),
        P("mp", "dp"),
        P("dp", None, "mp"),
        P("mp", "dp"),
        P(("dp", "mp"), None, None),
        P(None, "dp", "mp"),
        P("dp", "mp"),
        P("mp", "dp"),
        P(None, "dp", "mp"),
        P("mp", "dp"),
        P(None, None, ("dp", "mp")),
    )
    return jax.shard_map(
        on_device,
        mesh=mesh,
        in_specs=placed,
        out_specs=(
            P("dp", "mp"),
            P("dp", "mp"),
            P(("dp", "mp"), None, None),
            P(None, "dp", "mp"),
            P("dp", "mp"),
            P("mp", "dp"),
            P(None, "dp", "mp"),
            P("mp", "dp"),
            P(None, None, ("dp", "mp")),
        ),
        check_vma=False,
    )
```

```python
import functools

import jax
import jax.numpy as jnp
from jax import lax
from jax.experimental import pallas as pl
from jax.experimental.pallas import tpu as pltpu
from jax.sharding import PartitionSpec as P

DH = 128
KW = 4
RANK = 16
HALO = 16
EPSILON = 1e-06
WIDE = jnp.float32
NARROW = jnp.bfloat16
MESH = pl.DeviceIdType.MESH
EXACT = lax.Precision.HIGHEST


def coords():
    place = lax.axis_index("dp")
    return place // 8, lax.rem(place // 2, 4), lax.rem(place, 2)


def place_of(y, z, c):
    return (y * 4 + z) * 2 + c


def moved(dy, dz, other_core=False):
    y, z, c = coords()
    return place_of(lax.rem(y + dy + 4, 4), lax.rem(z + dz + 4, 4), 1 - c if other_core else c)


def greet(dp_peers=(), mp_peers=()):
    barrier = pltpu.get_barrier_semaphore()
    for peer in dp_peers:
        pl.semaphore_signal(barrier, inc=1, device_id={"dp": peer}, device_id_type=MESH)
    for peer in mp_peers:
        pl.semaphore_signal(barrier, inc=1, device_id={"mp": peer}, device_id_type=MESH)
    pl.semaphore_wait(barrier, len(dp_peers) + len(mp_peers))


class Mailbox:
    def __init__(self, send, recv):
        self.send, self.recv, self.copies = send, recv, []

    def push(self, src, dst, **device):
        k = len(self.copies)
        copy = pltpu.make_async_remote_copy(
            src_ref=src,
            dst_ref=dst,
            send_sem=self.send.at[k],
            recv_sem=self.recv.at[k],
            device_id=device,
            device_id_type=MESH,
        )
        copy.start()
        self.copies.append(copy)
        return copy

    def drain(self):
        for copy in self.copies:
            copy.wait_send()


def gather_steps(box, own, out):
    me = moved(0, 0)
    half = own.shape[0] // 2
    quarter = half // 2
    sibling = moved(0, 0, True)
    kinds = []
    for kind in range(2):
        base = kind * half
        parts = (pl.ds(base, half), pl.ds(base, quarter), pl.ds(base + quarter, quarter))
        if kind == 0:
            kinds.append((parts, lambda a, b: moved(a, b)))
        else:
            kinds.append((parts, lambda a, b: moved(b, a)))
    near, across, far, far_across, shared = [], [{}, {}], [[], []], [{}, {}], []

    def open_up():
        for parts, at in kinds:
            near.append([box.push(own.at[parts[0]], out.at[me, parts[0]], dp=at(s, 0)) for s in (1, -1)])
        for k, (parts, at) in enumerate(kinds):
            across[k][0] = [box.push(own.at[parts[0]], out.at[me, parts[0]], dp=at(0, s)) for s in (1, -1)]
        shared.append(box.push(own, out.at[me], dp=sibling))

    def pass_on(k, slot):
        parts, at = kinds[k]
        block = out.at[slot, parts[0]]
        return [box.push(block, block, dp=at(0, t)) for t in (1, -1)]

    def to_sibling(k, slot):
        block = out.at[slot, kinds[k][0][0]]
        shared.append(box.push(block, block, dp=sibling))

    def from_near(i, s):
        def step():
            for k, (parts, at) in enumerate(kinds):
                near[k][i].wait_recv()
                block = out.at[at(s, 0), parts[1 + i]]
                far[k].append(box.push(block, block, dp=at(-s, 0)))
            for k, (parts, at) in enumerate(kinds):
                across[k][s] = pass_on(k, at(s, 0))
                to_sibling(k, at(s, 0))

        return step

    def from_far(k):
        def step():
            for copy in far[k]:
                copy.wait_recv()
            slot = kinds[k][1](2, 0)
            across[k][2] = pass_on(k, slot)
            to_sibling(k, slot)

        return step

    def from_across(k, f):
        def step():
            parts, at = kinds[k]
            far_across[k][f] = []
            for i, s in enumerate((-1, 1)):
                across[k][f][i].wait_recv()
                slot = at(f, s)
                block = out.at[slot, parts[1 + i]]
                far_across[k][f].append(box.push(block, block, dp=at(0, -s)))
                to_sibling(k, slot)

        return step

    def from_far_across(k, f):
        def step():
            for copy in far_across[k][f]:
                copy.wait_recv()
            to_sibling(k, kinds[k][1](f, 2))

        return step

    def close():
        for copy in shared:
            copy.wait_recv()

    steps = [open_up, from_near(0, -1), from_near(1, 1), from_far(0), from_far(1)]
    steps += [from_across(k, f) for f in (0, -1, 1, 2) for k in range(2)]
    steps += [from_far_across(k, f) for f in (0, -1, 1, 2) for k in range(2)]
    return steps + [close]


def gather_peers():
    return [moved(1, 0), moved(-1, 0), moved(0, 1), moved(0, -1), moved(0, 0, True)]


GATHER_COPIES = 71


def half_dot(left, right, dims=(((1,), (0,)), ((), ()))):
    high = right.astype(NARROW)
    low = (right - high.astype(WIDE)).astype(NARROW)
    return lax.dot_general(left, high, dims, preferred_element_type=WIDE) + lax.dot_general(
        left, low, dims, preferred_element_type=WIDE
    )


TURNED = (((0,), (0,)), ((), ()))


def two_parts(value):
    high = value.astype(NARROW)
    return high, (value - high.astype(WIDE)).astype(NARROW)


def wide_dot(left, right, left_dim=1, right_dim=0):
    left_high, left_low = two_parts(left)
    right_high, right_low = two_parts(right)

    def part(one, two):
        return lax.dot_general(one, two, (((left_dim,), (right_dim,)), ((), ())), preferred_element_type=WIDE)

    return part(left_high, right_high) + (part(left_high, right_low) + part(left_low, right_high))


def convolve(pre_ref, taps_ref, part, head, inner, aux):
    count = aux.shape[0]
    cols = slice(part * inner + head * DH, part * inner + (head + 1) * DH)
    taps = taps_ref[:, head * DH : (head + 1) * DH]
    total = pre_ref[pl.ds(HALO, count), cols] * taps[part : part + 1]
    for j in range(1, KW):
        shifted = pre_ref[pl.ds(HALO - j, count), cols]
        total = total + shifted * aux[:, j : j + 1] * taps[3 * j + part : 3 * j + part + 1]
    return total


def spread_taps(taps_ref, taps):
    for j in range(KW):
        taps[3 * j : 3 * j + 3, :] = taps_ref[j].astype(WIDE)


def masks(aux, seg_row):
    same = aux[:, 6:7] == seg_row
    shape = (aux.shape[0], aux.shape[0])
    row = lax.broadcasted_iota(jnp.int32, shape, 0)
    col = lax.broadcasted_iota(jnp.int32, shape, 1)
    return row, col, same


def each(step, *lists):
    return [step(*items) for items in zip(*lists)]


def lower_inverses(lowers, row, col, tick):
    near = [jnp.where(row // 8 == col // 8, lower, 0.0) for lower in lowers]
    square = each(lambda a: wide_dot(a, a), near)
    inverse = [jnp.where(row == col, 1.0, 0.0) - a for a in near]
    inverse = each(lambda x, s: x + wide_dot(x, s), inverse, square)
    square = each(lambda s: wide_dot(s, s), square)
    inverse = each(lambda x, s: x + wide_dot(x, s), inverse, square)
    size = 8
    while size < row.shape[0]:
        link = (row // (2 * size) == col // (2 * size)) & (row // size != col // size)
        middle = each(lambda lower, x: wide_dot(jnp.where(link, lower, 0.0), x), lowers, inverse)
        inverse = each(lambda x, y: x - wide_dot(x, y), inverse, middle)
        size *= 2
        tick()
    return inverse


def mixer_forward(heads, pre_ref, taps_ref, aux, seg_row, out_ref, reach_ref, map_ref, offset_ref, kept, tick):
    q_ref, k_ref, v_ref, t_ref, w_ref, u_ref = kept
    count = aux.shape[0]
    inner = out_ref.shape[1]
    linked, ending = aux[:, 4:5], aux[:, 5:6]
    row, col, same = masks(aux, seg_row)
    rate = [aux[:, 8 + h : 9 + h] for h in heads]
    cols = [slice(h * DH, (h + 1) * DH) for h in heads]

    def act(part):
        convs = [convolve(pre_ref, taps_ref, part, h, inner, aux) for h in heads]
        return [conv * jax.nn.sigmoid(conv) for conv in convs]

    def unit(a):
        return a * lax.rsqrt(jnp.sum(a * a, axis=1, keepdims=True) + EPSILON)

    k = each(unit, act(1))
    gram = each(lambda b: wide_dot(b, b, 1, 1), k)
    lowers = each(lambda g, r: jnp.where((row > col) & same, g * r, 0.0), gram, rate)
    q, v = each(unit, act(0)), act(2)
    for i in range(len(heads)):
        q_ref[:, cols[i]] = q[i]
        k_ref[:, cols[i]] = k[i]
        v_ref[:, cols[i]] = v[i]
    scores = each(lambda a, b: jnp.where((row >= col) & same, wide_dot(a, b, 1, 1), 0.0), q, k)
    tick()
    inverse = lower_inverses(lowers, row, col, tick)
    written = each(
        lambda t, a, b, r: wide_dot(t, jnp.concatenate([a, b * linked], axis=1) * r), inverse, v, k, rate
    )
    ends = each(lambda b, w: wide_dot(b * ending, w, 0, 0), k, written)
    mixed = each(wide_dot, scores, written)
    eye = jnp.where(row[:DH, :DH] == col[:DH, :DH], 1.0, 0.0)
    last = aux[count - 1 :, 4:5]
    for i, h in enumerate(heads):
        t_ref[h] = inverse[i]
        w_ref[:, cols[i]] = written[i][:, :DH]
        u_ref[:, cols[i]] = written[i][:, DH:]
        offset_ref[h] = ends[i][:, :DH].astype(offset_ref.dtype)
        map_ref[h] = (eye * last - ends[i][:, DH:]).astype(map_ref.dtype)
        out_ref[:, cols[i]] = mixed[i][:, :DH]
        reach_ref[:, cols[i]] = q[i] * linked - mixed[i][:, DH:]
    tick()


def mixer_backward(heads, pre_ref, taps_ref, aux, seg_row, kept, state_ref, grad_ref, d_out_ref, d_ext, between):
    q_ref, k_ref, v_ref, t_ref, w_ref, u_ref = kept
    count = aux.shape[0]
    inner = d_out_ref.shape[1]
    linked, ending = aux[:, 4:5], aux[:, 5:6]
    row, col, same = masks(aux, seg_row)
    upto = (row >= col) & same
    below = (row > col) & same

    def take(ref):
        return [ref[:, h * DH : (h + 1) * DH] for h in heads]

    rate = [aux[:, 8 + h : 9 + h] for h in heads]
    q, k, v, d_out = take(q_ref), take(k_ref), take(v_ref), take(d_out_ref)
    state, grad = [state_ref[h] for h in heads], [grad_ref[h] for h in heads]
    written = each(lambda w, u, s: w - wide_dot(u, s), take(w_ref), take(u_ref), state)
    scores = each(lambda a, b: jnp.where(upto, wide_dot(a, b, 1, 1), 0.0), q, k)
    d_written = each(
        lambda a, d, b, g: wide_dot(a, d, 0, 0) + wide_dot(b * ending, g), scores, d_out, k, grad
    )
    d_right = each(lambda t, d: wide_dot(t, d, 0, 0), [t_ref[h] for h in heads], d_written)
    d_scores = each(lambda d, w: jnp.where(upto, wide_dot(d, w, 1, 1), 0.0), d_out, written)
    between()
    d_lower = each(lambda d, w: jnp.where(below, -wide_dot(d, w, 1, 1), 0.0), d_right, written)
    d_q = each(
        lambda ds, b, d, s: wide_dot(ds, b) + linked * wide_dot(d, s, 1, 1), d_scores, k, d_out, state
    )
    d_k = each(
        lambda ds, a, w, g: wide_dot(ds, a, 0, 0) + ending * wide_dot(w, g, 1, 1), d_scores, q, written, grad
    )
    d_rate = each(
        lambda d, a, b, s: jnp.sum(d * (a - linked * wide_dot(b, s)), axis=1, keepdims=True), d_right, v, k, state
    )
    d_rate = each(
        lambda r, d, b: r + jnp.sum(d * wide_dot(b, b, 1, 1), axis=1, keepdims=True), d_rate, d_lower, k
    )
    d_k = each(lambda dk, r, d, s: dk - (linked * r) * wide_dot(d, s, 1, 1), d_k, rate, d_right, state)
    d_gram = each(lambda d, r: d * r, d_lower, rate)
    d_k = each(lambda dk, d, b: dk + wide_dot(d, b) + wide_dot(d, b, 0, 0), d_k, d_gram, k)
    d_v = each(lambda r, d: r * d, rate, d_right)
    for i, h in enumerate(heads):
        for part, (unit, d) in enumerate(((q[i], d_q[i]), (k[i], d_k[i]), (None, d_v[i]))):
            cols = slice(h * DH, (h + 1) * DH)
            conv = convolve(pre_ref, taps_ref, part, h, inner, aux)
            gate = jax.nn.sigmoid(conv)
            if unit is not None:
                act = conv * gate
                scale = lax.rsqrt(jnp.sum(act * act, axis=1, keepdims=True) + EPSILON)
                d = (d - unit * jnp.sum(unit * d, axis=1, keepdims=True)) * scale
            d_conv = d * gate * (1.0 + conv * (1.0 - gate))
            d_ext[part, :HALO, cols] = jnp.zeros((HALO, DH), WIDE)
            d_ext[part, HALO:, cols] = d_conv * taps_ref[part : part + 1, cols]
            for j in range(1, KW):
                term = d_conv * taps_ref[3 * j + part : 3 * j + part + 1, cols] * aux[:, j : j + 1]
                d_ext[part, pl.ds(HALO - j, count), cols] += term
    return each(lambda d, r: d * r * (1.0 - r), d_rate, rate)


def inverse_rms(values):
    return lax.rsqrt(jnp.mean(values * values, axis=-1, keepdims=True) + EPSILON)


def norm_back(values, scale, gain, grad_out):
    weighted = grad_out * gain
    return scale * weighted - values * scale**3 * jnp.mean(weighted * values, axis=-1, keepdims=True)


def dot(left, right):
    return jnp.dot(left, right, preferred_element_type=WIDE)


def dot_nt(left, right):
    return lax.dot_general(left, right, (((1,), (1,)), ((), ())), preferred_element_type=WIDE)


def dot_tn(left, right):
    return lax.dot_general(left, right, (((0,), (0,)), ((), ())), preferred_element_type=WIDE)


class Chain:
    def __init__(self, box, a_ref, sib_a, chip_a, row_a):
        self.box, self.a_ref, self.sib_a, self.chip_a, self.row_a = box, a_ref, sib_a, chip_a, row_a
        self.y, self.z, self.c = coords()
        self.first = self.c == 0
        self.sibling = moved(0, 0, True)
        self.z_peers = {k: moved(0, k) for k in (1, 2, 3)}
        self.y_peers = {k: moved(k, 0) for k in (1, 2, 3)}
        self.mine = pl.ds(pl.multiple_of(2 * self.c, 2), 2)
        self.theirs = pl.ds(pl.multiple_of(2 * (1 - self.c), 2), 2)

    def peers(self):
        return [self.sibling] + list(self.z_peers.values()) + list(self.y_peers.values())

    def swap(self, ref, sib):
        return self.box.push(ref.at[self.theirs], sib, dp=self.sibling)

    def ordered(self, ref, sib, h):
        own, other = ref[2 * self.c + h], sib[h]
        return jnp.where(self.first, own, other), jnp.where(self.first, other, own)

    def spread(self, refs, place, peers):
        return [self.box.push(ref.at[place], ref.at[place], dp=peers[k]) for k in (2, 1, 3) for ref in refs]

    def start_forward(self, b_ref, sib_b, chip_b, row_b, pass_on):
        self.b_ref, self.sib_b, self.chip_b, self.row_b, self.pass_on = b_ref, sib_b, chip_b, row_b, pass_on
        self.pair = [self.swap(self.a_ref, self.sib_a), self.swap(b_ref, sib_b)]

    def chips_forward(self):
        for copy in self.pair:
            copy.wait_recv()
        self.lower = []
        for h in range(2):
            a_low, a_high = self.ordered(self.a_ref, self.sib_a, h)
            b_low, b_high = self.ordered(self.b_ref, self.sib_b, h)
            self.lower.append((a_low, b_low))
            self.chip_a[self.z, h] = lax.dot(a_high, a_low, preferred_element_type=WIDE).astype(NARROW)
            self.chip_b[self.z, h] = (
                lax.dot(a_high, b_low, preferred_element_type=WIDE) + b_high.astype(WIDE)
            ).astype(NARROW)
        self.ring = self.spread((self.chip_a, self.chip_b), self.z, self.z_peers)

    def rows_forward(self):
        for copy in self.ring:
            copy.wait_recv()
        for h in range(2):
            total_a, total_b = self.chip_a[0, h].astype(WIDE), self.chip_b[0, h].astype(WIDE)
            for i in range(1, 4):
                total_a = half_dot(self.chip_a[i, h], total_a)
                total_b = half_dot(self.chip_a[i, h], total_b) + self.chip_b[i, h].astype(WIDE)
            self.row_a[self.y, h] = total_a.astype(NARROW)
            self.row_b[self.y, h] = total_b.astype(NARROW)
        self.ring = self.spread((self.row_a, self.row_b), self.y, self.y_peers)

    def finish_forward(self, out):
        for copy in self.ring:
            copy.wait_recv()
        for h in range(2):
            state = jnp.zeros((DH, DH), WIDE)
            for i in range(3):
                longer = half_dot(self.row_a[i, h], state) + self.row_b[i, h].astype(WIDE)
                state = jnp.where(i < self.y, longer, state)
            for i in range(3):
                longer = half_dot(self.chip_a[i, h], state) + self.chip_b[i, h].astype(WIDE)
                state = jnp.where(i < self.z, longer, state)
            a_low, b_low = self.lower[h]
            middle = half_dot(a_low, state) + b_low.astype(WIDE)
            out[2 * self.c + h] = jnp.where(self.first, state, middle)
            self.pass_on[h] = jnp.where(self.first, middle, state)
        self.box.push(self.pass_on, out.at[self.mine], dp=self.sibling).wait_recv()

    def start_backward(self, g_ref, sib_g, chip_g, row_g, pass_on):
        self.g_ref, self.sib_g, self.chip_g, self.row_g, self.pass_on = g_ref, sib_g, chip_g, row_g, pass_on
        self.pair = [self.swap(g_ref, sib_g)]

    def chips_backward(self):
        for copy in self.pair:
            copy.wait_recv()
        self.upper_g = []
        for h in range(2):
            a_low, _ = self.ordered(self.a_ref, self.sib_a, h)
            g_low, g_high = self.ordered(self.g_ref, self.sib_g, h)
            self.upper_g.append(g_high)
            self.chip_g[self.z, h] = (
                lax.dot_general(a_low, g_high, TURNED, preferred_element_type=WIDE) + g_low.astype(WIDE)
            ).astype(NARROW)
        self.ring = self.spread((self.chip_g,), self.z, self.z_peers)

    def rows_backward(self):
        for copy in self.ring:
            copy.wait_recv()
        for h in range(2):
            total = self.chip_g[3, h].astype(WIDE)
            for i in (2, 1, 0):
                total = half_dot(self.chip_a[i, h], total, TURNED) + self.chip_g[i, h].astype(WIDE)
            self.row_g[self.y, h] = total.astype(NARROW)
        self.ring = self.spread((self.row_g,), self.y, self.y_peers)

    def finish_backward(self, out):
        for copy in self.ring:
            copy.wait_recv()
        for h in range(2):
            grad = jnp.zeros((DH, DH), WIDE)
            for i in (3, 2, 1):
                longer = half_dot(self.row_a[i, h], grad, TURNED) + self.row_g[i, h].astype(WIDE)
                grad = jnp.where(i > self.y, longer, grad)
            for i in (3, 2, 1):
                longer = half_dot(self.chip_a[i, h], grad, TURNED) + self.chip_g[i, h].astype(WIDE)
                grad = jnp.where(i > self.z, longer, grad)
            _, a_high = self.ordered(self.a_ref, self.sib_a, h)
            middle = half_dot(a_high, grad, TURNED) + self.upper_g[h].astype(WIDE)
            out[2 * self.c + h] = jnp.where(self.first, middle, grad)
            self.pass_on[h] = jnp.where(self.first, grad, middle)
        self.box.push(self.pass_on, out.at[self.mine], dp=self.sibling).wait_recv()


def columns(i, width):
    return pl.ds(pl.multiple_of(i * width, width), width)


class MpSum:
    ORDER = (2, 1, 3)

    def __init__(self, box, part, landed):
        self.box, self.part, self.landed = box, part, landed
        self.m = lax.axis_index("mp")
        self.peers = {k: lax.rem(self.m + k, 4) for k in (1, 2, 3)}
        self.copies = ([], [])
        self.half = part.shape[1] // 2

    def owner(self, k):
        return lax.rem(self.m + k, 4)

    def rows(self, half):
        return pl.ds(half * self.half, self.half)

    def send(self, k, half):
        rows = self.rows(half)
        self.copies[half].append(
            self.box.push(self.part.at[k, rows], self.landed.at[k - 1, rows], mp=self.peers[k])
        )

    def send_half(self, half):
        for k in self.ORDER:
            self.send(k, half)

    def total(self, half):
        for copy in self.copies[half]:
            copy.wait_recv()
        rows = self.rows(half)
        total = self.part[0, rows].astype(WIDE)
        for k in range(3):
            total = total + self.landed[k, rows].astype(WIDE)
        return total

    def share(self, out):
        width = self.part.shape[2]
        shared = []
        for half in range(2):
            rows = self.rows(half)
            out[rows, columns(self.m, width)] = self.total(half).astype(out.dtype)
            block = out.at[rows, columns(self.m, width)]
            shared += [self.box.push(block, block, mp=self.peers[k]) for k in self.ORDER]
        return shared


def unpack_ranks(block, spread, ranks, first, tiles):
    for q in range(4):
        for t in range(tiles):
            at = first + q * tiles + t
            spread[t, pl.ds(q, 32, stride=4), :] = block[at // 64, pl.ds(at % 64, 32, stride=64), :]
    for t in range(tiles):
        ranks[:, t * 128 : (t + 1) * 128] = spread[t].astype(ranks.dtype)


def front_kernel(
    x_ref, seg_ref, adapters, norm_ref, gain_ref, bias_ref, taps_ref, wide_ref, thin_ref, late_ref, late_thin,
    wide_out, thin_out, late_out, pre_out, xn_out, kept_out, t_out, aux_ref, picks_ref, u_ref,
    reach, ranks, a_ref, sib_a, chip_a, row_a, state_out, mixer_out, normed, u_out_ref, branch,
    pre, xn_ref, kept, t_ref, wide_all, thin_all, late_all, thin_own, late_own, halo_x, seg_ext, xn_ext, pre_wide, block, spread, b_beta,
    b_ref, out_zero, sib_b, chip_b, row_b, pass_on, part, landed, taps, send, recv, local,
):
    count, model = x_ref.shape
    heads = a_ref.shape[0]
    inner = heads * DH
    m = lax.axis_index("mp")
    place = lax.axis_index("dp")
    before, after = lax.rem(place + 31, 32), lax.rem(place + 1, 32)
    mp_peers = {k: lax.rem(m + k, 4) for k in (1, 2, 3)}
    box = Mailbox(send, recv)
    chain = Chain(box, a_ref, sib_a, chip_a, row_a)
    greet([before, after] + chain.peers(), list(mp_peers.values()))
    me = moved(0, 0)
    seg_row = seg_ref[...].astype(WIDE)
    seg_ext[HALO:] = jnp.broadcast_to(seg_row, (128, count)).T
    edges = [
        box.push(x_ref.at[pl.ds(count - HALO, HALO)], halo_x, dp=after),
        box.push(seg_ext.at[pl.ds(count, HALO)], seg_ext.at[pl.ds(0, HALO)], dp=after),
    ]
    thin_rows = thin_ref.shape[0]
    mine = pl.ds(pl.multiple_of(m * thin_rows, thin_rows), thin_rows)
    crossing = [box.push(thin_ref, thin_own.at[mine], mp=peer) for peer in mp_peers.values()]
    late_cols = pl.ds(late_ref.shape[1], late_thin.shape[1])
    late_crossing = [box.push(late_thin, late_own.at[mine, late_cols], mp=peer) for peer in mp_peers.values()]
    keep = [
        pltpu.make_async_copy(wide_ref, wide_all.at[me], local.at[0]),
        pltpu.make_async_copy(thin_ref, thin_own.at[mine], local.at[1]),
        pltpu.make_async_copy(late_ref, late_own.at[:, pl.ds(0, late_ref.shape[1])], local.at[2]),
        pltpu.make_async_copy(late_thin, late_own.at[mine, late_cols], local.at[3]),
    ]
    for copy in keep:
        copy.start()
    wide_steps = gather_steps(box, wide_ref, wide_all)
    thin_steps = gather_steps(box, thin_own, thin_all)
    late_steps = gather_steps(box, late_own, late_all)
    wide_steps.pop(0)()
    share = model // 4
    keep[1].wait()
    for copy in crossing:
        copy.wait_recv()
    keep_thin = pltpu.make_async_copy(thin_own, thin_all.at[me], local.at[4])
    keep_thin.start()
    thin_steps.pop(0)()

    def normal(rows):
        rows = rows.astype(WIDE)
        return (rows * inverse_rms(rows) * norm_ref[0:1, :]).astype(NARROW)

    xn_ref[...] = normal(x_ref[...])
    xn_ext[HALO:] = xn_ref[...]
    for one, two in zip(wide_steps, thin_steps):
        one()
        two()
    keep[0].wait()
    keep_thin.wait()
    keep[2].wait()
    keep[3].wait()
    for copy in late_crossing:
        copy.wait_recv()
    keep_late = pltpu.make_async_copy(late_own, late_all.at[me], local.at[5])
    keep_late.start()
    late_steps.pop(0)()
    to_hbm = [
        pltpu.make_async_copy(wide_all, wide_out, local.at[6]),
        pltpu.make_async_copy(thin_all, thin_out, local.at[7]),
    ]
    for copy in to_hbm:
        copy.start()

    def tick(steps):
        for _ in range(min(steps, len(late_steps))):
            late_steps.pop(0)()

    for copy in edges:
        copy.wait_recv()
    xn_ext[:HALO] = normal(halo_x[...])
    seg_ext[:HALO] = jnp.where(place == 0, -1.0, seg_ext[:HALO])
    spread_taps(taps_ref, taps)
    lanes = lax.broadcasted_iota(jnp.int32, seg_ext.shape, 1)
    seg_all = seg_ext[...]
    per_token = jnp.zeros(seg_all.shape, WIDE)
    for s in range(adapters.shape[0]):
        per_token = jnp.where(seg_all == float(s), adapters[s].astype(WIDE), per_token)
    picks_ext = jnp.where(per_token == (lanes // RANK).astype(WIDE), 1.0, 0.0)
    picks_ref[...] = picks_ext[HALO:]
    tiles = inner // 128
    for i in range(2):
        lane_block = slice(3 * inner + i * 128, 3 * inner + (i + 1) * 128)
        block[i] = wide_all[:, :, lane_block].reshape(model, 128).astype(WIDE)
    for q in range(4):
        b_beta[pl.ds(q, 32, stride=4), :] = block[0, pl.ds(q, 32, stride=64), :]
    unpack_ranks(block.at[pl.ds(1, 1)], spread, ranks.at[:, pl.ds(0, 4 * inner)], 0, 4 * tiles)
    beta = pltpu.roll(b_beta[...], 64, 1)
    beta_lane = lax.broadcasted_iota(jnp.int32, beta.shape, 1)
    beta = jnp.where((beta_lane >= 8) & (beta_lane < 8 + heads), beta, 0.0)
    ranks[:, 4 * inner :] = beta.astype(NARROW)
    tick(1)
    u_ext = dot(xn_ext[...], thin_all[...].reshape(model, thin_all.shape[2]))
    u_ext = (u_ext * jnp.concatenate([picks_ext] * 4, axis=1)).astype(NARROW)
    u_ref[...] = u_ext[HALO:]
    tick(1)
    for j in range(3):
        cols = slice(j * inner, (j + 1) * inner)
        value = dot(xn_ext[...], wide_all[:, :, cols].reshape(model, inner)) + dot(
            u_ext[:, j * 128 : (j + 1) * 128], ranks[:, cols]
        )
        value = value.astype(NARROW)
        pre[:, cols] = value
        pre_wide[:, cols] = value.astype(WIDE)
        tick(1)
    w_beta = wide_all[:, :, 3 * inner : 3 * inner + 128].reshape(model, 128)
    logits = dot(xn_ref[...], w_beta) + dot(u_ref[:, 384:], ranks[:, 4 * inner :])
    seg = seg_all[HALO:]
    lane = lanes[HALO:]
    for h in range(heads):
        logits = jnp.where(lane == 8 + h, logits + bias_ref[h], logits)
    aux = jnp.where((lane >= 8) & (lane < 8 + heads), jax.nn.sigmoid(logits), 0.0)
    for j in range(KW):
        aux = jnp.where((lane == j) & (seg_ext[pl.ds(HALO - j, count)] == seg), 1.0, aux)
    aux = jnp.where((lane == 4) & (seg == seg_ext[HALO - 1 : HALO]), 1.0, aux)
    aux = jnp.where((lane == 5) & (seg == seg_ext[HALO + count - 1 : HALO + count]), 1.0, aux)
    aux = jnp.where(lane == 6, seg, aux)
    aux_ref[...] = aux
    mixer_forward(
        list(range(heads)), pre_wide, taps, aux, seg_row, out_zero, reach, a_ref, b_ref,
        (*(kept.at[i] for i in range(3)), t_ref, *(kept.at[i] for i in (3, 4))), lambda: tick(2),
    )
    for i, (source, target) in enumerate(((pre, pre_out), (xn_ref, xn_out), (kept, kept_out), (t_ref, t_out))):
        to_hbm.append(pltpu.make_async_copy(source, target, local.at[9 + i]))
        to_hbm[-1].start()
    chain.start_forward(b_ref, sib_b, chip_b, row_b, pass_on)
    tick(2)
    chain.chips_forward()
    tick(2)
    chain.rows_forward()
    tick(len(late_steps))
    chain.finish_forward(state_out)
    keep_late.wait()
    keep_late_out = pltpu.make_async_copy(late_all, late_out, local.at[8])
    keep_late_out.start()
    for h in range(heads):
        cols = slice(h * DH, (h + 1) * DH)
        rows = out_zero[:, cols] + wide_dot(reach[:, cols], state_out[h])
        mixer_out[:, cols] = rows
        normed[:, cols] = (rows * inverse_rms(rows) * gain_ref[0:1, :]).astype(NARROW)
    u_out = (dot_nt(normed[...], ranks[:, 3 * inner : 4 * inner]) * picks_ref[...]).astype(NARROW)
    u_out_ref[...] = u_out
    one = MpSum(box, part, landed)
    for k in (2, 1, 3, 0):
        groups = pl.ds(one.owner(k) * (share // 64), share // 64)
        w_out = late_all[groups, :, :inner].reshape(share, inner)
        b_mix = late_all[groups, :, inner + 256 : inner + 384].reshape(share, 128)
        part[k] = (dot_nt(normed[...], w_out) + dot_nt(u_out, b_mix)).astype(NARROW)
        if k:
            one.send(k, 0)
    one.send_half(1)
    for copy in one.share(branch):
        copy.wait_recv()
    for copy in to_hbm + [keep_late_out]:
        copy.wait()
    box.drain()


def front(x, seg_row, adapters, norm, gain, bias, taps, wide, thin, late, late_thin):
    count, model = x.shape
    inner = taps.shape[2]
    heads = inner // DH
    share = model // 4
    vmem = pl.BlockSpec(memory_space=pltpu.VMEM)
    anywhere = pl.BlockSpec(memory_space=pl.ANY)
    smem = pl.BlockSpec(memory_space=pltpu.SMEM)
    two = (2, DH, DH)
    square = (heads, DH, DH)
    by_head = ((count, inner), WIDE)
    thin_all, late_all = (32, 64, thin.shape[1]), (32, 64, late.shape[1] + late_thin.shape[1])
    early = [
        ((HALO + count, 3 * inner), NARROW),
        ((count, model), NARROW),
        ((5, count, inner), WIDE),
        ((heads, count, count), WIDE),
    ]
    results = [
        ((32,) + wide.shape, NARROW),
        (thin_all, NARROW),
        (late_all, NARROW),
        *early,
        ((count, 128), WIDE),
        ((count, 128), WIDE),
        ((count, 512), NARROW),
        by_head,
        ((128, 4 * inner + 128), NARROW),
        (square, NARROW),
        (two, NARROW),
        ((4,) + two, NARROW),
        ((4,) + two, NARROW),
        (square, WIDE),
        by_head,
        ((count, inner), NARROW),
        ((count, 128), NARROW),
        ((count, model), NARROW),
    ]
    scratch = early + [
        ((32,) + wide.shape, NARROW),
        (thin_all, NARROW),
        (late_all, NARROW),
        (thin_all[1:], NARROW),
        (late_all[1:], NARROW),
        ((HALO, model), NARROW),
        ((HALO + count, 128), WIDE),
        ((HALO + count, model), NARROW),
        ((HALO + count, 3 * inner), WIDE),
        ((2, model, 128), WIDE),
        ((4 * inner // 128, 128, 128), WIDE),
        ((128, 128), WIDE),
        (square, NARROW),
        by_head,
        (two, NARROW),
        ((4,) + two, NARROW),
        ((4,) + two, NARROW),
        (two, WIDE),
        ((4, count, share), NARROW),
        ((3, count, share), NARROW),
        ((16, inner), WIDE),
    ]
    copies = 3 * GATHER_COPIES + 2 + 3 + 3 + 2 + 6 + 6 + 1 + 12
    return pl.pallas_call(
        front_kernel,
        out_shape=tuple(jax.ShapeDtypeStruct(*r) for r in results),
        in_specs=[vmem] * 2 + [smem] + [vmem] * 2 + [smem, vmem] + [anywhere] * 4,
        out_specs=tuple([anywhere] * 7 + [vmem] * (len(results) - 7)),
        scratch_shapes=[pltpu.VMEM(*s) for s in scratch]
        + [
            pltpu.SemaphoreType.DMA((copies,)),
            pltpu.SemaphoreType.DMA((copies,)),
            pltpu.SemaphoreType.DMA((13,)),
        ],
        compiler_params=pltpu.CompilerParams(
            collective_id=0, has_side_effects=True, vmem_limit_bytes=60 << 20
        ),
        name="front",
    )(x, seg_row, adapters, norm, gain, bias, taps, wide, thin, late, late_thin)


def middle_kernel(
    a_ref, sib_a, chip_a, row_a, reach, mixer_out, normed, u_out_ref, branch, picks_ref, x_ref, g_full, norm_ref, gain_ref,
    ranks_one, late_ref, wide_ref,
    output, grad_out, d_one_out, d_mixer_out, g_b_ffn, g_a_down, g_a_out, g_shared,
    late, w_gu, w_down, packed, block, spread, ranks, sib_g, chip_g, row_g, pass_on, g_maps,
    part, landed, hidden_one, xn_two, gate, up, hidden, ffn_part, ffn_landed,
    d_gate_up, d_xn, extra, extra_landed, d_branch, e_down_ref, u_two_ref,
    send, recv, local,
):
    count = x_ref.shape[0]
    heads = a_ref.shape[0]
    inner = heads * DH
    ff = gate.shape[1]
    model = x_ref.shape[1]
    share = output.shape[1]
    m = lax.axis_index("mp")
    loads = [
        pltpu.make_async_copy(late_ref, late, local.at[0]),
        pltpu.make_async_copy(wide_ref.at[:, pl.ds(3 * ff, packed.shape[1])], packed, local.at[1]),
        pltpu.make_async_copy(wide_ref.at[:, pl.ds(0, ff)], w_gu.at[:, pl.ds(0, ff)], local.at[2]),
        pltpu.make_async_copy(wide_ref.at[:, pl.ds(ff, ff)], w_gu.at[:, pl.ds(ff, ff)], local.at[3]),
        pltpu.make_async_copy(wide_ref.at[:, pl.ds(2 * ff, ff)], w_down, local.at[4]),
    ]
    for load in loads:
        load.start()
    box = Mailbox(send, recv)
    chain = Chain(box, a_ref, sib_a, chip_a, row_a)
    mp_peers = {k: lax.rem(m + k, 4) for k in (1, 2, 3)}
    greet(chain.peers(), list(mp_peers.values()))
    picks = picks_ref[...]
    u_out = u_out_ref[...]
    a_out = ranks_one.at[:, pl.ds(3 * inner, inner)]
    a_down = ranks.at[:, pl.ds(2 * ff, ff)]
    w_out, a_two = late.at[:, pl.ds(0, inner)], late.at[:, pl.ds(inner, 256)]
    b_mix, b_down = late.at[:, pl.ds(inner + 256, 128)], late.at[:, pl.ds(inner + 384, 128)]

    rows = x_ref[...].astype(WIDE) + branch[...].astype(WIDE)
    hidden_one[...] = rows
    scale_two = inverse_rms(rows)
    xn_two[...] = (rows * scale_two * norm_ref[0:1, :]).astype(NARROW)
    two_picks = jnp.concatenate([picks, picks], axis=1)
    loads[0].wait()
    u_two_ref[...] = (dot(xn_two[...], a_two[...]) * two_picks).astype(NARROW)
    for load in loads[1:4]:
        load.wait()
    for i in range(3):
        block[i] = packed[:, i * 128 : (i + 1) * 128].astype(WIDE)
    unpack_ranks(block, spread, ranks, 0, 3 * ff // 128)
    gate[...] = dot(xn_two[...], w_gu[:, :ff]) + dot(u_two_ref[:, :128], ranks[:, :ff])
    up[...] = dot(xn_two[...], w_gu[:, ff:]) + dot(u_two_ref[:, 128:], ranks[:, ff : 2 * ff])
    hidden[...] = (gate[...] * jax.nn.sigmoid(gate[...]) * up[...]).astype(NARROW)
    loads[4].wait()

    e_down = (dot(g_full[...], b_down[...]) * picks).astype(NARROW)
    e_down_ref[...] = e_down
    d_hidden = dot(g_full[...], w_down[...]) + dot(e_down, a_down[...])
    sig = jax.nn.sigmoid(gate[...])
    d_gate_up[:, :ff] = (d_hidden * up[...] * sig * (1.0 + gate[...] * (1.0 - sig))).astype(NARROW)
    d_gate_up[:, ff:] = (d_hidden * gate[...] * sig).astype(NARROW)
    e_two = [
        (dot_nt(d_gate_up[:, j * ff : (j + 1) * ff], ranks[:, j * ff : (j + 1) * ff]) * picks).astype(NARROW)
        for j in range(2)
    ]
    two = MpSum(box, part, landed)
    for k in (2, 1, 3, 0):
        rows = columns(two.owner(k), share)
        part[k] = (
            dot_nt(d_gate_up[...], w_gu[rows, :]) + dot_nt(jnp.concatenate(e_two, axis=1), a_two[rows, :])
        ).astype(NARROW)
        if k:
            two.send(k, 0)
    two.send_half(1)
    u_down = (dot_nt(hidden[...], a_down[...]) * picks).astype(NARROW)
    for j, value in enumerate((e_two[0], e_two[1], u_out, u_down)):
        extra[j] = value
    shared = two.share(d_xn)
    extra_sent = [box.push(extra.at[mp_peers[k]], extra_landed.at[k - 1], mp=mp_peers[k]) for k in MpSum.ORDER]
    three = MpSum(box, ffn_part, ffn_landed)
    for k in (2, 1, 3, 0):
        rows = columns(three.owner(k), share)
        ffn_part[k] = (dot_nt(hidden[...], w_down[rows, :]) + dot_nt(u_down, b_down[rows, :])).astype(NARROW)
    for copy in shared:
        copy.wait_recv()
    three.send_half(0)
    three.send_half(1)

    rows = hidden_one[...]
    scale_two = inverse_rms(rows)
    d_one = g_full[...].astype(WIDE) + norm_back(rows, scale_two, norm_ref[0:1, :], d_xn[...].astype(WIDE))
    d_one_out[...] = d_one
    d_branch[...] = d_one.astype(NARROW)
    e_out = (dot(d_branch[...], b_mix[...]) * picks).astype(NARROW)
    d_normed = dot(d_branch[...], w_out[...]) + dot(e_out, a_out[...])
    for h in range(heads):
        cols = slice(h * DH, (h + 1) * DH)
        rows = mixer_out[:, cols]
        d_rows = norm_back(rows, inverse_rms(rows), gain_ref[0:1, :], d_normed[:, cols])
        d_mixer_out[:, cols] = d_rows
        g_maps[h] = wide_dot(reach[:, cols], d_rows, 0, 0).astype(NARROW)
    chain.start_backward(g_maps, sib_g, chip_g, row_g, pass_on)
    g_a_out[...] = dot_tn(e_out, normed[...]).astype(NARROW)
    chain.chips_backward()
    for j in range(2):
        cols = slice(j * ff, (j + 1) * ff)
        g_b_ffn[:, cols] = dot_tn(u_two_ref[:, j * 128 : (j + 1) * 128], d_gate_up[:, cols]).astype(NARROW)
    chain.rows_backward()
    g_a_down[...] = dot_tn(e_down_ref[...], hidden[...]).astype(NARROW)
    for copy in extra_sent:
        copy.wait_recv()
    factor = extra[m].astype(WIDE)
    for k in range(3):
        factor = factor + extra_landed[k].astype(WIDE)
    left = jnp.where(m < 2, xn_two[...], jnp.where(m == 2, d_branch[...], g_full[...]))
    g_shared[...] = dot_tn(left, factor.astype(NARROW)).astype(NARROW)
    chain.finish_backward(grad_out)
    for half in range(2):
        rows = three.rows(half)
        output[rows] = (hidden_one[rows, columns(m, share)] + three.total(half)).astype(NARROW)
    box.drain()


def middle(kept_maps, forward, x, g, norm, gain, ranks, late, wide):
    operands = (*kept_maps, *forward, x, g, norm, gain, ranks)
    count, inner = forward[0].shape
    heads = inner // DH
    model = x.shape[1]
    share = model // 4
    ff = (wide.shape[1] - 384) // 3
    vmem = pl.BlockSpec(memory_space=pltpu.VMEM)
    anywhere = pl.BlockSpec(memory_space=pl.ANY)
    two = (2, DH, DH)
    copies = 1 + 3 + 3 + 1 + 12 + 3 + 6
    results = [
        ((count, share), NARROW),
        ((heads, DH, DH), WIDE),
        ((count, model), WIDE),
        ((count, inner), WIDE),
        ((128, 2 * ff), NARROW),
        ((128, ff), NARROW),
        ((128, inner), NARROW),
        ((model, 128), NARROW),
    ]
    scratch = [
        (late.shape, NARROW),
        ((model, 2 * ff), NARROW),
        ((model, ff), NARROW),
        ((model, 384), NARROW),
        ((3, model, 128), WIDE),
        ((3 * ff // 128, 128, 128), WIDE),
        ((128, 3 * ff), NARROW),
        (two, NARROW),
        ((4,) + two, NARROW),
        ((4,) + two, NARROW),
        (two, WIDE),
        ((heads, DH, DH), NARROW),
        ((4, count, share), NARROW),
        ((3, count, share), NARROW),
        ((count, model), WIDE),
        ((count, model), NARROW),
        ((count, ff), WIDE),
        ((count, ff), WIDE),
        ((count, ff), NARROW),
        ((4, count, share), NARROW),
        ((3, count, share), NARROW),
        ((count, 2 * ff), NARROW),
        ((count, model), NARROW),
        ((4, count, 128), NARROW),
        ((3, count, 128), NARROW),
        ((count, model), NARROW),
        ((count, 128), NARROW),
        ((count, 256), NARROW),
    ]
    return pl.pallas_call(
        middle_kernel,
        out_shape=tuple(jax.ShapeDtypeStruct(*r) for r in results),
        in_specs=[vmem] * len(operands) + [anywhere] * 2,
        out_specs=tuple([vmem] * len(results)),
        scratch_shapes=[pltpu.VMEM(*v) for v in scratch]
        + [
            pltpu.SemaphoreType.DMA((copies,)),
            pltpu.SemaphoreType.DMA((copies,)),
            pltpu.SemaphoreType.DMA((5,)),
        ],
        compiler_params=pltpu.CompilerParams(
            collective_id=2, has_side_effects=True, vmem_limit_bytes=60 << 20
        ),
        name="middle",
    )(*operands, late, wide)


class DpSum:
    SCRATCH = 6

    @staticmethod
    def scratch(rows, width):
        small = rows // 4
        return [
            ((2, 4, rows, width), NARROW),
            ((4, rows, width), NARROW),
            ((3, rows, width), NARROW),
            ((4, small, width), WIDE),
            ((3, small, width), WIDE),
            ((small, width), WIDE),
        ]

    def __init__(self, box, full, landed_core, landed_y, by_z, landed_z, result):
        self.box, self.full, self.landed_core = box, full, landed_core
        self.landed_y, self.by_z, self.landed_z, self.result = landed_y, by_z, landed_z, result
        self.y, self.z, self.c = coords()

    def over_cores(self):
        self.pair = self.box.push(self.full.at[1 - self.c], self.landed_core, dp=moved(0, 0, True))

    def over_y(self):
        self.pair.wait_recv()
        mine = self.full.at[self.c]
        for i in range(4):
            mine[i] = (mine[i].astype(WIDE) + self.landed_core[i].astype(WIDE)).astype(NARROW)
        self.copies = [
            self.box.push(mine.at[lax.rem(self.y + k, 4)], self.landed_y.at[k - 1], dp=moved(k, 0)) for k in (2, 1, 3)
        ]

    def over_z(self):
        for copy in self.copies:
            copy.wait_recv()
        total = self.full[self.c, self.y].astype(WIDE)
        for k in range(3):
            total = total + self.landed_y[k].astype(WIDE)
        self.by_z[...] = total.reshape(self.by_z.shape)
        self.copies = [
            self.box.push(self.by_z.at[lax.rem(self.z + k, 4)], self.landed_z.at[k - 1], dp=moved(0, k))
            for k in (2, 1, 3)
        ]

    def finish(self):
        for copy in self.copies:
            copy.wait_recv()
        total = self.by_z[self.z]
        for k in range(3):
            total = total + self.landed_z[k]
        self.result[...] = total


def tail_kernel(
    taps_ref, aux_ref, seg_ref, state_ref, grad_ref, d_out_ref,
    u_ref, norm_ref, picks_ref, ranks, shared_two, g_b_ffn, g_a_out, g_a_down,
    pre_in, kept_in, t_in, x_in, xn_in, d_one_in, wide_ref, thin_ref,
    grad_input, out_a_in, out_heads, out_beta, out_a_out, out_ffn, out_a_down, out_res,
    pre_ref, kept_all, t_ref, x_ref, xn_ref, d_one_ref, w_in, a_one, d_ext, pre_wide, taps, halo, d_pre, e_one, part, landed, extra_landed, sums, sums_landed, pair, early_pair, ends,
    *rest,
):
    one, two, three, four = (rest[i * DpSum.SCRATCH : (i + 1) * DpSum.SCRATCH] for i in range(4))
    send, recv, local = rest[4 * DpSum.SCRATCH :]
    count, model = x_in.shape
    inner = d_out_ref.shape[1]
    heads = inner // DH
    ff = g_a_down.shape[1]
    m = lax.axis_index("mp")
    c = lax.rem(lax.axis_index("dp"), 2)
    before, after = (lax.rem(lax.axis_index("dp") + k, 32) for k in (31, 1))
    mp_peers = {k: lax.rem(m + k, 4) for k in (1, 2, 3)}
    dp_peers = [before, after, moved(0, 0, True)]
    dp_peers += [moved(k, 0) for k in (1, 2, 3)] + [moved(0, k) for k in (1, 2, 3)]
    loads = [
        pltpu.make_async_copy(source, target, local.at[i])
        for i, (source, target) in enumerate(
            (
                (pre_in, pre_ref),
                (kept_in, kept_all),
                (t_in, t_ref),
                (wide_ref.at[:, pl.ds(0, w_in.shape[1])], w_in),
                (thin_ref.at[:, pl.ds(0, a_one.shape[1])], a_one),
                (x_in, x_ref),
                (xn_in, xn_ref),
                (d_one_in, d_one_ref),
            )
        )
    ]
    for load in loads:
        load.start()
    greet(dp_peers, list(mp_peers.values()))
    box = Mailbox(send, recv)
    early_sum, heads_sum, two_sum, one_sum = (DpSum(box, *refs) for refs in (four, one, two, three))

    def halves(refs, values):
        half = refs[0].shape[3]
        missing = 2 * half - sum(value.shape[1] for value in values)
        values = values + [jnp.zeros((128, missing), NARROW)] if missing else values
        values = jnp.concatenate(values, axis=1)
        for i in range(2):
            refs[0][i] = values[:, i * half : (i + 1) * half].reshape(4, 32, half)

    def by_core(value):
        value = value.reshape(4, 4, 2, model // 32, 128)
        return [value[:, :, i].reshape(4, model // 8, 128) for i in range(2)]

    halves(four, [g_b_ffn[...], g_a_out[...], g_a_down[...]])
    early_sum.over_cores()
    for i, value in enumerate(by_core(shared_two[...])):
        two[0][i] = value
    two_sum.over_cores()
    aux = aux_ref[...]
    spread_taps(taps_ref, taps)
    for load in loads[:3]:
        load.wait()
    pre_wide[...] = pre_ref[...].astype(WIDE)
    kept = (*(kept_all.at[i] for i in range(3)), t_ref, *(kept_all.at[i] for i in (3, 4)))
    lanes = lax.broadcasted_iota(jnp.int32, aux.shape, 1)
    d_logit = jnp.zeros(aux.shape, WIDE)
    def between():
        early_sum.over_y()
        two_sum.over_y()

    found = mixer_backward(
        list(range(heads)), pre_wide, taps, aux, seg_ref[...].astype(WIDE), kept, state_ref, grad_ref, d_out_ref, d_ext,
        between,
    )
    for h, value in enumerate(found):
        d_logit = jnp.where(lanes == 8 + h, value, d_logit)
    edges = [box.push(d_ext.at[i, pl.ds(HALO - 8, 8)], halo.at[i], dp=before) for i in range(3)]
    early_sum.over_z()
    two_sum.over_z()
    picks = picks_ref[...]
    d_logit = d_logit.astype(NARROW)
    for copy in edges:
        copy.wait_recv()
    for i in range(3):
        ref = d_ext.at[i]
        cols = slice(i * inner, (i + 1) * inner)
        d_pre[: count - 16, cols] = ref[HALO : HALO + count - 16].astype(NARROW)
        ending = ref[HALO + count - 16 :]
        d_pre[count - 16 :, cols] = jnp.concatenate([ending[:8], ending[8:] + halo[i]], axis=0).astype(NARROW)
    for j in range(3):
        cols = slice(j * inner, (j + 1) * inner)
        e_one[j] = (dot_nt(d_pre[:, cols], ranks[:, cols]) * picks).astype(NARROW)
    e_one[3] = (dot_nt(d_logit, ranks[:, 4 * inner :]) * picks).astype(NARROW)
    extra_sent = [box.push(e_one.at[mp_peers[k]], extra_landed.at[k - 1], mp=mp_peers[k]) for k in MpSum.ORDER]
    grads = [dot_tn(u_ref[:, j * 128 : (j + 1) * 128], d_pre[:, j * inner : (j + 1) * inner]) for j in range(3)]
    grads.append(dot_tn(u_ref[:, 384:], d_logit))
    halves(one, [value.astype(NARROW) for value in grads])
    heads_sum.over_cores()
    for load in loads[3:]:
        load.wait()
    share = grad_input.shape[1]
    total = MpSum(box, part, landed)
    row_sum = jnp.zeros((count, 128), WIDE)
    all_e = jnp.concatenate([e_one[j] for j in range(4)], axis=1)
    for k in (2, 1, 3, 0):
        owner = total.owner(k)
        rows = columns(owner, share)
        value = (
            dot_nt(d_pre[...], w_in[rows, : 3 * inner])
            + dot_nt(d_logit, w_in[rows, 3 * inner :])
            + dot_nt(all_e, a_one[rows, :])
        )
        part[k] = value.astype(NARROW)
        if k:
            total.send(k, 0)
            total.send(k, 1)
        weighted = value * norm_ref[0:1, rows] * x_ref[:, rows].astype(WIDE)
        row_sum = row_sum + jnp.sum(weighted, axis=1, keepdims=True)
    sums[...] = row_sum.T[:8]
    sums_sent = [box.push(sums, sums_landed.at[k - 1], mp=mp_peers[k]) for k in MpSum.ORDER]
    heads_sum.over_y()
    early_sum.finish()
    early_pair[c] = four[5][...]
    early_paired = box.push(four[5], early_pair.at[c], dp=moved(0, 0, True))
    for copy in extra_sent:
        copy.wait_recv()
    factor = e_one[m].astype(WIDE)
    for k in range(3):
        factor = factor + extra_landed[k].astype(WIDE)
    for i, value in enumerate(by_core(dot_tn(xn_ref[...], factor.astype(NARROW)).astype(NARROW))):
        three[0][i] = value
    one_sum.over_cores()
    heads_sum.over_z()
    one_sum.over_y()
    rank_rows = model // 128

    def to_owners(slot, result):
        ends[slot, m] = result[columns(m, rank_rows)]
        return [
            box.push(result.at[columns(mp_peers[k], rank_rows)], ends.at[slot, m], mp=mp_peers[k])
            for k in MpSum.ORDER
        ]

    two_sum.finish()
    owners = to_owners(1, two[5])
    heads_sum.finish()
    pair[c] = one[5][...]
    paired = box.push(one[5], pair.at[c], dp=moved(0, 0, True))
    one_sum.over_z()
    x_all = x_ref[...].astype(WIDE)
    scale = inverse_rms(x_all)
    mine = columns(m, share)
    one_sum.finish()
    owners += to_owners(0, three[5])
    for copy in sums_sent:
        copy.wait_recv()
    rows = sums[...] + sums_landed[0] + sums_landed[1] + sums_landed[2]
    mean = jnp.concatenate([rows] * 16, axis=0).T[:, :1] / model
    scale_three = scale * scale * scale * mean
    for half in range(2):
        at = total.rows(half)
        here = slice(half * (count // 2), (half + 1) * (count // 2))
        grad_input[at] = d_one_ref[at, mine] + (
            scale[here] * norm_ref[0:1, mine] * total.total(half) - x_ref[at, mine].astype(WIDE) * scale_three[here]
        )
    paired.wait_recv()
    early_paired.wait_recv()

    def own_ranks(pair):
        both = jnp.concatenate([pair[0], pair[1]], axis=1)
        return jnp.where(c == 0, both[:4], both[4:])

    rows = own_ranks(pair)
    for j in range(3):
        out_heads[j] = rows[:, j * inner : (j + 1) * inner]
    out_beta[...] = rows[:, 3 * inner + 8 : 3 * inner + 8 + heads]
    rows = own_ranks(early_pair)
    for j in range(2):
        out_ffn[j] = rows[:, j * ff : (j + 1) * ff]
    out_a_out[...] = rows[:, 2 * ff : 2 * ff + inner]
    out_a_down[...] = rows[:, 2 * ff + inner : 3 * ff + inner]
    for copy in owners:
        copy.wait_recv()
    for j in range(4):
        out_a_in[j] = ends[0, j]
    for j in range(2):
        out_a_in[4 + j] = ends[1, j]
        out_res[j] = ends[1, 2 + j]
    box.drain()


def tail(mixer, tokens, grads, kept, wide, thin):
    model = kept[3].shape[1]
    count, inner = mixer[-1].shape
    heads = inner // DH
    share = model // 4
    ff = grads[3].shape[1]

    def half_of(width):
        return -(-width // 256) * 128

    half, early_half = half_of(3 * inner + 128), half_of(3 * ff + inner)
    vmem = pl.BlockSpec(memory_space=pltpu.VMEM)
    anywhere = pl.BlockSpec(memory_space=pl.ANY)
    copies = 3 + 3 + 6 + 3 + 4 * 7 + 2 + 6
    results = [
        (count, share), (6, model // 128, 128), (3, 4, inner), (4, heads),
        (4, inner), (2, 4, ff), (4, ff), (2, model // 128, 128),
    ]
    scratch = [(x.shape, x.dtype) for x in kept] + [
        ((model, 3 * inner + 128), NARROW),
        ((model, 512), NARROW),
        ((3, HALO + count, inner), WIDE),
        ((HALO + count, 3 * inner), WIDE),
        ((16, inner), WIDE),
        ((3, 8, inner), WIDE),
        ((count, 3 * inner), NARROW),
        ((4, count, 128), NARROW),
        ((4, count, share), NARROW),
        ((3, count, share), NARROW),
        ((3, count, 128), NARROW),
        ((8, count), WIDE),
        ((3, 8, count), WIDE),
        ((2, 8, half), WIDE),
        ((2, 8, early_half), WIDE),
        ((2, 4, model // 128, 128), WIDE),
    ]
    scratch += DpSum.scratch(32, half) + DpSum.scratch(model // 8, 128) + DpSum.scratch(model // 8, 128)
    scratch += DpSum.scratch(32, early_half)
    operands = (*mixer, *tokens, *grads)
    return pl.pallas_call(
        tail_kernel,
        out_shape=tuple(jax.ShapeDtypeStruct(r, WIDE) for r in results),
        in_specs=[vmem] * len(operands) + [anywhere] * (len(kept) + 2),
        out_specs=tuple([vmem] * len(results)),
        scratch_shapes=[pltpu.VMEM(*s) for s in scratch]
        + [
            pltpu.SemaphoreType.DMA((copies,)),
            pltpu.SemaphoreType.DMA((copies,)),
            pltpu.SemaphoreType.DMA((8,)),
        ],
        compiler_params=pltpu.CompilerParams(
            collective_id=3, has_side_effects=True, vmem_limit_bytes=60 << 20
        ),
        name="tail",
    )(*operands, *kept, wide, thin)


def hand_over_kernel(*refs):
    half = len(refs) // 2
    for source, target in zip(refs[:half], refs[half:]):
        target[...] = source[...]


def hand_over(*arrays):
    vmem = pl.BlockSpec(memory_space=pltpu.VMEM)
    return pl.pallas_call(
        hand_over_kernel,
        out_shape=tuple(jax.ShapeDtypeStruct(x.shape, x.dtype) for x in arrays),
        in_specs=[vmem] * len(arrays),
        out_specs=tuple([vmem] * len(arrays)),
        name="hand_over",
    )(*arrays)


def on_device(
    layer_in, cotangent, segments, adapters, norm_one, norm_two, out_gain, beta_bias, conv_taps,
    w_qkv, w_beta, w_out, w_gate_up, w_down, a_in, b_heads, b_beta, a_out, b_ffn, a_down, b_res,
):
    heads = w_beta.shape[1]
    inner = heads * DH
    ff = w_down.shape[0]

    def pack_ranks(parts, blocks):
        flat = jnp.concatenate(parts, axis=1).reshape(-1, 128)
        flat = jnp.pad(flat, ((0, 64 * blocks - flat.shape[0]), (0, 0)))
        return flat.reshape(blocks, 64, 128).transpose(1, 0, 2).reshape(64, blocks * 128)

    last = jnp.concatenate(
        [
            w_gate_up.reshape(64, 2 * ff),
            w_down.T,
            pack_ranks([b_ffn.transpose(1, 0, 2).reshape(4, 2 * ff), a_down.T], 3),
        ],
        axis=1,
    )
    g_full = lax.all_gather(cotangent, "mp", axis=1, tiled=True)
    last = lax.all_gather(last, "dp", axis=0, tiled=True)
    beta = jnp.concatenate([w_beta, jnp.zeros((64, 64 - heads), NARROW), jnp.pad(b_beta, ((0, 60), (0, 0)))], axis=1)
    wide = jnp.concatenate(
        [
            w_qkv.reshape(64, 3 * inner),
            jnp.pad(beta, ((0, 0), (8, 56 - heads))),
            pack_ranks([b_heads.transpose(1, 0, 2).reshape(4, 3 * inner), a_out.T], 1),
        ],
        axis=1,
    )
    a_flat = a_in.reshape(16, 768)
    late_thin = jnp.concatenate([a_flat[:, 512:], b_res.transpose(2, 0, 1).reshape(16, 256)], axis=1)
    seg_row = segments[None, :]
    (
        wide, thin, late, pre, xn_one, kept, t_map, aux, picks, u_one, reach, ranks,
        maps, sib_a, chip_a, row_a, state_in, mixer_out, normed, u_out, branch,
    ) = front(
        layer_in, seg_row, adapters, norm_one[None, :], out_gain[None, :],
        beta_bias, conv_taps, wide, a_flat[:, :512], w_out.T, late_thin,
    )
    wide, thin, late = (x.reshape(2048, -1) for x in (wide, thin, late))
    output, state_grad, d_hidden_one, d_mixer, grad_b_ffn, grad_a_down, grad_a_out, shared_two = middle(
        (maps, sib_a, chip_a, row_a), (reach, mixer_out, normed, u_out, branch, picks),
        layer_in, g_full, norm_two[None, :], out_gain[None, :], ranks, late, last,
    )
    grad_input, d_a_in, d_b_heads, d_b_beta, d_a_out, d_b_ffn, d_a_down, d_b_res = tail(
        (conv_taps, aux, seg_row, state_in, state_grad, d_mixer),
        (u_one, norm_one[None, :], picks, ranks),
        (shared_two, grad_b_ffn, grad_a_out, grad_a_down),
        (pre, kept, t_map, layer_in, xn_one, d_hidden_one),
        wide,
        thin,
    )
    output, grad_input, d_a_in, d_b_heads, d_b_beta, d_a_out, d_b_ffn, d_a_down, d_b_res = hand_over(
        output, grad_input, d_a_in, d_b_heads, d_b_beta, d_a_out, d_b_ffn, d_a_down, d_b_res
    )
    return (
        output, grad_input, d_a_in.transpose(1, 0, 2), d_b_heads, d_b_beta, d_a_out.T, d_b_ffn, d_a_down.T,
        d_b_res.transpose(0, 2, 1),
    )


def solution(mesh):
    placed = (
        P("dp", None),
        P("dp", "mp"),
        P("dp"),
        P(),
        P(),
        P(),
        P(),
        P("mp"),
        P(None, None, "mp"),
        P("dp", None, "mp"),
        P("dp", "mp"),
        P("mp", "dp"),
        P("dp", None, "mp"),
        P("mp", "dp"),
        P(("dp", "mp"), None, None),
        P(None, "dp", "mp"),
        P("dp", "mp"),
        P("mp", "dp"),
        P(None, "dp", "mp"),
        P("mp", "dp"),
        P(None, None, ("dp", "mp")),
    )
    return jax.shard_map(
        on_device,
        mesh=mesh,
        in_specs=placed,
        out_specs=(
            P("dp", "mp"),
            P("dp", "mp"),
            P(("dp", "mp"), None, None),
            P(None, "dp", "mp"),
            P("dp", "mp"),
            P("mp", "dp"),
            P(None, "dp", "mp"),
            P("mp", "dp"),
            P(None, None, ("dp", "mp")),
        ),
        check_vma=False,
    )
```

```python
import functools

import jax
import jax.numpy as jnp
from jax import lax
from jax.experimental import pallas as pl
from jax.experimental.pallas import tpu as pltpu
from jax.sharding import PartitionSpec as P

DH = 128
KW = 4
RANK = 16
HALO = 16
EPSILON = 1e-06
WIDE = jnp.float32
NARROW = jnp.bfloat16
MESH = pl.DeviceIdType.MESH
EXACT = lax.Precision.HIGHEST


def coords():
    place = lax.axis_index("dp")
    return place // 8, lax.rem(place // 2, 4), lax.rem(place, 2)


def place_of(y, z, c):
    return (y * 4 + z) * 2 + c


def moved(dy, dz, other_core=False):
    y, z, c = coords()
    return place_of(lax.rem(y + dy + 4, 4), lax.rem(z + dz + 4, 4), 1 - c if other_core else c)


def greet(dp_peers=(), mp_peers=()):
    barrier = pltpu.get_barrier_semaphore()
    for peer in dp_peers:
        pl.semaphore_signal(barrier, inc=1, device_id={"dp": peer}, device_id_type=MESH)
    for peer in mp_peers:
        pl.semaphore_signal(barrier, inc=1, device_id={"mp": peer}, device_id_type=MESH)
    pl.semaphore_wait(barrier, len(dp_peers) + len(mp_peers))


class Mailbox:
    def __init__(self, send, recv):
        self.send, self.recv, self.copies = send, recv, []

    def push(self, src, dst, **device):
        k = len(self.copies)
        copy = pltpu.make_async_remote_copy(
            src_ref=src,
            dst_ref=dst,
            send_sem=self.send.at[k],
            recv_sem=self.recv.at[k],
            device_id=device,
            device_id_type=MESH,
        )
        copy.start()
        self.copies.append(copy)
        return copy

    def drain(self):
        for copy in self.copies:
            copy.wait_send()


def gather_steps(box, own, out):
    me = moved(0, 0)
    half = own.shape[0] // 2
    quarter = half // 2
    sibling = moved(0, 0, True)
    kinds = []
    for kind in range(2):
        base = kind * half
        parts = (pl.ds(base, half), pl.ds(base, quarter), pl.ds(base + quarter, quarter))
        if kind == 0:
            kinds.append((parts, lambda a, b: moved(a, b)))
        else:
            kinds.append((parts, lambda a, b: moved(b, a)))
    near, across, far, far_across, shared = [], [{}, {}], [[], []], [{}, {}], []

    def open_up():
        for parts, at in kinds:
            near.append([box.push(own.at[parts[0]], out.at[me, parts[0]], dp=at(s, 0)) for s in (1, -1)])
        for k, (parts, at) in enumerate(kinds):
            across[k][0] = [box.push(own.at[parts[0]], out.at[me, parts[0]], dp=at(0, s)) for s in (1, -1)]
        shared.append(box.push(own, out.at[me], dp=sibling))

    def pass_on(k, slot):
        parts, at = kinds[k]
        block = out.at[slot, parts[0]]
        return [box.push(block, block, dp=at(0, t)) for t in (1, -1)]

    def to_sibling(k, slot):
        block = out.at[slot, kinds[k][0][0]]
        shared.append(box.push(block, block, dp=sibling))

    def from_near(i, s):
        def step():
            for k, (parts, at) in enumerate(kinds):
                near[k][i].wait_recv()
                block = out.at[at(s, 0), parts[1 + i]]
                far[k].append(box.push(block, block, dp=at(-s, 0)))
            for k, (parts, at) in enumerate(kinds):
                across[k][s] = pass_on(k, at(s, 0))
                to_sibling(k, at(s, 0))

        return step

    def from_far(k):
        def step():
            for copy in far[k]:
                copy.wait_recv()
            slot = kinds[k][1](2, 0)
            across[k][2] = pass_on(k, slot)
            to_sibling(k, slot)

        return step

    def from_across(k, f):
        def step():
            parts, at = kinds[k]
            far_across[k][f] = []
            for i, s in enumerate((-1, 1)):
                across[k][f][i].wait_recv()
                slot = at(f, s)
                block = out.at[slot, parts[1 + i]]
                far_across[k][f].append(box.push(block, block, dp=at(0, -s)))
                to_sibling(k, slot)

        return step

    def from_far_across(k, f):
        def step():
            for copy in far_across[k][f]:
                copy.wait_recv()
            to_sibling(k, kinds[k][1](f, 2))

        return step

    def close():
        for copy in shared:
            copy.wait_recv()

    steps = [open_up, from_near(0, -1), from_near(1, 1), from_far(0), from_far(1)]
    steps += [from_across(k, f) for f in (0, -1, 1, 2) for k in range(2)]
    steps += [from_far_across(k, f) for f in (0, -1, 1, 2) for k in range(2)]
    return steps + [close]


def gather_peers():
    return [moved(1, 0), moved(-1, 0), moved(0, 1), moved(0, -1), moved(0, 0, True)]


GATHER_COPIES = 71


def half_dot(left, right, dims=(((1,), (0,)), ((), ()))):
    high = right.astype(NARROW)
    low = (right - high.astype(WIDE)).astype(NARROW)
    return lax.dot_general(left, high, dims, preferred_element_type=WIDE) + lax.dot_general(
        left, low, dims, preferred_element_type=WIDE
    )


TURNED = (((0,), (0,)), ((), ()))


def two_parts(value):
    high = value.astype(NARROW)
    return high, (value - high.astype(WIDE)).astype(NARROW)


def wide_dot(left, right, left_dim=1, right_dim=0):
    left_high, left_low = two_parts(left)
    right_high, right_low = two_parts(right)

    def part(one, two):
        return lax.dot_general(one, two, (((left_dim,), (right_dim,)), ((), ())), preferred_element_type=WIDE)

    return part(left_high, right_high) + (part(left_high, right_low) + part(left_low, right_high))


def convolve(pre_ref, taps_ref, part, head, inner, aux):
    count = aux.shape[0]
    cols = slice(part * inner + head * DH, part * inner + (head + 1) * DH)
    taps = taps_ref[:, head * DH : (head + 1) * DH]
    total = pre_ref[pl.ds(HALO, count), cols] * taps[part : part + 1]
    for j in range(1, KW):
        shifted = pre_ref[pl.ds(HALO - j, count), cols]
        total = total + shifted * aux[:, j : j + 1] * taps[3 * j + part : 3 * j + part + 1]
    return total


def spread_taps(taps_ref, taps):
    for j in range(KW):
        taps[3 * j : 3 * j + 3, :] = taps_ref[j].astype(WIDE)


def masks(aux, seg_row):
    same = aux[:, 6:7] == seg_row
    shape = (aux.shape[0], aux.shape[0])
    row = lax.broadcasted_iota(jnp.int32, shape, 0)
    col = lax.broadcasted_iota(jnp.int32, shape, 1)
    return row, col, same


def each(step, *lists):
    return [step(*items) for items in zip(*lists)]


def lower_inverses(lowers, row, col, tick):
    near = [jnp.where(row // 8 == col // 8, lower, 0.0) for lower in lowers]
    square = each(lambda a: wide_dot(a, a), near)
    inverse = [jnp.where(row == col, 1.0, 0.0) - a for a in near]
    inverse = each(lambda x, s: x + wide_dot(x, s), inverse, square)
    square = each(lambda s: wide_dot(s, s), square)
    inverse = each(lambda x, s: x + wide_dot(x, s), inverse, square)
    size = 8
    while size < row.shape[0]:
        link = (row // (2 * size) == col // (2 * size)) & (row // size != col // size)
        middle = each(lambda lower, x: wide_dot(jnp.where(link, lower, 0.0), x), lowers, inverse)
        inverse = each(lambda x, y: x - wide_dot(x, y), inverse, middle)
        size *= 2
        tick()
    return inverse


def mixer_forward(heads, pre_ref, taps_ref, aux, seg_row, out_ref, reach_ref, map_ref, offset_ref, kept, tick):
    q_ref, k_ref, v_ref, t_ref, w_ref, u_ref = kept
    count = aux.shape[0]
    inner = out_ref.shape[1]
    linked, ending = aux[:, 4:5], aux[:, 5:6]
    row, col, same = masks(aux, seg_row)
    rate = [aux[:, 8 + h : 9 + h] for h in heads]
    cols = [slice(h * DH, (h + 1) * DH) for h in heads]

    def act(part):
        convs = [convolve(pre_ref, taps_ref, part, h, inner, aux) for h in heads]
        return [conv * jax.nn.sigmoid(conv) for conv in convs]

    def unit(a):
        return a * lax.rsqrt(jnp.sum(a * a, axis=1, keepdims=True) + EPSILON)

    k = each(unit, act(1))
    gram = each(lambda b: wide_dot(b, b, 1, 1), k)
    lowers = each(lambda g, r: jnp.where((row > col) & same, g * r, 0.0), gram, rate)
    q, v = each(unit, act(0)), act(2)
    for i in range(len(heads)):
        q_ref[:, cols[i]] = q[i]
        k_ref[:, cols[i]] = k[i]
        v_ref[:, cols[i]] = v[i]
    scores = each(lambda a, b: jnp.where((row >= col) & same, wide_dot(a, b, 1, 1), 0.0), q, k)
    tick()
    inverse = lower_inverses(lowers, row, col, tick)
    written = each(
        lambda t, a, b, r: wide_dot(t, jnp.concatenate([a, b * linked], axis=1) * r), inverse, v, k, rate
    )
    ends = each(lambda b, w: wide_dot(b * ending, w, 0, 0), k, written)
    mixed = each(wide_dot, scores, written)
    eye = jnp.where(row[:DH, :DH] == col[:DH, :DH], 1.0, 0.0)
    last = aux[count - 1 :, 4:5]
    for i, h in enumerate(heads):
        t_ref[h] = inverse[i]
        w_ref[:, cols[i]] = written[i][:, :DH]
        u_ref[:, cols[i]] = written[i][:, DH:]
        offset_ref[h] = ends[i][:, :DH].astype(offset_ref.dtype)
        map_ref[h] = (eye * last - ends[i][:, DH:]).astype(map_ref.dtype)
        out_ref[:, cols[i]] = mixed[i][:, :DH]
        reach_ref[:, cols[i]] = q[i] * linked - mixed[i][:, DH:]
    tick()


def mixer_backward(heads, pre_ref, taps_ref, aux, seg_row, kept, state_ref, grad_ref, d_out_ref, d_ext, between):
    q_ref, k_ref, v_ref, t_ref, w_ref, u_ref = kept
    count = aux.shape[0]
    inner = d_out_ref.shape[1]
    linked, ending = aux[:, 4:5], aux[:, 5:6]
    row, col, same = masks(aux, seg_row)
    upto = (row >= col) & same
    below = (row > col) & same

    def take(ref):
        return [ref[:, h * DH : (h + 1) * DH] for h in heads]

    rate = [aux[:, 8 + h : 9 + h] for h in heads]
    q, k, v, d_out = take(q_ref), take(k_ref), take(v_ref), take(d_out_ref)
    state, grad = [state_ref[h] for h in heads], [grad_ref[h] for h in heads]
    written = each(lambda w, u, s: w - wide_dot(u, s), take(w_ref), take(u_ref), state)
    scores = each(lambda a, b: jnp.where(upto, wide_dot(a, b, 1, 1), 0.0), q, k)
    d_written = each(
        lambda a, d, b, g: wide_dot(a, d, 0, 0) + wide_dot(b * ending, g), scores, d_out, k, grad
    )
    d_right = each(lambda t, d: wide_dot(t, d, 0, 0), [t_ref[h] for h in heads], d_written)
    d_scores = each(lambda d, w: jnp.where(upto, wide_dot(d, w, 1, 1), 0.0), d_out, written)
    between()
    d_lower = each(lambda d, w: jnp.where(below, -wide_dot(d, w, 1, 1), 0.0), d_right, written)
    d_q = each(
        lambda ds, b, d, s: wide_dot(ds, b) + linked * wide_dot(d, s, 1, 1), d_scores, k, d_out, state
    )
    d_k = each(
        lambda ds, a, w, g: wide_dot(ds, a, 0, 0) + ending * wide_dot(w, g, 1, 1), d_scores, q, written, grad
    )
    d_rate = each(
        lambda d, a, b, s: jnp.sum(d * (a - linked * wide_dot(b, s)), axis=1, keepdims=True), d_right, v, k, state
    )
    d_rate = each(
        lambda r, d, b: r + jnp.sum(d * wide_dot(b, b, 1, 1), axis=1, keepdims=True), d_rate, d_lower, k
    )
    d_k = each(lambda dk, r, d, s: dk - (linked * r) * wide_dot(d, s, 1, 1), d_k, rate, d_right, state)
    d_gram = each(lambda d, r: d * r, d_lower, rate)
    d_k = each(lambda dk, d, b: dk + wide_dot(d, b) + wide_dot(d, b, 0, 0), d_k, d_gram, k)
    d_v = each(lambda r, d: r * d, rate, d_right)
    for i, h in enumerate(heads):
        for part, (unit, d) in enumerate(((q[i], d_q[i]), (k[i], d_k[i]), (None, d_v[i]))):
            cols = slice(h * DH, (h + 1) * DH)
            conv = convolve(pre_ref, taps_ref, part, h, inner, aux)
            gate = jax.nn.sigmoid(conv)
            if unit is not None:
                act = conv * gate
                scale = lax.rsqrt(jnp.sum(act * act, axis=1, keepdims=True) + EPSILON)
                d = (d - unit * jnp.sum(unit * d, axis=1, keepdims=True)) * scale
            d_conv = d * gate * (1.0 + conv * (1.0 - gate))
            d_ext[part, :HALO, cols] = jnp.zeros((HALO, DH), WIDE)
            d_ext[part, HALO:, cols] = d_conv * taps_ref[part : part + 1, cols]
            for j in range(1, KW):
                term = d_conv * taps_ref[3 * j + part : 3 * j + part + 1, cols] * aux[:, j : j + 1]
                d_ext[part, pl.ds(HALO - j, count), cols] += term
    return each(lambda d, r: d * r * (1.0 - r), d_rate, rate)


def inverse_rms(values):
    return lax.rsqrt(jnp.mean(values * values, axis=-1, keepdims=True) + EPSILON)


def norm_back(values, scale, gain, grad_out):
    weighted = grad_out * gain
    return scale * weighted - values * scale**3 * jnp.mean(weighted * values, axis=-1, keepdims=True)


def dot(left, right):
    return jnp.dot(left, right, preferred_element_type=WIDE)


def dot_nt(left, right):
    return lax.dot_general(left, right, (((1,), (1,)), ((), ())), preferred_element_type=WIDE)


def dot_tn(left, right):
    return lax.dot_general(left, right, (((0,), (0,)), ((), ())), preferred_element_type=WIDE)


class Chain:
    def __init__(self, box, a_ref, sib_a, chip_a, row_a):
        self.box, self.a_ref, self.sib_a, self.chip_a, self.row_a = box, a_ref, sib_a, chip_a, row_a
        self.y, self.z, self.c = coords()
        self.first = self.c == 0
        self.sibling = moved(0, 0, True)
        self.z_peers = {k: moved(0, k) for k in (1, 2, 3)}
        self.y_peers = {k: moved(k, 0) for k in (1, 2, 3)}
        self.mine = pl.ds(pl.multiple_of(2 * self.c, 2), 2)
        self.theirs = pl.ds(pl.multiple_of(2 * (1 - self.c), 2), 2)

    def peers(self):
        return [self.sibling] + list(self.z_peers.values()) + list(self.y_peers.values())

    def swap(self, ref, sib):
        return self.box.push(ref.at[self.theirs], sib, dp=self.sibling)

    def ordered(self, ref, sib, h):
        own, other = ref[2 * self.c + h], sib[h]
        return jnp.where(self.first, own, other), jnp.where(self.first, other, own)

    def spread(self, refs, place, peers):
        return [self.box.push(ref.at[place], ref.at[place], dp=peers[k]) for k in (2, 1, 3) for ref in refs]

    def start_forward(self, b_ref, sib_b, chip_b, row_b, pass_on):
        self.b_ref, self.sib_b, self.chip_b, self.row_b, self.pass_on = b_ref, sib_b, chip_b, row_b, pass_on
        self.pair = [self.swap(self.a_ref, self.sib_a), self.swap(b_ref, sib_b)]

    def chips_forward(self):
        for copy in self.pair:
            copy.wait_recv()
        self.lower = []
        for h in range(2):
            a_low, a_high = self.ordered(self.a_ref, self.sib_a, h)
            b_low, b_high = self.ordered(self.b_ref, self.sib_b, h)
            self.lower.append((a_low, b_low))
            self.chip_a[self.z, h] = lax.dot(a_high, a_low, preferred_element_type=WIDE).astype(NARROW)
            self.chip_b[self.z, h] = (
                lax.dot(a_high, b_low, preferred_element_type=WIDE) + b_high.astype(WIDE)
            ).astype(NARROW)
        self.ring = self.spread((self.chip_a, self.chip_b), self.z, self.z_peers)

    def rows_forward(self):
        for copy in self.ring:
            copy.wait_recv()
        for h in range(2):
            total_a, total_b = self.chip_a[0, h].astype(WIDE), self.chip_b[0, h].astype(WIDE)
            for i in range(1, 4):
                total_a = half_dot(self.chip_a[i, h], total_a)
                total_b = half_dot(self.chip_a[i, h], total_b) + self.chip_b[i, h].astype(WIDE)
            self.row_a[self.y, h] = total_a.astype(NARROW)
            self.row_b[self.y, h] = total_b.astype(NARROW)
        self.ring = self.spread((self.row_a, self.row_b), self.y, self.y_peers)

    def finish_forward(self, out):
        for copy in self.ring:
            copy.wait_recv()
        for h in range(2):
            state = jnp.zeros((DH, DH), WIDE)
            for i in range(3):
                longer = half_dot(self.row_a[i, h], state) + self.row_b[i, h].astype(WIDE)
                state = jnp.where(i < self.y, longer, state)
            for i in range(3):
                longer = half_dot(self.chip_a[i, h], state) + self.chip_b[i, h].astype(WIDE)
                state = jnp.where(i < self.z, longer, state)
            a_low, b_low = self.lower[h]
            middle = half_dot(a_low, state) + b_low.astype(WIDE)
            out[2 * self.c + h] = jnp.where(self.first, state, middle)
            self.pass_on[h] = jnp.where(self.first, middle, state)
        self.box.push(self.pass_on, out.at[self.mine], dp=self.sibling).wait_recv()

    def start_backward(self, g_ref, sib_g, chip_g, row_g, pass_on):
        self.g_ref, self.sib_g, self.chip_g, self.row_g, self.pass_on = g_ref, sib_g, chip_g, row_g, pass_on
        self.pair = [self.swap(g_ref, sib_g)]

    def chips_backward(self):
        for copy in self.pair:
            copy.wait_recv()
        self.upper_g = []
        for h in range(2):
            a_low, _ = self.ordered(self.a_ref, self.sib_a, h)
            g_low, g_high = self.ordered(self.g_ref, self.sib_g, h)
            self.upper_g.append(g_high)
            self.chip_g[self.z, h] = (
                lax.dot_general(a_low, g_high, TURNED, preferred_element_type=WIDE) + g_low.astype(WIDE)
            ).astype(NARROW)
        self.ring = self.spread((self.chip_g,), self.z, self.z_peers)

    def rows_backward(self):
        for copy in self.ring:
            copy.wait_recv()
        for h in range(2):
            total = self.chip_g[3, h].astype(WIDE)
            for i in (2, 1, 0):
                total = half_dot(self.chip_a[i, h], total, TURNED) + self.chip_g[i, h].astype(WIDE)
            self.row_g[self.y, h] = total.astype(NARROW)
        self.ring = self.spread((self.row_g,), self.y, self.y_peers)

    def finish_backward(self, out):
        for copy in self.ring:
            copy.wait_recv()
        for h in range(2):
            grad = jnp.zeros((DH, DH), WIDE)
            for i in (3, 2, 1):
                longer = half_dot(self.row_a[i, h], grad, TURNED) + self.row_g[i, h].astype(WIDE)
                grad = jnp.where(i > self.y, longer, grad)
            for i in (3, 2, 1):
                longer = half_dot(self.chip_a[i, h], grad, TURNED) + self.chip_g[i, h].astype(WIDE)
                grad = jnp.where(i > self.z, longer, grad)
            _, a_high = self.ordered(self.a_ref, self.sib_a, h)
            middle = half_dot(a_high, grad, TURNED) + self.upper_g[h].astype(WIDE)
            out[2 * self.c + h] = jnp.where(self.first, middle, grad)
            self.pass_on[h] = jnp.where(self.first, grad, middle)
        self.box.push(self.pass_on, out.at[self.mine], dp=self.sibling).wait_recv()


def columns(i, width):
    return pl.ds(pl.multiple_of(i * width, width), width)


class MpSum:
    ORDER = (2, 1, 3)

    def __init__(self, box, part, landed):
        self.box, self.part, self.landed = box, part, landed
        self.m = lax.axis_index("mp")
        self.peers = {k: lax.rem(self.m + k, 4) for k in (1, 2, 3)}
        self.copies = ([], [])
        self.half = part.shape[1] // 2

    def owner(self, k):
        return lax.rem(self.m + k, 4)

    def rows(self, half):
        return pl.ds(half * self.half, self.half)

    def send(self, k, half):
        rows = self.rows(half)
        self.copies[half].append(
            self.box.push(self.part.at[k, rows], self.landed.at[k - 1, rows], mp=self.peers[k])
        )

    def send_half(self, half):
        for k in self.ORDER:
            self.send(k, half)

    def total(self, half):
        for copy in self.copies[half]:
            copy.wait_recv()
        rows = self.rows(half)
        total = self.part[0, rows].astype(WIDE)
        for k in range(3):
            total = total + self.landed[k, rows].astype(WIDE)
        return total

    def share(self, out):
        width = self.part.shape[2]
        shared = []
        for half in range(2):
            rows = self.rows(half)
            out[rows, columns(self.m, width)] = self.total(half).astype(out.dtype)
            block = out.at[rows, columns(self.m, width)]
            shared += [self.box.push(block, block, mp=self.peers[k]) for k in self.ORDER]
        return shared


def unpack_ranks(block, spread, ranks, first, tiles):
    for q in range(4):
        for t in range(tiles):
            at = first + q * tiles + t
            spread[t, pl.ds(q, 32, stride=4), :] = block[at // 64, pl.ds(at % 64, 32, stride=64), :]
    for t in range(tiles):
        ranks[:, t * 128 : (t + 1) * 128] = spread[t].astype(ranks.dtype)


def front_kernel(
    x_ref, g_own, seg_ref, adapters, norm_ref, gain_ref, bias_ref, taps_ref, wide_ref, thin_ref, late_ref, late_thin,
    last_ref,
    wide_out, thin_out, late_out, last_out, pre_out, xn_out, kept_out, t_out, aux_ref, picks_ref, u_ref,
    reach, ranks, a_ref, sib_a, chip_a, row_a, state_out, mixer_out, normed, u_out_ref, branch, g_full,
    pre, xn_ref, kept, t_ref, wide_all, thin_all, late_all, thin_own, late_own, halo_x, seg_ext, xn_ext, pre_wide, block, spread, b_beta,
    b_ref, out_zero, sib_b, chip_b, row_b, pass_on, part, landed, taps, send, recv, local,
):
    count, model = x_ref.shape
    heads = a_ref.shape[0]
    inner = heads * DH
    m = lax.axis_index("mp")
    place = lax.axis_index("dp")
    before, after = lax.rem(place + 31, 32), lax.rem(place + 1, 32)
    mp_peers = {k: lax.rem(m + k, 4) for k in (1, 2, 3)}
    box = Mailbox(send, recv)
    chain = Chain(box, a_ref, sib_a, chip_a, row_a)
    greet([before, after] + chain.peers(), list(mp_peers.values()))
    me = moved(0, 0)
    seg_row = seg_ref[...].astype(WIDE)
    seg_ext[HALO:] = jnp.broadcast_to(seg_row, (128, count)).T
    edges = [
        box.push(x_ref.at[pl.ds(count - HALO, HALO)], halo_x, dp=after),
        box.push(seg_ext.at[pl.ds(count, HALO)], seg_ext.at[pl.ds(0, HALO)], dp=after),
    ]
    thin_rows = thin_ref.shape[0]
    mine = pl.ds(pl.multiple_of(m * thin_rows, thin_rows), thin_rows)
    crossing = [box.push(thin_ref, thin_own.at[mine], mp=peer) for peer in mp_peers.values()]
    late_cols = pl.ds(late_ref.shape[1], late_thin.shape[1])
    late_crossing = [box.push(late_thin, late_own.at[mine, late_cols], mp=peer) for peer in mp_peers.values()]
    keep = [
        pltpu.make_async_copy(wide_ref, wide_all.at[me], local.at[0]),
        pltpu.make_async_copy(thin_ref, thin_own.at[mine], local.at[1]),
        pltpu.make_async_copy(late_ref, late_own.at[:, pl.ds(0, late_ref.shape[1])], local.at[2]),
        pltpu.make_async_copy(late_thin, late_own.at[mine, late_cols], local.at[3]),
    ]
    for copy in keep:
        copy.start()
    wide_steps = gather_steps(box, wide_ref, wide_all)
    thin_steps = gather_steps(box, thin_own, thin_all)
    late_steps = gather_steps(box, late_own, late_all)
    last_steps = gather_steps(box, last_ref, last_out)
    wide_steps.pop(0)()
    share = g_own.shape[1]
    g_full[:, columns(m, share)] = g_own[...]
    keep[1].wait()
    for copy in crossing:
        copy.wait_recv()
    keep_thin = pltpu.make_async_copy(thin_own, thin_all.at[me], local.at[4])
    keep_thin.start()
    thin_steps.pop(0)()
    g_sent = [box.push(g_own, g_full.at[:, columns(m, share)], mp=mp_peers[k]) for k in MpSum.ORDER]

    def normal(rows):
        rows = rows.astype(WIDE)
        return (rows * inverse_rms(rows) * norm_ref[0:1, :]).astype(NARROW)

    xn_ref[...] = normal(x_ref[...])
    xn_ext[HALO:] = xn_ref[...]
    for i, (one, two) in enumerate(zip(wide_steps, thin_steps)):
        if i == 12:
            keep[2].wait()
            keep[3].wait()
            for copy in late_crossing:
                copy.wait_recv()
            keep_late = pltpu.make_async_copy(late_own, late_all.at[me], local.at[5])
            keep_late.start()
            late_steps[0]()
            keep_last = pltpu.make_async_copy(last_ref, last_out.at[me], local.at[13])
            keep_last.start()
            last_steps[0]()
        one()
        two()
    keep[0].wait()
    keep_thin.wait()
    rounds = [
        late_steps[1:3],
        late_steps[3:5],
        [],
        late_steps[5:9],
        late_steps[9:13],
        [],
        last_steps[1:2],
        last_steps[2:3],
        [],
        late_steps[13:17],
        late_steps[17:21],
        late_steps[21:22],
        [],
        [],
        [],
        last_steps[3:7],
        last_steps[7:13],
        last_steps[13:22],
    ]
    to_hbm = [
        pltpu.make_async_copy(wide_all, wide_out, local.at[6]),
        pltpu.make_async_copy(thin_all, thin_out, local.at[7]),
    ]
    for copy in to_hbm:
        copy.start()

    def tick():
        for step in rounds.pop(0):
            step()

    for copy in edges:
        copy.wait_recv()
    xn_ext[:HALO] = normal(halo_x[...])
    seg_ext[:HALO] = jnp.where(place == 0, -1.0, seg_ext[:HALO])
    spread_taps(taps_ref, taps)
    lanes = lax.broadcasted_iota(jnp.int32, seg_ext.shape, 1)
    seg_all = seg_ext[...]
    per_token = jnp.zeros(seg_all.shape, WIDE)
    for s in range(adapters.shape[0]):
        per_token = jnp.where(seg_all == float(s), adapters[s].astype(WIDE), per_token)
    picks_ext = jnp.where(per_token == (lanes // RANK).astype(WIDE), 1.0, 0.0)
    picks_ref[...] = picks_ext[HALO:]
    tiles = inner // 128
    for i in range(2):
        lane_block = slice(3 * inner + i * 128, 3 * inner + (i + 1) * 128)
        block[i] = wide_all[:, :, lane_block].reshape(model, 128).astype(WIDE)
    for q in range(4):
        b_beta[pl.ds(q, 32, stride=4), :] = block[0, pl.ds(q, 32, stride=64), :]
    unpack_ranks(block.at[pl.ds(1, 1)], spread, ranks.at[:, pl.ds(0, 4 * inner)], 0, 4 * tiles)
    beta = pltpu.roll(b_beta[...], 64, 1)
    beta_lane = lax.broadcasted_iota(jnp.int32, beta.shape, 1)
    beta = jnp.where((beta_lane >= 8) & (beta_lane < 8 + heads), beta, 0.0)
    ranks[:, 4 * inner :] = beta.astype(NARROW)
    tick()
    u_ext = dot(xn_ext[...], thin_all[...].reshape(model, thin_all.shape[2]))
    u_ext = (u_ext * jnp.concatenate([picks_ext] * 4, axis=1)).astype(NARROW)
    u_ref[...] = u_ext[HALO:]
    tick()
    for j in range(3):
        cols = slice(j * inner, (j + 1) * inner)
        value = dot(xn_ext[...], wide_all[:, :, cols].reshape(model, inner)) + dot(
            u_ext[:, j * 128 : (j + 1) * 128], ranks[:, cols]
        )
        value = value.astype(NARROW)
        pre[:, cols] = value
        pre_wide[:, cols] = value.astype(WIDE)
        tick()
    w_beta = wide_all[:, :, 3 * inner : 3 * inner + 128].reshape(model, 128)
    logits = dot(xn_ref[...], w_beta) + dot(u_ref[:, 384:], ranks[:, 4 * inner :])
    seg = seg_all[HALO:]
    lane = lanes[HALO:]
    for h in range(heads):
        logits = jnp.where(lane == 8 + h, logits + bias_ref[h], logits)
    aux = jnp.where((lane >= 8) & (lane < 8 + heads), jax.nn.sigmoid(logits), 0.0)
    for j in range(KW):
        aux = jnp.where((lane == j) & (seg_ext[pl.ds(HALO - j, count)] == seg), 1.0, aux)
    aux = jnp.where((lane == 4) & (seg == seg_ext[HALO - 1 : HALO]), 1.0, aux)
    aux = jnp.where((lane == 5) & (seg == seg_ext[HALO + count - 1 : HALO + count]), 1.0, aux)
    aux = jnp.where(lane == 6, seg, aux)
    aux_ref[...] = aux
    mixer_forward(
        list(range(heads)), pre_wide, taps, aux, seg_row, out_zero, reach, a_ref, b_ref,
        (*(kept.at[i] for i in range(3)), t_ref, *(kept.at[i] for i in (3, 4))), tick,
    )
    for i, (source, target) in enumerate(((pre, pre_out), (xn_ref, xn_out), (kept, kept_out), (t_ref, t_out))):
        to_hbm.append(pltpu.make_async_copy(source, target, local.at[9 + i]))
        to_hbm[-1].start()
    chain.start_forward(b_ref, sib_b, chip_b, row_b, pass_on)
    tick()
    chain.chips_forward()
    tick()
    chain.rows_forward()
    tick()
    chain.finish_forward(state_out)
    tick()
    keep_late.wait()
    keep_late_out = pltpu.make_async_copy(late_all, late_out, local.at[8])
    keep_late_out.start()
    for h in range(heads):
        cols = slice(h * DH, (h + 1) * DH)
        rows = out_zero[:, cols] + wide_dot(reach[:, cols], state_out[h])
        mixer_out[:, cols] = rows
        normed[:, cols] = (rows * inverse_rms(rows) * gain_ref[0:1, :]).astype(NARROW)
    u_out = (dot_nt(normed[...], ranks[:, 3 * inner : 4 * inner]) * picks_ref[...]).astype(NARROW)
    u_out_ref[...] = u_out
    one = MpSum(box, part, landed)
    for k in (2, 1, 3, 0):
        groups = pl.ds(one.owner(k) * (share // 64), share // 64)
        w_out = late_all[groups, :, :inner].reshape(share, inner)
        b_mix = late_all[groups, :, inner + 256 : inner + 384].reshape(share, 128)
        part[k] = (dot_nt(normed[...], w_out) + dot_nt(u_out, b_mix)).astype(NARROW)
        if k:
            one.send(k, 0)
    one.send_half(1)
    tick()
    shared = one.share(branch)
    tick()
    for copy in g_sent + shared:
        copy.wait_recv()
    for copy in to_hbm + [keep_late_out, keep_last]:
        copy.wait()
    box.drain()


def front(x, g, seg_row, adapters, norm, gain, bias, taps, wide, thin, late, late_thin, last):
    count, model = x.shape
    inner = taps.shape[2]
    heads = inner // DH
    share = model // 4
    vmem = pl.BlockSpec(memory_space=pltpu.VMEM)
    anywhere = pl.BlockSpec(memory_space=pl.ANY)
    smem = pl.BlockSpec(memory_space=pltpu.SMEM)
    two = (2, DH, DH)
    square = (heads, DH, DH)
    by_head = ((count, inner), WIDE)
    thin_all, late_all = (32, 64, thin.shape[1]), (32, 64, late.shape[1] + late_thin.shape[1])
    early = [
        ((HALO + count, 3 * inner), NARROW),
        ((count, model), NARROW),
        ((5, count, inner), WIDE),
        ((heads, count, count), WIDE),
    ]
    results = [
        ((32,) + wide.shape, NARROW),
        (thin_all, NARROW),
        (late_all, NARROW),
        ((32,) + last.shape, NARROW),
        *early,
        ((count, 128), WIDE),
        ((count, 128), WIDE),
        ((count, 512), NARROW),
        by_head,
        ((128, 4 * inner + 128), NARROW),
        (square, NARROW),
        (two, NARROW),
        ((4,) + two, NARROW),
        ((4,) + two, NARROW),
        (square, WIDE),
        by_head,
        ((count, inner), NARROW),
        ((count, 128), NARROW),
        ((count, model), NARROW),
        ((count, model), NARROW),
    ]
    scratch = early + [
        ((32,) + wide.shape, NARROW),
        (thin_all, NARROW),
        (late_all, NARROW),
        (thin_all[1:], NARROW),
        (late_all[1:], NARROW),
        ((HALO, model), NARROW),
        ((HALO + count, 128), WIDE),
        ((HALO + count, model), NARROW),
        ((HALO + count, 3 * inner), WIDE),
        ((2, model, 128), WIDE),
        ((4 * inner // 128, 128, 128), WIDE),
        ((128, 128), WIDE),
        (square, NARROW),
        by_head,
        (two, NARROW),
        ((4,) + two, NARROW),
        ((4,) + two, NARROW),
        (two, WIDE),
        ((4, count, share), NARROW),
        ((3, count, share), NARROW),
        ((16, inner), WIDE),
    ]
    copies = 4 * GATHER_COPIES + 2 + 3 + 3 + 3 + 2 + 6 + 6 + 1 + 12
    return pl.pallas_call(
        front_kernel,
        out_shape=tuple(jax.ShapeDtypeStruct(*r) for r in results),
        in_specs=[vmem] * 3 + [smem] + [vmem] * 2 + [smem, vmem] + [anywhere] * 5,
        out_specs=tuple([anywhere] * 8 + [vmem] * (len(results) - 8)),
        scratch_shapes=[pltpu.VMEM(*s) for s in scratch]
        + [
            pltpu.SemaphoreType.DMA((copies,)),
            pltpu.SemaphoreType.DMA((copies,)),
            pltpu.SemaphoreType.DMA((14,)),
        ],
        compiler_params=pltpu.CompilerParams(
            collective_id=0, has_side_effects=True, vmem_limit_bytes=60 << 20
        ),
        name="front",
    )(x, g, seg_row, adapters, norm, gain, bias, taps, wide, thin, late, late_thin, last)


def middle_kernel(
    a_ref, sib_a, chip_a, row_a, reach, mixer_out, normed, u_out_ref, branch, picks_ref, x_ref, g_full, norm_ref, gain_ref,
    ranks_one, late_ref, wide_ref,
    output, grad_out, d_one_out, d_mixer_out, g_b_ffn, g_a_down, g_a_out, g_shared,
    late, w_gu, w_down, packed, block, spread, ranks, sib_g, chip_g, row_g, pass_on, g_maps,
    part, landed, hidden_one, xn_two, gate, up, hidden, ffn_part, ffn_landed,
    d_gate_up, d_xn, extra, extra_landed, d_branch, e_down_ref, u_two_ref,
    send, recv, local,
):
    count = x_ref.shape[0]
    heads = a_ref.shape[0]
    inner = heads * DH
    ff = gate.shape[1]
    model = x_ref.shape[1]
    share = output.shape[1]
    m = lax.axis_index("mp")
    loads = [
        pltpu.make_async_copy(late_ref, late, local.at[0]),
        pltpu.make_async_copy(wide_ref.at[:, pl.ds(3 * ff, packed.shape[1])], packed, local.at[1]),
        pltpu.make_async_copy(wide_ref.at[:, pl.ds(0, ff)], w_gu.at[:, pl.ds(0, ff)], local.at[2]),
        pltpu.make_async_copy(wide_ref.at[:, pl.ds(ff, ff)], w_gu.at[:, pl.ds(ff, ff)], local.at[3]),
        pltpu.make_async_copy(wide_ref.at[:, pl.ds(2 * ff, ff)], w_down, local.at[4]),
    ]
    for load in loads:
        load.start()
    box = Mailbox(send, recv)
    chain = Chain(box, a_ref, sib_a, chip_a, row_a)
    mp_peers = {k: lax.rem(m + k, 4) for k in (1, 2, 3)}
    greet(chain.peers(), list(mp_peers.values()))
    picks = picks_ref[...]
    u_out = u_out_ref[...]
    a_out = ranks_one.at[:, pl.ds(3 * inner, inner)]
    a_down = ranks.at[:, pl.ds(2 * ff, ff)]
    w_out, a_two = late.at[:, pl.ds(0, inner)], late.at[:, pl.ds(inner, 256)]
    b_mix, b_down = late.at[:, pl.ds(inner + 256, 128)], late.at[:, pl.ds(inner + 384, 128)]

    rows = x_ref[...].astype(WIDE) + branch[...].astype(WIDE)
    hidden_one[...] = rows
    scale_two = inverse_rms(rows)
    xn_two[...] = (rows * scale_two * norm_ref[0:1, :]).astype(NARROW)
    two_picks = jnp.concatenate([picks, picks], axis=1)
    loads[0].wait()
    u_two_ref[...] = (dot(xn_two[...], a_two[...]) * two_picks).astype(NARROW)
    for load in loads[1:4]:
        load.wait()
    for i in range(3):
        block[i] = packed[:, i * 128 : (i + 1) * 128].astype(WIDE)
    unpack_ranks(block, spread, ranks, 0, 3 * ff // 128)
    gate[...] = dot(xn_two[...], w_gu[:, :ff]) + dot(u_two_ref[:, :128], ranks[:, :ff])
    up[...] = dot(xn_two[...], w_gu[:, ff:]) + dot(u_two_ref[:, 128:], ranks[:, ff : 2 * ff])
    hidden[...] = (gate[...] * jax.nn.sigmoid(gate[...]) * up[...]).astype(NARROW)
    loads[4].wait()

    e_down = (dot(g_full[...], b_down[...]) * picks).astype(NARROW)
    e_down_ref[...] = e_down
    d_hidden = dot(g_full[...], w_down[...]) + dot(e_down, a_down[...])
    sig = jax.nn.sigmoid(gate[...])
    d_gate_up[:, :ff] = (d_hidden * up[...] * sig * (1.0 + gate[...] * (1.0 - sig))).astype(NARROW)
    d_gate_up[:, ff:] = (d_hidden * gate[...] * sig).astype(NARROW)
    e_two = [
        (dot_nt(d_gate_up[:, j * ff : (j + 1) * ff], ranks[:, j * ff : (j + 1) * ff]) * picks).astype(NARROW)
        for j in range(2)
    ]
    two = MpSum(box, part, landed)
    for k in (2, 1, 3, 0):
        rows = columns(two.owner(k), share)
        part[k] = (
            dot_nt(d_gate_up[...], w_gu[rows, :]) + dot_nt(jnp.concatenate(e_two, axis=1), a_two[rows, :])
        ).astype(NARROW)
        if k:
            two.send(k, 0)
    two.send_half(1)
    u_down = (dot_nt(hidden[...], a_down[...]) * picks).astype(NARROW)
    for j, value in enumerate((e_two[0], e_two[1], u_out, u_down)):
        extra[j] = value
    shared = two.share(d_xn)
    extra_sent = [box.push(extra.at[mp_peers[k]], extra_landed.at[k - 1], mp=mp_peers[k]) for k in MpSum.ORDER]
    three = MpSum(box, ffn_part, ffn_landed)
    for k in (2, 1, 3, 0):
        rows = columns(three.owner(k), share)
        ffn_part[k] = (dot_nt(hidden[...], w_down[rows, :]) + dot_nt(u_down, b_down[rows, :])).astype(NARROW)
    for copy in shared:
        copy.wait_recv()
    three.send_half(0)
    three.send_half(1)

    rows = hidden_one[...]
    scale_two = inverse_rms(rows)
    d_one = g_full[...].astype(WIDE) + norm_back(rows, scale_two, norm_ref[0:1, :], d_xn[...].astype(WIDE))
    d_one_out[...] = d_one
    d_branch[...] = d_one.astype(NARROW)
    e_out = (dot(d_branch[...], b_mix[...]) * picks).astype(NARROW)
    d_normed = dot(d_branch[...], w_out[...]) + dot(e_out, a_out[...])
    for h in range(heads):
        cols = slice(h * DH, (h + 1) * DH)
        rows = mixer_out[:, cols]
        d_rows = norm_back(rows, inverse_rms(rows), gain_ref[0:1, :], d_normed[:, cols])
        d_mixer_out[:, cols] = d_rows
        g_maps[h] = wide_dot(reach[:, cols], d_rows, 0, 0).astype(NARROW)
    chain.start_backward(g_maps, sib_g, chip_g, row_g, pass_on)
    g_a_out[...] = dot_tn(e_out, normed[...]).astype(NARROW)
    chain.chips_backward()
    for j in range(2):
        cols = slice(j * ff, (j + 1) * ff)
        g_b_ffn[:, cols] = dot_tn(u_two_ref[:, j * 128 : (j + 1) * 128], d_gate_up[:, cols]).astype(NARROW)
    chain.rows_backward()
    g_a_down[...] = dot_tn(e_down_ref[...], hidden[...]).astype(NARROW)
    for copy in extra_sent:
        copy.wait_recv()
    factor = extra[m].astype(WIDE)
    for k in range(3):
        factor = factor + extra_landed[k].astype(WIDE)
    left = jnp.where(m < 2, xn_two[...], jnp.where(m == 2, d_branch[...], g_full[...]))
    g_shared[...] = dot_tn(left, factor.astype(NARROW)).astype(NARROW)
    chain.finish_backward(grad_out)
    for half in range(2):
        rows = three.rows(half)
        output[rows] = (hidden_one[rows, columns(m, share)] + three.total(half)).astype(NARROW)
    box.drain()


def middle(kept_maps, forward, x, g, norm, gain, ranks, late, wide):
    operands = (*kept_maps, *forward, x, g, norm, gain, ranks)
    count, inner = forward[0].shape
    heads = inner // DH
    model = x.shape[1]
    share = model // 4
    ff = (wide.shape[1] - 384) // 3
    vmem = pl.BlockSpec(memory_space=pltpu.VMEM)
    anywhere = pl.BlockSpec(memory_space=pl.ANY)
    two = (2, DH, DH)
    copies = 1 + 3 + 3 + 1 + 12 + 3 + 6
    results = [
        ((count, share), NARROW),
        ((heads, DH, DH), WIDE),
        ((count, model), WIDE),
        ((count, inner), WIDE),
        ((128, 2 * ff), NARROW),
        ((128, ff), NARROW),
        ((128, inner), NARROW),
        ((model, 128), NARROW),
    ]
    scratch = [
        (late.shape, NARROW),
        ((model, 2 * ff), NARROW),
        ((model, ff), NARROW),
        ((model, 384), NARROW),
        ((3, model, 128), WIDE),
        ((3 * ff // 128, 128, 128), WIDE),
        ((128, 3 * ff), NARROW),
        (two, NARROW),
        ((4,) + two, NARROW),
        ((4,) + two, NARROW),
        (two, WIDE),
        ((heads, DH, DH), NARROW),
        ((4, count, share), NARROW),
        ((3, count, share), NARROW),
        ((count, model), WIDE),
        ((count, model), NARROW),
        ((count, ff), WIDE),
        ((count, ff), WIDE),
        ((count, ff), NARROW),
        ((4, count, share), NARROW),
        ((3, count, share), NARROW),
        ((count, 2 * ff), NARROW),
        ((count, model), NARROW),
        ((4, count, 128), NARROW),
        ((3, count, 128), NARROW),
        ((count, model), NARROW),
        ((count, 128), NARROW),
        ((count, 256), NARROW),
    ]
    return pl.pallas_call(
        middle_kernel,
        out_shape=tuple(jax.ShapeDtypeStruct(*r) for r in results),
        in_specs=[vmem] * len(operands) + [anywhere] * 2,
        out_specs=tuple([vmem] * len(results)),
        scratch_shapes=[pltpu.VMEM(*v) for v in scratch]
        + [
            pltpu.SemaphoreType.DMA((copies,)),
            pltpu.SemaphoreType.DMA((copies,)),
            pltpu.SemaphoreType.DMA((5,)),
        ],
        compiler_params=pltpu.CompilerParams(
            collective_id=2, has_side_effects=True, vmem_limit_bytes=60 << 20
        ),
        name="middle",
    )(*operands, late, wide)


class DpSum:
    SCRATCH = 6

    @staticmethod
    def scratch(rows, width):
        small = rows // 4
        return [
            ((2, 4, rows, width), NARROW),
            ((4, rows, width), NARROW),
            ((3, rows, width), NARROW),
            ((4, small, width), WIDE),
            ((3, small, width), WIDE),
            ((small, width), WIDE),
        ]

    def __init__(self, box, full, landed_core, landed_y, by_z, landed_z, result):
        self.box, self.full, self.landed_core = box, full, landed_core
        self.landed_y, self.by_z, self.landed_z, self.result = landed_y, by_z, landed_z, result
        self.y, self.z, self.c = coords()

    def over_cores(self):
        self.pair = self.box.push(self.full.at[1 - self.c], self.landed_core, dp=moved(0, 0, True))

    def over_y(self):
        self.pair.wait_recv()
        mine = self.full.at[self.c]
        for i in range(4):
            mine[i] = (mine[i].astype(WIDE) + self.landed_core[i].astype(WIDE)).astype(NARROW)
        self.copies = [
            self.box.push(mine.at[lax.rem(self.y + k, 4)], self.landed_y.at[k - 1], dp=moved(k, 0)) for k in (2, 1, 3)
        ]

    def over_z(self):
        for copy in self.copies:
            copy.wait_recv()
        total = self.full[self.c, self.y].astype(WIDE)
        for k in range(3):
            total = total + self.landed_y[k].astype(WIDE)
        self.by_z[...] = total.reshape(self.by_z.shape)
        self.copies = [
            self.box.push(self.by_z.at[lax.rem(self.z + k, 4)], self.landed_z.at[k - 1], dp=moved(0, k))
            for k in (2, 1, 3)
        ]

    def finish(self):
        for copy in self.copies:
            copy.wait_recv()
        total = self.by_z[self.z]
        for k in range(3):
            total = total + self.landed_z[k]
        self.result[...] = total


def tail_kernel(
    taps_ref, aux_ref, seg_ref, state_ref, grad_ref, d_out_ref,
    u_ref, norm_ref, picks_ref, ranks, shared_two, g_b_ffn, g_a_out, g_a_down,
    pre_in, kept_in, t_in, x_in, xn_in, d_one_in, wide_ref, thin_ref,
    grad_input, out_a_in, out_heads, out_beta, out_a_out, out_ffn, out_a_down, out_res,
    pre_ref, kept_all, t_ref, x_ref, xn_ref, d_one_ref, w_in, a_one, d_ext, pre_wide, taps, halo, d_pre, e_one, part, landed, extra_landed, sums, sums_landed, pair, early_pair, ends,
    *rest,
):
    one, two, three, four = (rest[i * DpSum.SCRATCH : (i + 1) * DpSum.SCRATCH] for i in range(4))
    send, recv, local = rest[4 * DpSum.SCRATCH :]
    count, model = x_in.shape
    inner = d_out_ref.shape[1]
    heads = inner // DH
    ff = g_a_down.shape[1]
    m = lax.axis_index("mp")
    c = lax.rem(lax.axis_index("dp"), 2)
    before, after = (lax.rem(lax.axis_index("dp") + k, 32) for k in (31, 1))
    mp_peers = {k: lax.rem(m + k, 4) for k in (1, 2, 3)}
    dp_peers = [before, after, moved(0, 0, True)]
    dp_peers += [moved(k, 0) for k in (1, 2, 3)] + [moved(0, k) for k in (1, 2, 3)]
    loads = [
        pltpu.make_async_copy(source, target, local.at[i])
        for i, (source, target) in enumerate(
            (
                (pre_in, pre_ref),
                (kept_in, kept_all),
                (t_in, t_ref),
                (wide_ref.at[:, pl.ds(0, w_in.shape[1])], w_in),
                (thin_ref.at[:, pl.ds(0, a_one.shape[1])], a_one),
                (x_in, x_ref),
                (xn_in, xn_ref),
                (d_one_in, d_one_ref),
            )
        )
    ]
    for load in loads:
        load.start()
    greet(dp_peers, list(mp_peers.values()))
    box = Mailbox(send, recv)
    early_sum, heads_sum, two_sum, one_sum = (DpSum(box, *refs) for refs in (four, one, two, three))

    def halves(refs, values):
        half = refs[0].shape[3]
        missing = 2 * half - sum(value.shape[1] for value in values)
        values = values + [jnp.zeros((128, missing), NARROW)] if missing else values
        values = jnp.concatenate(values, axis=1)
        for i in range(2):
            refs[0][i] = values[:, i * half : (i + 1) * half].reshape(4, 32, half)

    def by_core(value):
        value = value.reshape(4, 4, 2, model // 32, 128)
        return [value[:, :, i].reshape(4, model // 8, 128) for i in range(2)]

    halves(four, [g_b_ffn[...], g_a_out[...], g_a_down[...]])
    early_sum.over_cores()
    for i, value in enumerate(by_core(shared_two[...])):
        two[0][i] = value
    two_sum.over_cores()
    aux = aux_ref[...]
    spread_taps(taps_ref, taps)
    for load in loads[:3]:
        load.wait()
    pre_wide[...] = pre_ref[...].astype(WIDE)
    kept = (*(kept_all.at[i] for i in range(3)), t_ref, *(kept_all.at[i] for i in (3, 4)))
    lanes = lax.broadcasted_iota(jnp.int32, aux.shape, 1)
    d_logit = jnp.zeros(aux.shape, WIDE)
    def between():
        early_sum.over_y()
        two_sum.over_y()

    found = mixer_backward(
        list(range(heads)), pre_wide, taps, aux, seg_ref[...].astype(WIDE), kept, state_ref, grad_ref, d_out_ref, d_ext,
        between,
    )
    for h, value in enumerate(found):
        d_logit = jnp.where(lanes == 8 + h, value, d_logit)
    edges = [box.push(d_ext.at[i, pl.ds(HALO - 8, 8)], halo.at[i], dp=before) for i in range(3)]
    early_sum.over_z()
    two_sum.over_z()
    picks = picks_ref[...]
    d_logit = d_logit.astype(NARROW)
    for copy in edges:
        copy.wait_recv()
    for i in range(3):
        ref = d_ext.at[i]
        cols = slice(i * inner, (i + 1) * inner)
        d_pre[: count - 16, cols] = ref[HALO : HALO + count - 16].astype(NARROW)
        ending = ref[HALO + count - 16 :]
        d_pre[count - 16 :, cols] = jnp.concatenate([ending[:8], ending[8:] + halo[i]], axis=0).astype(NARROW)
    for j in range(3):
        cols = slice(j * inner, (j + 1) * inner)
        e_one[j] = (dot_nt(d_pre[:, cols], ranks[:, cols]) * picks).astype(NARROW)
    e_one[3] = (dot_nt(d_logit, ranks[:, 4 * inner :]) * picks).astype(NARROW)
    extra_sent = [box.push(e_one.at[mp_peers[k]], extra_landed.at[k - 1], mp=mp_peers[k]) for k in MpSum.ORDER]
    grads = [dot_tn(u_ref[:, j * 128 : (j + 1) * 128], d_pre[:, j * inner : (j + 1) * inner]) for j in range(3)]
    grads.append(dot_tn(u_ref[:, 384:], d_logit))
    halves(one, [value.astype(NARROW) for value in grads])
    heads_sum.over_cores()
    for load in loads[3:]:
        load.wait()
    share = grad_input.shape[1]
    total = MpSum(box, part, landed)
    row_sum = jnp.zeros((count, 128), WIDE)
    all_e = jnp.concatenate([e_one[j] for j in range(4)], axis=1)
    for k in (2, 1, 3, 0):
        owner = total.owner(k)
        rows = columns(owner, share)
        value = (
            dot_nt(d_pre[...], w_in[rows, : 3 * inner])
            + dot_nt(d_logit, w_in[rows, 3 * inner :])
            + dot_nt(all_e, a_one[rows, :])
        )
        part[k] = value.astype(NARROW)
        if k:
            total.send(k, 0)
            total.send(k, 1)
        weighted = value * norm_ref[0:1, rows] * x_ref[:, rows].astype(WIDE)
        row_sum = row_sum + jnp.sum(weighted, axis=1, keepdims=True)
    sums[...] = row_sum.T[:8]
    sums_sent = [box.push(sums, sums_landed.at[k - 1], mp=mp_peers[k]) for k in MpSum.ORDER]
    heads_sum.over_y()
    early_sum.finish()
    early_pair[c] = four[5][...]
    early_paired = box.push(four[5], early_pair.at[c], dp=moved(0, 0, True))
    for copy in extra_sent:
        copy.wait_recv()
    factor = e_one[m].astype(WIDE)
    for k in range(3):
        factor = factor + extra_landed[k].astype(WIDE)
    for i, value in enumerate(by_core(dot_tn(xn_ref[...], factor.astype(NARROW)).astype(NARROW))):
        three[0][i] = value
    one_sum.over_cores()
    heads_sum.over_z()
    one_sum.over_y()
    rank_rows = model // 128

    def to_owners(slot, result):
        ends[slot, m] = result[columns(m, rank_rows)]
        return [
            box.push(result.at[columns(mp_peers[k], rank_rows)], ends.at[slot, m], mp=mp_peers[k])
            for k in MpSum.ORDER
        ]

    two_sum.finish()
    owners = to_owners(1, two[5])
    heads_sum.finish()
    pair[c] = one[5][...]
    paired = box.push(one[5], pair.at[c], dp=moved(0, 0, True))
    one_sum.over_z()
    x_all = x_ref[...].astype(WIDE)
    scale = inverse_rms(x_all)
    mine = columns(m, share)
    one_sum.finish()
    owners += to_owners(0, three[5])
    for copy in sums_sent:
        copy.wait_recv()
    rows = sums[...] + sums_landed[0] + sums_landed[1] + sums_landed[2]
    mean = jnp.concatenate([rows] * 16, axis=0).T[:, :1] / model
    scale_three = scale * scale * scale * mean
    for half in range(2):
        at = total.rows(half)
        here = slice(half * (count // 2), (half + 1) * (count // 2))
        grad_input[at] = d_one_ref[at, mine] + (
            scale[here] * norm_ref[0:1, mine] * total.total(half) - x_ref[at, mine].astype(WIDE) * scale_three[here]
        )
    paired.wait_recv()
    early_paired.wait_recv()

    def own_ranks(pair):
        both = jnp.concatenate([pair[0], pair[1]], axis=1)
        return jnp.where(c == 0, both[:4], both[4:])

    rows = own_ranks(pair)
    for j in range(3):
        out_heads[j] = rows[:, j * inner : (j + 1) * inner]
    out_beta[...] = rows[:, 3 * inner + 8 : 3 * inner + 8 + heads]
    rows = own_ranks(early_pair)
    for j in range(2):
        out_ffn[j] = rows[:, j * ff : (j + 1) * ff]
    out_a_out[...] = rows[:, 2 * ff : 2 * ff + inner]
    out_a_down[...] = rows[:, 2 * ff + inner : 3 * ff + inner]
    for copy in owners:
        copy.wait_recv()
    for j in range(4):
        out_a_in[j] = ends[0, j]
    for j in range(2):
        out_a_in[4 + j] = ends[1, j]
        out_res[j] = ends[1, 2 + j]
    box.drain()


def tail(mixer, tokens, grads, kept, wide, thin):
    model = kept[3].shape[1]
    count, inner = mixer[-1].shape
    heads = inner // DH
    share = model // 4
    ff = grads[3].shape[1]

    def half_of(width):
        return -(-width // 256) * 128

    half, early_half = half_of(3 * inner + 128), half_of(3 * ff + inner)
    vmem = pl.BlockSpec(memory_space=pltpu.VMEM)
    anywhere = pl.BlockSpec(memory_space=pl.ANY)
    copies = 3 + 3 + 6 + 3 + 4 * 7 + 2 + 6
    results = [
        (count, share), (6, model // 128, 128), (3, 4, inner), (4, heads),
        (4, inner), (2, 4, ff), (4, ff), (2, model // 128, 128),
    ]
    scratch = [(x.shape, x.dtype) for x in kept] + [
        ((model, 3 * inner + 128), NARROW),
        ((model, 512), NARROW),
        ((3, HALO + count, inner), WIDE),
        ((HALO + count, 3 * inner), WIDE),
        ((16, inner), WIDE),
        ((3, 8, inner), WIDE),
        ((count, 3 * inner), NARROW),
        ((4, count, 128), NARROW),
        ((4, count, share), NARROW),
        ((3, count, share), NARROW),
        ((3, count, 128), NARROW),
        ((8, count), WIDE),
        ((3, 8, count), WIDE),
        ((2, 8, half), WIDE),
        ((2, 8, early_half), WIDE),
        ((2, 4, model // 128, 128), WIDE),
    ]
    scratch += DpSum.scratch(32, half) + DpSum.scratch(model // 8, 128) + DpSum.scratch(model // 8, 128)
    scratch += DpSum.scratch(32, early_half)
    operands = (*mixer, *tokens, *grads)
    return pl.pallas_call(
        tail_kernel,
        out_shape=tuple(jax.ShapeDtypeStruct(r, WIDE) for r in results),
        in_specs=[vmem] * len(operands) + [anywhere] * (len(kept) + 2),
        out_specs=tuple([vmem] * len(results)),
        scratch_shapes=[pltpu.VMEM(*s) for s in scratch]
        + [
            pltpu.SemaphoreType.DMA((copies,)),
            pltpu.SemaphoreType.DMA((copies,)),
            pltpu.SemaphoreType.DMA((8,)),
        ],
        compiler_params=pltpu.CompilerParams(
            collective_id=3, has_side_effects=True, vmem_limit_bytes=60 << 20
        ),
        name="tail",
    )(*operands, *kept, wide, thin)


def hand_over_kernel(*refs):
    half = len(refs) // 2
    for source, target in zip(refs[:half], refs[half:]):
        target[...] = source[...]


def hand_over(*arrays):
    vmem = pl.BlockSpec(memory_space=pltpu.VMEM)
    return pl.pallas_call(
        hand_over_kernel,
        out_shape=tuple(jax.ShapeDtypeStruct(x.shape, x.dtype) for x in arrays),
        in_specs=[vmem] * len(arrays),
        out_specs=tuple([vmem] * len(arrays)),
        name="hand_over",
    )(*arrays)


def on_device(
    layer_in, cotangent, segments, adapters, norm_one, norm_two, out_gain, beta_bias, conv_taps,
    w_qkv, w_beta, w_out, w_gate_up, w_down, a_in, b_heads, b_beta, a_out, b_ffn, a_down, b_res,
):
    heads = w_beta.shape[1]
    inner = heads * DH
    ff = w_down.shape[0]

    def pack_ranks(parts, blocks):
        flat = jnp.concatenate(parts, axis=1).reshape(-1, 128)
        flat = jnp.pad(flat, ((0, 64 * blocks - flat.shape[0]), (0, 0)))
        return flat.reshape(blocks, 64, 128).transpose(1, 0, 2).reshape(64, blocks * 128)

    last = jnp.concatenate(
        [
            w_gate_up.reshape(64, 2 * ff),
            w_down.T,
            pack_ranks([b_ffn.transpose(1, 0, 2).reshape(4, 2 * ff), a_down.T], 3),
        ],
        axis=1,
    )
    beta = jnp.concatenate([w_beta, jnp.zeros((64, 64 - heads), NARROW), jnp.pad(b_beta, ((0, 60), (0, 0)))], axis=1)
    wide = jnp.concatenate(
        [
            w_qkv.reshape(64, 3 * inner),
            jnp.pad(beta, ((0, 0), (8, 56 - heads))),
            pack_ranks([b_heads.transpose(1, 0, 2).reshape(4, 3 * inner), a_out.T], 1),
        ],
        axis=1,
    )
    a_flat = a_in.reshape(16, 768)
    late_thin = jnp.concatenate([a_flat[:, 512:], b_res.transpose(2, 0, 1).reshape(16, 256)], axis=1)
    seg_row = segments[None, :]
    (
        wide, thin, late, last, pre, xn_one, kept, t_map, aux, picks, u_one, reach, ranks,
        maps, sib_a, chip_a, row_a, state_in, mixer_out, normed, u_out, branch, g_full,
    ) = front(
        layer_in, cotangent, seg_row, adapters, norm_one[None, :], out_gain[None, :],
        beta_bias, conv_taps, wide, a_flat[:, :512], w_out.T, late_thin, last,
    )
    wide, thin, late, last = (x.reshape(2048, -1) for x in (wide, thin, late, last))
    output, state_grad, d_hidden_one, d_mixer, grad_b_ffn, grad_a_down, grad_a_out, shared_two = middle(
        (maps, sib_a, chip_a, row_a), (reach, mixer_out, normed, u_out, branch, picks),
        layer_in, g_full, norm_two[None, :], out_gain[None, :], ranks, late, last,
    )
    grad_input, d_a_in, d_b_heads, d_b_beta, d_a_out, d_b_ffn, d_a_down, d_b_res = tail(
        (conv_taps, aux, seg_row, state_in, state_grad, d_mixer),
        (u_one, norm_one[None, :], picks, ranks),
        (shared_two, grad_b_ffn, grad_a_out, grad_a_down),
        (pre, kept, t_map, layer_in, xn_one, d_hidden_one),
        wide,
        thin,
    )
    output, grad_input, d_a_in, d_b_heads, d_b_beta, d_a_out, d_b_ffn, d_a_down, d_b_res = hand_over(
        output, grad_input, d_a_in, d_b_heads, d_b_beta, d_a_out, d_b_ffn, d_a_down, d_b_res
    )
    return (
        output, grad_input, d_a_in.transpose(1, 0, 2), d_b_heads, d_b_beta, d_a_out.T, d_b_ffn, d_a_down.T,
        d_b_res.transpose(0, 2, 1),
    )


def solution(mesh):
    placed = (
        P("dp", None),
        P("dp", "mp"),
        P("dp"),
        P(),
        P(),
        P(),
        P(),
        P("mp"),
        P(None, None, "mp"),
        P("dp", None, "mp"),
        P("dp", "mp"),
        P("mp", "dp"),
        P("dp", None, "mp"),
        P("mp", "dp"),
        P(("dp", "mp"), None, None),
        P(None, "dp", "mp"),
        P("dp", "mp"),
        P("mp", "dp"),
        P(None, "dp", "mp"),
        P("mp", "dp"),
        P(None, None, ("dp", "mp")),
    )
    return jax.shard_map(
        on_device,
        mesh=mesh,
        in_specs=placed,
        out_specs=(
            P("dp", "mp"),
            P("dp", "mp"),
            P(("dp", "mp"), None, None),
            P(None, "dp", "mp"),
            P("dp", "mp"),
            P("mp", "dp"),
            P(None, "dp", "mp"),
            P("mp", "dp"),
            P(None, None, ("dp", "mp")),
        ),
        check_vma=False,
    )
```

```python
import functools

import jax
import jax.numpy as jnp
from jax import lax
from jax.experimental import pallas as pl
from jax.experimental.pallas import tpu as pltpu
from jax.sharding import PartitionSpec as P

DH = 128
KW = 4
RANK = 16
HALO = 16
EPSILON = 1e-06
WIDE = jnp.float32
NARROW = jnp.bfloat16
MESH = pl.DeviceIdType.MESH
EXACT = lax.Precision.HIGHEST


def coords():
    place = lax.axis_index("dp")
    return place // 8, lax.rem(place // 2, 4), lax.rem(place, 2)


def place_of(y, z, c):
    return (y * 4 + z) * 2 + c


def moved(dy, dz, other_core=False):
    y, z, c = coords()
    return place_of(lax.rem(y + dy + 4, 4), lax.rem(z + dz + 4, 4), 1 - c if other_core else c)


def greet(dp_peers=(), mp_peers=()):
    barrier = pltpu.get_barrier_semaphore()
    for peer in dp_peers:
        pl.semaphore_signal(barrier, inc=1, device_id={"dp": peer}, device_id_type=MESH)
    for peer in mp_peers:
        pl.semaphore_signal(barrier, inc=1, device_id={"mp": peer}, device_id_type=MESH)
    pl.semaphore_wait(barrier, len(dp_peers) + len(mp_peers))


class Mailbox:
    def __init__(self, send, recv):
        self.send, self.recv, self.copies = send, recv, []

    def push(self, src, dst, **device):
        k = len(self.copies)
        copy = pltpu.make_async_remote_copy(
            src_ref=src,
            dst_ref=dst,
            send_sem=self.send.at[k],
            recv_sem=self.recv.at[k],
            device_id=device,
            device_id_type=MESH,
        )
        copy.start()
        self.copies.append(copy)
        return copy

    def drain(self):
        for copy in self.copies:
            copy.wait_send()


def gather_steps(box, own, out):
    me = moved(0, 0)
    half = own.shape[0] // 2
    quarter = half // 2
    sibling = moved(0, 0, True)
    kinds = []
    for kind in range(2):
        base = kind * half
        parts = (pl.ds(base, half), pl.ds(base, quarter), pl.ds(base + quarter, quarter))
        if kind == 0:
            kinds.append((parts, lambda a, b: moved(a, b)))
        else:
            kinds.append((parts, lambda a, b: moved(b, a)))
    near, across, far, far_across, shared = [], [{}, {}], [[], []], [{}, {}], []

    def open_up():
        for parts, at in kinds:
            near.append([box.push(own.at[parts[0]], out.at[me, parts[0]], dp=at(s, 0)) for s in (1, -1)])
        for k, (parts, at) in enumerate(kinds):
            across[k][0] = [box.push(own.at[parts[0]], out.at[me, parts[0]], dp=at(0, s)) for s in (1, -1)]
        shared.append(box.push(own, out.at[me], dp=sibling))

    def pass_on(k, slot):
        parts, at = kinds[k]
        block = out.at[slot, parts[0]]
        return [box.push(block, block, dp=at(0, t)) for t in (1, -1)]

    def to_sibling(k, slot):
        block = out.at[slot, kinds[k][0][0]]
        shared.append(box.push(block, block, dp=sibling))

    def from_near(i, s):
        def step():
            for k, (parts, at) in enumerate(kinds):
                near[k][i].wait_recv()
                block = out.at[at(s, 0), parts[1 + i]]
                far[k].append(box.push(block, block, dp=at(-s, 0)))
            for k, (parts, at) in enumerate(kinds):
                across[k][s] = pass_on(k, at(s, 0))
                to_sibling(k, at(s, 0))

        return step

    def from_far(k):
        def step():
            for copy in far[k]:
                copy.wait_recv()
            slot = kinds[k][1](2, 0)
            across[k][2] = pass_on(k, slot)
            to_sibling(k, slot)

        return step

    def from_across(k, f):
        def step():
            parts, at = kinds[k]
            far_across[k][f] = []
            for i, s in enumerate((-1, 1)):
                across[k][f][i].wait_recv()
                slot = at(f, s)
                block = out.at[slot, parts[1 + i]]
                far_across[k][f].append(box.push(block, block, dp=at(0, -s)))
                to_sibling(k, slot)

        return step

    def from_far_across(k, f):
        def step():
            for copy in far_across[k][f]:
                copy.wait_recv()
            to_sibling(k, kinds[k][1](f, 2))

        return step

    def close():
        for copy in shared:
            copy.wait_recv()

    steps = [open_up, from_near(0, -1), from_near(1, 1), from_far(0), from_far(1)]
    steps += [from_across(k, f) for f in (0, -1, 1, 2) for k in range(2)]
    steps += [from_far_across(k, f) for f in (0, -1, 1, 2) for k in range(2)]
    return steps + [close]


def gather_peers():
    return [moved(1, 0), moved(-1, 0), moved(0, 1), moved(0, -1), moved(0, 0, True)]


GATHER_COPIES = 71


def half_dot(left, right):
    high = right.astype(NARROW)
    low = (right - high.astype(WIDE)).astype(NARROW)
    both = lax.dot(left, jnp.concatenate([high, low], axis=1), preferred_element_type=WIDE)
    return both[:, : right.shape[1]] + both[:, right.shape[1] :]


def two_parts(value):
    high = value.astype(NARROW)
    return high, (value - high.astype(WIDE)).astype(NARROW)


def wide_dot(left, right, left_dim=1, right_dim=0):
    left_high, left_low = two_parts(left)
    right_high, right_low = two_parts(right)

    def part(one, two):
        return lax.dot_general(one, two, (((left_dim,), (right_dim,)), ((), ())), preferred_element_type=WIDE)

    return part(left_high, right_high) + (part(left_high, right_low) + part(left_low, right_high))


def convolve(pre_ref, taps_ref, part, head, inner, aux):
    count = aux.shape[0]
    cols = slice(part * inner + head * DH, part * inner + (head + 1) * DH)
    taps = taps_ref[:, head * DH : (head + 1) * DH]
    total = pre_ref[pl.ds(HALO, count), cols] * taps[part : part + 1]
    for j in range(1, KW):
        shifted = pre_ref[pl.ds(HALO - j, count), cols]
        total = total + shifted * aux[:, j : j + 1] * taps[3 * j + part : 3 * j + part + 1]
    return total


def spread_taps(taps_ref, taps):
    for part in range(3):
        rows = taps_ref[part].astype(WIDE)
        for j in range(KW):
            taps[3 * j + part : 3 * j + part + 1, :] = rows[j : j + 1]


def masks(aux, seg_row):
    same = aux[:, 6:7] == seg_row
    shape = (aux.shape[0], aux.shape[0])
    row = lax.broadcasted_iota(jnp.int32, shape, 0)
    col = lax.broadcasted_iota(jnp.int32, shape, 1)
    return row, col, same


def each(step, *lists):
    return [step(*items) for items in zip(*lists)]


def lower_inverses(lowers, row, col, tick):
    near = [jnp.where(row // 8 == col // 8, lower, 0.0) for lower in lowers]
    square = each(lambda a: wide_dot(a, a), near)
    inverse = [jnp.where(row == col, 1.0, 0.0) - a for a in near]
    inverse = each(lambda x, s: x + wide_dot(x, s), inverse, square)
    square = each(lambda s: wide_dot(s, s), square)
    inverse = each(lambda x, s: x + wide_dot(x, s), inverse, square)
    size = 8
    while size < row.shape[0]:
        link = (row // (2 * size) == col // (2 * size)) & (row // size != col // size)
        middle = each(lambda lower, x: wide_dot(jnp.where(link, lower, 0.0), x), lowers, inverse)
        inverse = each(lambda x, y: x - wide_dot(x, y), inverse, middle)
        size *= 2
        tick()
    return inverse


def mixer_forward(heads, pre_ref, taps_ref, aux, seg_row, out_ref, reach_ref, map_ref, offset_ref, kept, tick):
    q_ref, k_ref, v_ref, t_ref, w_ref, u_ref = kept
    count = aux.shape[0]
    inner = out_ref.shape[1]
    linked, ending = aux[:, 4:5], aux[:, 5:6]
    row, col, same = masks(aux, seg_row)
    rate = [aux[:, 8 + h : 9 + h] for h in heads]
    cols = [slice(h * DH, (h + 1) * DH) for h in heads]

    def act(part):
        convs = [convolve(pre_ref, taps_ref, part, h, inner, aux) for h in heads]
        return [conv * jax.nn.sigmoid(conv) for conv in convs]

    def unit(a):
        return a * lax.rsqrt(jnp.sum(a * a, axis=1, keepdims=True) + EPSILON)

    k = each(unit, act(1))
    gram = each(lambda b: wide_dot(b, b, 1, 1), k)
    lowers = each(lambda g, r: jnp.where((row > col) & same, g * r, 0.0), gram, rate)
    q, v = each(unit, act(0)), act(2)
    for i in range(len(heads)):
        q_ref[:, cols[i]] = q[i]
        k_ref[:, cols[i]] = k[i]
        v_ref[:, cols[i]] = v[i]
    scores = each(lambda a, b: jnp.where((row >= col) & same, wide_dot(a, b, 1, 1), 0.0), q, k)
    tick()
    inverse = lower_inverses(lowers, row, col, tick)
    written = each(
        lambda t, a, b, r: wide_dot(t, jnp.concatenate([a, b * linked], axis=1) * r), inverse, v, k, rate
    )
    ends = each(lambda b, w: wide_dot(b * ending, w, 0, 0), k, written)
    mixed = each(wide_dot, scores, written)
    eye = jnp.where(row[:DH, :DH] == col[:DH, :DH], 1.0, 0.0)
    last = aux[count - 1 :, 4:5]
    for i, h in enumerate(heads):
        t_ref[h] = inverse[i]
        w_ref[:, cols[i]] = written[i][:, :DH]
        u_ref[:, cols[i]] = written[i][:, DH:]
        offset_ref[h] = ends[i][:, :DH].astype(offset_ref.dtype)
        map_ref[h] = (eye * last - ends[i][:, DH:]).astype(map_ref.dtype)
        out_ref[:, cols[i]] = mixed[i][:, :DH]
        reach_ref[:, cols[i]] = q[i] * linked - mixed[i][:, DH:]
    tick()


def mixer_backward(heads, pre_ref, taps_ref, aux, seg_row, kept, state_ref, grad_ref, d_out_ref, d_ext, between):
    q_ref, k_ref, v_ref, t_ref, w_ref, u_ref = kept
    count = aux.shape[0]
    inner = d_out_ref.shape[1]
    linked, ending = aux[:, 4:5], aux[:, 5:6]
    row, col, same = masks(aux, seg_row)
    upto = (row >= col) & same
    below = (row > col) & same

    def take(ref):
        return [ref[:, h * DH : (h + 1) * DH] for h in heads]

    rate = [aux[:, 8 + h : 9 + h] for h in heads]
    q, k, v, d_out = take(q_ref), take(k_ref), take(v_ref), take(d_out_ref)
    state, grad = [state_ref[h] for h in heads], [grad_ref[h] for h in heads]
    written = each(lambda w, u, s: w - wide_dot(u, s), take(w_ref), take(u_ref), state)
    scores = each(lambda a, b: jnp.where(upto, wide_dot(a, b, 1, 1), 0.0), q, k)
    d_written = each(
        lambda a, d, b, g: wide_dot(a, d, 0, 0) + wide_dot(b * ending, g), scores, d_out, k, grad
    )
    d_right = each(lambda t, d: wide_dot(t, d, 0, 0), [t_ref[h] for h in heads], d_written)
    d_scores = each(lambda d, w: jnp.where(upto, wide_dot(d, w, 1, 1), 0.0), d_out, written)
    between()
    d_lower = each(lambda d, w: jnp.where(below, -wide_dot(d, w, 1, 1), 0.0), d_right, written)
    d_q = each(
        lambda ds, b, d, s: wide_dot(ds, b) + linked * wide_dot(d, s, 1, 1), d_scores, k, d_out, state
    )
    d_k = each(
        lambda ds, a, w, g: wide_dot(ds, a, 0, 0) + ending * wide_dot(w, g, 1, 1), d_scores, q, written, grad
    )
    d_rate = each(
        lambda d, a, b, s: jnp.sum(d * (a - linked * wide_dot(b, s)), axis=1, keepdims=True), d_right, v, k, state
    )
    d_rate = each(
        lambda r, d, b: r + jnp.sum(d * wide_dot(b, b, 1, 1), axis=1, keepdims=True), d_rate, d_lower, k
    )
    d_k = each(lambda dk, r, d, s: dk - (linked * r) * wide_dot(d, s, 1, 1), d_k, rate, d_right, state)
    d_gram = each(lambda d, r: d * r, d_lower, rate)
    d_k = each(lambda dk, d, b: dk + wide_dot(d, b) + wide_dot(d, b, 0, 0), d_k, d_gram, k)
    d_v = each(lambda r, d: r * d, rate, d_right)
    for i, h in enumerate(heads):
        for part, (unit, d) in enumerate(((q[i], d_q[i]), (k[i], d_k[i]), (None, d_v[i]))):
            cols = slice(h * DH, (h + 1) * DH)
            conv = convolve(pre_ref, taps_ref, part, h, inner, aux)
            gate = jax.nn.sigmoid(conv)
            if unit is not None:
                act = conv * gate
                scale = lax.rsqrt(jnp.sum(act * act, axis=1, keepdims=True) + EPSILON)
                d = (d - unit * jnp.sum(unit * d, axis=1, keepdims=True)) * scale
            d_conv = d * gate * (1.0 + conv * (1.0 - gate))
            d_ext[part, :HALO, cols] = jnp.zeros((HALO, DH), WIDE)
            d_ext[part, HALO:, cols] = d_conv * taps_ref[part : part + 1, cols]
            for j in range(1, KW):
                term = d_conv * taps_ref[3 * j + part : 3 * j + part + 1, cols] * aux[:, j : j + 1]
                d_ext[part, pl.ds(HALO - j, count), cols] += term
    return each(lambda d, r: d * r * (1.0 - r), d_rate, rate)


def inverse_rms(values):
    return lax.rsqrt(jnp.mean(values * values, axis=-1, keepdims=True) + EPSILON)


def norm_back(values, scale, gain, grad_out):
    weighted = grad_out * gain
    return scale * weighted - values * scale**3 * jnp.mean(weighted * values, axis=-1, keepdims=True)


def dot(left, right):
    return jnp.dot(left, right, preferred_element_type=WIDE)


def dot_nt(left, right):
    return lax.dot_general(left, right, (((1,), (1,)), ((), ())), preferred_element_type=WIDE)


def dot_tn(left, right):
    return lax.dot_general(left, right, (((0,), (0,)), ((), ())), preferred_element_type=WIDE)


class Chain:
    def __init__(self, box, a_ref, sib_a, chip_a, row_a):
        self.box, self.a_ref, self.sib_a, self.chip_a, self.row_a = box, a_ref, sib_a, chip_a, row_a
        self.y, self.z, self.c = coords()
        self.first = self.c == 0
        self.sibling = moved(0, 0, True)
        self.z_peers = {k: moved(0, k) for k in (1, 2, 3)}
        self.y_peers = {k: moved(k, 0) for k in (1, 2, 3)}
        self.mine = pl.ds(pl.multiple_of(2 * self.c, 2), 2)
        self.theirs = pl.ds(pl.multiple_of(2 * (1 - self.c), 2), 2)

    def peers(self):
        return [self.sibling] + list(self.z_peers.values()) + list(self.y_peers.values())

    def swap(self, ref, sib):
        return self.box.push(ref.at[self.theirs], sib, dp=self.sibling)

    def ordered(self, ref, sib, h):
        own, other = ref[2 * self.c + h], sib[h]
        return jnp.where(self.first, own, other), jnp.where(self.first, other, own)

    def spread(self, refs, place, peers):
        return [self.box.push(ref.at[place], ref.at[place], dp=peers[k]) for k in (2, 1, 3) for ref in refs]

    def start_forward(self, b_ref, sib_b, chip_b, row_b, pass_on):
        self.b_ref, self.sib_b, self.chip_b, self.row_b, self.pass_on = b_ref, sib_b, chip_b, row_b, pass_on
        self.pair = [self.swap(self.a_ref, self.sib_a), self.swap(b_ref, sib_b)]

    def chips_forward(self):
        for copy in self.pair:
            copy.wait_recv()
        self.lower = []
        for h in range(2):
            a_low, a_high = self.ordered(self.a_ref, self.sib_a, h)
            b_low, b_high = self.ordered(self.b_ref, self.sib_b, h)
            self.lower.append((a_low, b_low))
            self.chip_a[self.z, h] = lax.dot(a_high, a_low, preferred_element_type=WIDE).astype(NARROW)
            self.chip_b[self.z, h] = (
                lax.dot(a_high, b_low, preferred_element_type=WIDE) + b_high.astype(WIDE)
            ).astype(NARROW)
        self.ring = self.spread((self.chip_a, self.chip_b), self.z, self.z_peers)

    def rows_forward(self):
        for copy in self.ring:
            copy.wait_recv()
        for h in range(2):
            total_a, total_b = self.chip_a[0, h].astype(WIDE), self.chip_b[0, h].astype(WIDE)
            for i in range(1, 4):
                total_a = half_dot(self.chip_a[i, h], total_a)
                total_b = half_dot(self.chip_a[i, h], total_b) + self.chip_b[i, h].astype(WIDE)
            self.row_a[self.y, h] = total_a.astype(NARROW)
            self.row_b[self.y, h] = total_b.astype(NARROW)
        self.ring = self.spread((self.row_a, self.row_b), self.y, self.y_peers)
        self.ready_forward()

    def ready_forward(self):
        eye = jnp.where(
            lax.broadcasted_iota(jnp.int32, (DH, DH), 0) == lax.broadcasted_iota(jnp.int32, (DH, DH), 1), 1.0, 0.0
        )
        self.within = []
        for h in range(2):
            a, b = eye, jnp.zeros((DH, DH), WIDE)
            for i in range(3):
                step = self.chip_a[i, h]
                longer_a, longer_b = half_dot(step, a), half_dot(step, b) + self.chip_b[i, h].astype(WIDE)
                a, b = jnp.where(i < self.z, longer_a, a), jnp.where(i < self.z, longer_b, b)
            a_low, b_low = self.lower[h]
            a_mid, b_mid = half_dot(a_low, a), half_dot(a_low, b) + b_low.astype(WIDE)
            self.within.append(((a.astype(NARROW), b), (a_mid.astype(NARROW), b_mid)))

    def finish_forward(self, out):
        for copy in self.ring:
            copy.wait_recv()
        for h in range(2):
            state = self.row_b[0, h].astype(WIDE)
            state = jnp.where(self.y > 0, state, 0.0)
            for i in range(1, 3):
                longer = half_dot(self.row_a[i, h], state) + self.row_b[i, h].astype(WIDE)
                state = jnp.where(i < self.y, longer, state)
            (a, b), (a_mid, b_mid) = self.within[h]
            start, middle = half_dot(a, state) + b, half_dot(a_mid, state) + b_mid
            out[2 * self.c + h] = jnp.where(self.first, start, middle)
            self.pass_on[h] = jnp.where(self.first, middle, start)
        self.box.push(self.pass_on, out.at[self.mine], dp=self.sibling).wait_recv()

    def start_backward(self, g_ref, sib_g, chip_g, row_g, pass_on):
        self.g_ref, self.sib_g, self.chip_g, self.row_g, self.pass_on = g_ref, sib_g, chip_g, row_g, pass_on
        self.pair = [self.swap(g_ref, sib_g)]

    def turn(self, chip_t, row_t, pair_t):
        self.chip_t, self.row_t, self.pair_t = chip_t, row_t, pair_t

        def turned(value):
            return value.astype(WIDE).T.astype(NARROW)

        for h in range(2):
            for i in range(4):
                chip_t[i, h] = turned(self.chip_a[i, h])
                row_t[i, h] = turned(self.row_a[i, h])
            low, high = self.ordered(self.a_ref, self.sib_a, h)
            pair_t[0, h] = turned(low)
            pair_t[1, h] = turned(high)

    def chips_backward(self):
        for copy in self.pair:
            copy.wait_recv()
        self.upper_g = []
        for h in range(2):
            g_low, g_high = self.ordered(self.g_ref, self.sib_g, h)
            self.upper_g.append(g_high)
            self.chip_g[self.z, h] = (
                lax.dot(self.pair_t[0, h], g_high, preferred_element_type=WIDE) + g_low.astype(WIDE)
            ).astype(NARROW)
        self.ring = self.spread((self.chip_g,), self.z, self.z_peers)

    def rows_backward(self):
        for copy in self.ring:
            copy.wait_recv()
        for h in range(2):
            total = self.chip_g[3, h].astype(WIDE)
            for i in (2, 1, 0):
                total = half_dot(self.chip_t[i, h], total) + self.chip_g[i, h].astype(WIDE)
            self.row_g[self.y, h] = total.astype(NARROW)
        self.ring = self.spread((self.row_g,), self.y, self.y_peers)
        self.ready_backward()

    def ready_backward(self):
        eye = jnp.where(
            lax.broadcasted_iota(jnp.int32, (DH, DH), 0) == lax.broadcasted_iota(jnp.int32, (DH, DH), 1), 1.0, 0.0
        )
        self.within = []
        for h in range(2):
            a, b = eye, jnp.zeros((DH, DH), WIDE)
            for i in (3, 2, 1):
                step = self.chip_t[i, h]
                longer_a, longer_b = half_dot(step, a), half_dot(step, b) + self.chip_g[i, h].astype(WIDE)
                a, b = jnp.where(i > self.z, longer_a, a), jnp.where(i > self.z, longer_b, b)
            high = self.pair_t[1, h]
            a_mid, b_mid = half_dot(high, a), half_dot(high, b) + self.upper_g[h].astype(WIDE)
            self.within.append(((a.astype(NARROW), b), (a_mid.astype(NARROW), b_mid)))

    def finish_backward(self, out):
        for copy in self.ring:
            copy.wait_recv()
        for h in range(2):
            grad = self.row_g[3, h].astype(WIDE)
            grad = jnp.where(self.y < 3, grad, 0.0)
            for i in (2, 1):
                longer = half_dot(self.row_t[i, h], grad) + self.row_g[i, h].astype(WIDE)
                grad = jnp.where(i > self.y, longer, grad)
            (a, b), (a_mid, b_mid) = self.within[h]
            start, middle = half_dot(a, grad) + b, half_dot(a_mid, grad) + b_mid
            out[2 * self.c + h] = jnp.where(self.first, middle, start)
            self.pass_on[h] = jnp.where(self.first, start, middle)
        self.box.push(self.pass_on, out.at[self.mine], dp=self.sibling).wait_recv()


def columns(i, width):
    return pl.ds(pl.multiple_of(i * width, width), width)


class MpSum:
    ORDER = (2, 1, 3)

    def __init__(self, box, part, landed):
        self.box, self.part, self.landed = box, part, landed
        self.m = lax.axis_index("mp")
        self.peers = {k: lax.rem(self.m + k, 4) for k in (1, 2, 3)}
        self.copies = ([], [])
        self.half = part.shape[1] // 2

    def owner(self, k):
        return lax.rem(self.m + k, 4)

    def rows(self, half):
        return pl.ds(half * self.half, self.half)

    def send(self, k, half):
        rows = self.rows(half)
        self.copies[half].append(
            self.box.push(self.part.at[k, rows], self.landed.at[k - 1, rows], mp=self.peers[k])
        )

    def send_half(self, half):
        for k in self.ORDER:
            self.send(k, half)

    def total(self, half):
        for copy in self.copies[half]:
            copy.wait_recv()
        rows = self.rows(half)
        total = self.part[0, rows].astype(WIDE)
        for k in range(3):
            total = total + self.landed[k, rows].astype(WIDE)
        return total

    def share(self, out):
        width = self.part.shape[2]
        shared = []
        for half in range(2):
            rows = self.rows(half)
            out[rows, columns(self.m, width)] = self.total(half).astype(out.dtype)
            block = out.at[rows, columns(self.m, width)]
            shared += [self.box.push(block, block, mp=self.peers[k]) for k in self.ORDER]
        return shared


def unpack_ranks(block, spread, ranks, first, tiles):
    for q in range(4):
        for t in range(tiles):
            at = first + q * tiles + t
            spread[t, pl.ds(q, 32, stride=4), :] = block[at // 64, pl.ds(at % 64, 32, stride=64), :]
    for t in range(tiles):
        ranks[:, t * 128 : (t + 1) * 128] = spread[t].astype(ranks.dtype)


def front_kernel(
    x_ref, g_own, seg_ref, adapters, norm_ref, gain_ref, bias_ref, taps_ref, w_qkv, block_one, a_in, b_res, late_ref,
    gate_up, down, block_two,
    wide_out, thin_out, late_out, last_out, pre_out, xn_out, kept_out, t_out, aux_ref, picks_ref, u_ref,
    reach, ranks, a_ref, sib_a, chip_a, row_a, state_out, mixer_out, normed, u_out_ref, branch, g_full,
    wide_ref, thin_ref, late_thin, last_ref, pre, xn_ref, kept, t_ref, wide_all, thin_all, late_all, thin_own, late_own, halo_x, seg_ext, xn_ext, pre_wide, block, spread, b_beta,
    b_ref, out_zero, sib_b, chip_b, row_b, pass_on, part, landed, taps, send, recv, local, own_sems,
):
    count, model = x_ref.shape
    heads = a_ref.shape[0]
    inner = heads * DH
    m = lax.axis_index("mp")
    place = lax.axis_index("dp")
    before, after = lax.rem(place + 31, 32), lax.rem(place + 1, 32)
    mp_peers = {k: lax.rem(m + k, 4) for k in (1, 2, 3)}
    box = Mailbox(send, recv)
    chain = Chain(box, a_ref, sib_a, chip_a, row_a)
    parts = [(a_in.at[j], thin_ref.at[:, pl.ds(128 * j, 128)]) for j in range(4)]
    parts += [(a_in.at[4 + j], late_thin.at[:, pl.ds(128 * j, 128)]) for j in range(2)]
    parts += [(b_res.at[j], late_thin.at[:, pl.ds(256 + 128 * j, 128)]) for j in range(2)]
    parts += [(w_qkv.at[j], wide_ref.at[:, pl.ds(inner * j, inner)]) for j in range(3)]
    parts += [(block_one, wide_ref.at[:, pl.ds(3 * inner, 256)])]
    at = 0
    for source in (gate_up, down, block_two):
        parts.append((source, last_ref.at[:, pl.ds(at, source.shape[1])]))
        at += source.shape[1]
    parts = [pltpu.make_async_copy(*pair, own_sems.at[i]) for i, pair in enumerate(parts)]
    for copy in parts:
        copy.start()
    greet([before, after] + chain.peers(), list(mp_peers.values()))
    for copy in parts:
        copy.wait()
    me = moved(0, 0)
    seg_row = seg_ref[...].astype(WIDE)
    seg_ext[HALO:] = jnp.broadcast_to(seg_row, (128, count)).T
    edges = [
        box.push(x_ref.at[pl.ds(count - HALO, HALO)], halo_x, dp=after),
        box.push(seg_ext.at[pl.ds(count, HALO)], seg_ext.at[pl.ds(0, HALO)], dp=after),
    ]
    thin_rows = thin_ref.shape[0]
    mine = pl.ds(pl.multiple_of(m * thin_rows, thin_rows), thin_rows)
    crossing = [box.push(thin_ref, thin_own.at[mine], mp=peer) for peer in mp_peers.values()]
    late_cols = pl.ds(late_ref.shape[1], late_thin.shape[1])
    late_crossing = [box.push(late_thin, late_own.at[mine, late_cols], mp=peer) for peer in mp_peers.values()]
    keep = [
        pltpu.make_async_copy(wide_ref, wide_all.at[me], local.at[0]),
        pltpu.make_async_copy(thin_ref, thin_own.at[mine], local.at[1]),
        pltpu.make_async_copy(late_ref, late_own.at[:, pl.ds(0, late_ref.shape[1])], local.at[2]),
        pltpu.make_async_copy(late_thin, late_own.at[mine, late_cols], local.at[3]),
    ]
    for copy in keep:
        copy.start()
    wide_steps = gather_steps(box, wide_ref, wide_all)
    thin_steps = gather_steps(box, thin_own, thin_all)
    late_steps = gather_steps(box, late_own, late_all)
    last_steps = gather_steps(box, last_ref, last_out)
    wide_steps.pop(0)()
    share = g_own.shape[1]
    g_full[:, columns(m, share)] = g_own[...]
    keep[1].wait()
    for copy in crossing:
        copy.wait_recv()
    keep_thin = pltpu.make_async_copy(thin_own, thin_all.at[me], local.at[4])
    keep_thin.start()
    thin_steps.pop(0)()
    g_sent = [box.push(g_own, g_full.at[:, columns(m, share)], mp=mp_peers[k]) for k in MpSum.ORDER]

    def normal(rows):
        rows = rows.astype(WIDE)
        return (rows * inverse_rms(rows) * norm_ref[0:1, :]).astype(NARROW)

    xn_ref[...] = normal(x_ref[...])
    xn_ext[HALO:] = xn_ref[...]
    for i, (one, two) in enumerate(zip(wide_steps, thin_steps)):
        if i == 12:
            keep[2].wait()
            keep[3].wait()
            for copy in late_crossing:
                copy.wait_recv()
            keep_late = pltpu.make_async_copy(late_own, late_all.at[me], local.at[5])
            keep_late.start()
            late_steps[0]()
            keep_last = pltpu.make_async_copy(last_ref, last_out.at[me], local.at[13])
            keep_last.start()
            last_steps[0]()
        one()
        two()
    keep[0].wait()
    keep_thin.wait()
    rounds = [
        late_steps[1:3],
        late_steps[3:5],
        [],
        late_steps[5:9],
        late_steps[9:13],
        [],
        last_steps[1:2],
        last_steps[2:3],
        [],
        late_steps[13:17],
        late_steps[17:21],
        late_steps[21:22],
        [],
        [],
        [],
        last_steps[3:7],
        last_steps[7:13],
        last_steps[13:22],
    ]
    to_hbm = [
        pltpu.make_async_copy(wide_all, wide_out, local.at[6]),
        pltpu.make_async_copy(thin_all, thin_out, local.at[7]),
    ]
    for copy in to_hbm:
        copy.start()

    def tick():
        for step in rounds.pop(0):
            step()

    for copy in edges:
        copy.wait_recv()
    xn_ext[:HALO] = normal(halo_x[...])
    seg_ext[:HALO] = jnp.where(place == 0, -1.0, seg_ext[:HALO])
    spread_taps(taps_ref, taps)
    lanes = lax.broadcasted_iota(jnp.int32, seg_ext.shape, 1)
    seg_all = seg_ext[...]
    per_token = jnp.zeros(seg_all.shape, WIDE)
    for s in range(adapters.shape[0]):
        per_token = jnp.where(seg_all == float(s), adapters[s].astype(WIDE), per_token)
    picks_ext = jnp.where(per_token == (lanes // RANK).astype(WIDE), 1.0, 0.0)
    picks_ref[...] = picks_ext[HALO:]
    tiles = inner // 128
    for i in range(2):
        lane_block = slice(3 * inner + i * 128, 3 * inner + (i + 1) * 128)
        block[i] = wide_all[:, :, lane_block].reshape(model, 128).astype(WIDE)
    for q in range(4):
        b_beta[pl.ds(q, 32, stride=4), :] = block[0, pl.ds(q, 32, stride=64), :]
    unpack_ranks(block.at[pl.ds(1, 1)], spread, ranks.at[:, pl.ds(0, 4 * inner)], 0, 4 * tiles)
    beta = pltpu.roll(b_beta[...], 64, 1)
    beta_lane = lax.broadcasted_iota(jnp.int32, beta.shape, 1)
    beta = jnp.where((beta_lane >= 8) & (beta_lane < 8 + heads), beta, 0.0)
    ranks[:, 4 * inner :] = beta.astype(NARROW)
    tick()
    u_ext = dot(xn_ext[...], thin_all[...].reshape(model, thin_all.shape[2]))
    u_ext = (u_ext * jnp.concatenate([picks_ext] * 4, axis=1)).astype(NARROW)
    u_ref[...] = u_ext[HALO:]
    tick()
    for j in range(3):
        cols = slice(j * inner, (j + 1) * inner)
        value = dot(xn_ext[...], wide_all[:, :, cols].reshape(model, inner)) + dot(
            u_ext[:, j * 128 : (j + 1) * 128], ranks[:, cols]
        )
        value = value.astype(NARROW)
        pre[:, cols] = value
        pre_wide[:, cols] = value.astype(WIDE)
        tick()
    w_beta = wide_all[:, :, 3 * inner : 3 * inner + 128].reshape(model, 128)
    logits = dot(xn_ref[...], w_beta) + dot(u_ref[:, 384:], ranks[:, 4 * inner :])
    seg = seg_all[HALO:]
    lane = lanes[HALO:]
    for h in range(heads):
        logits = jnp.where(lane == 8 + h, logits + bias_ref[h], logits)
    aux = jnp.where((lane >= 8) & (lane < 8 + heads), jax.nn.sigmoid(logits), 0.0)
    for j in range(KW):
        aux = jnp.where((lane == j) & (seg_ext[pl.ds(HALO - j, count)] == seg), 1.0, aux)
    aux = jnp.where((lane == 4) & (seg == seg_ext[HALO - 1 : HALO]), 1.0, aux)
    aux = jnp.where((lane == 5) & (seg == seg_ext[HALO + count - 1 : HALO + count]), 1.0, aux)
    aux = jnp.where(lane == 6, seg, aux)
    aux_ref[...] = aux
    mixer_forward(
        list(range(heads)), pre_wide, taps, aux, seg_row, out_zero, reach, a_ref, b_ref,
        (*(kept.at[i] for i in range(3)), t_ref, *(kept.at[i] for i in (3, 4))), tick,
    )
    for i, (source, target) in enumerate(((pre, pre_out), (xn_ref, xn_out), (kept, kept_out), (t_ref, t_out))):
        to_hbm.append(pltpu.make_async_copy(source, target, local.at[9 + i]))
        to_hbm[-1].start()
    chain.start_forward(b_ref, sib_b, chip_b, row_b, pass_on)
    tick()
    chain.chips_forward()
    tick()
    chain.rows_forward()
    tick()
    chain.finish_forward(state_out)
    tick()
    keep_late.wait()
    keep_late_out = pltpu.make_async_copy(late_all, late_out, local.at[8])
    keep_late_out.start()
    for h in range(heads):
        cols = slice(h * DH, (h + 1) * DH)
        rows = out_zero[:, cols] + wide_dot(reach[:, cols], state_out[h])
        mixer_out[:, cols] = rows
        normed[:, cols] = (rows * inverse_rms(rows) * gain_ref[0:1, :]).astype(NARROW)
    u_out = (dot_nt(normed[...], ranks[:, 3 * inner : 4 * inner]) * picks_ref[...]).astype(NARROW)
    u_out_ref[...] = u_out
    one = MpSum(box, part, landed)
    for k in (2, 1, 3, 0):
        groups = pl.ds(one.owner(k) * (share // 64), share // 64)
        w_out = late_all[groups, :, :inner].reshape(share, inner)
        b_mix = late_all[groups, :, inner + 256 : inner + 384].reshape(share, 128)
        part[k] = (dot_nt(normed[...], w_out) + dot_nt(u_out, b_mix)).astype(NARROW)
        if k:
            one.send(k, 0)
    one.send_half(1)
    tick()
    shared = one.share(branch)
    tick()
    for copy in g_sent + shared:
        copy.wait_recv()
    for copy in to_hbm + [keep_late_out, keep_last]:
        copy.wait()
    box.drain()


def front(x, g, seg_row, adapters, norm, gain, bias, taps, *weights):
    w_qkv, block_one, a_in, _, late, gate_up, down, block_two = weights
    count, model = x.shape
    inner = taps.shape[2]
    heads = inner // DH
    share = model // 4
    vmem = pl.BlockSpec(memory_space=pltpu.VMEM)
    anywhere = pl.BlockSpec(memory_space=pl.ANY)
    smem = pl.BlockSpec(memory_space=pltpu.SMEM)
    two = (2, DH, DH)
    square = (heads, DH, DH)
    by_head = ((count, inner), WIDE)
    wide, last = (64, 3 * inner + 256), (64, gate_up.shape[1] + down.shape[1] + block_two.shape[1])
    thin_all, late_all = (32, 64, 512), (32, 64, late.shape[1] + 512)
    early = [
        ((HALO + count, 3 * inner), NARROW),
        ((count, model), NARROW),
        ((5, count, inner), WIDE),
        ((heads, count, count), WIDE),
    ]
    results = [
        ((32,) + wide, NARROW),
        (thin_all, NARROW),
        (late_all, NARROW),
        ((32,) + last, NARROW),
        *early,
        ((count, 128), WIDE),
        ((count, 128), WIDE),
        ((count, 512), NARROW),
        by_head,
        ((128, 4 * inner + 128), NARROW),
        (square, NARROW),
        (two, NARROW),
        ((4,) + two, NARROW),
        ((4,) + two, NARROW),
        (square, WIDE),
        by_head,
        ((count, inner), NARROW),
        ((count, 128), NARROW),
        ((count, model), NARROW),
        ((count, model), NARROW),
    ]
    scratch = [(wide, NARROW), ((16, 512), NARROW), ((16, 512), NARROW), (last, NARROW)] + early + [
        ((32,) + wide, NARROW),
        (thin_all, NARROW),
        (late_all, NARROW),
        (thin_all[1:], NARROW),
        (late_all[1:], NARROW),
        ((HALO, model), NARROW),
        ((HALO + count, 128), WIDE),
        ((HALO + count, model), NARROW),
        ((HALO + count, 3 * inner), WIDE),
        ((2, model, 128), WIDE),
        ((4 * inner // 128, 128, 128), WIDE),
        ((128, 128), WIDE),
        (square, NARROW),
        by_head,
        (two, NARROW),
        ((4,) + two, NARROW),
        ((4,) + two, NARROW),
        (two, WIDE),
        ((4, count, share), NARROW),
        ((3, count, share), NARROW),
        ((16, inner), WIDE),
    ]
    copies = 4 * GATHER_COPIES + 2 + 3 + 3 + 3 + 2 + 6 + 6 + 1 + 12
    return pl.pallas_call(
        front_kernel,
        out_shape=tuple(jax.ShapeDtypeStruct(*r) for r in results),
        in_specs=[vmem] * 3 + [smem] + [vmem] * 2 + [smem, vmem] + [anywhere] * 8,
        out_specs=tuple([anywhere] * 8 + [vmem] * (len(results) - 8)),
        scratch_shapes=[pltpu.VMEM(*s) for s in scratch]
        + [
            pltpu.SemaphoreType.DMA((copies,)),
            pltpu.SemaphoreType.DMA((copies,)),
            pltpu.SemaphoreType.DMA((14,)),
            pltpu.SemaphoreType.DMA((15,)),
        ],
        compiler_params=pltpu.CompilerParams(
            collective_id=0, has_side_effects=True, vmem_limit_bytes=60 << 20
        ),
        name="front",
    )(x, g, seg_row, adapters, norm, gain, bias, taps, *weights)


def middle_kernel(
    a_ref, sib_a, chip_a, row_a, reach, mixer_out, normed, u_out_ref, branch, picks_ref, x_ref, g_full, norm_ref, gain_ref,
    ranks_one, late_ref, wide_ref,
    output, grad_out, d_one_out, d_mixer_out, g_b_ffn, g_a_down, g_a_out, g_shared,
    late, w_gu, w_down, packed, block, spread, ranks, sib_g, chip_g, row_g, pass_on, g_maps, chip_t, row_t, pair_t,
    part, landed, hidden_one, xn_two, gate, up, hidden, ffn_part, ffn_landed,
    d_gate_up, d_xn, extra, extra_landed, d_branch, e_down_ref, u_two_ref,
    send, recv, local,
):
    count = x_ref.shape[0]
    heads = a_ref.shape[0]
    inner = heads * DH
    ff = gate.shape[1]
    model = x_ref.shape[1]
    share = output.shape[1]
    m = lax.axis_index("mp")
    loads = [
        pltpu.make_async_copy(late_ref, late, local.at[0]),
        pltpu.make_async_copy(wide_ref.at[:, pl.ds(3 * ff, packed.shape[1])], packed, local.at[1]),
        pltpu.make_async_copy(wide_ref.at[:, pl.ds(0, ff)], w_gu.at[:, pl.ds(0, ff)], local.at[2]),
        pltpu.make_async_copy(wide_ref.at[:, pl.ds(ff, ff)], w_gu.at[:, pl.ds(ff, ff)], local.at[3]),
        pltpu.make_async_copy(wide_ref.at[:, pl.ds(2 * ff, ff)], w_down, local.at[4]),
    ]
    for load in loads:
        load.start()
    box = Mailbox(send, recv)
    chain = Chain(box, a_ref, sib_a, chip_a, row_a)
    mp_peers = {k: lax.rem(m + k, 4) for k in (1, 2, 3)}
    greet(chain.peers(), list(mp_peers.values()))
    picks = picks_ref[...]
    u_out = u_out_ref[...]
    a_out = ranks_one.at[:, pl.ds(3 * inner, inner)]
    a_down = ranks.at[:, pl.ds(2 * ff, ff)]
    w_out, a_two = late.at[:, pl.ds(0, inner)], late.at[:, pl.ds(inner, 256)]
    b_mix, b_down = late.at[:, pl.ds(inner + 256, 128)], late.at[:, pl.ds(inner + 384, 128)]

    rows = x_ref[...].astype(WIDE) + branch[...].astype(WIDE)
    hidden_one[...] = rows
    scale_two = inverse_rms(rows)
    xn_two[...] = (rows * scale_two * norm_ref[0:1, :]).astype(NARROW)
    two_picks = jnp.concatenate([picks, picks], axis=1)
    loads[0].wait()
    u_two_ref[...] = (dot(xn_two[...], a_two[...]) * two_picks).astype(NARROW)
    for load in loads[1:4]:
        load.wait()
    for i in range(3):
        block[i] = packed[:, i * 128 : (i + 1) * 128].astype(WIDE)
    unpack_ranks(block, spread, ranks, 0, 3 * ff // 128)
    gate[...] = dot(xn_two[...], w_gu[:, :ff]) + dot(u_two_ref[:, :128], ranks[:, :ff])
    up[...] = dot(xn_two[...], w_gu[:, ff:]) + dot(u_two_ref[:, 128:], ranks[:, ff : 2 * ff])
    hidden[...] = (gate[...] * jax.nn.sigmoid(gate[...]) * up[...]).astype(NARROW)
    loads[4].wait()

    e_down = (dot(g_full[...], b_down[...]) * picks).astype(NARROW)
    e_down_ref[...] = e_down
    d_hidden = dot(g_full[...], w_down[...]) + dot(e_down, a_down[...])
    sig = jax.nn.sigmoid(gate[...])
    d_gate_up[:, :ff] = (d_hidden * up[...] * sig * (1.0 + gate[...] * (1.0 - sig))).astype(NARROW)
    d_gate_up[:, ff:] = (d_hidden * gate[...] * sig).astype(NARROW)
    e_two = [
        (dot_nt(d_gate_up[:, j * ff : (j + 1) * ff], ranks[:, j * ff : (j + 1) * ff]) * picks).astype(NARROW)
        for j in range(2)
    ]
    two = MpSum(box, part, landed)
    for k in (2, 1, 3, 0):
        rows = columns(two.owner(k), share)
        part[k] = (
            dot_nt(d_gate_up[...], w_gu[rows, :]) + dot_nt(jnp.concatenate(e_two, axis=1), a_two[rows, :])
        ).astype(NARROW)
        if k:
            two.send(k, 0)
    two.send_half(1)
    chain.turn(chip_t, row_t, pair_t)
    u_down = (dot_nt(hidden[...], a_down[...]) * picks).astype(NARROW)
    for j, value in enumerate((e_two[0], e_two[1], u_out, u_down)):
        extra[j] = value
    shared = two.share(d_xn)
    extra_sent = [box.push(extra.at[mp_peers[k]], extra_landed.at[k - 1], mp=mp_peers[k]) for k in MpSum.ORDER]
    three = MpSum(box, ffn_part, ffn_landed)
    for k in (2, 1, 3, 0):
        rows = columns(three.owner(k), share)
        ffn_part[k] = (dot_nt(hidden[...], w_down[rows, :]) + dot_nt(u_down, b_down[rows, :])).astype(NARROW)
    for copy in shared:
        copy.wait_recv()
    three.send_half(0)
    three.send_half(1)

    rows = hidden_one[...]
    scale_two = inverse_rms(rows)
    d_one = g_full[...].astype(WIDE) + norm_back(rows, scale_two, norm_ref[0:1, :], d_xn[...].astype(WIDE))
    d_one_out[...] = d_one
    d_branch[...] = d_one.astype(NARROW)
    e_out = (dot(d_branch[...], b_mix[...]) * picks).astype(NARROW)
    d_normed = dot(d_branch[...], w_out[...]) + dot(e_out, a_out[...])
    for h in range(heads):
        cols = slice(h * DH, (h + 1) * DH)
        rows = mixer_out[:, cols]
        d_rows = norm_back(rows, inverse_rms(rows), gain_ref[0:1, :], d_normed[:, cols])
        d_mixer_out[:, cols] = d_rows
        g_maps[h] = wide_dot(reach[:, cols], d_rows, 0, 0).astype(NARROW)
    chain.start_backward(g_maps, sib_g, chip_g, row_g, pass_on)
    g_a_out[...] = dot_tn(e_out, normed[...]).astype(NARROW)
    chain.chips_backward()
    for j in range(2):
        cols = slice(j * ff, (j + 1) * ff)
        g_b_ffn[:, cols] = dot_tn(u_two_ref[:, j * 128 : (j + 1) * 128], d_gate_up[:, cols]).astype(NARROW)
    chain.rows_backward()
    g_a_down[...] = dot_tn(e_down_ref[...], hidden[...]).astype(NARROW)
    for copy in extra_sent:
        copy.wait_recv()
    factor = extra[m].astype(WIDE)
    for k in range(3):
        factor = factor + extra_landed[k].astype(WIDE)
    left = jnp.where(m < 2, xn_two[...], jnp.where(m == 2, d_branch[...], g_full[...]))
    g_shared[...] = dot_tn(left, factor.astype(NARROW)).astype(NARROW)
    chain.finish_backward(grad_out)
    for half in range(2):
        rows = three.rows(half)
        output[rows] = (hidden_one[rows, columns(m, share)] + three.total(half)).astype(NARROW)
    box.drain()


def middle(kept_maps, forward, x, g, norm, gain, ranks, late, wide):
    operands = (*kept_maps, *forward, x, g, norm, gain, ranks)
    count, inner = forward[0].shape
    heads = inner // DH
    model = x.shape[1]
    share = model // 4
    ff = (wide.shape[1] - 384) // 3
    vmem = pl.BlockSpec(memory_space=pltpu.VMEM)
    anywhere = pl.BlockSpec(memory_space=pl.ANY)
    two = (2, DH, DH)
    copies = 1 + 3 + 3 + 1 + 12 + 3 + 6
    results = [
        ((count, share), NARROW),
        ((heads, DH, DH), WIDE),
        ((count, model), WIDE),
        ((count, inner), WIDE),
        ((128, 2 * ff), NARROW),
        ((128, ff), NARROW),
        ((128, inner), NARROW),
        ((model, 128), NARROW),
    ]
    scratch = [
        (late.shape, NARROW),
        ((model, 2 * ff), NARROW),
        ((model, ff), NARROW),
        ((model, 384), NARROW),
        ((3, model, 128), WIDE),
        ((3 * ff // 128, 128, 128), WIDE),
        ((128, 3 * ff), NARROW),
        (two, NARROW),
        ((4,) + two, NARROW),
        ((4,) + two, NARROW),
        (two, WIDE),
        ((heads, DH, DH), NARROW),
        ((4,) + two, NARROW),
        ((4,) + two, NARROW),
        ((2,) + two, NARROW),
        ((4, count, share), NARROW),
        ((3, count, share), NARROW),
        ((count, model), WIDE),
        ((count, model), NARROW),
        ((count, ff), WIDE),
        ((count, ff), WIDE),
        ((count, ff), NARROW),
        ((4, count, share), NARROW),
        ((3, count, share), NARROW),
        ((count, 2 * ff), NARROW),
        ((count, model), NARROW),
        ((4, count, 128), NARROW),
        ((3, count, 128), NARROW),
        ((count, model), NARROW),
        ((count, 128), NARROW),
        ((count, 256), NARROW),
    ]
    return pl.pallas_call(
        middle_kernel,
        out_shape=tuple(jax.ShapeDtypeStruct(*r) for r in results),
        in_specs=[vmem] * len(operands) + [anywhere] * 2,
        out_specs=tuple([vmem] * len(results)),
        scratch_shapes=[pltpu.VMEM(*v) for v in scratch]
        + [
            pltpu.SemaphoreType.DMA((copies,)),
            pltpu.SemaphoreType.DMA((copies,)),
            pltpu.SemaphoreType.DMA((5,)),
        ],
        compiler_params=pltpu.CompilerParams(
            collective_id=2, has_side_effects=True, vmem_limit_bytes=60 << 20
        ),
        name="middle",
    )(*operands, late, wide)


class DpSum:
    SCRATCH = 6

    @staticmethod
    def scratch(rows, width):
        small = rows // 4
        return [
            ((2, 4, rows, width), NARROW),
            ((4, rows, width), NARROW),
            ((3, rows, width), NARROW),
            ((4, small, width), WIDE),
            ((3, small, width), WIDE),
            ((small, width), WIDE),
        ]

    def __init__(self, box, full, landed_core, landed_y, by_z, landed_z, result):
        self.box, self.full, self.landed_core = box, full, landed_core
        self.landed_y, self.by_z, self.landed_z, self.result = landed_y, by_z, landed_z, result
        self.y, self.z, self.c = coords()

    def over_cores(self):
        self.pair = self.box.push(self.full.at[1 - self.c], self.landed_core, dp=moved(0, 0, True))

    def over_y(self):
        self.pair.wait_recv()
        mine = self.full.at[self.c]
        for i in range(4):
            mine[i] = (mine[i].astype(WIDE) + self.landed_core[i].astype(WIDE)).astype(NARROW)
        self.copies = [
            self.box.push(mine.at[lax.rem(self.y + k, 4)], self.landed_y.at[k - 1], dp=moved(k, 0)) for k in (2, 1, 3)
        ]

    def over_z(self):
        for copy in self.copies:
            copy.wait_recv()
        total = self.full[self.c, self.y].astype(WIDE)
        for k in range(3):
            total = total + self.landed_y[k].astype(WIDE)
        self.by_z[...] = total.reshape(self.by_z.shape)
        self.copies = [
            self.box.push(self.by_z.at[lax.rem(self.z + k, 4)], self.landed_z.at[k - 1], dp=moved(0, k))
            for k in (2, 1, 3)
        ]

    def finish(self):
        for copy in self.copies:
            copy.wait_recv()
        total = self.by_z[self.z]
        for k in range(3):
            total = total + self.landed_z[k]
        self.result[...] = total


def tail_kernel(
    taps_ref, aux_ref, seg_ref, state_ref, grad_ref, d_out_ref,
    u_ref, norm_ref, picks_ref, ranks, shared_two, g_b_ffn, g_a_out, g_a_down,
    pre_in, kept_in, t_in, x_in, xn_in, d_one_in, wide_ref, thin_ref,
    grad_input, out_a_in, out_heads, out_beta, out_a_out, out_ffn, out_a_down, out_res,
    pre_ref, kept_all, t_ref, x_ref, xn_ref, d_one_ref, w_in, a_one, d_ext, pre_wide, taps, halo, d_pre, e_one, part, landed, extra_landed, sums, sums_landed, pair, early_pair, ends,
    *rest,
):
    one, two, three, four = (rest[i * DpSum.SCRATCH : (i + 1) * DpSum.SCRATCH] for i in range(4))
    send, recv, local = rest[4 * DpSum.SCRATCH :]
    count, model = x_in.shape
    inner = d_out_ref.shape[1]
    heads = inner // DH
    ff = g_a_down.shape[1]
    m = lax.axis_index("mp")
    c = lax.rem(lax.axis_index("dp"), 2)
    before, after = (lax.rem(lax.axis_index("dp") + k, 32) for k in (31, 1))
    mp_peers = {k: lax.rem(m + k, 4) for k in (1, 2, 3)}
    dp_peers = [before, after, moved(0, 0, True)]
    dp_peers += [moved(k, 0) for k in (1, 2, 3)] + [moved(0, k) for k in (1, 2, 3)]
    loads = [
        pltpu.make_async_copy(source, target, local.at[i])
        for i, (source, target) in enumerate(
            (
                (pre_in, pre_ref),
                (kept_in, kept_all),
                (t_in, t_ref),
                (wide_ref.at[:, pl.ds(0, w_in.shape[1])], w_in),
                (thin_ref.at[:, pl.ds(0, a_one.shape[1])], a_one),
                (x_in, x_ref),
                (xn_in, xn_ref),
                (d_one_in, d_one_ref),
            )
        )
    ]
    for load in loads:
        load.start()
    greet(dp_peers, list(mp_peers.values()))
    box = Mailbox(send, recv)
    early_sum, heads_sum, two_sum, one_sum = (DpSum(box, *refs) for refs in (four, one, two, three))

    def halves(refs, values):
        half = refs[0].shape[3]
        missing = 2 * half - sum(value.shape[1] for value in values)
        values = values + [jnp.zeros((128, missing), NARROW)] if missing else values
        values = jnp.concatenate(values, axis=1)
        for i in range(2):
            refs[0][i] = values[:, i * half : (i + 1) * half].reshape(4, 32, half)

    def by_core(value):
        value = value.reshape(4, 4, 2, model // 32, 128)
        return [value[:, :, i].reshape(4, model // 8, 128) for i in range(2)]

    halves(four, [g_b_ffn[...], g_a_out[...], g_a_down[...]])
    early_sum.over_cores()
    for i, value in enumerate(by_core(shared_two[...])):
        two[0][i] = value
    two_sum.over_cores()
    aux = aux_ref[...]
    spread_taps(taps_ref, taps)
    for load in loads[:3]:
        load.wait()
    pre_wide[...] = pre_ref[...].astype(WIDE)
    kept = (*(kept_all.at[i] for i in range(3)), t_ref, *(kept_all.at[i] for i in (3, 4)))
    lanes = lax.broadcasted_iota(jnp.int32, aux.shape, 1)
    d_logit = jnp.zeros(aux.shape, WIDE)
    def between():
        early_sum.over_y()
        two_sum.over_y()

    found = mixer_backward(
        list(range(heads)), pre_wide, taps, aux, seg_ref[...].astype(WIDE), kept, state_ref, grad_ref, d_out_ref, d_ext,
        between,
    )
    for h, value in enumerate(found):
        d_logit = jnp.where(lanes == 8 + h, value, d_logit)
    edges = [box.push(d_ext.at[i, pl.ds(HALO - 8, 8)], halo.at[i], dp=before) for i in range(3)]
    early_sum.over_z()
    two_sum.over_z()
    picks = picks_ref[...]
    d_logit = d_logit.astype(NARROW)
    for copy in edges:
        copy.wait_recv()
    for i in range(3):
        ref = d_ext.at[i]
        cols = slice(i * inner, (i + 1) * inner)
        d_pre[: count - 16, cols] = ref[HALO : HALO + count - 16].astype(NARROW)
        ending = ref[HALO + count - 16 :]
        d_pre[count - 16 :, cols] = jnp.concatenate([ending[:8], ending[8:] + halo[i]], axis=0).astype(NARROW)
    for j in range(3):
        cols = slice(j * inner, (j + 1) * inner)
        e_one[j] = (dot_nt(d_pre[:, cols], ranks[:, cols]) * picks).astype(NARROW)
    e_one[3] = (dot_nt(d_logit, ranks[:, 4 * inner :]) * picks).astype(NARROW)
    extra_sent = [box.push(e_one.at[mp_peers[k]], extra_landed.at[k - 1], mp=mp_peers[k]) for k in MpSum.ORDER]
    grads = [dot_tn(u_ref[:, j * 128 : (j + 1) * 128], d_pre[:, j * inner : (j + 1) * inner]) for j in range(3)]
    grads.append(dot_tn(u_ref[:, 384:], d_logit))
    halves(one, [value.astype(NARROW) for value in grads])
    heads_sum.over_cores()
    for load in loads[3:]:
        load.wait()
    share = grad_input.shape[1]
    total = MpSum(box, part, landed)
    row_sum = jnp.zeros((count, 128), WIDE)
    all_e = jnp.concatenate([e_one[j] for j in range(4)], axis=1)
    for k in (2, 1, 3, 0):
        owner = total.owner(k)
        rows = columns(owner, share)
        value = (
            dot_nt(d_pre[...], w_in[rows, : 3 * inner])
            + dot_nt(d_logit, w_in[rows, 3 * inner :])
            + dot_nt(all_e, a_one[rows, :])
        )
        part[k] = value.astype(NARROW)
        if k:
            total.send(k, 0)
            total.send(k, 1)
        weighted = value * norm_ref[0:1, rows] * x_ref[:, rows].astype(WIDE)
        row_sum = row_sum + jnp.sum(weighted, axis=1, keepdims=True)
    sums[...] = row_sum.T[:8]
    sums_sent = [box.push(sums, sums_landed.at[k - 1], mp=mp_peers[k]) for k in MpSum.ORDER]
    heads_sum.over_y()
    early_sum.finish()
    early_pair[c] = four[5][...]
    early_paired = box.push(four[5], early_pair.at[c], dp=moved(0, 0, True))
    for copy in extra_sent:
        copy.wait_recv()
    factor = e_one[m].astype(WIDE)
    for k in range(3):
        factor = factor + extra_landed[k].astype(WIDE)
    for i, value in enumerate(by_core(dot_tn(xn_ref[...], factor.astype(NARROW)).astype(NARROW))):
        three[0][i] = value
    one_sum.over_cores()
    heads_sum.over_z()
    one_sum.over_y()
    rank_rows = model // 128

    def to_owners(slot, result):
        ends[slot, m] = result[columns(m, rank_rows)]
        return [
            box.push(result.at[columns(mp_peers[k], rank_rows)], ends.at[slot, m], mp=mp_peers[k])
            for k in MpSum.ORDER
        ]

    two_sum.finish()
    owners = to_owners(1, two[5])
    heads_sum.finish()
    pair[c] = one[5][...]
    paired = box.push(one[5], pair.at[c], dp=moved(0, 0, True))
    one_sum.over_z()
    x_all = x_ref[...].astype(WIDE)
    scale = inverse_rms(x_all)
    mine = columns(m, share)
    one_sum.finish()
    owners += to_owners(0, three[5])
    for copy in sums_sent:
        copy.wait_recv()
    rows = sums[...] + sums_landed[0] + sums_landed[1] + sums_landed[2]
    mean = jnp.concatenate([rows] * 16, axis=0).T[:, :1] / model
    scale_three = scale * scale * scale * mean
    for half in range(2):
        at = total.rows(half)
        here = slice(half * (count // 2), (half + 1) * (count // 2))
        grad_input[at] = d_one_ref[at, mine] + (
            scale[here] * norm_ref[0:1, mine] * total.total(half) - x_ref[at, mine].astype(WIDE) * scale_three[here]
        )
    paired.wait_recv()
    early_paired.wait_recv()

    def own_ranks(pair):
        both = jnp.concatenate([pair[0], pair[1]], axis=1)
        return jnp.where(c == 0, both[:4], both[4:])

    rows = own_ranks(pair)
    for j in range(3):
        out_heads[j] = rows[:, j * inner : (j + 1) * inner]
    out_beta[...] = rows[:, 3 * inner + 8 : 3 * inner + 8 + heads]
    rows = own_ranks(early_pair)
    for j in range(2):
        out_ffn[j] = rows[:, j * ff : (j + 1) * ff]
    out_a_out[...] = rows[:, 2 * ff : 2 * ff + inner]
    out_a_down[...] = rows[:, 2 * ff + inner : 3 * ff + inner]
    for copy in owners:
        copy.wait_recv()
    for j in range(4):
        out_a_in[j] = ends[0, j]
    for j in range(2):
        out_a_in[4 + j] = ends[1, j]
        out_res[j] = ends[1, 2 + j]
    box.drain()


def tail(mixer, tokens, grads, kept, wide, thin):
    model = kept[3].shape[1]
    count, inner = mixer[-1].shape
    heads = inner // DH
    share = model // 4
    ff = grads[3].shape[1]

    def half_of(width):
        return -(-width // 256) * 128

    half, early_half = half_of(3 * inner + 128), half_of(3 * ff + inner)
    vmem = pl.BlockSpec(memory_space=pltpu.VMEM)
    anywhere = pl.BlockSpec(memory_space=pl.ANY)
    copies = 3 + 3 + 6 + 3 + 4 * 7 + 2 + 6
    results = [
        (count, share), (6, model // 128, 128), (3, 4, inner), (4, heads),
        (4, inner), (2, 4, ff), (4, ff), (2, model // 128, 128),
    ]
    scratch = [(x.shape, x.dtype) for x in kept] + [
        ((model, 3 * inner + 128), NARROW),
        ((model, 512), NARROW),
        ((3, HALO + count, inner), WIDE),
        ((HALO + count, 3 * inner), WIDE),
        ((16, inner), WIDE),
        ((3, 8, inner), WIDE),
        ((count, 3 * inner), NARROW),
        ((4, count, 128), NARROW),
        ((4, count, share), NARROW),
        ((3, count, share), NARROW),
        ((3, count, 128), NARROW),
        ((8, count), WIDE),
        ((3, 8, count), WIDE),
        ((2, 8, half), WIDE),
        ((2, 8, early_half), WIDE),
        ((2, 4, model // 128, 128), WIDE),
    ]
    scratch += DpSum.scratch(32, half) + DpSum.scratch(model // 8, 128) + DpSum.scratch(model // 8, 128)
    scratch += DpSum.scratch(32, early_half)
    operands = (*mixer, *tokens, *grads)
    return pl.pallas_call(
        tail_kernel,
        out_shape=tuple(jax.ShapeDtypeStruct(r, WIDE) for r in results),
        in_specs=[vmem] * len(operands) + [anywhere] * (len(kept) + 2),
        out_specs=tuple([vmem] * len(results)),
        scratch_shapes=[pltpu.VMEM(*s) for s in scratch]
        + [
            pltpu.SemaphoreType.DMA((copies,)),
            pltpu.SemaphoreType.DMA((copies,)),
            pltpu.SemaphoreType.DMA((8,)),
        ],
        compiler_params=pltpu.CompilerParams(
            collective_id=3, has_side_effects=True, vmem_limit_bytes=60 << 20
        ),
        name="tail",
    )(*operands, *kept, wide, thin)


def hand_over_kernel(*refs):
    half = len(refs) // 2
    for source, target in zip(refs[:half], refs[half:]):
        target[...] = source[...]


def hand_over(*arrays):
    vmem = pl.BlockSpec(memory_space=pltpu.VMEM)
    return pl.pallas_call(
        hand_over_kernel,
        out_shape=tuple(jax.ShapeDtypeStruct(x.shape, x.dtype) for x in arrays),
        in_specs=[vmem] * len(arrays),
        out_specs=tuple([vmem] * len(arrays)),
        name="hand_over",
    )(*arrays)


def on_device(
    layer_in, cotangent, segments, adapters, norm_one, norm_two, out_gain, beta_bias, conv_taps,
    w_qkv, w_beta, w_out, w_gate_up, w_down, a_in, b_heads, b_beta, a_out, b_ffn, a_down, b_res,
):
    heads = w_beta.shape[1]
    inner = heads * DH
    ff = w_down.shape[0]

    def pack_ranks(parts, blocks):
        flat = jnp.concatenate(parts, axis=1).reshape(-1, 128)
        flat = jnp.pad(flat, ((0, 64 * blocks - flat.shape[0]), (0, 0)))
        return flat.reshape(blocks, 64, 128).transpose(1, 0, 2).reshape(64, blocks * 128)

    beta = jnp.concatenate([w_beta, jnp.zeros((64, 64 - heads), NARROW), jnp.pad(b_beta, ((0, 60), (0, 0)))], axis=1)
    block_one = jnp.concatenate(
        [
            jnp.pad(beta, ((0, 0), (8, 56 - heads))),
            pack_ranks([b_heads.transpose(1, 0, 2).reshape(4, 3 * inner), a_out.T], 1),
        ],
        axis=1,
    )
    block_two = pack_ranks([b_ffn.transpose(1, 0, 2).reshape(4, 2 * ff), a_down.T], 3)
    conv_taps = conv_taps.transpose(1, 0, 2)
    seg_row = segments[None, :]
    (
        wide, thin, late, last, pre, xn_one, kept, t_map, aux, picks, u_one, reach, ranks,
        maps, sib_a, chip_a, row_a, state_in, mixer_out, normed, u_out, branch, g_full,
    ) = front(
        layer_in, cotangent, seg_row, adapters, norm_one[None, :], out_gain[None, :],
        beta_bias, conv_taps, w_qkv.transpose(1, 0, 2), block_one, a_in.transpose(1, 0, 2), b_res.transpose(0, 2, 1),
        w_out.T, w_gate_up.reshape(64, 2 * ff), w_down.T, block_two,
    )
    wide, thin, late, last = (x.reshape(2048, -1) for x in (wide, thin, late, last))
    output, state_grad, d_hidden_one, d_mixer, grad_b_ffn, grad_a_down, grad_a_out, shared_two = middle(
        (maps, sib_a, chip_a, row_a), (reach, mixer_out, normed, u_out, branch, picks),
        layer_in, g_full, norm_two[None, :], out_gain[None, :], ranks, late, last,
    )
    grad_input, d_a_in, d_b_heads, d_b_beta, d_a_out, d_b_ffn, d_a_down, d_b_res = tail(
        (conv_taps, aux, seg_row, state_in, state_grad, d_mixer),
        (u_one, norm_one[None, :], picks, ranks),
        (shared_two, grad_b_ffn, grad_a_out, grad_a_down),
        (pre, kept, t_map, layer_in, xn_one, d_hidden_one),
        wide,
        thin,
    )
    output, grad_input, d_a_in, d_b_heads, d_b_beta, d_a_out, d_b_ffn, d_a_down, d_b_res = hand_over(
        output, grad_input, d_a_in, d_b_heads, d_b_beta, d_a_out, d_b_ffn, d_a_down, d_b_res
    )
    return (
        output, grad_input, d_a_in.transpose(1, 0, 2), d_b_heads, d_b_beta, d_a_out.T, d_b_ffn, d_a_down.T,
        d_b_res.transpose(0, 2, 1),
    )


def solution(mesh):
    placed = (
        P("dp", None),
        P("dp", "mp"),
        P("dp"),
        P(),
        P(),
        P(),
        P(),
        P("mp"),
        P(None, None, "mp"),
        P("dp", None, "mp"),
        P("dp", "mp"),
        P("mp", "dp"),
        P("dp", None, "mp"),
        P("mp", "dp"),
        P(("dp", "mp"), None, None),
        P(None, "dp", "mp"),
        P("dp", "mp"),
        P("mp", "dp"),
        P(None, "dp", "mp"),
        P("mp", "dp"),
        P(None, None, ("dp", "mp")),
    )
    return jax.shard_map(
        on_device,
        mesh=mesh,
        in_specs=placed,
        out_specs=(
            P("dp", "mp"),
            P("dp", "mp"),
            P(("dp", "mp"), None, None),
            P(None, "dp", "mp"),
            P("dp", "mp"),
            P("mp", "dp"),
            P(None, "dp", "mp"),
            P("mp", "dp"),
            P(None, None, ("dp", "mp")),
        ),
        check_vma=False,
    )
```

```python
import functools

import jax
import jax.numpy as jnp
from jax import lax
from jax.experimental import pallas as pl
from jax.experimental.pallas import tpu as pltpu
from jax.sharding import PartitionSpec as P

DH = 128
KW = 4
RANK = 16
HALO = 16
EPSILON = 1e-06
WIDE = jnp.float32
NARROW = jnp.bfloat16
MESH = pl.DeviceIdType.MESH
EXACT = lax.Precision.HIGHEST


def coords():
    place = lax.axis_index("dp")
    return place // 8, lax.rem(place // 2, 4), lax.rem(place, 2)


def place_of(y, z, c):
    return (y * 4 + z) * 2 + c


def moved(dy, dz, other_core=False):
    y, z, c = coords()
    return place_of(lax.rem(y + dy + 4, 4), lax.rem(z + dz + 4, 4), 1 - c if other_core else c)


def greet(dp_peers=(), mp_peers=()):
    barrier = pltpu.get_barrier_semaphore()
    for peer in dp_peers:
        pl.semaphore_signal(barrier, inc=1, device_id={"dp": peer}, device_id_type=MESH)
    for peer in mp_peers:
        pl.semaphore_signal(barrier, inc=1, device_id={"mp": peer}, device_id_type=MESH)
    pl.semaphore_wait(barrier, len(dp_peers) + len(mp_peers))


class Mailbox:
    def __init__(self, send, recv):
        self.send, self.recv, self.copies = send, recv, []

    def push(self, src, dst, **device):
        k = len(self.copies)
        copy = pltpu.make_async_remote_copy(
            src_ref=src,
            dst_ref=dst,
            send_sem=self.send.at[k],
            recv_sem=self.recv.at[k],
            device_id=device,
            device_id_type=MESH,
        )
        copy.start()
        self.copies.append(copy)
        return copy

    def drain(self):
        for copy in self.copies:
            copy.wait_send()


def gather_steps(box, own, out):
    me = moved(0, 0)
    half = own.shape[0] // 2
    quarter = half // 2
    sibling = moved(0, 0, True)
    kinds = []
    for kind in range(2):
        base = kind * half
        parts = (pl.ds(base, half), pl.ds(base, quarter), pl.ds(base + quarter, quarter))
        if kind == 0:
            kinds.append((parts, lambda a, b: moved(a, b)))
        else:
            kinds.append((parts, lambda a, b: moved(b, a)))
    near, across, far, far_across, shared = [], [{}, {}], [[], []], [{}, {}], []

    def open_up():
        for parts, at in kinds:
            near.append([box.push(own.at[parts[0]], out.at[me, parts[0]], dp=at(s, 0)) for s in (1, -1)])
        for k, (parts, at) in enumerate(kinds):
            across[k][0] = [box.push(own.at[parts[0]], out.at[me, parts[0]], dp=at(0, s)) for s in (1, -1)]
        shared.append(box.push(own, out.at[me], dp=sibling))

    def pass_on(k, slot):
        parts, at = kinds[k]
        block = out.at[slot, parts[0]]
        return [box.push(block, block, dp=at(0, t)) for t in (1, -1)]

    def to_sibling(k, slot):
        block = out.at[slot, kinds[k][0][0]]
        shared.append(box.push(block, block, dp=sibling))

    def from_near(i, s):
        def step():
            for k, (parts, at) in enumerate(kinds):
                near[k][i].wait_recv()
                block = out.at[at(s, 0), parts[1 + i]]
                far[k].append(box.push(block, block, dp=at(-s, 0)))
            for k, (parts, at) in enumerate(kinds):
                across[k][s] = pass_on(k, at(s, 0))
                to_sibling(k, at(s, 0))

        return step

    def from_far(k):
        def step():
            for copy in far[k]:
                copy.wait_recv()
            slot = kinds[k][1](2, 0)
            across[k][2] = pass_on(k, slot)
            to_sibling(k, slot)

        return step

    def from_across(k, f):
        def step():
            parts, at = kinds[k]
            far_across[k][f] = []
            for i, s in enumerate((-1, 1)):
                across[k][f][i].wait_recv()
                slot = at(f, s)
                block = out.at[slot, parts[1 + i]]
                far_across[k][f].append(box.push(block, block, dp=at(0, -s)))
                to_sibling(k, slot)

        return step

    def from_far_across(k, f):
        def step():
            for copy in far_across[k][f]:
                copy.wait_recv()
            to_sibling(k, kinds[k][1](f, 2))

        return step

    def close():
        for copy in shared:
            copy.wait_recv()

    steps = [open_up, from_near(0, -1), from_near(1, 1), from_far(0), from_far(1)]
    steps += [from_across(k, f) for f in (0, -1, 1, 2) for k in range(2)]
    steps += [from_far_across(k, f) for f in (0, -1, 1, 2) for k in range(2)]
    return steps + [close]


def gather_peers():
    return [moved(1, 0), moved(-1, 0), moved(0, 1), moved(0, -1), moved(0, 0, True)]


GATHER_COPIES = 71


def half_dot(left, right):
    high = right.astype(NARROW)
    low = (right - high.astype(WIDE)).astype(NARROW)
    both = lax.dot(left, jnp.concatenate([high, low], axis=1), preferred_element_type=WIDE)
    return both[:, : right.shape[1]] + both[:, right.shape[1] :]


def two_parts(value):
    high = value.astype(NARROW)
    return high, (value - high.astype(WIDE)).astype(NARROW)


def wide_dot(left, right, left_dim=1, right_dim=0):
    left_high, left_low = two_parts(left)
    right_high, right_low = two_parts(right)

    def part(one, two):
        return lax.dot_general(one, two, (((left_dim,), (right_dim,)), ((), ())), preferred_element_type=WIDE)

    return part(left_high, right_high) + (part(left_high, right_low) + part(left_low, right_high))


def convolve(pre_ref, taps_ref, part, head, inner, aux):
    count = aux.shape[0]
    cols = slice(part * inner + head * DH, part * inner + (head + 1) * DH)
    taps = taps_ref[:, head * DH : (head + 1) * DH]
    total = pre_ref[pl.ds(HALO, count), cols] * taps[part : part + 1]
    for j in range(1, KW):
        shifted = pre_ref[pl.ds(HALO - j, count), cols]
        total = total + shifted * aux[:, j : j + 1] * taps[3 * j + part : 3 * j + part + 1]
    return total


def spread_taps(taps_ref, taps):
    for part in range(3):
        rows = taps_ref[part].astype(WIDE)
        for j in range(KW):
            taps[3 * j + part : 3 * j + part + 1, :] = rows[j : j + 1]


def masks(aux, seg_row):
    same = aux[:, 6:7] == seg_row
    shape = (aux.shape[0], aux.shape[0])
    row = lax.broadcasted_iota(jnp.int32, shape, 0)
    col = lax.broadcasted_iota(jnp.int32, shape, 1)
    return row, col, same


def each(step, *lists):
    return [step(*items) for items in zip(*lists)]


def lower_inverses(lowers, row, col, tick):
    near = [jnp.where(row // 8 == col // 8, lower, 0.0) for lower in lowers]
    square = each(lambda a: wide_dot(a, a), near)
    inverse = [jnp.where(row == col, 1.0, 0.0) - a for a in near]
    inverse = each(lambda x, s: x + wide_dot(x, s), inverse, square)
    square = each(lambda s: wide_dot(s, s), square)
    inverse = each(lambda x, s: x + wide_dot(x, s), inverse, square)
    size = 8
    while size < row.shape[0]:
        link = (row // (2 * size) == col // (2 * size)) & (row // size != col // size)
        middle = each(lambda lower, x: wide_dot(jnp.where(link, lower, 0.0), x), lowers, inverse)
        inverse = each(lambda x, y: x - wide_dot(x, y), inverse, middle)
        size *= 2
        tick()
    return inverse


def mixer_forward(heads, pre_ref, taps_ref, aux, seg_row, out_ref, reach_ref, map_ref, offset_ref, kept, tick):
    q_ref, k_ref, v_ref, t_ref, w_ref, u_ref = kept
    count = aux.shape[0]
    inner = out_ref.shape[1]
    linked, ending = aux[:, 4:5], aux[:, 5:6]
    row, col, same = masks(aux, seg_row)
    rate = [aux[:, 8 + h : 9 + h] for h in heads]
    cols = [slice(h * DH, (h + 1) * DH) for h in heads]

    def act(part):
        convs = [convolve(pre_ref, taps_ref, part, h, inner, aux) for h in heads]
        return [conv * jax.nn.sigmoid(conv) for conv in convs]

    def unit(a):
        return a * lax.rsqrt(jnp.sum(a * a, axis=1, keepdims=True) + EPSILON)

    k = each(unit, act(1))
    gram = each(lambda b: wide_dot(b, b, 1, 1), k)
    lowers = each(lambda g, r: jnp.where((row > col) & same, g * r, 0.0), gram, rate)
    q, v = each(unit, act(0)), act(2)
    for i in range(len(heads)):
        q_ref[:, cols[i]] = q[i]
        k_ref[:, cols[i]] = k[i]
        v_ref[:, cols[i]] = v[i]
    scores = each(lambda a, b: jnp.where((row >= col) & same, wide_dot(a, b, 1, 1), 0.0), q, k)
    tick()
    inverse = lower_inverses(lowers, row, col, tick)
    written = each(
        lambda t, a, b, r: wide_dot(t, jnp.concatenate([a, b * linked], axis=1) * r), inverse, v, k, rate
    )
    ends = each(lambda b, w: wide_dot(b * ending, w, 0, 0), k, written)
    mixed = each(wide_dot, scores, written)
    eye = jnp.where(row[:DH, :DH] == col[:DH, :DH], 1.0, 0.0)
    last = aux[count - 1 :, 4:5]
    for i, h in enumerate(heads):
        t_ref[h] = inverse[i]
        w_ref[:, cols[i]] = written[i][:, :DH]
        u_ref[:, cols[i]] = written[i][:, DH:]
        offset_ref[h] = ends[i][:, :DH].astype(offset_ref.dtype)
        map_ref[h] = (eye * last - ends[i][:, DH:]).astype(map_ref.dtype)
        out_ref[:, cols[i]] = mixed[i][:, :DH]
        reach_ref[:, cols[i]] = q[i] * linked - mixed[i][:, DH:]
    tick()


def mixer_backward(heads, pre_ref, taps_ref, aux, seg_row, kept, state_ref, grad_ref, d_out_ref, d_ext, between):
    q_ref, k_ref, v_ref, t_ref, w_ref, u_ref = kept
    count = aux.shape[0]
    inner = d_out_ref.shape[1]
    linked, ending = aux[:, 4:5], aux[:, 5:6]
    row, col, same = masks(aux, seg_row)
    upto = (row >= col) & same
    below = (row > col) & same

    def take(ref):
        return [ref[:, h * DH : (h + 1) * DH] for h in heads]

    rate = [aux[:, 8 + h : 9 + h] for h in heads]
    q, k, v, d_out = take(q_ref), take(k_ref), take(v_ref), take(d_out_ref)
    state, grad = [state_ref[h] for h in heads], [grad_ref[h] for h in heads]
    written = each(lambda w, u, s: w - wide_dot(u, s), take(w_ref), take(u_ref), state)
    scores = each(lambda a, b: jnp.where(upto, wide_dot(a, b, 1, 1), 0.0), q, k)
    d_written = each(
        lambda a, d, b, g: wide_dot(a, d, 0, 0) + wide_dot(b * ending, g), scores, d_out, k, grad
    )
    d_right = each(lambda t, d: wide_dot(t, d, 0, 0), [t_ref[h] for h in heads], d_written)
    d_scores = each(lambda d, w: jnp.where(upto, wide_dot(d, w, 1, 1), 0.0), d_out, written)
    between()
    d_lower = each(lambda d, w: jnp.where(below, -wide_dot(d, w, 1, 1), 0.0), d_right, written)
    d_q = each(
        lambda ds, b, d, s: wide_dot(ds, b) + linked * wide_dot(d, s, 1, 1), d_scores, k, d_out, state
    )
    d_k = each(
        lambda ds, a, w, g: wide_dot(ds, a, 0, 0) + ending * wide_dot(w, g, 1, 1), d_scores, q, written, grad
    )
    d_rate = each(
        lambda d, a, b, s: jnp.sum(d * (a - linked * wide_dot(b, s)), axis=1, keepdims=True), d_right, v, k, state
    )
    d_rate = each(
        lambda r, d, b: r + jnp.sum(d * wide_dot(b, b, 1, 1), axis=1, keepdims=True), d_rate, d_lower, k
    )
    d_k = each(lambda dk, r, d, s: dk - (linked * r) * wide_dot(d, s, 1, 1), d_k, rate, d_right, state)
    d_gram = each(lambda d, r: d * r, d_lower, rate)
    d_k = each(lambda dk, d, b: dk + wide_dot(d, b) + wide_dot(d, b, 0, 0), d_k, d_gram, k)
    d_v = each(lambda r, d: r * d, rate, d_right)
    for i, h in enumerate(heads):
        for part, (unit, d) in enumerate(((q[i], d_q[i]), (k[i], d_k[i]), (None, d_v[i]))):
            cols = slice(h * DH, (h + 1) * DH)
            conv = convolve(pre_ref, taps_ref, part, h, inner, aux)
            gate = jax.nn.sigmoid(conv)
            if unit is not None:
                act = conv * gate
                scale = lax.rsqrt(jnp.sum(act * act, axis=1, keepdims=True) + EPSILON)
                d = (d - unit * jnp.sum(unit * d, axis=1, keepdims=True)) * scale
            d_conv = d * gate * (1.0 + conv * (1.0 - gate))
            d_ext[part, :HALO, cols] = jnp.zeros((HALO, DH), WIDE)
            d_ext[part, HALO:, cols] = d_conv * taps_ref[part : part + 1, cols]
            for j in range(1, KW):
                term = d_conv * taps_ref[3 * j + part : 3 * j + part + 1, cols] * aux[:, j : j + 1]
                d_ext[part, pl.ds(HALO - j, count), cols] += term
    return each(lambda d, r: d * r * (1.0 - r), d_rate, rate)


def inverse_rms(values):
    return lax.rsqrt(jnp.mean(values * values, axis=-1, keepdims=True) + EPSILON)


def norm_back(values, scale, gain, grad_out):
    weighted = grad_out * gain
    return scale * weighted - values * scale**3 * jnp.mean(weighted * values, axis=-1, keepdims=True)


def dot(left, right):
    return jnp.dot(left, right, preferred_element_type=WIDE)


def dot_nt(left, right):
    return lax.dot_general(left, right, (((1,), (1,)), ((), ())), preferred_element_type=WIDE)


def dot_tn(left, right):
    return lax.dot_general(left, right, (((0,), (0,)), ((), ())), preferred_element_type=WIDE)


class Chain:
    def __init__(self, box, a_ref, sib_a, chip_a, row_a):
        self.box, self.a_ref, self.sib_a, self.chip_a, self.row_a = box, a_ref, sib_a, chip_a, row_a
        self.y, self.z, self.c = coords()
        self.first = self.c == 0
        self.sibling = moved(0, 0, True)
        self.z_peers = {k: moved(0, k) for k in (1, 2, 3)}
        self.y_peers = {k: moved(k, 0) for k in (1, 2, 3)}
        self.mine = pl.ds(pl.multiple_of(2 * self.c, 2), 2)
        self.theirs = pl.ds(pl.multiple_of(2 * (1 - self.c), 2), 2)

    def peers(self):
        return [self.sibling] + list(self.z_peers.values()) + list(self.y_peers.values())

    def swap(self, ref, sib):
        return self.box.push(ref.at[self.theirs], sib, dp=self.sibling)

    def ordered(self, ref, sib, h):
        own, other = ref[2 * self.c + h], sib[h]
        return jnp.where(self.first, own, other), jnp.where(self.first, other, own)

    def spread(self, refs, place, peers):
        return [self.box.push(ref.at[place], ref.at[place], dp=peers[k]) for k in (2, 1, 3) for ref in refs]

    def start_forward(self, b_ref, sib_b, chip_b, row_b, pass_on):
        self.b_ref, self.sib_b, self.chip_b, self.row_b, self.pass_on = b_ref, sib_b, chip_b, row_b, pass_on
        self.pair = [self.swap(self.a_ref, self.sib_a), self.swap(b_ref, sib_b)]

    def chips_forward(self):
        for copy in self.pair:
            copy.wait_recv()
        self.lower = []
        for h in range(2):
            a_low, a_high = self.ordered(self.a_ref, self.sib_a, h)
            b_low, b_high = self.ordered(self.b_ref, self.sib_b, h)
            self.lower.append((a_low, b_low))
            self.chip_a[self.z, h] = lax.dot(a_high, a_low, preferred_element_type=WIDE).astype(NARROW)
            self.chip_b[self.z, h] = (
                lax.dot(a_high, b_low, preferred_element_type=WIDE) + b_high.astype(WIDE)
            ).astype(NARROW)
        self.ring = self.spread((self.chip_a, self.chip_b), self.z, self.z_peers)

    def rows_forward(self):
        for copy in self.ring:
            copy.wait_recv()
        for h in range(2):
            total_a, total_b = self.chip_a[0, h].astype(WIDE), self.chip_b[0, h].astype(WIDE)
            for i in range(1, 4):
                total_a = half_dot(self.chip_a[i, h], total_a)
                total_b = half_dot(self.chip_a[i, h], total_b) + self.chip_b[i, h].astype(WIDE)
            self.row_a[self.y, h] = total_a.astype(NARROW)
            self.row_b[self.y, h] = total_b.astype(NARROW)
        self.ring = self.spread((self.row_a, self.row_b), self.y, self.y_peers)
        self.ready_forward()

    def ready_forward(self):
        eye = jnp.where(
            lax.broadcasted_iota(jnp.int32, (DH, DH), 0) == lax.broadcasted_iota(jnp.int32, (DH, DH), 1), 1.0, 0.0
        )
        self.within = []
        for h in range(2):
            a, b = eye, jnp.zeros((DH, DH), WIDE)
            for i in range(3):
                step = self.chip_a[i, h]
                longer_a, longer_b = half_dot(step, a), half_dot(step, b) + self.chip_b[i, h].astype(WIDE)
                a, b = jnp.where(i < self.z, longer_a, a), jnp.where(i < self.z, longer_b, b)
            a_low, b_low = self.lower[h]
            a_mid, b_mid = half_dot(a_low, a), half_dot(a_low, b) + b_low.astype(WIDE)
            self.within.append(((a.astype(NARROW), b), (a_mid.astype(NARROW), b_mid)))

    def finish_forward(self, out):
        for copy in self.ring:
            copy.wait_recv()
        for h in range(2):
            state = self.row_b[0, h].astype(WIDE)
            state = jnp.where(self.y > 0, state, 0.0)
            for i in range(1, 3):
                longer = half_dot(self.row_a[i, h], state) + self.row_b[i, h].astype(WIDE)
                state = jnp.where(i < self.y, longer, state)
            (a, b), (a_mid, b_mid) = self.within[h]
            start, middle = half_dot(a, state) + b, half_dot(a_mid, state) + b_mid
            out[2 * self.c + h] = jnp.where(self.first, start, middle)
            self.pass_on[h] = jnp.where(self.first, middle, start)
        self.box.push(self.pass_on, out.at[self.mine], dp=self.sibling).wait_recv()

    def start_backward(self, g_ref, sib_g, chip_g, row_g, pass_on):
        self.g_ref, self.sib_g, self.chip_g, self.row_g, self.pass_on = g_ref, sib_g, chip_g, row_g, pass_on
        self.pair = [self.swap(g_ref, sib_g)]

    def turn(self, chip_t, row_t, pair_t):
        self.chip_t, self.row_t, self.pair_t = chip_t, row_t, pair_t

        def turned(value):
            return value.astype(WIDE).T.astype(NARROW)

        for h in range(2):
            for i in range(4):
                chip_t[i, h] = turned(self.chip_a[i, h])
                row_t[i, h] = turned(self.row_a[i, h])
            low, high = self.ordered(self.a_ref, self.sib_a, h)
            pair_t[0, h] = turned(low)
            pair_t[1, h] = turned(high)

    def chips_backward(self):
        for copy in self.pair:
            copy.wait_recv()
        self.upper_g = []
        for h in range(2):
            g_low, g_high = self.ordered(self.g_ref, self.sib_g, h)
            self.upper_g.append(g_high)
            self.chip_g[self.z, h] = (
                lax.dot(self.pair_t[0, h], g_high, preferred_element_type=WIDE) + g_low.astype(WIDE)
            ).astype(NARROW)
        self.ring = self.spread((self.chip_g,), self.z, self.z_peers)

    def rows_backward(self):
        for copy in self.ring:
            copy.wait_recv()
        for h in range(2):
            total = self.chip_g[3, h].astype(WIDE)
            for i in (2, 1, 0):
                total = half_dot(self.chip_t[i, h], total) + self.chip_g[i, h].astype(WIDE)
            self.row_g[self.y, h] = total.astype(NARROW)
        self.ring = self.spread((self.row_g,), self.y, self.y_peers)
        self.ready_backward()

    def ready_backward(self):
        eye = jnp.where(
            lax.broadcasted_iota(jnp.int32, (DH, DH), 0) == lax.broadcasted_iota(jnp.int32, (DH, DH), 1), 1.0, 0.0
        )
        self.within = []
        for h in range(2):
            a, b = eye, jnp.zeros((DH, DH), WIDE)
            for i in (3, 2, 1):
                step = self.chip_t[i, h]
                longer_a, longer_b = half_dot(step, a), half_dot(step, b) + self.chip_g[i, h].astype(WIDE)
                a, b = jnp.where(i > self.z, longer_a, a), jnp.where(i > self.z, longer_b, b)
            high = self.pair_t[1, h]
            a_mid, b_mid = half_dot(high, a), half_dot(high, b) + self.upper_g[h].astype(WIDE)
            self.within.append(((a.astype(NARROW), b), (a_mid.astype(NARROW), b_mid)))

    def finish_backward(self, out):
        for copy in self.ring:
            copy.wait_recv()
        for h in range(2):
            grad = self.row_g[3, h].astype(WIDE)
            grad = jnp.where(self.y < 3, grad, 0.0)
            for i in (2, 1):
                longer = half_dot(self.row_t[i, h], grad) + self.row_g[i, h].astype(WIDE)
                grad = jnp.where(i > self.y, longer, grad)
            (a, b), (a_mid, b_mid) = self.within[h]
            start, middle = half_dot(a, grad) + b, half_dot(a_mid, grad) + b_mid
            out[2 * self.c + h] = jnp.where(self.first, middle, start)
            self.pass_on[h] = jnp.where(self.first, start, middle)
        self.box.push(self.pass_on, out.at[self.mine], dp=self.sibling).wait_recv()


def columns(i, width):
    return pl.ds(pl.multiple_of(i * width, width), width)


class MpSum:
    ORDER = (2, 1, 3)

    def __init__(self, box, part, landed):
        self.box, self.part, self.landed = box, part, landed
        self.m = lax.axis_index("mp")
        self.peers = {k: lax.rem(self.m + k, 4) for k in (1, 2, 3)}
        self.copies = ([], [])
        self.half = part.shape[1] // 2

    def owner(self, k):
        return lax.rem(self.m + k, 4)

    def rows(self, half):
        return pl.ds(half * self.half, self.half)

    def send(self, k, half):
        rows = self.rows(half)
        self.copies[half].append(
            self.box.push(self.part.at[k, rows], self.landed.at[k - 1, rows], mp=self.peers[k])
        )

    def send_half(self, half):
        for k in self.ORDER:
            self.send(k, half)

    def total(self, half):
        for copy in self.copies[half]:
            copy.wait_recv()
        rows = self.rows(half)
        total = self.part[0, rows].astype(WIDE)
        for k in range(3):
            total = total + self.landed[k, rows].astype(WIDE)
        return total

    def share(self, out):
        width = self.part.shape[2]
        shared = []
        for half in range(2):
            rows = self.rows(half)
            out[rows, columns(self.m, width)] = self.total(half).astype(out.dtype)
            block = out.at[rows, columns(self.m, width)]
            shared += [self.box.push(block, block, mp=self.peers[k]) for k in self.ORDER]
        return shared


def unpack_ranks(block, spread, ranks, first, tiles):
    for q in range(4):
        for t in range(tiles):
            at = first + q * tiles + t
            spread[t, pl.ds(q, 32, stride=4), :] = block[at // 64, pl.ds(at % 64, 32, stride=64), :]
    for t in range(tiles):
        ranks[:, t * 128 : (t + 1) * 128] = spread[t, :128].astype(ranks.dtype)


def front_kernel(
    x_ref, g_own, seg_ref, adapters, norm_ref, gain_ref, bias_ref, taps_ref, w_qkv, block_one, a_in, b_res, late_ref,
    gate_up, down, block_two,
    wide_out, thin_out, late_out, last_out, pre_out, xn_out, kept_out, t_out, reach_out, ranks_out, aux_ref, picks_ref, u_ref,
     a_ref, sib_a, chip_a, row_a, state_out, mixer_out, normed, u_out_ref, branch, g_full,
    wide_ref, thin_ref, late_thin, last_ref, pre, xn_ref, kept, t_ref, reach, ranks, wide_all, thin_all, late_all, thin_own, late_own, halo_x, seg_ext, xn_ext, pre_wide, block, spread, b_beta,
    b_ref, out_zero, sib_b, chip_b, row_b, pass_on, part, landed, taps, send, recv, local, own_sems,
):
    count, model = x_ref.shape
    heads = a_ref.shape[0]
    inner = heads * DH
    m = lax.axis_index("mp")
    place = lax.axis_index("dp")
    before, after = lax.rem(place + 31, 32), lax.rem(place + 1, 32)
    mp_peers = {k: lax.rem(m + k, 4) for k in (1, 2, 3)}
    box = Mailbox(send, recv)
    chain = Chain(box, a_ref, sib_a, chip_a, row_a)
    parts = [(a_in.at[j], thin_ref.at[:, pl.ds(128 * j, 128)]) for j in range(4)]
    parts += [(a_in.at[4 + j], late_thin.at[:, pl.ds(128 * j, 128)]) for j in range(2)]
    parts += [(b_res.at[j], late_thin.at[:, pl.ds(256 + 128 * j, 128)]) for j in range(2)]
    parts += [(w_qkv.at[j], wide_ref.at[:, pl.ds(inner * j, inner)]) for j in range(3)]
    parts += [(block_one, wide_ref.at[:, pl.ds(3 * inner, 256)])]
    at = 0
    for source in (gate_up, down, block_two):
        parts.append((source, last_ref.at[:, pl.ds(at, source.shape[1])]))
        at += source.shape[1]
    parts = [pltpu.make_async_copy(*pair, own_sems.at[i]) for i, pair in enumerate(parts)]
    for copy in parts:
        copy.start()
    greet([before, after] + chain.peers(), list(mp_peers.values()))
    for copy in parts:
        copy.wait()
    me = moved(0, 0)
    seg_row = seg_ref[...].astype(WIDE)
    seg_ext[HALO:] = jnp.broadcast_to(seg_row, (128, count)).T
    edges = [
        box.push(x_ref.at[pl.ds(count - HALO, HALO)], halo_x, dp=after),
        box.push(seg_ext.at[pl.ds(count, HALO)], seg_ext.at[pl.ds(0, HALO)], dp=after),
    ]
    thin_rows = thin_ref.shape[0]
    mine = pl.ds(pl.multiple_of(m * thin_rows, thin_rows), thin_rows)
    crossing = [box.push(thin_ref, thin_own.at[mine], mp=peer) for peer in mp_peers.values()]
    late_cols = pl.ds(late_ref.shape[1], late_thin.shape[1])
    late_crossing = [box.push(late_thin, late_own.at[mine, late_cols], mp=peer) for peer in mp_peers.values()]
    keep = [
        pltpu.make_async_copy(wide_ref, wide_all.at[me], local.at[0]),
        pltpu.make_async_copy(thin_ref, thin_own.at[mine], local.at[1]),
        pltpu.make_async_copy(late_ref, late_own.at[:, pl.ds(0, late_ref.shape[1])], local.at[2]),
        pltpu.make_async_copy(late_thin, late_own.at[mine, late_cols], local.at[3]),
    ]
    for copy in keep:
        copy.start()
    wide_steps = gather_steps(box, wide_ref, wide_all)
    thin_steps = gather_steps(box, thin_own, thin_all)
    late_steps = gather_steps(box, late_own, late_all)
    last_steps = gather_steps(box, last_ref, last_out)
    wide_steps.pop(0)()
    share = g_own.shape[1]
    g_full[:, columns(m, share)] = g_own[...]
    keep[1].wait()
    for copy in crossing:
        copy.wait_recv()
    keep_thin = pltpu.make_async_copy(thin_own, thin_all.at[me], local.at[4])
    keep_thin.start()
    thin_steps.pop(0)()
    g_sent = [box.push(g_own, g_full.at[:, columns(m, share)], mp=mp_peers[k]) for k in MpSum.ORDER]

    def normal(rows):
        rows = rows.astype(WIDE)
        return (rows * inverse_rms(rows) * norm_ref[0:1, :]).astype(NARROW)

    xn_ref[...] = normal(x_ref[...])
    xn_ext[HALO:] = xn_ref[...]
    for i, (one, two) in enumerate(zip(wide_steps, thin_steps)):
        if i == 12:
            keep[2].wait()
            keep[3].wait()
            for copy in late_crossing:
                copy.wait_recv()
            keep_late = pltpu.make_async_copy(late_own, late_all.at[me], local.at[5])
            keep_late.start()
            late_steps[0]()
            keep_last = pltpu.make_async_copy(last_ref, last_out.at[me], local.at[13])
            keep_last.start()
            last_steps[0]()
        one()
        two()
    keep[0].wait()
    keep_thin.wait()
    rounds = [
        late_steps[1:3],
        late_steps[3:5],
        [],
        late_steps[5:9],
        late_steps[9:13],
        [],
        last_steps[1:2],
        last_steps[2:3],
        [],
        late_steps[13:17],
        late_steps[17:21],
        late_steps[21:22],
        [],
        [],
        [],
        last_steps[3:7],
        last_steps[7:13],
        last_steps[13:22],
    ]
    to_hbm = [
        pltpu.make_async_copy(wide_all, wide_out, local.at[6]),
        pltpu.make_async_copy(thin_all, thin_out, local.at[7]),
    ]
    for copy in to_hbm:
        copy.start()

    def tick():
        for step in rounds.pop(0):
            step()

    for copy in edges:
        copy.wait_recv()
    xn_ext[:HALO] = normal(halo_x[...])
    seg_ext[:HALO] = jnp.where(place == 0, -1.0, seg_ext[:HALO])
    spread_taps(taps_ref, taps)
    lanes = lax.broadcasted_iota(jnp.int32, seg_ext.shape, 1)
    seg_all = seg_ext[...]
    per_token = jnp.zeros(seg_all.shape, WIDE)
    for s in range(adapters.shape[0]):
        per_token = jnp.where(seg_all == float(s), adapters[s].astype(WIDE), per_token)
    picks_ext = jnp.where(per_token == (lanes // RANK).astype(WIDE), 1.0, 0.0)
    picks_ref[...] = picks_ext[HALO:]
    tiles = inner // 128
    for i in range(2):
        lane_block = slice(3 * inner + i * 128, 3 * inner + (i + 1) * 128)
        block[i, :model] = wide_all[:, :, lane_block].reshape(model, 128).astype(WIDE)
    for q in range(4):
        b_beta[pl.ds(q, 32, stride=4), :] = block[0, pl.ds(q, 32, stride=64), :]
    unpack_ranks(block.at[pl.ds(1, 1)], spread, ranks.at[:, pl.ds(0, 4 * inner)], 0, 4 * tiles)
    beta = pltpu.roll(b_beta[:128], 64, 1)
    beta_lane = lax.broadcasted_iota(jnp.int32, beta.shape, 1)
    beta = jnp.where((beta_lane >= 8) & (beta_lane < 8 + heads), beta, 0.0)
    ranks[:, 4 * inner :] = beta.astype(NARROW)
    tick()
    u_ext = dot(xn_ext[...], thin_all[...].reshape(model, thin_all.shape[2]))
    u_ext = (u_ext * jnp.concatenate([picks_ext] * 4, axis=1)).astype(NARROW)
    u_ref[...] = u_ext[HALO:]
    tick()
    for j in range(3):
        cols = slice(j * inner, (j + 1) * inner)
        value = dot(xn_ext[...], wide_all[:, :, cols].reshape(model, inner)) + dot(
            u_ext[:, j * 128 : (j + 1) * 128], ranks[:, cols]
        )
        value = value.astype(NARROW)
        pre[:, cols] = value
        pre_wide[:, cols] = value.astype(WIDE)
        tick()
    w_beta = wide_all[:, :, 3 * inner : 3 * inner + 128].reshape(model, 128)
    logits = dot(xn_ref[...], w_beta) + dot(u_ref[:, 384:], ranks[:, 4 * inner :])
    seg = seg_all[HALO:]
    lane = lanes[HALO:]
    for h in range(heads):
        logits = jnp.where(lane == 8 + h, logits + bias_ref[h], logits)
    aux = jnp.where((lane >= 8) & (lane < 8 + heads), jax.nn.sigmoid(logits), 0.0)
    for j in range(KW):
        aux = jnp.where((lane == j) & (seg_ext[pl.ds(HALO - j, count)] == seg), 1.0, aux)
    aux = jnp.where((lane == 4) & (seg == seg_ext[HALO - 1 : HALO]), 1.0, aux)
    aux = jnp.where((lane == 5) & (seg == seg_ext[HALO + count - 1 : HALO + count]), 1.0, aux)
    aux = jnp.where(lane == 6, seg, aux)
    aux_ref[...] = aux
    mixer_forward(
        list(range(heads)), pre_wide, taps, aux, seg_row, out_zero, reach, a_ref, b_ref,
        (*(kept.at[i] for i in range(3)), t_ref, *(kept.at[i] for i in (3, 4))), tick,
    )
    for i, (source, target) in enumerate(((pre, pre_out), (xn_ref, xn_out), (kept, kept_out), (t_ref, t_out), (reach, reach_out), (ranks, ranks_out))):
        to_hbm.append(pltpu.make_async_copy(source, target, local.at[9 + i if i < 4 else 10 + i]))
        to_hbm[-1].start()
    chain.start_forward(b_ref, sib_b, chip_b, row_b, pass_on)
    tick()
    chain.chips_forward()
    tick()
    chain.rows_forward()
    tick()
    chain.finish_forward(state_out)
    tick()
    keep_late.wait()
    keep_late_out = pltpu.make_async_copy(late_all, late_out, local.at[8])
    keep_late_out.start()
    for h in range(heads):
        cols = slice(h * DH, (h + 1) * DH)
        rows = out_zero[:, cols] + wide_dot(reach[:, cols], state_out[h])
        mixer_out[:, cols] = rows
        normed[:, cols] = (rows * inverse_rms(rows) * gain_ref[0:1, :]).astype(NARROW)
    u_out = (dot_nt(normed[...], ranks[:, 3 * inner : 4 * inner]) * picks_ref[...]).astype(NARROW)
    u_out_ref[...] = u_out
    one = MpSum(box, part, landed)
    for k in (2, 1, 3, 0):
        groups = pl.ds(one.owner(k) * (share // 64), share // 64)
        w_out = late_all[groups, :, :inner].reshape(share, inner)
        b_mix = late_all[groups, :, inner + 256 : inner + 384].reshape(share, 128)
        part[k] = (dot_nt(normed[...], w_out) + dot_nt(u_out, b_mix)).astype(NARROW)
        if k:
            one.send(k, 0)
    one.send_half(1)
    tick()
    shared = one.share(branch)
    tick()
    for copy in g_sent + shared:
        copy.wait_recv()
    for copy in to_hbm + [keep_late_out, keep_last]:
        copy.wait()
    box.drain()


def front(x, g, seg_row, adapters, norm, gain, bias, taps, *weights):
    w_qkv, block_one, a_in, _, late, gate_up, down, block_two = weights
    count, model = x.shape
    inner = taps.shape[2]
    heads = inner // DH
    share = model // 4
    vmem = pl.BlockSpec(memory_space=pltpu.VMEM)
    anywhere = pl.BlockSpec(memory_space=pl.ANY)
    smem = pl.BlockSpec(memory_space=pltpu.SMEM)
    two = (2, DH, DH)
    square = (heads, DH, DH)
    by_head = ((count, inner), WIDE)
    wide, last = (64, 3 * inner + 256), (64, gate_up.shape[1] + down.shape[1] + block_two.shape[1])
    thin_all, late_all = (32, 64, 512), (32, 64, late.shape[1] + 512)
    early = [
        ((HALO + count, 3 * inner), NARROW),
        ((count, model), NARROW),
        ((5, count, inner), WIDE),
        ((heads, count, count), WIDE),
        by_head,
        ((128, 4 * inner + 128), NARROW),
    ]
    results = [
        ((32,) + wide, NARROW),
        (thin_all, NARROW),
        (late_all, NARROW),
        ((32,) + last, NARROW),
        *early,
        ((count, 128), WIDE),
        ((count, 128), WIDE),
        ((count, 512), NARROW),
        (square, NARROW),
        (two, NARROW),
        ((4,) + two, NARROW),
        ((4,) + two, NARROW),
        (square, WIDE),
        by_head,
        ((count, inner), NARROW),
        ((count, 128), NARROW),
        ((count, model), NARROW),
        ((count, model), NARROW),
    ]
    scratch = [(wide, NARROW), ((16, 512), NARROW), ((16, 512), NARROW), (last, NARROW)] + early + [
        ((32,) + wide, NARROW),
        (thin_all, NARROW),
        (late_all, NARROW),
        (thin_all[1:], NARROW),
        (late_all[1:], NARROW),
        ((HALO, model), NARROW),
        ((HALO + count, 128), WIDE),
        ((HALO + count, model), NARROW),
        ((HALO + count, 3 * inner), WIDE),
        ((2, model + 64, 128), WIDE),
        ((4 * inner // 128, 136, 128), WIDE),
        ((136, 128), WIDE),
        (square, NARROW),
        by_head,
        (two, NARROW),
        ((4,) + two, NARROW),
        ((4,) + two, NARROW),
        (two, WIDE),
        ((4, count, share), NARROW),
        ((3, count, share), NARROW),
        ((16, inner), WIDE),
    ]
    copies = 4 * GATHER_COPIES + 2 + 3 + 3 + 3 + 2 + 6 + 6 + 1 + 12
    return pl.pallas_call(
        front_kernel,
        out_shape=tuple(jax.ShapeDtypeStruct(*r) for r in results),
        in_specs=[vmem] * 3 + [smem] + [vmem] * 2 + [smem, vmem] + [anywhere] * 8,
        out_specs=tuple([anywhere] * 10 + [vmem] * (len(results) - 10)),
        scratch_shapes=[pltpu.VMEM(*s) for s in scratch]
        + [
            pltpu.SemaphoreType.DMA((copies,)),
            pltpu.SemaphoreType.DMA((copies,)),
            pltpu.SemaphoreType.DMA((16,)),
            pltpu.SemaphoreType.DMA((15,)),
        ],
        compiler_params=pltpu.CompilerParams(
            collective_id=0, has_side_effects=True, vmem_limit_bytes=60 << 20
        ),
        name="front",
    )(x, g, seg_row, adapters, norm, gain, bias, taps, *weights)


def middle_kernel(
    a_ref, sib_a, chip_a, row_a, reach, mixer_out, normed, u_out_ref, branch, picks_ref, x_ref, g_full, norm_ref, gain_ref,
    ranks_one, late_ref, wide_ref,
    d_one_hbm, output, grad_out, d_mixer_out, g_b_ffn, g_a_down, g_a_out, g_shared,
    d_one_out, late, w_gu, w_down, packed, block, spread, ranks, sib_g, chip_g, row_g, pass_on, g_maps, chip_t, row_t, pair_t,
    part, landed, hidden_one, xn_two, gate, up, hidden, ffn_part, ffn_landed,
    d_gate_up, d_xn, extra, extra_landed, d_branch, e_down_ref, u_two_ref,
    send, recv, local,
):
    count = x_ref.shape[0]
    heads = a_ref.shape[0]
    inner = heads * DH
    ff = gate.shape[1]
    model = x_ref.shape[1]
    share = output.shape[1]
    m = lax.axis_index("mp")
    loads = [
        pltpu.make_async_copy(late_ref.at[:, pl.ds(inner, 512)], late.at[:, pl.ds(inner, 512)], local.at[0]),
        pltpu.make_async_copy(wide_ref.at[:, pl.ds(3 * ff, packed.shape[1])], packed, local.at[1]),
        pltpu.make_async_copy(wide_ref.at[:, pl.ds(0, ff)], w_gu.at[:, pl.ds(0, ff)], local.at[2]),
        pltpu.make_async_copy(wide_ref.at[:, pl.ds(ff, ff)], w_gu.at[:, pl.ds(ff, ff)], local.at[3]),
        pltpu.make_async_copy(wide_ref.at[:, pl.ds(2 * ff, ff)], w_down, local.at[4]),
        pltpu.make_async_copy(late_ref.at[:, pl.ds(0, inner)], late.at[:, pl.ds(0, inner)], local.at[5]),
    ]
    for load in loads:
        load.start()
    box = Mailbox(send, recv)
    chain = Chain(box, a_ref, sib_a, chip_a, row_a)
    mp_peers = {k: lax.rem(m + k, 4) for k in (1, 2, 3)}
    greet(chain.peers(), list(mp_peers.values()))
    picks = picks_ref[...]
    u_out = u_out_ref[...]
    a_out = ranks_one.at[:, pl.ds(3 * inner, inner)]
    a_down = ranks.at[:, pl.ds(2 * ff, ff)]
    w_out, a_two = late.at[:, pl.ds(0, inner)], late.at[:, pl.ds(inner, 256)]
    b_mix, b_down = late.at[:, pl.ds(inner + 256, 128)], late.at[:, pl.ds(inner + 384, 128)]

    rows = x_ref[...].astype(WIDE) + branch[...].astype(WIDE)
    hidden_one[...] = rows
    scale_two = inverse_rms(rows)
    xn_two[...] = (rows * scale_two * norm_ref[0:1, :]).astype(NARROW)
    two_picks = jnp.concatenate([picks, picks], axis=1)
    loads[0].wait()
    u_two_ref[...] = (dot(xn_two[...], a_two[...]) * two_picks).astype(NARROW)
    loads[1].wait()
    for i in range(3):
        block[i, :model] = packed[:, i * 128 : (i + 1) * 128].astype(WIDE)
    unpack_ranks(block, spread, ranks, 0, 3 * ff // 128)
    loads[2].wait()
    loads[3].wait()
    gate[...] = dot(xn_two[...], w_gu[:, :ff]) + dot(u_two_ref[:, :128], ranks[:, :ff])
    up[...] = dot(xn_two[...], w_gu[:, ff:]) + dot(u_two_ref[:, 128:], ranks[:, ff : 2 * ff])
    hidden[...] = (gate[...] * jax.nn.sigmoid(gate[...]) * up[...]).astype(NARROW)
    loads[4].wait()

    e_down = (dot(g_full[...], b_down[...]) * picks).astype(NARROW)
    e_down_ref[...] = e_down
    d_hidden = dot(g_full[...], w_down[...]) + dot(e_down, a_down[...])
    sig = jax.nn.sigmoid(gate[...])
    d_gate_up[:, :ff] = (d_hidden * up[...] * sig * (1.0 + gate[...] * (1.0 - sig))).astype(NARROW)
    d_gate_up[:, ff:] = (d_hidden * gate[...] * sig).astype(NARROW)
    e_two = [
        (dot_nt(d_gate_up[:, j * ff : (j + 1) * ff], ranks[:, j * ff : (j + 1) * ff]) * picks).astype(NARROW)
        for j in range(2)
    ]
    two = MpSum(box, part, landed)
    for k in (2, 1, 3, 0):
        rows = columns(two.owner(k), share)
        part[k] = (
            dot_nt(d_gate_up[...], w_gu[rows, :]) + dot_nt(jnp.concatenate(e_two, axis=1), a_two[rows, :])
        ).astype(NARROW)
        if k:
            two.send(k, 0)
    two.send_half(1)
    chain.turn(chip_t, row_t, pair_t)
    u_down = (dot_nt(hidden[...], a_down[...]) * picks).astype(NARROW)
    for j, value in enumerate((e_two[0], e_two[1], u_out, u_down)):
        extra[j] = value
    shared = two.share(d_xn)
    extra_sent = [box.push(extra.at[mp_peers[k]], extra_landed.at[k - 1], mp=mp_peers[k]) for k in MpSum.ORDER]
    three = MpSum(box, ffn_part, ffn_landed)
    for k in (2, 1, 3, 0):
        rows = columns(three.owner(k), share)
        ffn_part[k] = (dot_nt(hidden[...], w_down[rows, :]) + dot_nt(u_down, b_down[rows, :])).astype(NARROW)
    for copy in shared:
        copy.wait_recv()
    three.send_half(0)
    three.send_half(1)

    rows = hidden_one[...]
    scale_two = inverse_rms(rows)
    d_one = g_full[...].astype(WIDE) + norm_back(rows, scale_two, norm_ref[0:1, :], d_xn[...].astype(WIDE))
    d_one_out[...] = d_one
    leaving = pltpu.make_async_copy(d_one_out, d_one_hbm, local.at[6])
    leaving.start()
    loads[5].wait()
    d_branch[...] = d_one.astype(NARROW)
    e_out = (dot(d_branch[...], b_mix[...]) * picks).astype(NARROW)
    d_normed = dot(d_branch[...], w_out[...]) + dot(e_out, a_out[...])
    for h in range(heads):
        cols = slice(h * DH, (h + 1) * DH)
        rows = mixer_out[:, cols]
        d_rows = norm_back(rows, inverse_rms(rows), gain_ref[0:1, :], d_normed[:, cols])
        d_mixer_out[:, cols] = d_rows
        g_maps[h] = wide_dot(reach[:, cols], d_rows, 0, 0).astype(NARROW)
    chain.start_backward(g_maps, sib_g, chip_g, row_g, pass_on)
    g_a_out[...] = dot_tn(e_out, normed[...]).astype(NARROW)
    chain.chips_backward()
    for j in range(2):
        cols = slice(j * ff, (j + 1) * ff)
        g_b_ffn[:, cols] = dot_tn(u_two_ref[:, j * 128 : (j + 1) * 128], d_gate_up[:, cols]).astype(NARROW)
    chain.rows_backward()
    g_a_down[...] = dot_tn(e_down_ref[...], hidden[...]).astype(NARROW)
    for copy in extra_sent:
        copy.wait_recv()
    factor = extra[m].astype(WIDE)
    for k in range(3):
        factor = factor + extra_landed[k].astype(WIDE)
    left = jnp.where(m < 2, xn_two[...], jnp.where(m == 2, d_branch[...], g_full[...]))
    g_shared[...] = dot_tn(left, factor.astype(NARROW)).astype(NARROW)
    chain.finish_backward(grad_out)
    for half in range(2):
        rows = three.rows(half)
        output[rows] = (hidden_one[rows, columns(m, share)] + three.total(half)).astype(NARROW)
    leaving.wait()
    box.drain()


def middle(kept_maps, forward, x, g, norm, gain, ranks, late, wide):
    operands = (*kept_maps, *forward, x, g, norm, gain, ranks)
    count, inner = forward[0].shape
    heads = inner // DH
    model = x.shape[1]
    share = model // 4
    ff = (wide.shape[1] - 384) // 3
    vmem = pl.BlockSpec(memory_space=pltpu.VMEM)
    anywhere = pl.BlockSpec(memory_space=pl.ANY)
    two = (2, DH, DH)
    copies = 1 + 3 + 3 + 1 + 12 + 3 + 6
    results = [
        ((count, model), WIDE),
        ((count, share), NARROW),
        ((heads, DH, DH), WIDE),
        ((count, inner), WIDE),
        ((128, 2 * ff), NARROW),
        ((128, ff), NARROW),
        ((128, inner), NARROW),
        ((model, 128), NARROW),
    ]
    scratch = [
        ((count, model), WIDE),
        (late.shape, NARROW),
        ((model, 2 * ff), NARROW),
        ((model, ff), NARROW),
        ((model, 384), NARROW),
        ((3, model + 64, 128), WIDE),
        ((3 * ff // 128, 136, 128), WIDE),
        ((128, 3 * ff), NARROW),
        (two, NARROW),
        ((4,) + two, NARROW),
        ((4,) + two, NARROW),
        (two, WIDE),
        ((heads, DH, DH), NARROW),
        ((4,) + two, NARROW),
        ((4,) + two, NARROW),
        ((2,) + two, NARROW),
        ((4, count, share), NARROW),
        ((3, count, share), NARROW),
        ((count, model), WIDE),
        ((count, model), NARROW),
        ((count, ff), WIDE),
        ((count, ff), WIDE),
        ((count, ff), NARROW),
        ((4, count, share), NARROW),
        ((3, count, share), NARROW),
        ((count, 2 * ff), NARROW),
        ((count, model), NARROW),
        ((4, count, 128), NARROW),
        ((3, count, 128), NARROW),
        ((count, model), NARROW),
        ((count, 128), NARROW),
        ((count, 256), NARROW),
    ]
    return pl.pallas_call(
        middle_kernel,
        out_shape=tuple(jax.ShapeDtypeStruct(*r) for r in results),
        in_specs=[vmem] * len(operands) + [anywhere] * 2,
        out_specs=tuple([anywhere] + [vmem] * (len(results) - 1)),
        scratch_shapes=[pltpu.VMEM(*v) for v in scratch]
        + [
            pltpu.SemaphoreType.DMA((copies,)),
            pltpu.SemaphoreType.DMA((copies,)),
            pltpu.SemaphoreType.DMA((7,)),
        ],
        compiler_params=pltpu.CompilerParams(
            collective_id=2, has_side_effects=True, vmem_limit_bytes=60 << 20
        ),
        name="middle",
    )(*operands, late, wide)


class DpSum:
    SCRATCH = 6

    @staticmethod
    def scratch(rows, width):
        small = rows // 4
        return [
            ((2, 4, rows, width), NARROW),
            ((4, rows, width), NARROW),
            ((3, rows, width), NARROW),
            ((4, small, width), WIDE),
            ((3, small, width), WIDE),
            ((small, width), WIDE),
        ]

    def __init__(self, box, full, landed_core, landed_y, by_z, landed_z, result):
        self.box, self.full, self.landed_core = box, full, landed_core
        self.landed_y, self.by_z, self.landed_z, self.result = landed_y, by_z, landed_z, result
        self.y, self.z, self.c = coords()

    def over_cores(self):
        self.pair = self.box.push(self.full.at[1 - self.c], self.landed_core, dp=moved(0, 0, True))

    def over_y(self):
        self.pair.wait_recv()
        mine = self.full.at[self.c]
        for i in range(4):
            mine[i] = (mine[i].astype(WIDE) + self.landed_core[i].astype(WIDE)).astype(NARROW)
        self.copies = [
            self.box.push(mine.at[lax.rem(self.y + k, 4)], self.landed_y.at[k - 1], dp=moved(k, 0)) for k in (2, 1, 3)
        ]

    def over_z(self):
        for copy in self.copies:
            copy.wait_recv()
        total = self.full[self.c, self.y].astype(WIDE)
        for k in range(3):
            total = total + self.landed_y[k].astype(WIDE)
        self.by_z[...] = total.reshape(self.by_z.shape)
        self.copies = [
            self.box.push(self.by_z.at[lax.rem(self.z + k, 4)], self.landed_z.at[k - 1], dp=moved(0, k))
            for k in (2, 1, 3)
        ]

    def finish(self):
        for copy in self.copies:
            copy.wait_recv()
        total = self.by_z[self.z]
        for k in range(3):
            total = total + self.landed_z[k]
        self.result[...] = total


def tail_kernel(
    taps_ref, aux_ref, seg_ref, state_ref, grad_ref, d_out_ref,
    u_ref, norm_ref, picks_ref, ranks, shared_two, g_b_ffn, g_a_out, g_a_down,
    pre_in, kept_in, t_in, x_in, xn_in, d_one_in, wide_ref, thin_ref,
    grad_input, out_a_in, out_heads, out_beta, out_a_out, out_ffn, out_a_down, out_res,
    pre_ref, kept_all, t_ref, x_ref, xn_ref, d_one_ref, w_in, a_one, d_ext, pre_wide, taps, halo, d_pre, e_one, part, landed, extra_landed, sums, sums_landed, pair, early_pair, ends,
    *rest,
):
    one, two, three, four = (rest[i * DpSum.SCRATCH : (i + 1) * DpSum.SCRATCH] for i in range(4))
    send, recv, local = rest[4 * DpSum.SCRATCH :]
    count, model = x_in.shape
    inner = d_out_ref.shape[1]
    heads = inner // DH
    ff = g_a_down.shape[1]
    m = lax.axis_index("mp")
    c = lax.rem(lax.axis_index("dp"), 2)
    before, after = (lax.rem(lax.axis_index("dp") + k, 32) for k in (31, 1))
    mp_peers = {k: lax.rem(m + k, 4) for k in (1, 2, 3)}
    dp_peers = [before, after, moved(0, 0, True)]
    dp_peers += [moved(k, 0) for k in (1, 2, 3)] + [moved(0, k) for k in (1, 2, 3)]
    loads = [
        pltpu.make_async_copy(source, target, local.at[i])
        for i, (source, target) in enumerate(
            (
                (pre_in, pre_ref),
                (kept_in, kept_all),
                (t_in, t_ref),
                (wide_ref.at[:, pl.ds(0, w_in.shape[1])], w_in),
                (thin_ref.at[:, pl.ds(0, a_one.shape[1])], a_one),
                (x_in, x_ref),
                (xn_in, xn_ref),
                (d_one_in, d_one_ref),
            )
        )
    ]
    for load in loads:
        load.start()
    greet(dp_peers, list(mp_peers.values()))
    box = Mailbox(send, recv)
    early_sum, heads_sum, two_sum, one_sum = (DpSum(box, *refs) for refs in (four, one, two, three))

    def halves(refs, values):
        half = refs[0].shape[3]
        missing = 2 * half - sum(value.shape[1] for value in values)
        values = values + [jnp.zeros((128, missing), NARROW)] if missing else values
        values = jnp.concatenate(values, axis=1)
        for i in range(2):
            refs[0][i] = values[:, i * half : (i + 1) * half].reshape(4, 32, half)

    def by_core(value):
        value = value.reshape(4, 4, 2, model // 32, 128)
        return [value[:, :, i].reshape(4, model // 8, 128) for i in range(2)]

    halves(four, [g_b_ffn[...], g_a_out[...], g_a_down[...]])
    early_sum.over_cores()
    for i, value in enumerate(by_core(shared_two[...])):
        two[0][i] = value
    two_sum.over_cores()
    aux = aux_ref[...]
    spread_taps(taps_ref, taps)
    for load in loads[:3]:
        load.wait()
    pre_wide[...] = pre_ref[...].astype(WIDE)
    kept = (*(kept_all.at[i] for i in range(3)), t_ref, *(kept_all.at[i] for i in (3, 4)))
    lanes = lax.broadcasted_iota(jnp.int32, aux.shape, 1)
    d_logit = jnp.zeros(aux.shape, WIDE)
    def between():
        early_sum.over_y()
        two_sum.over_y()

    found = mixer_backward(
        list(range(heads)), pre_wide, taps, aux, seg_ref[...].astype(WIDE), kept, state_ref, grad_ref, d_out_ref, d_ext,
        between,
    )
    for h, value in enumerate(found):
        d_logit = jnp.where(lanes == 8 + h, value, d_logit)
    edges = [box.push(d_ext.at[i, pl.ds(HALO - 8, 8)], halo.at[i], dp=before) for i in range(3)]
    early_sum.over_z()
    two_sum.over_z()
    picks = picks_ref[...]
    d_logit = d_logit.astype(NARROW)
    for copy in edges:
        copy.wait_recv()
    for i in range(3):
        ref = d_ext.at[i]
        cols = slice(i * inner, (i + 1) * inner)
        d_pre[: count - 16, cols] = ref[HALO : HALO + count - 16].astype(NARROW)
        ending = ref[HALO + count - 16 :]
        d_pre[count - 16 :, cols] = jnp.concatenate([ending[:8], ending[8:] + halo[i]], axis=0).astype(NARROW)
    for j in range(3):
        cols = slice(j * inner, (j + 1) * inner)
        e_one[j] = (dot_nt(d_pre[:, cols], ranks[:, cols]) * picks).astype(NARROW)
    e_one[3] = (dot_nt(d_logit, ranks[:, 4 * inner :]) * picks).astype(NARROW)
    extra_sent = [box.push(e_one.at[mp_peers[k]], extra_landed.at[k - 1], mp=mp_peers[k]) for k in MpSum.ORDER]
    grads = [dot_tn(u_ref[:, j * 128 : (j + 1) * 128], d_pre[:, j * inner : (j + 1) * inner]) for j in range(3)]
    grads.append(dot_tn(u_ref[:, 384:], d_logit))
    halves(one, [value.astype(NARROW) for value in grads])
    heads_sum.over_cores()
    for load in loads[3:]:
        load.wait()
    share = grad_input.shape[1]
    total = MpSum(box, part, landed)
    row_sum = jnp.zeros((count, 128), WIDE)
    all_e = jnp.concatenate([e_one[j] for j in range(4)], axis=1)
    for k in (2, 1, 3, 0):
        owner = total.owner(k)
        rows = columns(owner, share)
        value = (
            dot_nt(d_pre[...], w_in[rows, : 3 * inner])
            + dot_nt(d_logit, w_in[rows, 3 * inner :])
            + dot_nt(all_e, a_one[rows, :])
        )
        part[k] = value.astype(NARROW)
        if k:
            total.send(k, 0)
            total.send(k, 1)
        weighted = value * norm_ref[0:1, rows] * x_ref[:, rows].astype(WIDE)
        row_sum = row_sum + jnp.sum(weighted, axis=1, keepdims=True)
    sums[...] = row_sum.T[:8]
    sums_sent = [box.push(sums, sums_landed.at[k - 1], mp=mp_peers[k]) for k in MpSum.ORDER]
    heads_sum.over_y()
    early_sum.finish()
    early_pair[c] = four[5][...]
    early_paired = box.push(four[5], early_pair.at[c], dp=moved(0, 0, True))
    for copy in extra_sent:
        copy.wait_recv()
    factor = e_one[m].astype(WIDE)
    for k in range(3):
        factor = factor + extra_landed[k].astype(WIDE)
    for i, value in enumerate(by_core(dot_tn(xn_ref[...], factor.astype(NARROW)).astype(NARROW))):
        three[0][i] = value
    one_sum.over_cores()
    heads_sum.over_z()
    one_sum.over_y()
    rank_rows = model // 128

    def to_owners(slot, result):
        ends[slot, m] = result[columns(m, rank_rows)]
        return [
            box.push(result.at[columns(mp_peers[k], rank_rows)], ends.at[slot, m], mp=mp_peers[k])
            for k in MpSum.ORDER
        ]

    two_sum.finish()
    owners = to_owners(1, two[5])
    heads_sum.finish()
    pair[c] = one[5][...]
    paired = box.push(one[5], pair.at[c], dp=moved(0, 0, True))
    one_sum.over_z()
    x_all = x_ref[...].astype(WIDE)
    scale = inverse_rms(x_all)
    mine = columns(m, share)
    one_sum.finish()
    owners += to_owners(0, three[5])
    for copy in sums_sent:
        copy.wait_recv()
    rows = sums[...] + sums_landed[0] + sums_landed[1] + sums_landed[2]
    mean = jnp.concatenate([rows] * 16, axis=0).T[:, :1] / model
    scale_three = scale * scale * scale * mean
    for half in range(2):
        at = total.rows(half)
        here = slice(half * (count // 2), (half + 1) * (count // 2))
        grad_input[at] = d_one_ref[at, mine] + (
            scale[here] * norm_ref[0:1, mine] * total.total(half) - x_ref[at, mine].astype(WIDE) * scale_three[here]
        )
    paired.wait_recv()
    early_paired.wait_recv()

    def own_ranks(pair):
        both = jnp.concatenate([pair[0], pair[1]], axis=1)
        return jnp.where(c == 0, both[:4], both[4:])

    rows = own_ranks(pair)
    for j in range(3):
        out_heads[j] = rows[:, j * inner : (j + 1) * inner]
    out_beta[...] = rows[:, 3 * inner + 8 : 3 * inner + 8 + heads]
    rows = own_ranks(early_pair)
    for j in range(2):
        out_ffn[j] = rows[:, j * ff : (j + 1) * ff]
    out_a_out[...] = rows[:, 2 * ff : 2 * ff + inner]
    out_a_down[...] = rows[:, 2 * ff + inner : 3 * ff + inner]
    for copy in owners:
        copy.wait_recv()
    for j in range(4):
        out_a_in[j] = ends[0, j]
    for j in range(2):
        out_a_in[4 + j] = ends[1, j]
        out_res[j] = ends[1, 2 + j]
    box.drain()


def tail(mixer, tokens, grads, kept, wide, thin):
    model = kept[3].shape[1]
    count, inner = mixer[-1].shape
    heads = inner // DH
    share = model // 4
    ff = grads[3].shape[1]

    def half_of(width):
        return -(-width // 256) * 128

    half, early_half = half_of(3 * inner + 128), half_of(3 * ff + inner)
    vmem = pl.BlockSpec(memory_space=pltpu.VMEM)
    anywhere = pl.BlockSpec(memory_space=pl.ANY)
    copies = 3 + 3 + 6 + 3 + 4 * 7 + 2 + 6
    results = [
        (count, share), (6, model // 128, 128), (3, 4, inner), (4, heads),
        (4, inner), (2, 4, ff), (4, ff), (2, model // 128, 128),
    ]
    scratch = [(x.shape, x.dtype) for x in kept] + [
        ((model, 3 * inner + 128), NARROW),
        ((model, 512), NARROW),
        ((3, HALO + count, inner), WIDE),
        ((HALO + count, 3 * inner), WIDE),
        ((16, inner), WIDE),
        ((3, 8, inner), WIDE),
        ((count, 3 * inner), NARROW),
        ((4, count, 128), NARROW),
        ((4, count, share), NARROW),
        ((3, count, share), NARROW),
        ((3, count, 128), NARROW),
        ((8, count), WIDE),
        ((3, 8, count), WIDE),
        ((2, 8, half), WIDE),
        ((2, 8, early_half), WIDE),
        ((2, 4, model // 128, 128), WIDE),
    ]
    scratch += DpSum.scratch(32, half) + DpSum.scratch(model // 8, 128) + DpSum.scratch(model // 8, 128)
    scratch += DpSum.scratch(32, early_half)
    operands = (*mixer, *tokens, *grads)
    return pl.pallas_call(
        tail_kernel,
        out_shape=tuple(jax.ShapeDtypeStruct(r, WIDE) for r in results),
        in_specs=[vmem] * len(operands) + [anywhere] * (len(kept) + 2),
        out_specs=tuple([vmem] * len(results)),
        scratch_shapes=[pltpu.VMEM(*s) for s in scratch]
        + [
            pltpu.SemaphoreType.DMA((copies,)),
            pltpu.SemaphoreType.DMA((copies,)),
            pltpu.SemaphoreType.DMA((8,)),
        ],
        compiler_params=pltpu.CompilerParams(
            collective_id=3, has_side_effects=True, vmem_limit_bytes=60 << 20
        ),
        name="tail",
    )(*operands, *kept, wide, thin)


def hand_over_kernel(*refs):
    half = len(refs) // 2
    for source, target in zip(refs[:half], refs[half:]):
        target[...] = source[...]


def hand_over(*arrays):
    vmem = pl.BlockSpec(memory_space=pltpu.VMEM)
    return pl.pallas_call(
        hand_over_kernel,
        out_shape=tuple(jax.ShapeDtypeStruct(x.shape, x.dtype) for x in arrays),
        in_specs=[vmem] * len(arrays),
        out_specs=tuple([vmem] * len(arrays)),
        name="hand_over",
    )(*arrays)


def on_device(
    layer_in, cotangent, segments, adapters, norm_one, norm_two, out_gain, beta_bias, conv_taps,
    w_qkv, w_beta, w_out, w_gate_up, w_down, a_in, b_heads, b_beta, a_out, b_ffn, a_down, b_res,
):
    heads = w_beta.shape[1]
    inner = heads * DH
    ff = w_down.shape[0]

    def pack_ranks(parts, blocks):
        flat = jnp.concatenate(parts, axis=1).reshape(-1, 128)
        flat = jnp.pad(flat, ((0, 64 * blocks - flat.shape[0]), (0, 0)))
        return flat.reshape(blocks, 64, 128).transpose(1, 0, 2).reshape(64, blocks * 128)

    beta = jnp.concatenate([w_beta, jnp.zeros((64, 64 - heads), NARROW), jnp.pad(b_beta, ((0, 60), (0, 0)))], axis=1)
    block_one = jnp.concatenate(
        [
            jnp.pad(beta, ((0, 0), (8, 56 - heads))),
            pack_ranks([b_heads.transpose(1, 0, 2).reshape(4, 3 * inner), a_out.T], 1),
        ],
        axis=1,
    )
    block_two = pack_ranks([b_ffn.transpose(1, 0, 2).reshape(4, 2 * ff), a_down.T], 3)
    conv_taps = conv_taps.transpose(1, 0, 2)
    seg_row = segments[None, :]
    (
        wide, thin, late, last, pre, xn_one, kept, t_map, reach, ranks, aux, picks, u_one,
        maps, sib_a, chip_a, row_a, state_in, mixer_out, normed, u_out, branch, g_full,
    ) = front(
        layer_in, cotangent, seg_row, adapters, norm_one[None, :], out_gain[None, :],
        beta_bias, conv_taps, w_qkv.transpose(1, 0, 2), block_one, a_in.transpose(1, 0, 2), b_res.transpose(0, 2, 1),
        w_out.T, w_gate_up.reshape(64, 2 * ff), w_down.T, block_two,
    )
    wide, thin, late, last = (x.reshape(2048, -1) for x in (wide, thin, late, last))
    d_hidden_one, output, state_grad, d_mixer, grad_b_ffn, grad_a_down, grad_a_out, shared_two = middle(
        (maps, sib_a, chip_a, row_a), (reach, mixer_out, normed, u_out, branch, picks),
        layer_in, g_full, norm_two[None, :], out_gain[None, :], ranks, late, last,
    )
    grad_input, d_a_in, d_b_heads, d_b_beta, d_a_out, d_b_ffn, d_a_down, d_b_res = tail(
        (conv_taps, aux, seg_row, state_in, state_grad, d_mixer),
        (u_one, norm_one[None, :], picks, ranks),
        (shared_two, grad_b_ffn, grad_a_out, grad_a_down),
        (pre, kept, t_map, layer_in, xn_one, d_hidden_one),
        wide,
        thin,
    )
    output, grad_input, d_a_in, d_b_heads, d_b_beta, d_a_out, d_b_ffn, d_a_down, d_b_res = hand_over(
        output, grad_input, d_a_in, d_b_heads, d_b_beta, d_a_out, d_b_ffn, d_a_down, d_b_res
    )
    return (
        output, grad_input, d_a_in.transpose(1, 0, 2), d_b_heads, d_b_beta, d_a_out.T, d_b_ffn, d_a_down.T,
        d_b_res.transpose(0, 2, 1),
    )


def solution(mesh):
    placed = (
        P("dp", None),
        P("dp", "mp"),
        P("dp"),
        P(),
        P(),
        P(),
        P(),
        P("mp"),
        P(None, None, "mp"),
        P("dp", None, "mp"),
        P("dp", "mp"),
        P("mp", "dp"),
        P("dp", None, "mp"),
        P("mp", "dp"),
        P(("dp", "mp"), None, None),
        P(None, "dp", "mp"),
        P("dp", "mp"),
        P("mp", "dp"),
        P(None, "dp", "mp"),
        P("mp", "dp"),
        P(None, None, ("dp", "mp")),
    )
    return jax.shard_map(
        on_device,
        mesh=mesh,
        in_specs=placed,
        out_specs=(
            P("dp", "mp"),
            P("dp", "mp"),
            P(("dp", "mp"), None, None),
            P(None, "dp", "mp"),
            P("dp", "mp"),
            P("mp", "dp"),
            P(None, "dp", "mp"),
            P("mp", "dp"),
            P(None, None, ("dp", "mp")),
        ),
        check_vma=False,
    )
```
